128 devices in a mesh: hid: 16 (over z, y), ffn: 8 (over x, core).
Axes of the slice: x: 4, y: 4, z: 4, core: 2. Of those that a mesh axis runs over, the one named last changes fastest.
Arguments:
- tokens: bfloat16 [128, 2, 16384], P('ffn', None, 'hid'), may hold values from -6 to 6
- norm_gain: bfloat16 [16384], P('hid'), may hold values from 0.099609375 to 1.8984375
- query_weight: bfloat16 [16384, 8192], P('hid', 'ffn'), may hold values from -0.046875 to 0.046875
- w_keyval: bfloat16 [16384, 1024], P('hid', 'ffn'), may hold values from -0.046875 to 0.046875
- w_out: bfloat16 [8192, 16384], P('ffn', 'hid'), may hold values from -0.25 to 0.25
- cache_keys: bfloat16 [128, 8192, 512], P(('hid', 'ffn')), may hold values from -1024 to 1024
- cache_values: bfloat16 [128, 8192, 512], P(('hid', 'ffn')), may hold values from -6 to 6
- lengths: int32 [128], replicated, may hold values from 2048 to 8192, as said below
Outputs:
- layer_out: bfloat16 [128, 2, 16384], P('ffn', None, 'hid')
- new_entries: bfloat16 [128, 2, 1024], P(('hid', 'ffn'))
The draws below stay inside these ranges and needn't reach their ends.
Inputs may be any that keep to these rules, and one draw needn't show every extreme that they name: `lengths`: every prompt has from a quarter of 8192 to 8192 cached entries, and some prompt has exactly 8192.
All inputs are finite; a program needn't handle non-finite values.
Results may differ from the reference program's by a relative error of at most 0.02.
The reference program's roundings to bfloat16 on the way (of `normed`, `queries` and `attended`) count: a program that leaves them out, or rounds other values in their place, can miss the bound.
Values may be sent and summed in bfloat16 or wider, within the bound.
A program may use at most 128 MiB of HBM per device.

```python
import jax
import jax.numpy as jnp
from jax import lax

D = 16384
HEADS = 64
KV_HEADS = 4
HD = 128
LMAX = 8192
STEPS = 2
PROMPTS = 128


def draw_lengths(key, part):
    key = jax.random.fold_in(key, 5)
    shortest = LMAX // 4
    values = jax.random.randint(key, (PROMPTS,), shortest, LMAX + 1)
    shuffled = jax.random.permutation(jax.random.fold_in(key, 1), PROMPTS)
    values = values.at[shuffled[0]].set(LMAX)
    values = values.at[shuffled[1]].set(shortest)
    return values.astype(jnp.int32)


def draw_cache_keys(key, part):
    key = jax.random.fold_in(key, 11)
    standard = jnp.clip(jax.random.normal(key, (PROMPTS, LMAX, KV_HEADS * HD), jnp.float32), -6.0, 6.0)
    return (standard * 1.5).astype(jnp.bfloat16)


def block_levels(rng, dims, split, least, high):
    level = 1.0
    for dim, shards_of in split:
        draws = jax.random.uniform(jax.random.fold_in(jax.random.fold_in(rng, 6), dim), (shards_of,), jnp.float32, least / len(split), high / len(split))
        level = level * jnp.repeat(jnp.exp(draws), dims[dim] // shards_of).reshape((-1,) + (1,) * (len(dims) - 1 - dim))
    return level


def bell_draw(stream_key, shape, scale, limit, pieces=(), held_as=jnp.bfloat16):
    values = jax.random.normal(stream_key, shape, jnp.float32) * scale
    if len(pieces) > 0:
        values = block_levels(stream_key, shape, pieces, -0.22, 0.18) * values
    return jnp.clip(values, min=-limit, max=limit).astype(held_as)


def setup_inputs(seed: int = 0) -> dict:
    key_list = jax.random.split(jax.random.key(seed), 9)
    return {
        "tokens": bell_draw(key_list[0], (PROMPTS, STEPS, D), 1.0, 6.0, ((0, 8), (2, 16))),
        "norm_gain": jnp.clip(1.0 + 0.18 * jax.random.normal(key_list[1], (D,), jnp.float32), 0.099609375, 1.8984375).astype(jnp.bfloat16),
        "query_weight": bell_draw(key_list[2], (D, HEADS * HD), D ** -0.5, 0.046875, ((0, 16), (1, 8))),
        "w_keyval": bell_draw(key_list[3], (D, 2 * KV_HEADS * HD), D ** -0.5, 0.046875, ((0, 16), (1, 8))),
        "w_out": bell_draw(key_list[4], (HEADS * HD, D), (HEADS * HD // 16) ** -0.5, 0.25, ((0, 8), (1, 16))),
        "cache_keys": draw_cache_keys(jax.random.fold_in(key_list[8], 71), 0),
        "cache_values": bell_draw(key_list[6], (PROMPTS, LMAX, KV_HEADS * HD), 1.0, 6.0, ((0, 128),)),
        "lengths": draw_lengths(jax.random.fold_in(key_list[8], 71), 0),
    }


epsilon = 1e-05
rope_base = 500000.0

def rotate(vectors, positions):
    halfway = vectors.shape[-1] // 2
    exponent = jnp.arange(halfway, dtype=jnp.float32) * (2.0 / vectors.shape[-1])
    angles = positions[..., None] * rope_base ** (-exponent)
    cosine = jnp.cos(angles)
    sine_part = jnp.sin(angles)
    first_half = vectors[..., :halfway]
    second = vectors[..., halfway:]
    return jnp.concatenate([first_half * cosine - second * sine_part, second * cosine + first_half * sine_part], axis=-1)

def rounded(values):
    return lax.optimization_barrier(values.astype(jnp.bfloat16)).astype(jnp.float32)

def attend_prompt(prompt_items):
    queries, keys_new, values_new, cache_k, cache_v, length = prompt_items
    group_size = HEADS // KV_HEADS
    grouped_query_rows = queries.astype(jnp.float32).reshape(STEPS, KV_HEADS, group_size, HD)
    stored_keys = cache_k.astype(jnp.float32).reshape(LMAX, KV_HEADS, HD)
    stored_values = cache_v.astype(jnp.float32).reshape(LMAX, KV_HEADS, HD)
    factor = HD ** (-0.5)
    past_scores = jnp.einsum('sgjd,lgd->sgjl', grouped_query_rows, stored_keys) * factor
    live_mask = jnp.arange(LMAX, dtype=jnp.int32) < length
    past_scores = jnp.where(live_mask[None, None, None, :], past_scores, -jnp.inf)
    fresh_scores = jnp.einsum('sgjd,tgd->sgjt', grouped_query_rows, keys_new.astype(jnp.float32)) * factor
    causal = jnp.arange(STEPS)[:, None] >= jnp.arange(STEPS)[None, :]
    fresh_scores = jnp.where(causal[:, None, None, :], fresh_scores, -jnp.inf)
    highest = jnp.maximum(lax.optimization_barrier(jnp.max(past_scores, axis=-1)), lax.optimization_barrier(jnp.max(fresh_scores, axis=-1)))
    past_weights = rounded(jnp.exp(past_scores - highest[..., None]))
    current_step_weights = rounded(jnp.exp(fresh_scores - highest[..., None]))
    weight_sum = lax.optimization_barrier(jnp.sum(past_weights, axis=-1)) + lax.optimization_barrier(jnp.sum(current_step_weights, axis=-1))
    weighted = jnp.einsum('sgjl,lgd->sgjd', past_weights, stored_values)
    weighted = weighted + jnp.einsum('sgjt,tgd->sgjd', current_step_weights, values_new.astype(jnp.float32))
    return (weighted / weight_sum[..., None]).astype(jnp.bfloat16).reshape(STEPS, HEADS * HD)

def reference(tokens, norm_gain, query_weight, w_keyval, w_out, cache_keys, cache_values, lengths):
    widened = tokens.astype(jnp.float32)
    mean_square = lax.optimization_barrier(jnp.mean(widened * widened, axis=-1, keepdims=True))
    normed = (widened * lax.rsqrt(mean_square + epsilon) * norm_gain.astype(jnp.float32)).astype(jnp.bfloat16)
    flat_rows = normed.reshape(PROMPTS * STEPS, D)
    query_raw = jnp.dot(flat_rows, query_weight, preferred_element_type=jnp.float32).astype(jnp.bfloat16)
    key_value_unprojected = jnp.dot(flat_rows, w_keyval, preferred_element_type=jnp.float32).astype(jnp.bfloat16)
    query_raw = query_raw.reshape(PROMPTS, STEPS, HEADS, HD)
    key_value_unprojected = key_value_unprojected.reshape(PROMPTS, STEPS, 2 * KV_HEADS, HD)
    positions = (lengths[:, None] + jnp.arange(STEPS, dtype=jnp.int32)[None, :]).astype(jnp.float32)[..., None]
    queries = rotate(query_raw.astype(jnp.float32), positions).astype(jnp.bfloat16)
    appended_key_rows = rotate(key_value_unprojected[:, :, :KV_HEADS].astype(jnp.float32), positions).astype(jnp.bfloat16)
    appended_value_rows = key_value_unprojected[:, :, KV_HEADS:]
    new_entries = jnp.concatenate([appended_key_rows, appended_value_rows], axis=2).reshape(PROMPTS, STEPS, 2 * KV_HEADS * HD)
    attended = lax.map(attend_prompt, (queries, appended_key_rows, appended_value_rows, cache_keys, cache_values, lengths))
    layer_out = jnp.dot(attended.reshape(PROMPTS * STEPS, HEADS * HD), w_out, preferred_element_type=jnp.float32)
    layer_out = layer_out.astype(jnp.bfloat16).reshape(PROMPTS, STEPS, D)
    return (layer_out, new_entries)
```

```python
import functools

import jax
import jax.numpy as jnp
import numpy as np
from jax import lax
from jax.experimental import pallas as pl
from jax.experimental.pallas import tpu as pltpu
from jax.sharding import PartitionSpec as P

MESH = pl.DeviceIdType.MESH
F32 = jnp.float32
BF16 = jnp.bfloat16

HEADS = 64
KV_HEADS = 4
HD = 128
STEPS = 2
EPSILON = 1e-05
ROPE_BASE = 500000.0
SCALE = HD ** (-0.5) * 1.4426950408889634
MASKED = -1e30

NH = 16
NF = 8
NX = 4
OWN = 32
PR = 16
CHUNK = 1024
CACHE_COPIES = 4


def remote(src, dst, send_sem, recv_sem, device):
    return pltpu.make_async_remote_copy(
        src_ref=src,
        dst_ref=dst,
        send_sem=send_sem,
        recv_sem=recv_sem,
        device_id=device,
        device_id_type=MESH,
    )


def rotate(vectors, cosine, sine):
    return vectors * cosine + pltpu.roll(vectors, HD // 2, 1) * sine


def kernel(
    lengths, freq, tokens, gain, wq, wkv, wout, cache_k, cache_v,
    out, entries,
    tok_v, freq_v, gain_v, wq_v, wkv_v, wout_v, k_v, v_v,
    x_all, normed, ss_own, ss_recv, tot_all, part, part_recv,
    spread, msg, qkv, kx, vx, ne, scores, att_send, att_recv, att_f32, rows_all,
    opart, sib_recv, fin_send, fin_recv, fin_own, ent_v,
    local_sem, k_sem, v_sem,
    tok_ssem, tok_rsem, fwd_ssem, fwd_rsem, ss_ssem, ss_rsem, tot_ssem, tot_rsem,
    part_ssem, part_rsem, msg_ssem, msg_rsem, att_ssem, att_rsem, rows_ssem, rows_rsem,
    sib_ssem, sib_rsem, fin_ssem, fin_rsem,
):
    h = lax.axis_index("hid")
    f = lax.axis_index("ffn")
    cx = lax.div(f, 2)
    core = lax.rem(f, 2)
    sib = f + 1 - 2 * core
    lmax = cache_k.shape[1]

    barrier = pltpu.get_barrier_semaphore()

    def greet_hid(k, carry):
        pl.semaphore_signal(
            barrier, inc=1, device_id=(lax.rem(h + k, NH), f), device_id_type=MESH
        )
        return carry

    def greet_ffn(k, carry):
        pl.semaphore_signal(
            barrier, inc=1, device_id=(h, lax.rem(f + k, NF)), device_id_type=MESH
        )
        return carry

    lax.fori_loop(1, NH, greet_hid, 0)
    lax.fori_loop(1, NF, greet_ffn, 0)

    loads = []
    for i, (src, dst) in enumerate(
        [(tokens, tok_v), (gain, gain_v), (freq, freq_v), (wq, wq_v), (wkv, wkv_v)]
    ):
        copy = pltpu.make_async_copy(src, dst, local_sem.at[i])
        copy.start()
        loads.append(copy)
    span = lmax // CACHE_COPIES
    k_loads, v_loads = [], []
    for i in range(CACHE_COPIES):
        copy = pltpu.make_async_copy(
            cache_k.at[0, pl.ds(i * span, span)], k_v.at[pl.ds(i * span, span)], k_sem.at[i]
        )
        copy.start()
        k_loads.append(copy)
    for i in range(CACHE_COPIES):
        copy = pltpu.make_async_copy(
            cache_v.at[0, pl.ds(i * span, span)], v_v.at[pl.ds(i * span, span)], v_sem.at[i]
        )
        copy.start()
        v_loads.append(copy)
    wout_load = pltpu.make_async_copy(wout, wout_v, local_sem.at[5])
    wout_load.start()

    loads[0].wait()
    x_own = tok_v[...]
    x_f32 = x_own.astype(F32)
    sums = jnp.sum(x_f32 * x_f32, axis=1, keepdims=True)
    row_id = lax.broadcasted_iota(jnp.int32, (OWN, HD), 0)
    lane_id = lax.broadcasted_iota(jnp.int32, (OWN, HD), 1)
    diagonal = row_id == lane_id
    own_sums = jnp.sum(jnp.where(diagonal, sums, 0.0), axis=0, keepdims=True)
    ss_own[...] = jnp.broadcast_to(own_sums, (8, HD))

    pl.semaphore_wait(barrier, NH + NF - 2)

    def block(index):
        return x_all.at[pl.ds(pl.multiple_of(index * OWN, OWN), OWN)]

    tok_copies = []
    for k in range(1, NX):
        peer = 2 * lax.rem(cx + k, NX) + core
        copy = remote(tok_v, block(f), tok_ssem.at[k - 1], tok_rsem.at[k - 1], (h, peer))
        copy.start()
        tok_copies.append(copy)

    def ss_copy(k):
        return remote(
            ss_own, ss_recv.at[k - 1], ss_ssem.at[k - 1], ss_rsem.at[k - 1],
            (lax.rem(h + k, NH), f),
        )

    def ss_start(k, carry):
        ss_copy(k).start()
        return carry

    lax.fori_loop(1, NH, ss_start, 0)
    fwd_copies = [remote(tok_v, block(f), fwd_ssem.at[0], fwd_rsem.at[0], (h, sib))]
    fwd_copies[0].start()
    x_all[pl.ds(pl.multiple_of(f * OWN, OWN), OWN), :] = x_own

    def ss_add(k, total):
        ss_copy(k).wait()
        return total + ss_recv[k - 1]

    total = lax.fori_loop(1, NH, ss_add, ss_own[...])
    tot_all[f] = total
    tot_copies = []
    for k in range(1, NF):
        copy = remote(
            tot_all.at[f], tot_all.at[f], tot_ssem.at[k - 1], tot_rsem.at[k - 1],
            (h, lax.rem(f + k, NF)),
        )
        copy.start()
        tot_copies.append(copy)
    for k in range(1, NX):
        tok_copies[k - 1].wait_recv()
        came = 2 * lax.rem(cx + NX - k, NX) + core
        copy = remote(block(came), block(came), fwd_ssem.at[k], fwd_rsem.at[k], (h, sib))
        copy.start()
        fwd_copies.append(copy)

    length = lengths[h * NF + f]
    step_of = lax.div(lax.broadcasted_iota(jnp.int32, (PR, HD), 0), 8)
    loads[2].wait()
    angles = (step_of + length).astype(F32) * freq_v[...]
    cosine = jnp.cos(angles)
    sine = jnp.sin(angles)
    sine = jnp.where(
        lax.broadcasted_iota(jnp.int32, (PR, HD), 1) < HD // 2, -sine, sine
    )

    for copy in tot_copies:
        copy.wait()
    for copy in fwd_copies:
        copy.wait()
    for copy in tok_copies:
        copy.wait_send()
    loads[1].wait()
    width = x_all.shape[1]
    full = width * NH
    gain_row = gain_v[0:1, :].astype(F32)

    def normalise(b, carry):
        rows = pl.ds(pl.multiple_of(b * OWN, OWN), OWN)
        lane_sums = tot_all[b][0:1, :]
        row_sums = jnp.sum(jnp.where(diagonal, lane_sums, 0.0), axis=1, keepdims=True)
        inverse = lax.rsqrt(row_sums / full + EPSILON)
        normed[rows, :] = (x_all[rows, :].astype(F32) * inverse * gain_row).astype(BF16)
        return carry

    lax.fori_loop(0, NF, normalise, 0)

    loads[3].wait()
    loads[4].wait()
    lhs = normed[...]
    qcols = wq_v.shape[1]
    part[:, :qcols] = jnp.dot(lhs, wq_v[...], preferred_element_type=F32)
    part[:, qcols:] = jnp.dot(lhs, wkv_v[...], preferred_element_type=F32)

    def part_rows(index):
        return pl.ds(pl.multiple_of(index * PR, PR), PR)

    def part_copy(k):
        peer = lax.rem(h + k, NH)
        return remote(
            part.at[part_rows(peer)], part_recv.at[k - 1],
            part_ssem.at[k - 1], part_rsem.at[k - 1], (peer, f),
        )

    def part_start(k, carry):
        part_copy(k).start()
        return carry

    lax.fori_loop(1, NH, part_start, 0)

    def part_wait(k, carry):
        part_copy(k).wait()
        return carry

    lax.fori_loop(1, NH, part_wait, 0)
    summed = part[part_rows(h), :]
    for k in range(NH - 1):
        summed = summed + part_recv[k]

    for j in range(8):
        spread[pl.ds(j, PR, stride=8), :] = summed[:, j * HD : (j + 1) * HD]
    msg[:, :PR, :] = spread[...].reshape(NF, PR, HD).astype(BF16)
    spread[...] = jnp.zeros_like(spread)
    spread[pl.ds(0, PR, stride=8), :] = summed[:, qcols:]
    msg[:, PR:, :] = spread[...].reshape(NF, PR, HD).astype(BF16)
    qkv[f] = msg[f]
    msg_copies = []
    for k in range(1, NF):
        peer = lax.rem(f + k, NF)
        copy = remote(
            msg.at[peer], qkv.at[f], msg_ssem.at[k - 1], msg_rsem.at[k - 1], (h, peer)
        )
        copy.start()
        msg_copies.append(copy)
    for copy in msg_copies:
        copy.wait()

    kx[...] = jnp.zeros_like(kx)
    vx[...] = jnp.zeros_like(vx)
    for i in range(2 * KV_HEADS):
        raw = qkv[i, PR:, :].astype(F32)
        cols = pl.ds((i % KV_HEADS) * HD, HD)
        if i < KV_HEADS:
            raw = rotate(raw, cosine, sine)
            kx[:PR, cols] = raw.astype(BF16)
        else:
            vx[:PR, cols] = raw.astype(BF16)
        ne[0:1, i * HD : (i + 1) * HD] = raw[0:1]
        ne[1:2, i * HD : (i + 1) * HD] = raw[8:9]
    ent_v[...] = ne[0:2, :].astype(BF16)
    ent_copy = pltpu.make_async_copy(ent_v, entries, local_sem.at[6])
    ent_copy.start()

    queries = []
    for g in range(KV_HEADS):
        pair = [
            rotate(qkv[2 * g + i, :PR, :].astype(F32), cosine, sine).astype(BF16)
            for i in range(2)
        ]
        queries.append(jnp.concatenate(pair, axis=0))
    row32 = lax.broadcasted_iota(jnp.int32, (OWN, HD), 0)
    step_row = lax.rem(lax.div(row32, 8), 2)
    fresh_live = (lane_id == 0) | ((lane_id == 8) & (step_row == 1))
    nt = (((1,), (1,)), ((), ()))
    highs, fresh = [], []
    for g in range(KV_HEADS):
        s = lax.dot_general(
            queries[g], kx[:, g * HD : (g + 1) * HD], nt, preferred_element_type=F32
        )
        s = jnp.where(fresh_live, s * SCALE, MASKED)
        fresh.append(s)
        highs.append(s)

    for copy in k_loads:
        copy.wait()

    def score_step(c, carried):
        rows = pl.ds(pl.multiple_of(c * CHUNK, CHUNK), CHUNK)
        position = lax.broadcasted_iota(jnp.int32, (8, CHUNK), 1) + c * CHUNK
        cap = jnp.where(position < length, -MASKED, MASKED)
        cap = jnp.concatenate([cap] * (OWN // 8), axis=0)
        result = []
        for g in range(KV_HEADS):
            s = lax.dot_general(
                queries[g], k_v[rows, g * HD : (g + 1) * HD], nt, preferred_element_type=F32
            )
            s = jnp.minimum(s * SCALE, cap)
            scores[g * OWN : (g + 1) * OWN, rows] = s
            high = carried[g]
            for t in range(CHUNK // HD):
                high = jnp.maximum(high, s[:, t * HD : (t + 1) * HD])
            result.append(high)
        return tuple(result)

    highs = lax.fori_loop(0, lmax // CHUNK, score_step, tuple(highs))
    peaks = [
        jnp.broadcast_to(jnp.max(high, axis=1, keepdims=True), (OWN, HD)) for high in highs
    ]

    for copy in v_loads:
        copy.wait()
    state = []
    for g in range(KV_HEADS):
        weights = jnp.exp2(fresh[g] - peaks[g]).astype(BF16)
        state.append(weights.astype(F32))
        state.append(
            jnp.dot(weights, vx[:, g * HD : (g + 1) * HD], preferred_element_type=F32)
        )

    def value_step(c, carried):
        rows = pl.ds(pl.multiple_of(c * CHUNK, CHUNK), CHUNK)
        result = []
        for g in range(KV_HEADS):
            s = scores[g * OWN : (g + 1) * OWN, rows]
            total, acc = carried[2 * g], carried[2 * g + 1]
            pieces = []
            for t in range(CHUNK // HD):
                piece = jnp.exp2(s[:, t * HD : (t + 1) * HD] - peaks[g]).astype(BF16)
                total = total + piece.astype(F32)
                pieces.append(piece)
            weights = jnp.concatenate(pieces, axis=1)
            acc = acc + jnp.dot(
                weights, v_v[rows, g * HD : (g + 1) * HD], preferred_element_type=F32
            )
            result += [total, acc]
        return tuple(result)

    state = lax.fori_loop(0, lmax // CHUNK, value_step, tuple(state))
    for g in range(KV_HEADS):
        weight_sum = jnp.sum(state[2 * g], axis=1, keepdims=True)
        attended = (state[2 * g + 1] / weight_sum).astype(BF16)
        att_send[2 * g] = attended[:PR]
        att_send[2 * g + 1] = attended[PR:]

    att_recv[f] = att_send[f]
    att_copies = []
    for k in range(1, NF):
        peer = lax.rem(f + k, NF)
        copy = remote(
            att_send.at[peer], att_recv.at[f], att_ssem.at[k - 1], att_rsem.at[k - 1], (h, peer)
        )
        copy.start()
        att_copies.append(copy)
    for copy in att_copies:
        copy.wait()
    att_f32[...] = att_recv[...].astype(F32).reshape(NF * PR, HD)
    for j in range(8):
        rows_all[part_rows(h), j * HD : (j + 1) * HD] = att_f32[pl.ds(j, PR, stride=8), :].astype(
            BF16
        )

    def rows_copy(k):
        mine = rows_all.at[part_rows(h)]
        return remote(
            mine, mine, rows_ssem.at[k - 1], rows_rsem.at[k - 1], (lax.rem(h + k, NH), f)
        )

    def rows_start(k, carry):
        rows_copy(k).start()
        return carry

    def rows_wait(k, carry):
        rows_copy(k).wait()
        return carry

    lax.fori_loop(1, NH, rows_start, 0)
    wout_load.wait()
    lax.fori_loop(1, NH, rows_wait, 0)

    opart[...] = jnp.dot(rows_all[...], wout_v[...], preferred_element_type=F32)

    def out_rows(index):
        return pl.ds(pl.multiple_of(index * OWN, OWN), OWN)

    sib_copies = []
    for x in range(NX):
        copy = remote(
            opart.at[out_rows(2 * x + 1 - core)], sib_recv.at[x],
            sib_ssem.at[x], sib_rsem.at[x], (h, sib),
        )
        copy.start()
        sib_copies.append(copy)
    for copy in sib_copies:
        copy.wait()
    fin_copies = []
    for k in range(1, NX):
        x = lax.rem(cx + k, NX)
        fin_send[k - 1] = (opart[out_rows(2 * x + core), :] + sib_recv[x]).astype(BF16)
        copy = remote(
            fin_send.at[k - 1], fin_recv.at[k - 1],
            fin_ssem.at[k - 1], fin_rsem.at[k - 1], (h, 2 * x + core),
        )
        copy.start()
        fin_copies.append(copy)
    result = opart[out_rows(f), :] + sib_recv[cx]
    for k in range(1, NX):
        fin_copies[k - 1].wait()
        result = result + fin_recv[k - 1].astype(F32)
    fin_own[...] = result.astype(BF16)
    out_copy = pltpu.make_async_copy(fin_own, out, local_sem.at[7])
    out_copy.start()
    ent_copy.wait()
    out_copy.wait()


def body(tokens, norm_gain, query_weight, w_keyval, w_out, cache_keys, cache_values, lengths):
    width = tokens.shape[2]
    lmax = cache_keys.shape[1]
    qcols = query_weight.shape[1]
    kvcols = w_keyval.shape[1]
    halves = np.arange(HD // 2, dtype=np.float64) * (2.0 / HD)
    freq = (ROPE_BASE ** (-halves)).astype(np.float32)
    freq = jnp.asarray(np.tile(np.concatenate([freq, freq])[None, :], (PR, 1)))
    any_spec = pl.BlockSpec(memory_space=pl.ANY)
    dma = pltpu.SemaphoreType.DMA
    rows = NH * PR
    out, entries = pl.pallas_call(
        kernel,
        out_shape=(
            jax.ShapeDtypeStruct((OWN, width), BF16),
            jax.ShapeDtypeStruct((STEPS, 2 * KV_HEADS * HD), BF16),
        ),
        in_specs=[pl.BlockSpec(memory_space=pltpu.SMEM)] + [any_spec] * 8,
        out_specs=(any_spec, any_spec),
        scratch_shapes=[
            pltpu.VMEM((OWN, width), BF16),
            pltpu.VMEM((PR, HD), F32),
            pltpu.VMEM((1, width), BF16),
            pltpu.VMEM((width, qcols), BF16),
            pltpu.VMEM((width, kvcols), BF16),
            pltpu.VMEM((qcols, width), BF16),
            pltpu.VMEM((lmax, KV_HEADS * HD), BF16),
            pltpu.VMEM((lmax, KV_HEADS * HD), BF16),
            pltpu.VMEM((rows, width), BF16),
            pltpu.VMEM((rows, width), BF16),
            pltpu.VMEM((8, HD), F32),
            pltpu.VMEM((NH - 1, 8, HD), F32),
            pltpu.VMEM((NF, 8, HD), F32),
            pltpu.VMEM((rows, qcols + kvcols), F32),
            pltpu.VMEM((NH - 1, PR, qcols + kvcols), F32),
            pltpu.VMEM((NF * PR, HD), F32),
            pltpu.VMEM((NF, 2 * PR, HD), BF16),
            pltpu.VMEM((NF, 2 * PR, HD), BF16),
            pltpu.VMEM((HD, KV_HEADS * HD), BF16),
            pltpu.VMEM((HD, KV_HEADS * HD), BF16),
            pltpu.VMEM((8, 2 * KV_HEADS * HD), F32),
            pltpu.VMEM((KV_HEADS * OWN, lmax), F32),
            pltpu.VMEM((NF, PR, HD), BF16),
            pltpu.VMEM((NF, PR, HD), BF16),
            pltpu.VMEM((NF * PR, HD), F32),
            pltpu.VMEM((rows, qcols), BF16),
            pltpu.VMEM((rows, width), F32),
            pltpu.VMEM((NX, OWN, width), F32),
            pltpu.VMEM((NX - 1, OWN, width), BF16),
            pltpu.VMEM((NX - 1, OWN, width), BF16),
            pltpu.VMEM((OWN, width), BF16),
            pltpu.VMEM((STEPS, 2 * KV_HEADS * HD), BF16),
            dma((8,)),
            dma((CACHE_COPIES,)),
            dma((CACHE_COPIES,)),
            dma((NX - 1,)), dma((NX - 1,)),
            dma((NX,)), dma((NX,)),
            dma((NH - 1,)), dma((NH - 1,)),
            dma((NF - 1,)), dma((NF - 1,)),
            dma((NH - 1,)), dma((NH - 1,)),
            dma((NF - 1,)), dma((NF - 1,)),
            dma((NF - 1,)), dma((NF - 1,)),
            dma((NH - 1,)), dma((NH - 1,)),
            dma((NX,)), dma((NX,)),
            dma((NX - 1,)), dma((NX - 1,)),
        ],
        compiler_params=pltpu.CompilerParams(
            collective_id=0, has_side_effects=True, vmem_limit_bytes=56 * 2**20
        ),
        name="decode_block",
    )(
        lengths,
        freq,
        tokens.reshape(OWN, width),
        norm_gain.reshape(1, width),
        query_weight,
        w_keyval,
        w_out,
        cache_keys,
        cache_values,
    )
    return out.reshape(tokens.shape), entries.reshape(1, STEPS, 2 * KV_HEADS * HD)


def solution(mesh):
    in_specs = (
        P("ffn", None, "hid"),
        P("hid"),
        P("hid", "ffn"),
        P("hid", "ffn"),
        P("ffn", "hid"),
        P(("hid", "ffn"), None, None),
        P(("hid", "ffn"), None, None),
        P(),
    )
    out_specs = (P("ffn", None, "hid"), P(("hid", "ffn"), None, None))
    return jax.shard_map(body, mesh=mesh, in_specs=in_specs, out_specs=out_specs, check_vma=False)
```

```python
import functools

import jax
import jax.numpy as jnp
import numpy as np
from jax import lax
from jax.experimental import pallas as pl
from jax.experimental.pallas import tpu as pltpu
from jax.sharding import PartitionSpec as P

MESH = pl.DeviceIdType.MESH
F32 = jnp.float32
BF16 = jnp.bfloat16

HEADS = 64
KV_HEADS = 4
HD = 128
STEPS = 2
EPSILON = 1e-05
ROPE_BASE = 500000.0
SCALE = HD ** (-0.5) * 1.4426950408889634
MASKED = -1e30

NH = 16
NF = 8
NX = 4
NY = 4
LOW = 512
OWN = 32
PR = 16
CHUNK = 1024
CACHE_COPIES = 4


def remote(src, dst, send_sem, recv_sem, device):
    return pltpu.make_async_remote_copy(
        src_ref=src,
        dst_ref=dst,
        send_sem=send_sem,
        recv_sem=recv_sem,
        device_id=device,
        device_id_type=MESH,
    )


def rotate(vectors, cosine, sine):
    return vectors * cosine + pltpu.roll(vectors, HD // 2, 1) * sine


def kernel(
    lengths_hbm, freq, tokens, gain, wq, wkv, wout, cache_k, cache_v,
    out, entries,
    lengths, raw_v, tok_v, freq_v, gain_v, wq_v, wkv_v, wout_v, k_v, v_v,
    x_all, normed, ss_own, ss_recv, tot_all, part, relay_low, relay_high, left_low, left_high,
    right_low, right_high, mine, mine_recv,
    spread, msg, qkv, kx, vx, ne, scores, att_send, att_recv, att_f32, rows_all,
    opart, sib_recv, fin_send, fin_recv,
    local_sem, k_sem, v_sem,
    tok_ssem, tok_rsem, fwd_ssem, fwd_rsem, ss_ssem, ss_rsem, tot_ssem, tot_rsem,
    ring_ssem, ring_rsem, stage_ssem, stage_rsem, msg_ssem, msg_rsem, att_ssem, att_rsem, near_ssem, near_rsem, line_ssem, line_rsem,
    sib_ssem, sib_rsem, fin_ssem, fin_rsem,
):
    h = lax.axis_index("hid")
    f = lax.axis_index("ffn")
    z = lax.div(h, NY)
    y = lax.rem(h, NY)
    cx = lax.div(f, 2)
    core = lax.rem(f, 2)
    sib = f + 1 - 2 * core
    lmax = cache_k.shape[1]

    barrier = pltpu.get_barrier_semaphore()

    def greet_hid(k, carry):
        pl.semaphore_signal(
            barrier, inc=1, device_id=(lax.rem(h + k, NH), f), device_id_type=MESH
        )
        return carry

    def greet_ffn(k, carry):
        pl.semaphore_signal(
            barrier, inc=1, device_id=(h, lax.rem(f + k, NF)), device_id_type=MESH
        )
        return carry

    lax.fori_loop(1, NH, greet_hid, 0)
    lax.fori_loop(1, NF, greet_ffn, 0)

    loads = []
    for i, (src, dst) in enumerate(
        [(tokens, raw_v), (gain, gain_v), (freq, freq_v), (wq, wq_v), (wkv, wkv_v), (lengths_hbm, lengths)]
    ):
        copy = pltpu.make_async_copy(src, dst, local_sem.at[i])
        copy.start()
        loads.append(copy)
    span = lmax // CACHE_COPIES
    k_loads, v_loads = [], []
    for i in range(CACHE_COPIES):
        copy = pltpu.make_async_copy(
            cache_k.at[0, pl.ds(i * span, span)], k_v.at[pl.ds(i * span, span)], k_sem.at[i]
        )
        copy.start()
        k_loads.append(copy)
    for i in range(CACHE_COPIES):
        copy = pltpu.make_async_copy(
            cache_v.at[0, pl.ds(i * span, span)], v_v.at[pl.ds(i * span, span)], v_sem.at[i]
        )
        copy.start()
        v_loads.append(copy)
    wout_load = pltpu.make_async_copy(wout, wout_v, local_sem.at[6])
    wout_load.start()

    loads[0].wait()
    x_f32 = raw_v[...].astype(F32).reshape(tok_v.shape)
    x_own = x_f32.astype(BF16)
    tok_v[...] = x_own
    sums = jnp.sum(x_f32 * x_f32, axis=1, keepdims=True)
    row_id = lax.broadcasted_iota(jnp.int32, (OWN, HD), 0)
    lane_id = lax.broadcasted_iota(jnp.int32, (OWN, HD), 1)
    diagonal = row_id == lane_id
    own_sums = jnp.sum(jnp.where(diagonal, sums, 0.0), axis=0, keepdims=True)
    ss_own[...] = jnp.broadcast_to(own_sums, (8, HD))

    pl.semaphore_wait(barrier, NH + NF - 2)

    def block(index):
        return x_all.at[pl.ds(pl.multiple_of(index * OWN, OWN), OWN)]

    tok_copies = []
    for k in range(1, NX):
        peer = 2 * lax.rem(cx + k, NX) + core
        copy = remote(tok_v, block(f), tok_ssem.at[k - 1], tok_rsem.at[k - 1], (h, peer))
        copy.start()
        tok_copies.append(copy)

    def ss_copy(k):
        return remote(
            ss_own, ss_recv.at[k - 1], ss_ssem.at[k - 1], ss_rsem.at[k - 1],
            (lax.rem(h + k, NH), f),
        )

    def ss_start(k, carry):
        ss_copy(k).start()
        return carry

    lax.fori_loop(1, NH, ss_start, 0)
    fwd_copies = [remote(tok_v, block(f), fwd_ssem.at[0], fwd_rsem.at[0], (h, sib))]
    fwd_copies[0].start()
    x_all[pl.ds(pl.multiple_of(f * OWN, OWN), OWN), :] = x_own

    def ss_add(k, total):
        ss_copy(k).wait()
        return total + ss_recv[k - 1]

    total = lax.fori_loop(1, NH, ss_add, ss_own[...])
    tot_all[f] = total
    tot_copies = []
    for k in range(1, NF):
        copy = remote(
            tot_all.at[f], tot_all.at[f], tot_ssem.at[k - 1], tot_rsem.at[k - 1],
            (h, lax.rem(f + k, NF)),
        )
        copy.start()
        tot_copies.append(copy)
    for k in range(1, NX):
        tok_copies[k - 1].wait_recv()
        came = 2 * lax.rem(cx + NX - k, NX) + core
        copy = remote(block(came), block(came), fwd_ssem.at[k], fwd_rsem.at[k], (h, sib))
        copy.start()
        fwd_copies.append(copy)

    loads[5].wait()
    length = lengths[h * NF + f]
    step_of = lax.div(lax.broadcasted_iota(jnp.int32, (PR, HD), 0), 8)
    loads[2].wait()
    angles = (step_of + length).astype(F32) * freq_v[...]
    cosine = jnp.cos(angles)
    sine = jnp.sin(angles)
    sine = jnp.where(
        lax.broadcasted_iota(jnp.int32, (PR, HD), 1) < HD // 2, -sine, sine
    )

    for copy in tot_copies:
        copy.wait()
    for copy in fwd_copies:
        copy.wait()
    for copy in tok_copies:
        copy.wait_send()
    loads[1].wait()
    width = x_all.shape[1]
    full = width * NH
    gain_row = gain_v[...].astype(F32).reshape(1, width)

    def normalise(b, carry):
        rows = pl.ds(pl.multiple_of(b * OWN, OWN), OWN)
        lane_sums = tot_all[b][0:1, :]
        row_sums = jnp.sum(jnp.where(diagonal, lane_sums, 0.0), axis=1, keepdims=True)
        inverse = lax.rsqrt(row_sums / full + EPSILON)
        normed[rows, :] = (x_all[rows, :].astype(F32) * inverse * gain_row).astype(BF16)
        return carry

    lax.fori_loop(0, NF, normalise, 0)

    loads[3].wait()
    loads[4].wait()
    lhs = normed[...]
    qcols = wq_v.shape[1]
    for cols, weights in ((slice(0, qcols), wq_v), (slice(qcols, None), wkv_v)):
        product = jnp.dot(lhs, weights[...], preferred_element_type=F32)
        part[:, :, :, cols] = product.reshape(NY, NY, PR, product.shape[1])

    half = PR // 2
    low, high_cols = pl.ds(0, LOW), pl.ds(LOW, part.shape[3] - LOW)

    def ring(side):
        pos = (y, z)[side]

        def device(q):
            return (z * NY + q, f) if side == 0 else (q * NY + y, f)

        def view(q, cols):
            if side == 0:
                return part.at[:, q, pl.ds(0, half), cols]
            return part.at[q, :, pl.ds(half, half), cols]

        return pos, device, view

    after = {}
    for side in range(2):
        pos, device, view = ring(side)
        nxt, prv, far = lax.rem(pos + 1, NY), lax.rem(pos + 3, NY), lax.rem(pos + 2, NY)
        plan = [
            (view(far, low), relay_low, nxt),
            (view(far, high_cols), relay_high, prv),
            (view(nxt, high_cols), left_high, nxt),
            (view(prv, low), right_low, prv),
        ]
        copies = [
            remote(
                src, dst.at[side], ring_ssem.at[side, i], ring_rsem.at[side, i], device(to)
            )
            for i, (src, dst, to) in enumerate(plan)
        ]
        for copy in copies:
            copy.start()
        after[side] = copies
    for side in range(2):
        pos, device, view = ring(side)
        nxt, prv = lax.rem(pos + 1, NY), lax.rem(pos + 3, NY)
        plan = [
            (view(nxt, low), relay_low, left_low, nxt),
            (view(prv, high_cols), relay_high, right_high, prv),
        ]
        for i, (own, relay, dst, to) in enumerate(plan):
            after[side][i].wait_recv()
            relay[side] = relay[side] + own[...]
            copy = remote(
                relay.at[side], dst.at[side],
                ring_ssem.at[side, 4 + i], ring_rsem.at[side, 4 + i], device(to),
            )
            copy.start()
            after[side].append(copy)
    stage_copies = {}
    for side in range(2):
        pos, device, view = ring(side)
        for copy in after[side][2:]:
            copy.wait_recv()
        mine[side, :, :, :LOW] = view(pos, low)[...] + left_low[side] + right_low[side]
        mine[side, :, :, LOW:] = view(pos, high_cols)[...] + left_high[side] + right_high[side]
        other, other_device, _ = ring(1 - side)
        stage_copies[side] = []
        for k in range(1, NY):
            peer = lax.rem(other + k, NY)
            copy = remote(
                mine.at[side, peer], mine_recv.at[side, k - 1],
                stage_ssem.at[side, k - 1], stage_rsem.at[side, k - 1], other_device(peer),
            )
            copy.start()
            stage_copies[side].append(copy)
    halves = []
    for side in range(2):
        other = ring(1 - side)[0]
        total = mine[side, other]
        for k in range(1, NY):
            stage_copies[side][k - 1].wait()
            total = total + mine_recv[side, k - 1]
        halves.append(total)
        for copy in after[side]:
            copy.wait_send()
    summed = jnp.concatenate(halves, axis=0)

    for j in range(8):
        spread[pl.ds(j, PR, stride=8), :] = summed[:, j * HD : (j + 1) * HD]
    msg[:, :PR, :] = spread[...].reshape(NF, PR, HD).astype(BF16)
    spread[...] = jnp.zeros_like(spread)
    spread[pl.ds(0, PR, stride=8), :] = summed[:, qcols:]
    msg[:, PR:, :] = spread[...].reshape(NF, PR, HD).astype(BF16)
    qkv[f] = msg[f]
    msg_copies = []
    for k in range(1, NF):
        peer = lax.rem(f + k, NF)
        copy = remote(
            msg.at[peer], qkv.at[f], msg_ssem.at[k - 1], msg_rsem.at[k - 1], (h, peer)
        )
        copy.start()
        msg_copies.append(copy)
    for copy in msg_copies:
        copy.wait()

    kx[...] = jnp.zeros_like(kx)
    vx[...] = jnp.zeros_like(vx)
    for i in range(2 * KV_HEADS):
        raw = qkv[i, PR:, :].astype(F32)
        cols = pl.ds((i % KV_HEADS) * HD, HD)
        if i < KV_HEADS:
            raw = rotate(raw, cosine, sine)
            kx[:PR, cols] = raw.astype(BF16)
        else:
            vx[:PR, cols] = raw.astype(BF16)
        ne[0:1, i * HD : (i + 1) * HD] = raw[0:1]
        ne[1:2, i * HD : (i + 1) * HD] = raw[8:9]
    entries[...] = ne[0:2, :].reshape(entries.shape).astype(BF16)

    queries = []
    for g in range(KV_HEADS):
        pair = [
            rotate(qkv[2 * g + i, :PR, :].astype(F32), cosine, sine).astype(BF16)
            for i in range(2)
        ]
        queries.append(jnp.concatenate(pair, axis=0))
    row32 = lax.broadcasted_iota(jnp.int32, (OWN, HD), 0)
    step_row = lax.rem(lax.div(row32, 8), 2)
    fresh_live = (lane_id == 0) | ((lane_id == 8) & (step_row == 1))
    nt = (((1,), (1,)), ((), ()))
    highs, fresh = [], []
    for g in range(KV_HEADS):
        s = lax.dot_general(
            queries[g], kx[:, g * HD : (g + 1) * HD], nt, preferred_element_type=F32
        )
        s = jnp.where(fresh_live, s * SCALE, MASKED)
        fresh.append(s)
        highs.append(s)

    for copy in k_loads:
        copy.wait()

    def score_step(c, carried):
        rows = pl.ds(pl.multiple_of(c * CHUNK, CHUNK), CHUNK)
        position = lax.broadcasted_iota(jnp.int32, (8, CHUNK), 1) + c * CHUNK
        cap = jnp.where(position < length, -MASKED, MASKED)
        cap = jnp.concatenate([cap] * (OWN // 8), axis=0)
        result = []
        for g in range(KV_HEADS):
            s = lax.dot_general(
                queries[g], k_v[rows, g * HD : (g + 1) * HD], nt, preferred_element_type=F32
            )
            s = jnp.minimum(s * SCALE, cap)
            scores[g * OWN : (g + 1) * OWN, rows] = s
            high = carried[g]
            for t in range(CHUNK // HD):
                high = jnp.maximum(high, s[:, t * HD : (t + 1) * HD])
            result.append(high)
        return tuple(result)

    highs = lax.fori_loop(0, lmax // CHUNK, score_step, tuple(highs))
    peaks = [
        jnp.broadcast_to(jnp.max(high, axis=1, keepdims=True), (OWN, HD)) for high in highs
    ]

    for copy in v_loads:
        copy.wait()
    state = []
    for g in range(KV_HEADS):
        weights = jnp.exp2(fresh[g] - peaks[g]).astype(BF16)
        state.append(weights.astype(F32))
        state.append(
            jnp.dot(weights, vx[:, g * HD : (g + 1) * HD], preferred_element_type=F32)
        )

    def value_step(c, carried):
        rows = pl.ds(pl.multiple_of(c * CHUNK, CHUNK), CHUNK)
        result = []
        for g in range(KV_HEADS):
            s = scores[g * OWN : (g + 1) * OWN, rows]
            total, acc = carried[2 * g], carried[2 * g + 1]
            pieces = []
            for t in range(CHUNK // HD):
                piece = jnp.exp2(s[:, t * HD : (t + 1) * HD] - peaks[g]).astype(BF16)
                total = total + piece.astype(F32)
                pieces.append(piece)
            weights = jnp.concatenate(pieces, axis=1)
            acc = acc + jnp.dot(
                weights, v_v[rows, g * HD : (g + 1) * HD], preferred_element_type=F32
            )
            result += [total, acc]
        return tuple(result)

    state = lax.fori_loop(0, lmax // CHUNK, value_step, tuple(state))
    for g in range(KV_HEADS):
        weight_sum = jnp.sum(state[2 * g], axis=1, keepdims=True)
        attended = (state[2 * g + 1] / weight_sum).astype(BF16)
        att_send[2 * g] = attended[:PR]
        att_send[2 * g + 1] = attended[PR:]

    att_recv[f] = att_send[f]
    att_copies = []
    for k in range(1, NF):
        peer = lax.rem(f + k, NF)
        copy = remote(
            att_send.at[peer], att_recv.at[f], att_ssem.at[k - 1], att_rsem.at[k - 1], (h, peer)
        )
        copy.start()
        att_copies.append(copy)
    for copy in att_copies:
        copy.wait()
    att_f32[...] = att_recv[...].astype(F32).reshape(NF * PR, HD)
    for j in range(8):
        rows_all[z, y, :, j * HD : (j + 1) * HD] = att_f32[pl.ds(j, PR, stride=8), :].astype(BF16)

    width_half = rows_all.shape[3] // 2
    quarter = width_half // 2

    def rows_device(side, q):
        return (z * NY + q, f) if side == 0 else (q * NY + y, f)

    def rows_line(side, q, first, count):
        cols = pl.ds(side * width_half + first, count)
        return rows_all.at[q, :, :, cols] if side == 0 else rows_all.at[:, q, :, cols]

    near = {}
    for side in range(2):
        near[side] = []
        mine_rows = rows_all.at[z, y, :, pl.ds(side * width_half, width_half)]
        for k in range(1, NY):
            peer = lax.rem((y, z)[side] + k, NY)
            copy = remote(
                mine_rows, mine_rows,
                near_ssem.at[side, k - 1], near_rsem.at[side, k - 1], rows_device(side, peer),
            )
            copy.start()
            near[side].append(copy)
    lines = {}
    for side in range(2):
        pos = (z, y)[side]
        for copy in near[side]:
            copy.wait_recv()
        lines[side] = []
        block = rows_line(side, pos, 0, width_half)
        for i, step in enumerate((1, 3)):
            copy = remote(
                block, block, line_ssem.at[side, i], line_rsem.at[side, i],
                rows_device(1 - side, lax.rem(pos + step, NY)),
            )
            copy.start()
            lines[side].append(copy)
    for side in range(2):
        pos = (z, y)[side]
        for i, step in enumerate((1, 3)):
            lines[side][i].wait_recv()
            block = rows_line(side, lax.rem(pos + NY - step, NY), i * quarter, quarter)
            copy = remote(
                block, block, line_ssem.at[side, 2 + i], line_rsem.at[side, 2 + i],
                rows_device(1 - side, lax.rem(pos + step, NY)),
            )
            copy.start()
            lines[side].append(copy)
    wout_load.wait()
    for side in range(2):
        for copy in lines[side][2:]:
            copy.wait_recv()
        for copy in near[side] + lines[side]:
            copy.wait_send()

    opart[...] = jnp.dot(
        rows_all[...].reshape(opart.shape[0], wout_v.shape[0]),
        wout_v[...],
        preferred_element_type=F32,
    )

    def out_rows(index):
        return pl.ds(pl.multiple_of(index * OWN, OWN), OWN)

    sib_copies = []
    for x in range(NX):
        copy = remote(
            opart.at[out_rows(2 * x + 1 - core)], sib_recv.at[x],
            sib_ssem.at[x], sib_rsem.at[x], (h, sib),
        )
        copy.start()
        sib_copies.append(copy)
    for copy in sib_copies:
        copy.wait()
    fin_copies = []
    for k in range(1, NX):
        x = lax.rem(cx + k, NX)
        fin_send[k - 1] = (opart[out_rows(2 * x + core), :] + sib_recv[x]).astype(BF16)
        copy = remote(
            fin_send.at[k - 1], fin_recv.at[k - 1],
            fin_ssem.at[k - 1], fin_rsem.at[k - 1], (h, 2 * x + core),
        )
        copy.start()
        fin_copies.append(copy)
    result = opart[out_rows(f), :] + sib_recv[cx]
    for k in range(1, NX):
        fin_copies[k - 1].wait()
        result = result + fin_recv[k - 1].astype(F32)
    out[...] = result.reshape(out.shape).astype(BF16)


def hand_out(out, entries, out_hbm, entries_hbm, sem):
    copies = [
        pltpu.make_async_copy(out, out_hbm, sem.at[0]),
        pltpu.make_async_copy(entries, entries_hbm, sem.at[1]),
    ]
    for copy in copies:
        copy.start()
    for copy in copies:
        copy.wait()


def body(tokens, norm_gain, query_weight, w_keyval, w_out, cache_keys, cache_values, lengths):
    width = tokens.shape[2]
    lmax = cache_keys.shape[1]
    qcols = query_weight.shape[1]
    kvcols = w_keyval.shape[1]
    halves = np.arange(HD // 2, dtype=np.float64) * (2.0 / HD)
    freq = (ROPE_BASE ** (-halves)).astype(np.float32)
    freq = jnp.asarray(np.tile(np.concatenate([freq, freq])[None, :], (PR, 1)))
    any_spec = pl.BlockSpec(memory_space=pl.ANY)
    hbm_spec = pl.BlockSpec(memory_space=pltpu.HBM)
    vmem_spec = pl.BlockSpec(memory_space=pltpu.VMEM)
    dma = pltpu.SemaphoreType.DMA
    rows = NH * PR
    out, entries = pl.pallas_call(
        kernel,
        out_shape=(
            jax.ShapeDtypeStruct(tokens.shape, BF16),
            jax.ShapeDtypeStruct((1, STEPS, 2 * KV_HEADS * HD), BF16),
        ),
        in_specs=[hbm_spec] * 9,
        out_specs=(vmem_spec, vmem_spec),
        scratch_shapes=[
            pltpu.SMEM(lengths.shape, jnp.int32),
            pltpu.VMEM(tokens.shape, BF16),
            pltpu.VMEM((OWN, width), BF16),
            pltpu.VMEM((PR, HD), F32),
            pltpu.VMEM((width,), BF16),
            pltpu.VMEM((width, qcols), BF16),
            pltpu.VMEM((width, kvcols), BF16),
            pltpu.VMEM((qcols, width), BF16),
            pltpu.VMEM((lmax, KV_HEADS * HD), BF16),
            pltpu.VMEM((lmax, KV_HEADS * HD), BF16),
            pltpu.VMEM((rows, width), BF16),
            pltpu.VMEM((rows, width), BF16),
            pltpu.VMEM((8, HD), F32),
            pltpu.VMEM((NH - 1, 8, HD), F32),
            pltpu.VMEM((NF, 8, HD), F32),
            pltpu.VMEM((NY, NY, PR, qcols + kvcols), F32),
            pltpu.VMEM((2, NY, PR // 2, LOW), F32),
            pltpu.VMEM((2, NY, PR // 2, qcols + kvcols - LOW), F32),
            pltpu.VMEM((2, NY, PR // 2, LOW), F32),
            pltpu.VMEM((2, NY, PR // 2, qcols + kvcols - LOW), F32),
            pltpu.VMEM((2, NY, PR // 2, LOW), F32),
            pltpu.VMEM((2, NY, PR // 2, qcols + kvcols - LOW), F32),
            pltpu.VMEM((2, NY, PR // 2, qcols + kvcols), F32),
            pltpu.VMEM((2, NY - 1, PR // 2, qcols + kvcols), F32),
            pltpu.VMEM((NF * PR, HD), F32),
            pltpu.VMEM((NF, 2 * PR, HD), BF16),
            pltpu.VMEM((NF, 2 * PR, HD), BF16),
            pltpu.VMEM((HD, KV_HEADS * HD), BF16),
            pltpu.VMEM((HD, KV_HEADS * HD), BF16),
            pltpu.VMEM((8, 2 * KV_HEADS * HD), F32),
            pltpu.VMEM((KV_HEADS * OWN, lmax), F32),
            pltpu.VMEM((NF, PR, HD), BF16),
            pltpu.VMEM((NF, PR, HD), BF16),
            pltpu.VMEM((NF * PR, HD), F32),
            pltpu.VMEM((NY, NY, PR, qcols), BF16),
            pltpu.VMEM((rows, width), F32),
            pltpu.VMEM((NX, OWN, width), F32),
            pltpu.VMEM((NX - 1, OWN, width), BF16),
            pltpu.VMEM((NX - 1, OWN, width), BF16),
            dma((8,)),
            dma((CACHE_COPIES,)),
            dma((CACHE_COPIES,)),
            dma((NX - 1,)), dma((NX - 1,)),
            dma((NX,)), dma((NX,)),
            dma((NH - 1,)), dma((NH - 1,)),
            dma((NF - 1,)), dma((NF - 1,)),
            dma((2, 6)), dma((2, 6)),
            dma((2, NY - 1)), dma((2, NY - 1)),
            dma((NF - 1,)), dma((NF - 1,)),
            dma((NF - 1,)), dma((NF - 1,)),
            dma((2, NY - 1)), dma((2, NY - 1)),
            dma((2, 4)), dma((2, 4)),
            dma((NX,)), dma((NX,)),
            dma((NX - 1,)), dma((NX - 1,)),
        ],
        compiler_params=pltpu.CompilerParams(
            collective_id=0, has_side_effects=True, vmem_limit_bytes=48 * 2**20
        ),
        name="decode_block",
    )(
        *[
            pltpu.with_memory_space_constraint(array, pltpu.HBM)
            for array in (
                lengths, freq, tokens, norm_gain, query_weight, w_keyval, w_out,
                cache_keys, cache_values,
            )
        ],
    )
    return pl.pallas_call(
        hand_out,
        out_shape=tuple(jax.ShapeDtypeStruct(a.shape, a.dtype) for a in (out, entries)),
        in_specs=[any_spec, any_spec],
        out_specs=(any_spec, any_spec),
        scratch_shapes=[dma((2,))],
        name="hand_out",
    )(out, entries)


def solution(mesh):
    in_specs = (
        P("ffn", None, "hid"),
        P("hid"),
        P("hid", "ffn"),
        P("hid", "ffn"),
        P("ffn", "hid"),
        P(("hid", "ffn"), None, None),
        P(("hid", "ffn"), None, None),
        P(),
    )
    out_specs = (P("ffn", None, "hid"), P(("hid", "ffn"), None, None))
    return jax.shard_map(body, mesh=mesh, in_specs=in_specs, out_specs=out_specs, check_vma=False)
```

```python
import functools

import jax
import jax.numpy as jnp
import numpy as np
from jax import lax
from jax.experimental import pallas as pl
from jax.experimental.pallas import tpu as pltpu
from jax.sharding import PartitionSpec as P

MESH = pl.DeviceIdType.MESH
F32 = jnp.float32
BF16 = jnp.bfloat16

HEADS = 64
KV_HEADS = 4
HD = 128
STEPS = 2
EPSILON = 1e-05
ROPE_BASE = 500000.0
SCALE = HD ** (-0.5) * 1.4426950408889634
MASKED = -1e30

NH = 16
NF = 8
NX = 4
NY = 4
LOW = 512
OWN = 32
PR = 16
CHUNK = 1024
CACHE_COPIES = 4


def remote(src, dst, send_sem, recv_sem, device):
    return pltpu.make_async_remote_copy(
        src_ref=src,
        dst_ref=dst,
        send_sem=send_sem,
        recv_sem=recv_sem,
        device_id=device,
        device_id_type=MESH,
    )


def rotate(vectors, cosine, sine):
    return vectors * cosine + pltpu.roll(vectors, HD // 2, 1) * sine


def kernel(
    lengths_hbm, freq, tokens, gain, wq, wkv, wout, cache_k, cache_v,
    out, entries,
    lengths, raw_v, tok_v, freq_v, gain_v, wq_v, wkv_v, wout_v, k_v, v_v,
    x_all, normed, ss_own, ss_recv, tot_all, part, relay_low, relay_high, left_low, left_high,
    right_low, right_high, mine, mine_recv,
    spread, msg, qkv, kx, vx, ne, scores, att_send, att_recv, att_f32, rows_all,
    opart, sib_recv, fin_send, fin_recv,
    local_sem, k_sem, v_sem,
    tok_ssem, tok_rsem, fwd_ssem, fwd_rsem, ss_ssem, ss_rsem, tot_ssem, tot_rsem,
    ring_ssem, ring_rsem, stage_ssem, stage_rsem, msg_ssem, msg_rsem, att_ssem, att_rsem, line_ssem, line_rsem,
    sib_ssem, sib_rsem, fin_ssem, fin_rsem,
):
    h = lax.axis_index("hid")
    f = lax.axis_index("ffn")
    z = lax.div(h, NY)
    y = lax.rem(h, NY)
    cx = lax.div(f, 2)
    core = lax.rem(f, 2)
    sib = f + 1 - 2 * core
    lmax = cache_k.shape[1]

    barrier = pltpu.get_barrier_semaphore()

    def greet_hid(k, carry):
        pl.semaphore_signal(
            barrier, inc=1, device_id=(lax.rem(h + k, NH), f), device_id_type=MESH
        )
        return carry

    def greet_ffn(k, carry):
        pl.semaphore_signal(
            barrier, inc=1, device_id=(h, lax.rem(f + k, NF)), device_id_type=MESH
        )
        return carry

    lax.fori_loop(1, NH, greet_hid, 0)
    lax.fori_loop(1, NF, greet_ffn, 0)

    loads = []
    for i, (src, dst) in enumerate(
        [(tokens, raw_v), (gain, gain_v), (freq, freq_v), (wq, wq_v), (wkv, wkv_v), (lengths_hbm, lengths)]
    ):
        copy = pltpu.make_async_copy(src, dst, local_sem.at[i])
        copy.start()
        loads.append(copy)
    span = lmax // CACHE_COPIES
    k_loads = []
    for i in range(CACHE_COPIES):
        copy = pltpu.make_async_copy(
            cache_k.at[0, pl.ds(i * span, span)], k_v.at[pl.ds(i * span, span)], k_sem.at[i]
        )
        copy.start()
        k_loads.append(copy)
    loads[0].wait()
    x_f32 = raw_v[...].astype(F32).reshape(tok_v.shape)
    x_own = x_f32.astype(BF16)
    tok_v[...] = x_own
    sums = jnp.sum(x_f32 * x_f32, axis=1, keepdims=True)
    row_id = lax.broadcasted_iota(jnp.int32, (OWN, HD), 0)
    lane_id = lax.broadcasted_iota(jnp.int32, (OWN, HD), 1)
    diagonal = row_id == lane_id
    own_sums = jnp.sum(jnp.where(diagonal, sums, 0.0), axis=0, keepdims=True)
    ss_own[...] = jnp.broadcast_to(own_sums, (8, HD))

    pl.semaphore_wait(barrier, NH + NF - 2)

    def block(index):
        return x_all.at[pl.ds(pl.multiple_of(index * OWN, OWN), OWN)]

    tok_copies = []
    for k in range(1, NX):
        peer = 2 * lax.rem(cx + k, NX) + core
        copy = remote(tok_v, block(f), tok_ssem.at[k - 1], tok_rsem.at[k - 1], (h, peer))
        copy.start()
        tok_copies.append(copy)

    def ss_copy(k):
        return remote(
            ss_own, ss_recv.at[k - 1], ss_ssem.at[k - 1], ss_rsem.at[k - 1],
            (lax.rem(h + k, NH), f),
        )

    def ss_start(k, carry):
        ss_copy(k).start()
        return carry

    lax.fori_loop(1, NH, ss_start, 0)
    fwd_copies = [remote(tok_v, block(f), fwd_ssem.at[0], fwd_rsem.at[0], (h, sib))]
    fwd_copies[0].start()
    x_all[pl.ds(pl.multiple_of(f * OWN, OWN), OWN), :] = x_own

    def ss_add(k, total):
        ss_copy(k).wait()
        return total + ss_recv[k - 1]

    total = lax.fori_loop(1, NH, ss_add, ss_own[...])
    tot_all[f] = total
    tot_copies = []
    for k in range(1, NF):
        copy = remote(
            tot_all.at[f], tot_all.at[f], tot_ssem.at[k - 1], tot_rsem.at[k - 1],
            (h, lax.rem(f + k, NF)),
        )
        copy.start()
        tot_copies.append(copy)
    for k in range(1, NX):
        tok_copies[k - 1].wait_recv()
        came = 2 * lax.rem(cx + NX - k, NX) + core
        copy = remote(block(came), block(came), fwd_ssem.at[k], fwd_rsem.at[k], (h, sib))
        copy.start()
        fwd_copies.append(copy)

    loads[5].wait()
    length = lengths[h * NF + f]
    step_of = lax.div(lax.broadcasted_iota(jnp.int32, (PR, HD), 0), 8)
    loads[2].wait()
    angles = (step_of + length).astype(F32) * freq_v[...]
    cosine = jnp.cos(angles)
    sine = jnp.sin(angles)
    sine = jnp.where(
        lax.broadcasted_iota(jnp.int32, (PR, HD), 1) < HD // 2, -sine, sine
    )

    for copy in tot_copies:
        copy.wait()
    for copy in fwd_copies:
        copy.wait()
    for copy in tok_copies:
        copy.wait_send()
    loads[1].wait()
    width = x_all.shape[1]
    full = width * NH
    gain_row = gain_v[...].astype(F32).reshape(1, width)

    def normalise(b, carry):
        rows = pl.ds(pl.multiple_of(b * OWN, OWN), OWN)
        lane_sums = tot_all[b][0:1, :]
        row_sums = jnp.sum(jnp.where(diagonal, lane_sums, 0.0), axis=1, keepdims=True)
        inverse = lax.rsqrt(row_sums / full + EPSILON)
        normed[rows, :] = (x_all[rows, :].astype(F32) * inverse * gain_row).astype(BF16)
        return carry

    lax.fori_loop(0, NF, normalise, 0)

    loads[3].wait()
    loads[4].wait()
    lhs = normed[...]
    qcols = wq_v.shape[1]
    for cols, weights in ((slice(0, qcols), wq_v), (slice(qcols, None), wkv_v)):
        product = jnp.dot(lhs, weights[...], preferred_element_type=F32)
        part[:, :, :, cols] = product.reshape(NY, NY, PR, product.shape[1])

    half = PR // 2
    low, high_cols = pl.ds(0, LOW), pl.ds(LOW, part.shape[3] - LOW)

    def ring(side):
        pos = (y, z)[side]

        def device(q):
            return (z * NY + q, f) if side == 0 else (q * NY + y, f)

        def view(q, cols):
            if side == 0:
                return part.at[:, q, pl.ds(0, half), cols]
            return part.at[q, :, pl.ds(half, half), cols]

        return pos, device, view

    after = {}
    for side in range(2):
        pos, device, view = ring(side)
        nxt, prv, far = lax.rem(pos + 1, NY), lax.rem(pos + 3, NY), lax.rem(pos + 2, NY)
        plan = [
            (view(far, low), relay_low, nxt),
            (view(far, high_cols), relay_high, prv),
            (view(nxt, high_cols), left_high, nxt),
            (view(prv, low), right_low, prv),
        ]
        copies = [
            remote(
                src, dst.at[side], ring_ssem.at[side, i], ring_rsem.at[side, i], device(to)
            )
            for i, (src, dst, to) in enumerate(plan)
        ]
        for copy in copies:
            copy.start()
        after[side] = copies
    v_loads = []
    for i in range(CACHE_COPIES):
        copy = pltpu.make_async_copy(
            cache_v.at[0, pl.ds(i * span, span)], v_v.at[pl.ds(i * span, span)], v_sem.at[i]
        )
        copy.start()
        v_loads.append(copy)
    wout_load = pltpu.make_async_copy(wout, wout_v, local_sem.at[6])
    wout_load.start()
    for side in range(2):
        pos, device, view = ring(side)
        nxt, prv = lax.rem(pos + 1, NY), lax.rem(pos + 3, NY)
        plan = [
            (view(nxt, low), relay_low, left_low, nxt),
            (view(prv, high_cols), relay_high, right_high, prv),
        ]
        for i, (own, relay, dst, to) in enumerate(plan):
            after[side][i].wait_recv()
            relay[side] = relay[side] + own[...]
            copy = remote(
                relay.at[side], dst.at[side],
                ring_ssem.at[side, 4 + i], ring_rsem.at[side, 4 + i], device(to),
            )
            copy.start()
            after[side].append(copy)
    stage_copies = {}
    for side in range(2):
        pos, device, view = ring(side)
        for copy in after[side][2:]:
            copy.wait_recv()
        mine[side, :, :, :LOW] = view(pos, low)[...] + left_low[side] + right_low[side]
        mine[side, :, :, LOW:] = view(pos, high_cols)[...] + left_high[side] + right_high[side]
        other, other_device, _ = ring(1 - side)
        stage_copies[side] = []
        for k in range(1, NY):
            peer = lax.rem(other + k, NY)
            copy = remote(
                mine.at[side, peer], mine_recv.at[side, k - 1],
                stage_ssem.at[side, k - 1], stage_rsem.at[side, k - 1], other_device(peer),
            )
            copy.start()
            stage_copies[side].append(copy)
    halves = []
    for side in range(2):
        other = ring(1 - side)[0]
        total = mine[side, other]
        for k in range(1, NY):
            stage_copies[side][k - 1].wait()
            total = total + mine_recv[side, k - 1]
        halves.append(total)
        for copy in after[side]:
            copy.wait_send()
    summed = jnp.concatenate(halves, axis=0)

    for j in range(8):
        spread[pl.ds(j, PR, stride=8), :] = summed[:, j * HD : (j + 1) * HD]
    msg[:, :PR, :] = spread[...].reshape(NF, PR, HD).astype(BF16)
    spread[...] = jnp.zeros_like(spread)
    spread[pl.ds(0, PR, stride=8), :] = summed[:, qcols:]
    msg[:, PR:, :] = spread[...].reshape(NF, PR, HD).astype(BF16)
    qkv[f] = msg[f]
    msg_copies = []
    for k in range(1, NF):
        peer = lax.rem(f + k, NF)
        copy = remote(
            msg.at[peer], qkv.at[f], msg_ssem.at[k - 1], msg_rsem.at[k - 1], (h, peer)
        )
        copy.start()
        msg_copies.append(copy)
    for copy in msg_copies:
        copy.wait()

    kx[...] = jnp.zeros_like(kx)
    vx[...] = jnp.zeros_like(vx)
    for i in range(2 * KV_HEADS):
        raw = qkv[i, PR:, :].astype(F32)
        cols = pl.ds((i % KV_HEADS) * HD, HD)
        if i < KV_HEADS:
            raw = rotate(raw, cosine, sine)
            kx[:PR, cols] = raw.astype(BF16)
        else:
            vx[:PR, cols] = raw.astype(BF16)
        ne[0:1, i * HD : (i + 1) * HD] = raw[0:1]
        ne[1:2, i * HD : (i + 1) * HD] = raw[8:9]
    entries[...] = ne[0:2, :].reshape(entries.shape).astype(BF16)

    queries = []
    for g in range(KV_HEADS):
        pair = [
            rotate(qkv[2 * g + i, :PR, :].astype(F32), cosine, sine).astype(BF16)
            for i in range(2)
        ]
        queries.append(jnp.concatenate(pair, axis=0))
    row32 = lax.broadcasted_iota(jnp.int32, (OWN, HD), 0)
    step_row = lax.rem(lax.div(row32, 8), 2)
    fresh_live = (lane_id == 0) | ((lane_id == 8) & (step_row == 1))
    nt = (((1,), (1,)), ((), ()))
    highs, fresh = [], []
    for g in range(KV_HEADS):
        s = lax.dot_general(
            queries[g], kx[:, g * HD : (g + 1) * HD], nt, preferred_element_type=F32
        )
        s = jnp.where(fresh_live, s * SCALE, MASKED)
        fresh.append(s)
        highs.append(s)

    for copy in k_loads:
        copy.wait()

    def score_step(c, carried):
        rows = pl.ds(pl.multiple_of(c * CHUNK, CHUNK), CHUNK)
        position = lax.broadcasted_iota(jnp.int32, (8, CHUNK), 1) + c * CHUNK
        cap = jnp.where(position < length, -MASKED, MASKED)
        cap = jnp.concatenate([cap] * (OWN // 8), axis=0)
        result = []
        for g in range(KV_HEADS):
            s = lax.dot_general(
                queries[g], k_v[rows, g * HD : (g + 1) * HD], nt, preferred_element_type=F32
            )
            s = jnp.minimum(s * SCALE, cap)
            scores[g * OWN : (g + 1) * OWN, rows] = s
            high = carried[g]
            for t in range(CHUNK // HD):
                high = jnp.maximum(high, s[:, t * HD : (t + 1) * HD])
            result.append(high)
        return tuple(result)

    highs = lax.fori_loop(0, lmax // CHUNK, score_step, tuple(highs))
    peaks = [
        jnp.broadcast_to(jnp.max(high, axis=1, keepdims=True), (OWN, HD)) for high in highs
    ]

    for copy in v_loads:
        copy.wait()
    state = []
    for g in range(KV_HEADS):
        weights = jnp.exp2(fresh[g] - peaks[g]).astype(BF16)
        state.append(weights.astype(F32))
        state.append(
            jnp.dot(weights, vx[:, g * HD : (g + 1) * HD], preferred_element_type=F32)
        )

    def value_step(c, carried):
        rows = pl.ds(pl.multiple_of(c * CHUNK, CHUNK), CHUNK)
        result = []
        for g in range(KV_HEADS):
            s = scores[g * OWN : (g + 1) * OWN, rows]
            total, acc = carried[2 * g], carried[2 * g + 1]
            pieces = []
            for t in range(CHUNK // HD):
                piece = jnp.exp2(s[:, t * HD : (t + 1) * HD] - peaks[g]).astype(BF16)
                total = total + piece.astype(F32)
                pieces.append(piece)
            weights = jnp.concatenate(pieces, axis=1)
            acc = acc + jnp.dot(
                weights, v_v[rows, g * HD : (g + 1) * HD], preferred_element_type=F32
            )
            result += [total, acc]
        return tuple(result)

    state = lax.fori_loop(0, lmax // CHUNK, value_step, tuple(state))
    for g in range(KV_HEADS):
        weight_sum = jnp.sum(state[2 * g], axis=1, keepdims=True)
        attended = (state[2 * g + 1] / weight_sum).astype(BF16)
        att_send[2 * g] = attended[:PR]
        att_send[2 * g + 1] = attended[PR:]

    odd = lax.rem(y + z, 2)
    slot = lax.div((1 - odd) * y + odd * z, 2)
    own_copy = pltpu.make_async_copy(
        att_send.at[f], att_recv.at[odd, slot, f], att_rsem.at[odd, slot]
    )
    own_copy.start()
    for k in range(NY):
        chip = lax.rem(z + odd * k, NY) * NY + lax.rem(y + (1 - odd) * k, NY)
        for m in range(NF):
            if k + m > 0:
                peer = lax.rem(f + m, NF)
                remote(
                    att_send.at[peer], att_recv.at[odd, slot, f],
                    att_ssem.at[k], att_rsem.at[odd, slot], (chip, peer),
                ).start()

    line_copies = []
    for side in range(2):
        for i in range(2):
            whole = att_recv.at[side, i]
            pltpu.make_async_copy(whole, whole, att_rsem.at[side, i]).wait()
        pos = (z, y)[side]
        for i in range(2):
            att_f32[...] = att_recv[side, i].astype(F32).reshape(NF * PR, HD)
            for j in range(8):
                rows_all[side, pos, i, :, j * HD : (j + 1) * HD] = att_f32[
                    pl.ds(j, PR, stride=8), :
                ].astype(BF16)
        mine_rows = rows_all.at[side, pos]
        for k in range(1, NY):
            q = lax.rem(pos + k, NY)
            device = (q * NY + y, f) if side == 0 else (z * NY + q, f)
            copy = remote(
                mine_rows, mine_rows,
                line_ssem.at[side, k - 1], line_rsem.at[side, k - 1], device,
            )
            copy.start()
            line_copies.append(copy)
    wout_load.wait()
    for copy in line_copies:
        copy.wait_recv()

    product = jnp.dot(
        rows_all[...].reshape(opart.shape[0], wout_v.shape[0]),
        wout_v[...],
        preferred_element_type=F32,
    )
    for side in range(2):
        for q in range(NY):
            for i in range(2):
                far = 2 * i + (q + side) % 2
                home = q * NY + far if side == 0 else far * NY + q
                first = ((side * NY + q) * 2 + i) * PR
                opart[home * PR : (home + 1) * PR, :] = product[first : first + PR]

    def out_rows(index):
        return pl.ds(pl.multiple_of(index * OWN, OWN), OWN)

    sib_copies = []
    for x in range(NX):
        copy = remote(
            opart.at[out_rows(2 * x + 1 - core)], sib_recv.at[x],
            sib_ssem.at[x], sib_rsem.at[x], (h, sib),
        )
        copy.start()
        sib_copies.append(copy)
    for copy in sib_copies:
        copy.wait()
    fin_copies = []
    for k in range(1, NX):
        x = lax.rem(cx + k, NX)
        fin_send[k - 1] = (opart[out_rows(2 * x + core), :] + sib_recv[x]).astype(BF16)
        copy = remote(
            fin_send.at[k - 1], fin_recv.at[k - 1],
            fin_ssem.at[k - 1], fin_rsem.at[k - 1], (h, 2 * x + core),
        )
        copy.start()
        fin_copies.append(copy)
    result = opart[out_rows(f), :] + sib_recv[cx]
    for k in range(1, NX):
        fin_copies[k - 1].wait()
        result = result + fin_recv[k - 1].astype(F32)
    out[...] = result.reshape(out.shape).astype(BF16)
    for k in range(NY):
        sent = att_send.at[pl.ds(0, NF - 1)] if k == 0 else att_send
        pltpu.make_async_copy(sent, sent, att_ssem.at[k]).wait()
    for copy in line_copies:
        copy.wait_send()


def hand_out(out, entries, out_hbm, entries_hbm, sem):
    copies = [
        pltpu.make_async_copy(out, out_hbm, sem.at[0]),
        pltpu.make_async_copy(entries, entries_hbm, sem.at[1]),
    ]
    for copy in copies:
        copy.start()
    for copy in copies:
        copy.wait()


def body(tokens, norm_gain, query_weight, w_keyval, w_out, cache_keys, cache_values, lengths):
    width = tokens.shape[2]
    lmax = cache_keys.shape[1]
    qcols = query_weight.shape[1]
    kvcols = w_keyval.shape[1]
    halves = np.arange(HD // 2, dtype=np.float64) * (2.0 / HD)
    freq = (ROPE_BASE ** (-halves)).astype(np.float32)
    freq = jnp.asarray(np.tile(np.concatenate([freq, freq])[None, :], (PR, 1)))
    any_spec = pl.BlockSpec(memory_space=pl.ANY)
    hbm_spec = pl.BlockSpec(memory_space=pltpu.HBM)
    vmem_spec = pl.BlockSpec(memory_space=pltpu.VMEM)
    dma = pltpu.SemaphoreType.DMA
    rows = NH * PR
    out, entries = pl.pallas_call(
        kernel,
        out_shape=(
            pltpu.VMEM(tokens.shape, BF16),
            pltpu.VMEM((1, STEPS, 2 * KV_HEADS * HD), BF16),
        ),
        in_specs=[hbm_spec] * 9,
        out_specs=(vmem_spec, vmem_spec),
        scratch_shapes=[
            pltpu.SMEM(lengths.shape, jnp.int32),
            pltpu.VMEM(tokens.shape, BF16),
            pltpu.VMEM((OWN, width), BF16),
            pltpu.VMEM((PR, HD), F32),
            pltpu.VMEM((width,), BF16),
            pltpu.VMEM((width, qcols), BF16),
            pltpu.VMEM((width, kvcols), BF16),
            pltpu.VMEM((qcols, width), BF16),
            pltpu.VMEM((lmax, KV_HEADS * HD), BF16),
            pltpu.VMEM((lmax, KV_HEADS * HD), BF16),
            pltpu.VMEM((rows, width), BF16),
            pltpu.VMEM((rows, width), BF16),
            pltpu.VMEM((8, HD), F32),
            pltpu.VMEM((NH - 1, 8, HD), F32),
            pltpu.VMEM((NF, 8, HD), F32),
            pltpu.VMEM((NY, NY, PR, qcols + kvcols), F32),
            pltpu.VMEM((2, NY, PR // 2, LOW), F32),
            pltpu.VMEM((2, NY, PR // 2, qcols + kvcols - LOW), F32),
            pltpu.VMEM((2, NY, PR // 2, LOW), F32),
            pltpu.VMEM((2, NY, PR // 2, qcols + kvcols - LOW), F32),
            pltpu.VMEM((2, NY, PR // 2, LOW), F32),
            pltpu.VMEM((2, NY, PR // 2, qcols + kvcols - LOW), F32),
            pltpu.VMEM((2, NY, PR // 2, qcols + kvcols), F32),
            pltpu.VMEM((2, NY - 1, PR // 2, qcols + kvcols), F32),
            pltpu.VMEM((NF * PR, HD), F32),
            pltpu.VMEM((NF, 2 * PR, HD), BF16),
            pltpu.VMEM((NF, 2 * PR, HD), BF16),
            pltpu.VMEM((HD, KV_HEADS * HD), BF16),
            pltpu.VMEM((HD, KV_HEADS * HD), BF16),
            pltpu.VMEM((8, 2 * KV_HEADS * HD), F32),
            pltpu.VMEM((KV_HEADS * OWN, lmax), F32),
            pltpu.VMEM((NF, PR, HD), BF16),
            pltpu.VMEM((2, 2, NF, PR, HD), BF16),
            pltpu.VMEM((NF * PR, HD), F32),
            pltpu.VMEM((2, NY, 2, PR, qcols), BF16),
            pltpu.VMEM((rows, width), F32),
            pltpu.VMEM((NX, OWN, width), F32),
            pltpu.VMEM((NX - 1, OWN, width), BF16),
            pltpu.VMEM((NX - 1, OWN, width), BF16),
            dma((8,)),
            dma((CACHE_COPIES,)),
            dma((CACHE_COPIES,)),
            dma((NX - 1,)), dma((NX - 1,)),
            dma((NX,)), dma((NX,)),
            dma((NH - 1,)), dma((NH - 1,)),
            dma((NF - 1,)), dma((NF - 1,)),
            dma((2, 6)), dma((2, 6)),
            dma((2, NY - 1)), dma((2, NY - 1)),
            dma((NF - 1,)), dma((NF - 1,)),
            dma((NY,)), dma((2, 2)),
            dma((2, NY - 1)), dma((2, NY - 1)),
            dma((NX,)), dma((NX,)),
            dma((NX - 1,)), dma((NX - 1,)),
        ],
        compiler_params=pltpu.CompilerParams(
            collective_id=0, has_side_effects=True, vmem_limit_bytes=48 * 2**20
        ),
        name="decode_block",
    )(
        *[
            pltpu.with_memory_space_constraint(array, pltpu.HBM)
            for array in (
                lengths, freq, tokens, norm_gain, query_weight, w_keyval, w_out,
                cache_keys, cache_values,
            )
        ],
    )
    return pl.pallas_call(
        hand_out,
        out_shape=tuple(jax.ShapeDtypeStruct(a.shape, a.dtype) for a in (out, entries)),
        in_specs=[vmem_spec, vmem_spec],
        out_specs=(any_spec, any_spec),
        scratch_shapes=[dma((2,))],
        name="hand_out",
    )(out, entries)


def solution(mesh):
    in_specs = (
        P("ffn", None, "hid"),
        P("hid"),
        P("hid", "ffn"),
        P("hid", "ffn"),
        P("ffn", "hid"),
        P(("hid", "ffn"), None, None),
        P(("hid", "ffn"), None, None),
        P(),
    )
    out_specs = (P("ffn", None, "hid"), P(("hid", "ffn"), None, None))
    return jax.shard_map(body, mesh=mesh, in_specs=in_specs, out_specs=out_specs, check_vma=False)
```

```python
import functools

import jax
import jax.numpy as jnp
import numpy as np
from jax import lax
from jax.experimental import pallas as pl
from jax.experimental.pallas import tpu as pltpu
from jax.sharding import PartitionSpec as P

MESH = pl.DeviceIdType.MESH
F32 = jnp.float32
BF16 = jnp.bfloat16

HEADS = 64
KV_HEADS = 4
HD = 128
STEPS = 2
EPSILON = 1e-05
ROPE_BASE = 500000.0
SCALE = HD ** (-0.5) * 1.4426950408889634
MASKED = -1e30

NH = 16
NF = 8
NX = 4
NY = 4
LOW = 512
OWN = 32
PR = 16
CHUNK = 2048
CACHE_COPIES = 4
PAIRS = KV_HEADS // 2


def remote(src, dst, send_sem, recv_sem, device):
    return pltpu.make_async_remote_copy(
        src_ref=src,
        dst_ref=dst,
        send_sem=send_sem,
        recv_sem=recv_sem,
        device_id=device,
        device_id_type=MESH,
    )


def rotate(vectors, cosine, sine):
    return vectors * cosine + pltpu.roll(vectors, HD // 2, 1) * sine


def kernel(
    lengths_hbm, freq, tokens, gain, wq, wkv, wout, cache_k, cache_v,
    results,
    lengths, raw_v, tok_v, freq_v, gain_v, wq_v, wkv_v, wout_v, k_v, v_v,
    x_all, normed, ss_own, ss_recv, tot_all, part, relay_low, relay_high, left_low, left_high,
    right_low, right_high, mine, mine_recv,
    spread, msg, qkv, kx, vx, ne, scores, weighted, att_send, att_recv, att_f32, rows_all,
    opart, sib_recv, fin_send, fin_recv,
    local_sem, k_sem, v_sem,
    tok_ssem, tok_rsem, fwd_ssem, fwd_rsem, ss_ssem, ss_rsem, tot_ssem, tot_rsem,
    ring_ssem, ring_rsem, stage_ssem, stage_rsem, msg_ssem, msg_rsem, att_ssem, att_rsem, line_ssem, line_rsem,
    sib_ssem, sib_rsem, fin_ssem, fin_rsem,
):
    h = lax.axis_index("hid")
    f = lax.axis_index("ffn")
    z = lax.div(h, NY)
    y = lax.rem(h, NY)
    cx = lax.div(f, 2)
    core = lax.rem(f, 2)
    sib = f + 1 - 2 * core
    lmax = cache_k.shape[1]

    barrier = pltpu.get_barrier_semaphore()

    def greet_hid(k, carry):
        pl.semaphore_signal(
            barrier, inc=1, device_id=(lax.rem(h + k, NH), f), device_id_type=MESH
        )
        return carry

    def greet_ffn(k, carry):
        pl.semaphore_signal(
            barrier, inc=1, device_id=(h, lax.rem(f + k, NF)), device_id_type=MESH
        )
        return carry

    loads = []
    for i, (src, dst) in enumerate(
        [(tokens, raw_v), (gain, gain_v), (freq, freq_v), (wq, wq_v), (wkv, wkv_v), (lengths_hbm, lengths)]
    ):
        copy = pltpu.make_async_copy(src, dst, local_sem.at[i])
        copy.start()
        loads.append(copy)
    lax.fori_loop(1, NH, greet_hid, 0)
    lax.fori_loop(1, NF, greet_ffn, 0)

    span = lmax // CACHE_COPIES
    k_loads = []
    for i in range(CACHE_COPIES):
        copy = pltpu.make_async_copy(
            cache_k.at[0, pl.ds(i * span, span)], k_v.at[pl.ds(i * span, span)], k_sem.at[i]
        )
        copy.start()
        k_loads.append(copy)
    loads[0].wait()
    x_f32 = raw_v[...].astype(F32).reshape(tok_v.shape)
    x_own = x_f32.astype(BF16)
    tok_v[...] = x_own
    sums = jnp.sum(x_f32 * x_f32, axis=1, keepdims=True)
    row_id = lax.broadcasted_iota(jnp.int32, (OWN, HD), 0)
    lane_id = lax.broadcasted_iota(jnp.int32, (OWN, HD), 1)
    diagonal = row_id == lane_id
    own_sums = jnp.sum(jnp.where(diagonal, sums, 0.0), axis=0, keepdims=True)
    ss_own[...] = jnp.broadcast_to(own_sums, (8, HD))

    pl.semaphore_wait(barrier, NH + NF - 2)

    def block(index):
        return x_all.at[pl.ds(pl.multiple_of(index * OWN, OWN), OWN)]

    def ss_copy(k):
        return remote(
            ss_own, ss_recv.at[k - 1], ss_ssem.at[k - 1], ss_rsem.at[k - 1],
            (lax.rem(h + k, NH), f),
        )

    def ss_start(k, carry):
        ss_copy(k).start()
        return carry

    lax.fori_loop(1, NH, ss_start, 0)
    tok_copies = []
    for k in range(1, NX):
        peer = 2 * lax.rem(cx + k, NX) + core
        copy = remote(tok_v, block(f), tok_ssem.at[k - 1], tok_rsem.at[k - 1], (h, peer))
        copy.start()
        tok_copies.append(copy)
    fwd_copies = [remote(tok_v, block(f), fwd_ssem.at[0], fwd_rsem.at[0], (h, sib))]
    fwd_copies[0].start()
    x_all[pl.ds(pl.multiple_of(f * OWN, OWN), OWN), :] = x_own

    def ss_add(k, total):
        ss_copy(k).wait()
        return total + ss_recv[k - 1]

    total = lax.fori_loop(1, NH, ss_add, ss_own[...])
    tot_all[f] = total
    tot_copies = []
    for k in range(1, NF):
        copy = remote(
            tot_all.at[f], tot_all.at[f], tot_ssem.at[k - 1], tot_rsem.at[k - 1],
            (h, lax.rem(f + k, NF)),
        )
        copy.start()
        tot_copies.append(copy)
    for k in range(1, NX):
        tok_copies[k - 1].wait_recv()
        came = 2 * lax.rem(cx + NX - k, NX) + core
        copy = remote(block(came), block(came), fwd_ssem.at[k], fwd_rsem.at[k], (h, sib))
        copy.start()
        fwd_copies.append(copy)

    loads[5].wait()
    length = lengths[h * NF + f]
    step_of = lax.div(lax.broadcasted_iota(jnp.int32, (PR, HD), 0), 8)
    loads[2].wait()
    angles = (step_of + length).astype(F32) * freq_v[...]
    cosine = jnp.cos(angles)
    sine = jnp.sin(angles)
    sine = jnp.where(
        lax.broadcasted_iota(jnp.int32, (PR, HD), 1) < HD // 2, -sine, sine
    )

    for copy in tot_copies:
        copy.wait()
    loads[1].wait()
    width = x_all.shape[1]
    qcols = wq_v.shape[1]
    full = width * NH
    gain_row = gain_v[...].astype(F32).reshape(1, width)

    def project(parity):
        for x in range(NX):
            b = 2 * x + parity
            lane_sums = tot_all[b][0:1, :]
            row_sums = jnp.sum(jnp.where(diagonal, lane_sums, 0.0), axis=1, keepdims=True)
            inverse = lax.rsqrt(row_sums / full + EPSILON)
            normed[x * OWN : (x + 1) * OWN, :] = (
                block(b)[...].astype(F32) * inverse * gain_row
            ).astype(BF16)
        lhs = normed[...]
        for cols, weights in ((slice(0, qcols), wq_v), (slice(qcols, None), wkv_v)):
            product = jnp.dot(lhs, weights[...], preferred_element_type=F32)
            part[:, pl.ds(2 * parity, 2), :, cols] = product.reshape(NX, 2, PR, product.shape[1])

    loads[3].wait()
    loads[4].wait()
    project(core)
    for copy in fwd_copies:
        copy.wait()
    for copy in tok_copies:
        copy.wait_send()
    project(1 - core)

    half = PR // 2
    low, high_cols = pl.ds(0, LOW), pl.ds(LOW, part.shape[3] - LOW)

    def ring(side):
        pos = (y, z)[side]

        def device(q):
            return (z * NY + q, f) if side == 0 else (q * NY + y, f)

        def view(q, cols):
            if side == 0:
                return part.at[:, q, pl.ds(0, half), cols]
            return part.at[q, :, pl.ds(half, half), cols]

        return pos, device, view

    after = {}
    for side in range(2):
        pos, device, view = ring(side)
        nxt, prv, far = lax.rem(pos + 1, NY), lax.rem(pos + 3, NY), lax.rem(pos + 2, NY)
        plan = [
            (view(far, low), relay_low, nxt),
            (view(far, high_cols), relay_high, prv),
            (view(nxt, high_cols), left_high, nxt),
            (view(prv, low), right_low, prv),
        ]
        copies = [
            remote(
                src, dst.at[side], ring_ssem.at[side, i], ring_rsem.at[side, i], device(to)
            )
            for i, (src, dst, to) in enumerate(plan)
        ]
        after[side] = copies
    for first in (0, 2):
        for side in range(2):
            for copy in after[side][first : first + 2]:
                copy.start()
    v_loads = []
    for i in range(CACHE_COPIES):
        copy = pltpu.make_async_copy(
            cache_v.at[0, pl.ds(i * span, span)], v_v.at[pl.ds(i * span, span)], v_sem.at[i]
        )
        copy.start()
        v_loads.append(copy)
    wout_load = pltpu.make_async_copy(wout, wout_v, local_sem.at[6])
    wout_load.start()
    for side in range(2):
        pos, device, view = ring(side)
        nxt, prv = lax.rem(pos + 1, NY), lax.rem(pos + 3, NY)
        plan = [
            (view(nxt, low), relay_low, left_low, nxt),
            (view(prv, high_cols), relay_high, right_high, prv),
        ]
        for i, (own, relay, dst, to) in enumerate(plan):
            after[side][i].wait_recv()
            relay[side] = relay[side] + own[...]
            copy = remote(
                relay.at[side], dst.at[side],
                ring_ssem.at[side, 4 + i], ring_rsem.at[side, 4 + i], device(to),
            )
            copy.start()
            after[side].append(copy)
    stage_copies = {}
    for side in range(2):
        pos, device, view = ring(side)
        for copy in after[side][2:]:
            copy.wait_recv()
        mine[side, :, :, :LOW] = view(pos, low)[...] + left_low[side] + right_low[side]
        mine[side, :, :, LOW:] = view(pos, high_cols)[...] + left_high[side] + right_high[side]
        other, other_device, _ = ring(1 - side)
        stage_copies[side] = []
        for k in range(1, NY):
            peer = lax.rem(other + k, NY)
            copy = remote(
                mine.at[side, peer], mine_recv.at[side, k - 1],
                stage_ssem.at[side, k - 1], stage_rsem.at[side, k - 1], other_device(peer),
            )
            copy.start()
            stage_copies[side].append(copy)
    halves = []
    for side in range(2):
        other = ring(1 - side)[0]
        total = mine[side, other]
        for k in range(1, NY):
            stage_copies[side][k - 1].wait()
            total = total + mine_recv[side, k - 1]
        halves.append(total)
        for copy in after[side]:
            copy.wait_send()
    summed = jnp.concatenate(halves, axis=0)

    for j in range(8):
        spread[pl.ds(j, PR, stride=8), :] = summed[:, j * HD : (j + 1) * HD]
    msg[:, :PR, :] = spread[...].reshape(NF, PR, HD).astype(BF16)
    spread[...] = jnp.zeros_like(spread)
    spread[pl.ds(0, PR, stride=8), :] = summed[:, qcols:]
    msg[:, PR:, :] = spread[...].reshape(NF, PR, HD).astype(BF16)
    qkv[f] = msg[f]
    msg_copies = []
    for k in range(1, NF):
        peer = lax.rem(f + k, NF)
        copy = remote(
            msg.at[peer], qkv.at[f], msg_ssem.at[k - 1], msg_rsem.at[k - 1], (h, peer)
        )
        copy.start()
        msg_copies.append(copy)
    for copy in msg_copies:
        copy.wait()

    kx[...] = jnp.zeros_like(kx)
    vx[...] = jnp.zeros_like(vx)
    fresh_rows = []
    for i in range(2 * KV_HEADS):
        raw = qkv[i, PR:, :].astype(F32)
        cols = pl.ds((i % KV_HEADS) * HD, HD)
        if i < KV_HEADS:
            raw = rotate(raw, cosine, sine)
            kx[:PR, cols] = raw.astype(BF16)
        else:
            vx[:PR, cols] = raw.astype(BF16)
        fresh_rows.append(raw)

    rotated = [
        rotate(qkv[i, :PR, :].astype(F32), cosine, sine).astype(BF16) for i in range(NF)
    ]
    nothing = jnp.zeros((OWN, HD), BF16)
    queries = []
    for p in range(PAIRS):
        upper = jnp.concatenate(rotated[4 * p : 4 * p + 2], axis=0)
        lower = jnp.concatenate(rotated[4 * p + 2 : 4 * p + 4], axis=0)
        queries.append(
            jnp.concatenate(
                [
                    jnp.concatenate([upper, nothing], axis=1),
                    jnp.concatenate([nothing, lower], axis=1),
                ],
                axis=0,
            )
        )
    pair_rows, pair_cols = 2 * OWN, 2 * HD
    lane = lax.broadcasted_iota(jnp.int32, (pair_rows, HD), 1)
    step_row = lax.rem(lax.div(lax.broadcasted_iota(jnp.int32, (pair_rows, HD), 0), 8), 2)
    fresh_live = (lane == 0) | ((lane == 8) & (step_row == 1))
    nt = (((1,), (1,)), ((), ()))
    highs, fresh = [], []
    for p in range(PAIRS):
        s = lax.dot_general(
            queries[p], kx[:, p * pair_cols : (p + 1) * pair_cols], nt,
            preferred_element_type=F32,
        )
        s = jnp.where(fresh_live, s * SCALE, MASKED)
        fresh.append(s)
        highs.append(s)

    for copy in k_loads:
        copy.wait()

    def score_step(c, carried):
        rows = pl.ds(pl.multiple_of(c * CHUNK, CHUNK), CHUNK)
        position = lax.broadcasted_iota(jnp.int32, (8, CHUNK), 1) + c * CHUNK
        cap = jnp.where(position < length, -MASKED, MASKED)
        cap = jnp.concatenate([cap] * (pair_rows // 8), axis=0)
        result = []
        for p in range(PAIRS):
            s = lax.dot_general(
                queries[p], k_v[rows, p * pair_cols : (p + 1) * pair_cols], nt,
                preferred_element_type=F32,
            )
            s = jnp.minimum(s * SCALE, cap)
            scores[p * pair_rows : (p + 1) * pair_rows, rows] = s
            high = carried[p]
            for t in range(CHUNK // HD):
                high = jnp.maximum(high, s[:, t * HD : (t + 1) * HD])
            result.append(high)
        return tuple(result)

    highs = lax.fori_loop(0, lmax // CHUNK, score_step, tuple(highs))
    peaks = [
        jnp.broadcast_to(jnp.max(high, axis=1, keepdims=True), (pair_rows, HD)) for high in highs
    ]

    for copy in v_loads:
        copy.wait()
    totals = []
    for p in range(PAIRS):
        weights = jnp.exp2(fresh[p] - peaks[p]).astype(BF16)
        totals.append(weights.astype(F32))
        weighted[p] = jnp.dot(
            weights, vx[:, p * pair_cols : (p + 1) * pair_cols], preferred_element_type=F32
        )

    def value_step(c, carried):
        rows = pl.ds(pl.multiple_of(c * CHUNK, CHUNK), CHUNK)
        result = []
        for p in range(PAIRS):
            s = scores[p * pair_rows : (p + 1) * pair_rows, rows]
            total = carried[p]
            pieces = []
            for t in range(CHUNK // HD):
                piece = jnp.exp2(s[:, t * HD : (t + 1) * HD] - peaks[p]).astype(BF16)
                total = total + piece.astype(F32)
                pieces.append(piece)
            weighted[p] += jnp.dot(
                jnp.concatenate(pieces, axis=1),
                v_v[rows, p * pair_cols : (p + 1) * pair_cols],
                preferred_element_type=F32,
            )
            result.append(total)
        return tuple(result)

    totals = lax.fori_loop(0, lmax // CHUNK, value_step, tuple(totals))
    for p in range(PAIRS):
        weight_sum = jnp.sum(totals[p], axis=1, keepdims=True)
        for i in range(2):
            rows = slice(i * OWN, (i + 1) * OWN)
            attended = weighted[p, rows, i * HD : (i + 1) * HD] / weight_sum[rows]
            attended = attended.astype(BF16)
            att_send[4 * p + 2 * i] = attended[:PR]
            att_send[4 * p + 2 * i + 1] = attended[PR:]

    odd = lax.rem(y + z, 2)
    slot = lax.div((1 - odd) * y + odd * z, 2)
    own_copy = pltpu.make_async_copy(
        att_send.at[f], att_recv.at[odd, slot, f], att_rsem.at[odd, slot]
    )
    own_copy.start()
    for k in range(NY):
        chip = lax.rem(z + odd * k, NY) * NY + lax.rem(y + (1 - odd) * k, NY)
        for m in range(NF):
            if k + m > 0:
                peer = lax.rem(f + m, NF)
                remote(
                    att_send.at[peer], att_recv.at[odd, slot, f],
                    att_ssem.at[k], att_rsem.at[odd, slot], (chip, peer),
                ).start()

    for i in range(2 * KV_HEADS):
        ne[0:1, i * HD : (i + 1) * HD] = fresh_rows[i][0:1]
        ne[1:2, i * HD : (i + 1) * HD] = fresh_rows[i][8:9]
    results[PR:, :, :] = ne[0:2, :].reshape(1, STEPS, ne.shape[1]).astype(BF16)

    line_copies = []
    for side in range(2):
        for i in range(2):
            whole = att_recv.at[side, i]
            pltpu.make_async_copy(whole, whole, att_rsem.at[side, i]).wait()
        pos = (z, y)[side]
        for i in range(2):
            att_f32[...] = att_recv[side, i].astype(F32).reshape(NF * PR, HD)
            for j in range(8):
                rows_all[side, pos, i, :, j * HD : (j + 1) * HD] = att_f32[
                    pl.ds(j, PR, stride=8), :
                ].astype(BF16)
        mine_rows = rows_all.at[side, pos]
        for k in range(1, NY):
            q = lax.rem(pos + k, NY)
            device = (q * NY + y, f) if side == 0 else (z * NY + q, f)
            copy = remote(
                mine_rows, mine_rows,
                line_ssem.at[side, k - 1], line_rsem.at[side, k - 1], device,
            )
            copy.start()
            line_copies.append(copy)
    wout_load.wait()
    for copy in line_copies:
        copy.wait_recv()

    product = jnp.dot(
        rows_all[...].reshape(opart.shape[0], wout_v.shape[0]),
        wout_v[...],
        preferred_element_type=F32,
    )
    for side in range(2):
        for q in range(NY):
            for i in range(2):
                far = 2 * i + (q + side) % 2
                home = q * NY + far if side == 0 else far * NY + q
                first = ((side * NY + q) * 2 + i) * PR
                opart[home * PR : (home + 1) * PR, :] = product[first : first + PR]

    def out_rows(index):
        return pl.ds(pl.multiple_of(index * OWN, OWN), OWN)

    sib_copies = []
    for x in range(NX):
        copy = remote(
            opart.at[out_rows(2 * x + 1 - core)], sib_recv.at[x],
            sib_ssem.at[x], sib_rsem.at[x], (h, sib),
        )
        copy.start()
        sib_copies.append(copy)
    for copy in sib_copies:
        copy.wait()
    fin_copies = []
    for k in range(1, NX):
        x = lax.rem(cx + k, NX)
        fin_send[k - 1] = (opart[out_rows(2 * x + core), :] + sib_recv[x]).astype(BF16)
        copy = remote(
            fin_send.at[k - 1], fin_recv.at[k - 1],
            fin_ssem.at[k - 1], fin_rsem.at[k - 1], (h, 2 * x + core),
        )
        copy.start()
        fin_copies.append(copy)
    result = opart[out_rows(f), :] + sib_recv[cx]
    for k in range(1, NX):
        fin_copies[k - 1].wait()
        result = result + fin_recv[k - 1].astype(F32)
    results[:PR, :, :] = result.reshape(PR, STEPS, result.shape[1]).astype(BF16)
    for k in range(NY):
        sent = att_send.at[pl.ds(0, NF - 1)] if k == 0 else att_send
        pltpu.make_async_copy(sent, sent, att_ssem.at[k]).wait()
    for copy in line_copies:
        copy.wait_send()


def hand_out(results, out, entries, sem):
    rows = out.shape[0]
    copies = [
        pltpu.make_async_copy(results.at[pl.ds(0, rows)], out, sem.at[0]),
        pltpu.make_async_copy(results.at[pl.ds(rows, 1)], entries, sem.at[1]),
    ]
    for copy in copies:
        copy.start()
    for copy in copies:
        copy.wait()


def body(tokens, norm_gain, query_weight, w_keyval, w_out, cache_keys, cache_values, lengths):
    width = tokens.shape[2]
    lmax = cache_keys.shape[1]
    qcols = query_weight.shape[1]
    kvcols = w_keyval.shape[1]
    halves = np.arange(HD // 2, dtype=np.float64) * (2.0 / HD)
    freq = (ROPE_BASE ** (-halves)).astype(np.float32)
    freq = jnp.asarray(np.tile(np.concatenate([freq, freq])[None, :], (PR, 1)))
    any_spec = pl.BlockSpec(memory_space=pl.ANY)
    hbm_spec = pl.BlockSpec(memory_space=pltpu.HBM)
    vmem_spec = pl.BlockSpec(memory_space=pltpu.VMEM)
    dma = pltpu.SemaphoreType.DMA
    rows = NH * PR
    results = pl.pallas_call(
        kernel,
        out_shape=pltpu.VMEM((PR + 1, STEPS, width), BF16),
        in_specs=[hbm_spec] * 9,
        out_specs=vmem_spec,
        scratch_shapes=[
            pltpu.SMEM(lengths.shape, jnp.int32),
            pltpu.VMEM(tokens.shape, BF16),
            pltpu.VMEM((OWN, width), BF16),
            pltpu.VMEM((PR, HD), F32),
            pltpu.VMEM((width,), BF16),
            pltpu.VMEM((width, qcols), BF16),
            pltpu.VMEM((width, kvcols), BF16),
            pltpu.VMEM((qcols, width), BF16),
            pltpu.VMEM((lmax, KV_HEADS * HD), BF16),
            pltpu.VMEM((lmax, KV_HEADS * HD), BF16),
            pltpu.VMEM((rows, width), BF16),
            pltpu.VMEM((rows // 2, width), BF16),
            pltpu.VMEM((8, HD), F32),
            pltpu.VMEM((NH - 1, 8, HD), F32),
            pltpu.VMEM((NF, 8, HD), F32),
            pltpu.VMEM((NY, NY, PR, qcols + kvcols), F32),
            pltpu.VMEM((2, NY, PR // 2, LOW), F32),
            pltpu.VMEM((2, NY, PR // 2, qcols + kvcols - LOW), F32),
            pltpu.VMEM((2, NY, PR // 2, LOW), F32),
            pltpu.VMEM((2, NY, PR // 2, qcols + kvcols - LOW), F32),
            pltpu.VMEM((2, NY, PR // 2, LOW), F32),
            pltpu.VMEM((2, NY, PR // 2, qcols + kvcols - LOW), F32),
            pltpu.VMEM((2, NY, PR // 2, qcols + kvcols), F32),
            pltpu.VMEM((2, NY - 1, PR // 2, qcols + kvcols), F32),
            pltpu.VMEM((NF * PR, HD), F32),
            pltpu.VMEM((NF, 2 * PR, HD), BF16),
            pltpu.VMEM((NF, 2 * PR, HD), BF16),
            pltpu.VMEM((HD, KV_HEADS * HD), BF16),
            pltpu.VMEM((HD, KV_HEADS * HD), BF16),
            pltpu.VMEM((8, 2 * KV_HEADS * HD), F32),
            pltpu.VMEM((KV_HEADS * OWN, lmax), F32),
            pltpu.VMEM((PAIRS, 2 * OWN, 2 * HD), F32),
            pltpu.VMEM((NF, PR, HD), BF16),
            pltpu.VMEM((2, 2, NF, PR, HD), BF16),
            pltpu.VMEM((NF * PR, HD), F32),
            pltpu.VMEM((2, NY, 2, PR, qcols), BF16),
            pltpu.VMEM((rows, width), F32),
            pltpu.VMEM((NX, OWN, width), F32),
            pltpu.VMEM((NX - 1, OWN, width), BF16),
            pltpu.VMEM((NX - 1, OWN, width), BF16),
            dma((8,)),
            dma((CACHE_COPIES,)),
            dma((CACHE_COPIES,)),
            dma((NX - 1,)), dma((NX - 1,)),
            dma((NX,)), dma((NX,)),
            dma((NH - 1,)), dma((NH - 1,)),
            dma((NF - 1,)), dma((NF - 1,)),
            dma((2, 6)), dma((2, 6)),
            dma((2, NY - 1)), dma((2, NY - 1)),
            dma((NF - 1,)), dma((NF - 1,)),
            dma((NY,)), dma((2, 2)),
            dma((2, NY - 1)), dma((2, NY - 1)),
            dma((NX,)), dma((NX,)),
            dma((NX - 1,)), dma((NX - 1,)),
        ],
        compiler_params=pltpu.CompilerParams(
            collective_id=0, has_side_effects=True, vmem_limit_bytes=48 * 2**20
        ),
        name="decode_block",
    )(
        *[
            pltpu.with_memory_space_constraint(array, pltpu.HBM)
            for array in (
                lengths, freq, tokens, norm_gain, query_weight, w_keyval, w_out,
                cache_keys, cache_values,
            )
        ],
    )
    return pl.pallas_call(
        hand_out,
        out_shape=(
            jax.ShapeDtypeStruct(tokens.shape, BF16),
            jax.ShapeDtypeStruct((1, STEPS, 2 * KV_HEADS * HD), BF16),
        ),
        in_specs=[vmem_spec],
        out_specs=(any_spec, any_spec),
        scratch_shapes=[dma((2,))],
        name="hand_out",
    )(results)


def solution(mesh):
    in_specs = (
        P("ffn", None, "hid"),
        P("hid"),
        P("hid", "ffn"),
        P("hid", "ffn"),
        P("ffn", "hid"),
        P(("hid", "ffn"), None, None),
        P(("hid", "ffn"), None, None),
        P(),
    )
    out_specs = (P("ffn", None, "hid"), P(("hid", "ffn"), None, None))
    return jax.shard_map(body, mesh=mesh, in_specs=in_specs, out_specs=out_specs, check_vma=False)
```

```python
import functools

import jax
import jax.numpy as jnp
import numpy as np
from jax import lax
from jax.experimental import pallas as pl
from jax.experimental.pallas import tpu as pltpu
from jax.sharding import PartitionSpec as P

MESH = pl.DeviceIdType.MESH
F32 = jnp.float32
BF16 = jnp.bfloat16

HEADS = 64
KV_HEADS = 4
HD = 128
STEPS = 2
EPSILON = 1e-05
ROPE_BASE = 500000.0
SCALE = HD ** (-0.5) * 1.4426950408889634
MASKED = -1e30

NH = 16
NF = 8
NX = 4
NY = 4
LOW = 512
OWN = 32
PR = 16
CHUNK = 4096
CACHE_COPIES = 4
PAIRS = KV_HEADS // 2


def remote(src, dst, send_sem, recv_sem, device):
    return pltpu.make_async_remote_copy(
        src_ref=src,
        dst_ref=dst,
        send_sem=send_sem,
        recv_sem=recv_sem,
        device_id=device,
        device_id_type=MESH,
    )


def rotate(vectors, cosine, sine):
    return vectors * cosine + pltpu.roll(vectors, HD // 2, 1) * sine


def kernel(
    lengths_hbm, freq, tokens, gain, wq, wkv, wout, cache_k, cache_v,
    results,
    lengths, raw_v, tok_v, freq_v, gain_v, wq_v, wkv_v, wout_v, k_v, v_v,
    x_all, normed, ss_own, ss_recv, tot_all, part, relay_low, relay_high, left_low, left_high,
    right_low, right_high, mine, mine_recv,
    spread, msg, qkv, kx, vx, ne, scores, weighted, att_send, att_recv, att_f32, rows_all,
    opart, sib_recv, fin_send, fin_recv,
    local_sem, k_sem, v_sem,
    tok_ssem, tok_rsem, fwd_ssem, fwd_rsem, ss_ssem, ss_rsem, tot_ssem, tot_rsem,
    ring_ssem, ring_rsem, stage_ssem, stage_rsem, msg_ssem, msg_rsem, att_ssem, att_rsem, line_ssem, line_rsem,
    sib_ssem, sib_rsem, fin_ssem, fin_rsem,
):
    h = lax.axis_index("hid")
    f = lax.axis_index("ffn")
    z = lax.div(h, NY)
    y = lax.rem(h, NY)
    cx = lax.div(f, 2)
    core = lax.rem(f, 2)
    sib = f + 1 - 2 * core
    lmax = cache_k.shape[1]

    barrier = pltpu.get_barrier_semaphore()

    def greet_hid(k, carry):
        pl.semaphore_signal(
            barrier, inc=1, device_id=(lax.rem(h + k, NH), f), device_id_type=MESH
        )
        return carry

    def greet_ffn(k, carry):
        pl.semaphore_signal(
            barrier, inc=1, device_id=(h, lax.rem(f + k, NF)), device_id_type=MESH
        )
        return carry

    loads = []
    for i, (src, dst) in enumerate(
        [(tokens, raw_v), (gain, gain_v), (freq, freq_v), (wq, wq_v), (wkv, wkv_v), (lengths_hbm, lengths)]
    ):
        copy = pltpu.make_async_copy(src, dst, local_sem.at[i])
        copy.start()
        loads.append(copy)
    lax.fori_loop(1, NH, greet_hid, 0)
    lax.fori_loop(1, NF, greet_ffn, 0)

    span = lmax // CACHE_COPIES
    k_loads = []
    for i in range(CACHE_COPIES):
        copy = pltpu.make_async_copy(
            cache_k.at[0, pl.ds(i * span, span)], k_v.at[pl.ds(i * span, span)], k_sem.at[i]
        )
        copy.start()
        k_loads.append(copy)
    loads[0].wait()
    x_f32 = raw_v[...].astype(F32).reshape(tok_v.shape)
    x_own = x_f32.astype(BF16)
    tok_v[...] = x_own
    sums = jnp.sum(x_f32 * x_f32, axis=1, keepdims=True)
    row_id = lax.broadcasted_iota(jnp.int32, (OWN, HD), 0)
    lane_id = lax.broadcasted_iota(jnp.int32, (OWN, HD), 1)
    diagonal = row_id == lane_id
    own_sums = jnp.sum(jnp.where(diagonal, sums, 0.0), axis=0, keepdims=True)
    ss_own[...] = jnp.broadcast_to(own_sums, (8, HD))

    pl.semaphore_wait(barrier, NH + NF - 2)

    def block(index):
        return x_all.at[pl.ds(pl.multiple_of(index * OWN, OWN), OWN)]

    def ss_copy(k):
        return remote(
            ss_own, ss_recv.at[k - 1], ss_ssem.at[k - 1], ss_rsem.at[k - 1],
            (lax.rem(h + k, NH), f),
        )

    def ss_start(k, carry):
        ss_copy(k).start()
        return carry

    lax.fori_loop(1, NH, ss_start, 0)
    tok_copies = []
    for k in range(1, NX):
        peer = 2 * lax.rem(cx + k, NX) + core
        copy = remote(tok_v, block(f), tok_ssem.at[k - 1], tok_rsem.at[k - 1], (h, peer))
        copy.start()
        tok_copies.append(copy)
    fwd_copies = [remote(tok_v, block(f), fwd_ssem.at[0], fwd_rsem.at[0], (h, sib))]
    fwd_copies[0].start()
    x_all[pl.ds(pl.multiple_of(f * OWN, OWN), OWN), :] = x_own

    def ss_add(k, total):
        ss_copy(k).wait()
        return total + ss_recv[k - 1]

    total = lax.fori_loop(1, NH, ss_add, ss_own[...])
    tot_all[f] = total
    tot_copies = []
    for k in range(1, NF):
        copy = remote(
            tot_all.at[f], tot_all.at[f], tot_ssem.at[k - 1], tot_rsem.at[k - 1],
            (h, lax.rem(f + k, NF)),
        )
        copy.start()
        tot_copies.append(copy)
    for k in range(1, NX):
        tok_copies[k - 1].wait_recv()
        came = 2 * lax.rem(cx + NX - k, NX) + core
        copy = remote(block(came), block(came), fwd_ssem.at[k], fwd_rsem.at[k], (h, sib))
        copy.start()
        fwd_copies.append(copy)

    loads[5].wait()
    length = lengths[h * NF + f]
    step_of = lax.div(lax.broadcasted_iota(jnp.int32, (PR, HD), 0), 8)
    loads[2].wait()
    angles = (step_of + length).astype(F32) * freq_v[...]
    cosine = jnp.cos(angles)
    sine = jnp.sin(angles)
    sine = jnp.where(
        lax.broadcasted_iota(jnp.int32, (PR, HD), 1) < HD // 2, -sine, sine
    )

    for copy in tot_copies:
        copy.wait()
    loads[1].wait()
    width = x_all.shape[1]
    qcols = wq_v.shape[1]
    full = width * NH
    gain_row = gain_v[...].astype(F32).reshape(1, width)

    def project(parity):
        for x in range(NX):
            b = 2 * x + parity
            lane_sums = tot_all[b][0:1, :]
            row_sums = jnp.sum(jnp.where(diagonal, lane_sums, 0.0), axis=1, keepdims=True)
            inverse = lax.rsqrt(row_sums / full + EPSILON)
            normed[x * OWN : (x + 1) * OWN, :] = (
                block(b)[...].astype(F32) * inverse * gain_row
            ).astype(BF16)
        lhs = normed[...]
        for cols, weights in ((slice(0, qcols), wq_v), (slice(qcols, None), wkv_v)):
            product = jnp.dot(lhs, weights[...], preferred_element_type=F32)
            part[:, pl.ds(2 * parity, 2), :, cols] = product.reshape(NX, 2, PR, product.shape[1])

    loads[3].wait()
    loads[4].wait()
    project(core)
    for copy in fwd_copies:
        copy.wait()
    for copy in tok_copies:
        copy.wait_send()
    project(1 - core)

    half = PR // 2
    low, high_cols = pl.ds(0, LOW), pl.ds(LOW, part.shape[3] - LOW)

    def ring(side):
        pos = (y, z)[side]

        def device(q):
            return (z * NY + q, f) if side == 0 else (q * NY + y, f)

        def view(q, cols):
            if side == 0:
                return part.at[:, q, pl.ds(0, half), cols]
            return part.at[q, :, pl.ds(half, half), cols]

        return pos, device, view

    after = {}
    for side in range(2):
        pos, device, view = ring(side)
        nxt, prv, far = lax.rem(pos + 1, NY), lax.rem(pos + 3, NY), lax.rem(pos + 2, NY)
        plan = [
            (view(far, low), relay_low, nxt),
            (view(far, high_cols), relay_high, prv),
            (view(nxt, high_cols), left_high, nxt),
            (view(prv, low), right_low, prv),
        ]
        copies = [
            remote(
                src, dst.at[side], ring_ssem.at[side, i], ring_rsem.at[side, i], device(to)
            )
            for i, (src, dst, to) in enumerate(plan)
        ]
        after[side] = copies
    for first in (0, 2):
        for side in range(2):
            for copy in after[side][first : first + 2]:
                copy.start()
    v_loads = []
    for i in range(CACHE_COPIES):
        copy = pltpu.make_async_copy(
            cache_v.at[0, pl.ds(i * span, span)], v_v.at[pl.ds(i * span, span)], v_sem.at[i]
        )
        copy.start()
        v_loads.append(copy)
    wout_load = pltpu.make_async_copy(wout, wout_v, local_sem.at[6])
    wout_load.start()
    for side in range(2):
        pos, device, view = ring(side)
        nxt, prv = lax.rem(pos + 1, NY), lax.rem(pos + 3, NY)
        plan = [
            (view(nxt, low), relay_low, left_low, nxt),
            (view(prv, high_cols), relay_high, right_high, prv),
        ]
        for i, (own, relay, dst, to) in enumerate(plan):
            after[side][i].wait_recv()
            relay[side] = relay[side] + own[...]
            copy = remote(
                relay.at[side], dst.at[side],
                ring_ssem.at[side, 4 + i], ring_rsem.at[side, 4 + i], device(to),
            )
            copy.start()
            after[side].append(copy)
    stage_copies = {}
    for side in range(2):
        pos, device, view = ring(side)
        for copy in after[side][2:]:
            copy.wait_recv()
        mine[side, :, :, :LOW] = view(pos, low)[...] + left_low[side] + right_low[side]
        mine[side, :, :, LOW:] = view(pos, high_cols)[...] + left_high[side] + right_high[side]
        other, other_device, _ = ring(1 - side)
        stage_copies[side] = []
        for k in range(1, NY):
            peer = lax.rem(other + k, NY)
            copy = remote(
                mine.at[side, peer], mine_recv.at[side, k - 1],
                stage_ssem.at[side, k - 1], stage_rsem.at[side, k - 1], other_device(peer),
            )
            copy.start()
            stage_copies[side].append(copy)
    halves = []
    for side in range(2):
        other = ring(1 - side)[0]
        total = mine[side, other]
        for k in range(1, NY):
            stage_copies[side][k - 1].wait()
            total = total + mine_recv[side, k - 1]
        halves.append(total)
        for copy in after[side]:
            copy.wait_send()
    summed = jnp.concatenate(halves, axis=0)

    for j in range(8):
        spread[pl.ds(j, PR, stride=8), :] = summed[:, j * HD : (j + 1) * HD]
    msg[:, :PR, :] = spread[...].reshape(NF, PR, HD).astype(BF16)
    spread[...] = jnp.zeros_like(spread)
    spread[pl.ds(0, PR, stride=8), :] = summed[:, qcols:]
    msg[:, PR:, :] = spread[...].reshape(NF, PR, HD).astype(BF16)
    qkv[f] = msg[f]
    msg_copies = []
    for k in range(1, NF):
        peer = lax.rem(f + k, NF)
        copy = remote(
            msg.at[peer], qkv.at[f], msg_ssem.at[k - 1], msg_rsem.at[k - 1], (h, peer)
        )
        copy.start()
        msg_copies.append(copy)
    for copy in msg_copies:
        copy.wait()

    kx[...] = jnp.zeros_like(kx)
    vx[...] = jnp.zeros_like(vx)
    fresh_rows = []
    for i in range(2 * KV_HEADS):
        raw = qkv[i, PR:, :].astype(F32)
        cols = pl.ds((i % KV_HEADS) * HD, HD)
        if i < KV_HEADS:
            raw = rotate(raw, cosine, sine)
            kx[:PR, cols] = raw.astype(BF16)
        else:
            vx[:PR, cols] = raw.astype(BF16)
        fresh_rows.append(raw)

    rotated = [
        rotate(qkv[i, :PR, :].astype(F32), cosine, sine).astype(BF16) for i in range(NF)
    ]
    nothing = jnp.zeros((OWN, HD), BF16)
    queries = []
    for p in range(PAIRS):
        upper = jnp.concatenate(rotated[4 * p : 4 * p + 2], axis=0)
        lower = jnp.concatenate(rotated[4 * p + 2 : 4 * p + 4], axis=0)
        queries.append(
            jnp.concatenate(
                [
                    jnp.concatenate([upper, nothing], axis=1),
                    jnp.concatenate([nothing, lower], axis=1),
                ],
                axis=0,
            )
        )
    pair_rows, pair_cols = 2 * OWN, 2 * HD
    lane = lax.broadcasted_iota(jnp.int32, (pair_rows, HD), 1)
    step_row = lax.rem(lax.div(lax.broadcasted_iota(jnp.int32, (pair_rows, HD), 0), 8), 2)
    fresh_live = (lane == 0) | ((lane == 8) & (step_row == 1))
    nt = (((1,), (1,)), ((), ()))
    def attend(p):
        pair = pl.ds(p * pair_cols, pair_cols)
        rows_of = pl.ds(p * pair_rows, pair_rows)
        fresh = lax.dot_general(queries[p], kx[:, pair], nt, preferred_element_type=F32)
        fresh = jnp.where(fresh_live, fresh * SCALE, MASKED)

        def score_step(c, high):
            rows = pl.ds(pl.multiple_of(c * CHUNK, CHUNK), CHUNK)
            position = lax.broadcasted_iota(jnp.int32, (8, CHUNK), 1) + c * CHUNK
            cap = jnp.where(position < length, -MASKED, MASKED)
            cap = jnp.concatenate([cap] * (pair_rows // 8), axis=0)
            s = lax.dot_general(queries[p], k_v[rows, pair], nt, preferred_element_type=F32)
            s = jnp.minimum(s * SCALE, cap)
            scores[rows_of, rows] = s
            for t in range(CHUNK // HD):
                high = jnp.maximum(high, s[:, t * HD : (t + 1) * HD])
            return high

        high = lax.fori_loop(0, lmax // CHUNK, score_step, fresh)
        peak = jnp.broadcast_to(jnp.max(high, axis=1, keepdims=True), (pair_rows, HD))
        weights = jnp.exp2(fresh - peak).astype(BF16)
        weighted[p] = jnp.dot(weights, vx[:, pair], preferred_element_type=F32)

        def value_step(c, total):
            rows = pl.ds(pl.multiple_of(c * CHUNK, CHUNK), CHUNK)
            s = scores[rows_of, rows]
            pieces = []
            for t in range(CHUNK // HD):
                piece = jnp.exp2(s[:, t * HD : (t + 1) * HD] - peak).astype(BF16)
                total = total + piece.astype(F32)
                pieces.append(piece)
            weighted[p] += jnp.dot(
                jnp.concatenate(pieces, axis=1), v_v[rows, pair], preferred_element_type=F32
            )
            return total

        if p == 0:
            for copy in v_loads:
                copy.wait()
        total = lax.fori_loop(0, lmax // CHUNK, value_step, weights.astype(F32))
        weight_sum = jnp.sum(total, axis=1, keepdims=True)
        for i in range(2):
            rows = slice(i * OWN, (i + 1) * OWN)
            attended = weighted[p, rows, i * HD : (i + 1) * HD] / weight_sum[rows]
            attended = attended.astype(BF16)
            att_send[4 * p + 2 * i] = attended[:PR]
            att_send[4 * p + 2 * i + 1] = attended[PR:]

    odd = lax.rem(y + z, 2)
    slot = lax.rem(lax.div(y, 2) + lax.div(z, 2), 2)

    def send_attended(p):
        for m in range(4):
            peer = 4 * p + lax.rem(f + m, 4)
            landing = att_recv.at[odd, slot, f]

            @pl.when(peer == f)
            def _():
                pltpu.make_async_copy(
                    att_send.at[f], landing, att_rsem.at[odd, slot]
                ).start()

            for k in range(NY):
                chip = lax.rem(z + odd * k, NY) * NY + lax.rem(y + (1 - odd) * k, NY)
                copy = remote(
                    att_send.at[peer], landing, att_ssem.at[k], att_rsem.at[odd, slot],
                    (chip, peer),
                )
                if k == 0:
                    pl.when(peer != f)(copy.start)
                else:
                    copy.start()

    for copy in k_loads:
        copy.wait()
    for p in range(PAIRS):
        attend(p)
        send_attended(p)

    for i in range(2 * KV_HEADS):
        ne[0:1, i * HD : (i + 1) * HD] = fresh_rows[i][0:1]
        ne[1:2, i * HD : (i + 1) * HD] = fresh_rows[i][8:9]
    results[PR:, :, :] = ne[0:2, :].reshape(1, STEPS, ne.shape[1]).astype(BF16)

    line_copies = [[], []]
    for part_id in range(2):
        for side in range(2):
            whole = att_recv.at[side, part_id]
            pltpu.make_async_copy(whole, whole, att_rsem.at[side, part_id]).wait()
            pos = (z, y)[side]
            att_f32[...] = att_recv[side, part_id].astype(F32).reshape(NF * PR, HD)
            for j in range(8):
                rows_all[part_id, side, pos, :, j * HD : (j + 1) * HD] = att_f32[
                    pl.ds(j, PR, stride=8), :
                ].astype(BF16)
            mine_rows = rows_all.at[part_id, side, pos]
            for k in range(1, NY):
                q = lax.rem(pos + k, NY)
                device = (q * NY + y, f) if side == 0 else (z * NY + q, f)
                copy = remote(
                    mine_rows, mine_rows,
                    line_ssem.at[part_id, side, k - 1], line_rsem.at[part_id, side, k - 1],
                    device,
                )
                copy.start()
                line_copies[part_id].append(copy)
    wout_load.wait()

    def out_rows(index):
        return pl.ds(pl.multiple_of(index * OWN, OWN), OWN)

    sib_copies = [[], []]
    for part_id in range(2):
        for copy in line_copies[part_id]:
            copy.wait_recv()
        product = jnp.dot(
            rows_all[part_id].reshape(NH * PR // 2, wout_v.shape[0]),
            wout_v[...],
            preferred_element_type=F32,
        )
        for side in range(2):
            for q in range(NY):
                far = 2 * ((part_id + q // 2) % 2) + (q + side) % 2
                home = q * NY + far if side == 0 else far * NY + q
                first = (side * NY + q) * PR
                opart[home * PR : (home + 1) * PR, :] = product[first : first + PR]
        for e in range(2):
            x = 2 * lax.rem(1 + core + part_id, 2) + e
            copy = remote(
                opart.at[out_rows(2 * x + 1 - core)], sib_recv.at[part_id, e],
                sib_ssem.at[part_id, e], sib_rsem.at[part_id, e], (h, sib),
            )
            copy.start()
            sib_copies[part_id].append(copy)
    fin_copies = []
    for part_id in range(2):
        for copy in sib_copies[part_id]:
            copy.wait_recv()
        for e in range(2):
            x = 2 * lax.rem(core + part_id, 2) + e
            hop = lax.rem(x - cx + NX, NX)
            there = lax.rem(hop + NX - 1, NX)
            copy = remote(
                fin_send.at[part_id, e], fin_recv.at[there],
                fin_ssem.at[part_id, e], fin_rsem.at[there], (h, 2 * x + core),
            )
            fin_copies.append((hop, copy))

            @pl.when(hop != 0)
            def _():
                total = opart[out_rows(2 * x + core), :] + sib_recv[part_id, e]
                fin_send[part_id, e] = total.astype(BF16)
                copy.start()

    own_part = lax.rem(core + lax.div(cx, 2), 2)
    result = opart[out_rows(f), :] + sib_recv[own_part, lax.rem(cx, 2)]
    for k in range(1, NX):
        pltpu.make_async_copy(
            fin_recv.at[k - 1], fin_recv.at[k - 1], fin_rsem.at[k - 1]
        ).wait()
        result = result + fin_recv[k - 1].astype(F32)
    results[:PR, :, :] = result.reshape(PR, STEPS, result.shape[1]).astype(BF16)
    for hop, copy in fin_copies:
        pl.when(hop != 0)(copy.wait_send)
    for copies in sib_copies + line_copies:
        for copy in copies:
            copy.wait_send()
    for k in range(NY):
        sent = att_send.at[pl.ds(0, NF - 1)] if k == 0 else att_send
        pltpu.make_async_copy(sent, sent, att_ssem.at[k]).wait()


def hand_out(results, out, entries, sem):
    rows = out.shape[0]
    copies = [
        pltpu.make_async_copy(results.at[pl.ds(0, rows)], out, sem.at[0]),
        pltpu.make_async_copy(results.at[pl.ds(rows, 1)], entries, sem.at[1]),
    ]
    for copy in copies:
        copy.start()
    for copy in copies:
        copy.wait()


def body(tokens, norm_gain, query_weight, w_keyval, w_out, cache_keys, cache_values, lengths):
    width = tokens.shape[2]
    lmax = cache_keys.shape[1]
    qcols = query_weight.shape[1]
    kvcols = w_keyval.shape[1]
    halves = np.arange(HD // 2, dtype=np.float64) * (2.0 / HD)
    freq = (ROPE_BASE ** (-halves)).astype(np.float32)
    freq = jnp.asarray(np.tile(np.concatenate([freq, freq])[None, :], (PR, 1)))
    any_spec = pl.BlockSpec(memory_space=pl.ANY)
    hbm_spec = pl.BlockSpec(memory_space=pltpu.HBM)
    vmem_spec = pl.BlockSpec(memory_space=pltpu.VMEM)
    dma = pltpu.SemaphoreType.DMA
    rows = NH * PR
    results = pl.pallas_call(
        kernel,
        out_shape=pltpu.VMEM((PR + 1, STEPS, width), BF16),
        in_specs=[hbm_spec] * 9,
        out_specs=vmem_spec,
        scratch_shapes=[
            pltpu.SMEM(lengths.shape, jnp.int32),
            pltpu.VMEM(tokens.shape, BF16),
            pltpu.VMEM((OWN, width), BF16),
            pltpu.VMEM((PR, HD), F32),
            pltpu.VMEM((width,), BF16),
            pltpu.VMEM((width, qcols), BF16),
            pltpu.VMEM((width, kvcols), BF16),
            pltpu.VMEM((qcols, width), BF16),
            pltpu.VMEM((lmax, KV_HEADS * HD), BF16),
            pltpu.VMEM((lmax, KV_HEADS * HD), BF16),
            pltpu.VMEM((rows, width), BF16),
            pltpu.VMEM((rows // 2, width), BF16),
            pltpu.VMEM((8, HD), F32),
            pltpu.VMEM((NH - 1, 8, HD), F32),
            pltpu.VMEM((NF, 8, HD), F32),
            pltpu.VMEM((NY, NY, PR, qcols + kvcols), F32),
            pltpu.VMEM((2, NY, PR // 2, LOW), F32),
            pltpu.VMEM((2, NY, PR // 2, qcols + kvcols - LOW), F32),
            pltpu.VMEM((2, NY, PR // 2, LOW), F32),
            pltpu.VMEM((2, NY, PR // 2, qcols + kvcols - LOW), F32),
            pltpu.VMEM((2, NY, PR // 2, LOW), F32),
            pltpu.VMEM((2, NY, PR // 2, qcols + kvcols - LOW), F32),
            pltpu.VMEM((2, NY, PR // 2, qcols + kvcols), F32),
            pltpu.VMEM((2, NY - 1, PR // 2, qcols + kvcols), F32),
            pltpu.VMEM((NF * PR, HD), F32),
            pltpu.VMEM((NF, 2 * PR, HD), BF16),
            pltpu.VMEM((NF, 2 * PR, HD), BF16),
            pltpu.VMEM((HD, KV_HEADS * HD), BF16),
            pltpu.VMEM((HD, KV_HEADS * HD), BF16),
            pltpu.VMEM((8, 2 * KV_HEADS * HD), F32),
            pltpu.VMEM((KV_HEADS * OWN, lmax), F32),
            pltpu.VMEM((PAIRS, 2 * OWN, 2 * HD), F32),
            pltpu.VMEM((NF, PR, HD), BF16),
            pltpu.VMEM((2, 2, NF, PR, HD), BF16),
            pltpu.VMEM((NF * PR, HD), F32),
            pltpu.VMEM((2, 2, NY, PR, qcols), BF16),
            pltpu.VMEM((rows, width), F32),
            pltpu.VMEM((2, 2, OWN, width), F32),
            pltpu.VMEM((2, 2, OWN, width), BF16),
            pltpu.VMEM((NX - 1, OWN, width), BF16),
            dma((8,)),
            dma((CACHE_COPIES,)),
            dma((CACHE_COPIES,)),
            dma((NX - 1,)), dma((NX - 1,)),
            dma((NX,)), dma((NX,)),
            dma((NH - 1,)), dma((NH - 1,)),
            dma((NF - 1,)), dma((NF - 1,)),
            dma((2, 6)), dma((2, 6)),
            dma((2, NY - 1)), dma((2, NY - 1)),
            dma((NF - 1,)), dma((NF - 1,)),
            dma((NY,)), dma((2, 2)),
            dma((2, 2, NY - 1)), dma((2, 2, NY - 1)),
            dma((2, 2)), dma((2, 2)),
            dma((2, 2)), dma((NX - 1,)),
        ],
        compiler_params=pltpu.CompilerParams(
            collective_id=0, has_side_effects=True, vmem_limit_bytes=48 * 2**20
        ),
        name="decode_block",
    )(
        *[
            pltpu.with_memory_space_constraint(array, pltpu.HBM)
            for array in (
                lengths, freq, tokens, norm_gain, query_weight, w_keyval, w_out,
                cache_keys, cache_values,
            )
        ],
    )
    return pl.pallas_call(
        hand_out,
        out_shape=(
            jax.ShapeDtypeStruct(tokens.shape, BF16),
            jax.ShapeDtypeStruct((1, STEPS, 2 * KV_HEADS * HD), BF16),
        ),
        in_specs=[vmem_spec],
        out_specs=(any_spec, any_spec),
        scratch_shapes=[dma((2,))],
        name="hand_out",
    )(pltpu.with_memory_space_constraint(results, pltpu.VMEM))


def solution(mesh):
    in_specs = (
        P("ffn", None, "hid"),
        P("hid"),
        P("hid", "ffn"),
        P("hid", "ffn"),
        P("ffn", "hid"),
        P(("hid", "ffn"), None, None),
        P(("hid", "ffn"), None, None),
        P(),
    )
    out_specs = (P("ffn", None, "hid"), P(("hid", "ffn"), None, None))
    return jax.shard_map(body, mesh=mesh, in_specs=in_specs, out_specs=out_specs, check_vma=False)
```

```python
import functools

import jax
import jax.numpy as jnp
import numpy as np
from jax import lax
from jax.experimental import pallas as pl
from jax.experimental.pallas import tpu as pltpu
from jax.sharding import PartitionSpec as P

MESH = pl.DeviceIdType.MESH
F32 = jnp.float32
BF16 = jnp.bfloat16

HEADS = 64
KV_HEADS = 4
HD = 128
STEPS = 2
EPSILON = 1e-05
ROPE_BASE = 500000.0
SCALE = HD ** (-0.5) * 1.4426950408889634
MASKED = -1e30

NH = 16
NF = 8
NX = 4
NY = 4
LOW = 512
OWN = 32
PR = 16
CHUNK = 4096
CACHE_COPIES = 4
PAIRS = KV_HEADS // 2


def remote(src, dst, send_sem, recv_sem, device):
    return pltpu.make_async_remote_copy(
        src_ref=src,
        dst_ref=dst,
        send_sem=send_sem,
        recv_sem=recv_sem,
        device_id=device,
        device_id_type=MESH,
    )


def rotate(vectors, cosine, sine):
    return vectors * cosine + pltpu.roll(vectors, HD // 2, 1) * sine


def kernel(
    lengths_hbm, freq, tokens, gain, wq, wkv, wout, cache_k, cache_v,
    results,
    lengths, raw_v, tok_v, freq_v, gain_v, wq_v, wkv_v, wout_v, k_v, v_v,
    x_all, normed, ss_own, ss_recv, tot_all, part, relay_low, relay_high, left_low, left_high,
    right_low, right_high, mine, mine_recv,
    spread, msg, qkv, kx, vx, ne, scores, weighted, att_send, att_recv, att_f32, rows_all,
    opart, sib_recv, fin_send, fin_recv,
    local_sem, k_sem, v_sem,
    tok_ssem, tok_rsem, fwd_ssem, fwd_rsem, ss_ssem, ss_rsem, tot_ssem, tot_rsem,
    ring_ssem, ring_rsem, stage_ssem, stage_rsem, msg_ssem, msg_rsem, att_ssem, att_rsem, line_ssem, line_rsem,
    sib_ssem, sib_rsem, fin_ssem, fin_rsem,
):
    h = lax.axis_index("hid")
    f = lax.axis_index("ffn")
    z = lax.div(h, NY)
    y = lax.rem(h, NY)
    cx = lax.div(f, 2)
    core = lax.rem(f, 2)
    sib = f + 1 - 2 * core
    lmax = cache_k.shape[1]

    barrier = pltpu.get_barrier_semaphore()
    tokens_load = pltpu.make_async_copy(tokens, raw_v, local_sem.at[0])
    tokens_load.start()

    def greet_hid(k, carry):
        pl.semaphore_signal(
            barrier, inc=1, device_id=(lax.rem(h + k, NH), f), device_id_type=MESH
        )
        return carry

    def greet_ffn(k, carry):
        pl.semaphore_signal(
            barrier, inc=1, device_id=(h, lax.rem(f + k, NF)), device_id_type=MESH
        )
        return carry

    lax.fori_loop(1, NF, greet_ffn, 0)
    lax.fori_loop(1, NH, greet_hid, 0)

    loads = []
    for i, (src, dst) in enumerate(
        [(gain, gain_v), (freq, freq_v), (wq, wq_v), (wkv, wkv_v), (lengths_hbm, lengths)]
    ):
        copy = pltpu.make_async_copy(src, dst, local_sem.at[1 + i])
        copy.start()
        loads.append(copy)
    span = lmax // CACHE_COPIES
    k_loads = []
    for i in range(CACHE_COPIES):
        copy = pltpu.make_async_copy(
            cache_k.at[0, pl.ds(i * span, span)], k_v.at[pl.ds(i * span, span)], k_sem.at[i]
        )
        copy.start()
        k_loads.append(copy)
    wout_load = pltpu.make_async_copy(wout, wout_v, local_sem.at[6])
    wout_load.start()

    tokens_load.wait()
    x_f32 = raw_v[...].astype(F32).reshape(tok_v.shape)
    x_own = x_f32.astype(BF16)
    tok_v[...] = x_own
    pl.semaphore_wait(barrier, NH + NF - 2)

    def block(index):
        return x_all.at[pl.ds(pl.multiple_of(index * OWN, OWN), OWN)]

    tok_copies = []
    for k in (1, 3, 2):
        peer = 2 * lax.rem(cx + k, NX) + core
        copy = remote(tok_v, block(f), tok_ssem.at[k - 1], tok_rsem.at[k - 1], (h, peer))
        copy.start()
        tok_copies.append((k, copy))
    fwd_copies = [remote(tok_v, block(f), fwd_ssem.at[0], fwd_rsem.at[0], (h, sib))]
    fwd_copies[0].start()

    sums = jnp.sum(x_f32 * x_f32, axis=1, keepdims=True)
    row_id = lax.broadcasted_iota(jnp.int32, (OWN, HD), 0)
    lane_id = lax.broadcasted_iota(jnp.int32, (OWN, HD), 1)
    diagonal = row_id == lane_id
    own_sums = jnp.sum(jnp.where(diagonal, sums, 0.0), axis=0, keepdims=True)
    ss_own[...] = jnp.broadcast_to(own_sums, (8, HD))

    def ss_copy(k):
        return remote(
            ss_own, ss_recv.at[k - 1], ss_ssem.at[k - 1], ss_rsem.at[k - 1],
            (lax.rem(h + k, NH), f),
        )

    def ss_start(k, carry):
        ss_copy(k).start()
        return carry

    lax.fori_loop(1, NH, ss_start, 0)
    x_all[pl.ds(pl.multiple_of(f * OWN, OWN), OWN), :] = x_own

    def ss_add(k, total):
        ss_copy(k).wait_recv()
        return total + ss_recv[k - 1]

    total = lax.fori_loop(1, NH, ss_add, ss_own[...])
    tot_all[f] = total
    tot_copies = []
    for k in range(1, NF):
        copy = remote(
            tot_all.at[f], tot_all.at[f], tot_ssem.at[k - 1], tot_rsem.at[k - 1],
            (h, lax.rem(f + k, NF)),
        )
        copy.start()
        tot_copies.append(copy)
    for k, tok_copy in tok_copies:
        tok_copy.wait_recv()
        came = 2 * lax.rem(cx + NX - k, NX) + core
        copy = remote(block(came), block(came), fwd_ssem.at[k], fwd_rsem.at[k], (h, sib))
        copy.start()
        fwd_copies.append(copy)

    loads[4].wait()
    length = lengths[h * NF + f]
    step_of = lax.div(lax.broadcasted_iota(jnp.int32, (PR, HD), 0), 8)
    loads[1].wait()
    angles = (step_of + length).astype(F32) * freq_v[...]
    cosine = jnp.cos(angles)
    sine = jnp.sin(angles)
    sine = jnp.where(
        lax.broadcasted_iota(jnp.int32, (PR, HD), 1) < HD // 2, -sine, sine
    )

    kx[...] = jnp.zeros_like(kx)
    vx[...] = jnp.zeros_like(vx)
    for copy in tot_copies:
        copy.wait_recv()
    loads[0].wait()
    width = x_all.shape[1]
    qcols = wq_v.shape[1]
    full = width * NH
    gain_row = gain_v[...].astype(F32).reshape(1, width)

    def project(parity):
        for x in range(NX):
            b = 2 * x + parity
            lane_sums = tot_all[b][0:1, :]
            row_sums = jnp.sum(jnp.where(diagonal, lane_sums, 0.0), axis=1, keepdims=True)
            inverse = lax.rsqrt(row_sums / full + EPSILON)
            normed[x * OWN : (x + 1) * OWN, :] = (
                block(b)[...].astype(F32) * inverse * gain_row
            ).astype(BF16)
        lhs = normed[...]
        for cols, weights in ((slice(0, qcols), wq_v), (slice(qcols, None), wkv_v)):
            product = jnp.dot(lhs, weights[...], preferred_element_type=F32)
            part[:, pl.ds(2 * parity, 2), :, cols] = product.reshape(NX, 2, PR, product.shape[1])

    loads[2].wait()
    loads[3].wait()
    project(core)
    for copy in fwd_copies:
        copy.wait_recv()
    project(1 - core)

    half = PR // 2
    low, high_cols = pl.ds(0, LOW), pl.ds(LOW, part.shape[3] - LOW)

    def ring(side):
        pos = (y, z)[side]

        def device(q):
            return (z * NY + q, f) if side == 0 else (q * NY + y, f)

        def view(q, cols):
            if side == 0:
                return part.at[:, q, pl.ds(0, half), cols]
            return part.at[q, :, pl.ds(half, half), cols]

        return pos, device, view

    after = {}
    for side in range(2):
        pos, device, view = ring(side)
        nxt, prv, far = lax.rem(pos + 1, NY), lax.rem(pos + 3, NY), lax.rem(pos + 2, NY)
        plan = [
            (view(far, low), relay_low, nxt),
            (view(far, high_cols), relay_high, prv),
            (view(nxt, high_cols), left_high, nxt),
            (view(prv, low), right_low, prv),
        ]
        copies = [
            remote(
                src, dst.at[side], ring_ssem.at[side, i], ring_rsem.at[side, i], device(to)
            )
            for i, (src, dst, to) in enumerate(plan)
        ]
        after[side] = copies
    for first in (0, 2):
        for side in range(2):
            for copy in after[side][first : first + 2]:
                copy.start()
    v_loads = []
    for i in range(CACHE_COPIES):
        copy = pltpu.make_async_copy(
            cache_v.at[0, pl.ds(i * span, span)], v_v.at[pl.ds(i * span, span)], v_sem.at[i]
        )
        copy.start()
        v_loads.append(copy)

    def ss_sent(k, carry):
        ss_copy(k).wait_send()
        return carry

    lax.fori_loop(1, NH, ss_sent, 0)
    for copy in tot_copies + fwd_copies + [copy for _, copy in tok_copies]:
        copy.wait_send()
    for side in range(2):
        pos, device, view = ring(side)
        nxt, prv = lax.rem(pos + 1, NY), lax.rem(pos + 3, NY)
        plan = [
            (view(nxt, low), relay_low, left_low, nxt),
            (view(prv, high_cols), relay_high, right_high, prv),
        ]
        for i, (own, relay, dst, to) in enumerate(plan):
            after[side][i].wait_recv()
            relay[side] = relay[side] + own[...]
            copy = remote(
                relay.at[side], dst.at[side],
                ring_ssem.at[side, 4 + i], ring_rsem.at[side, 4 + i], device(to),
            )
            copy.start()
            after[side].append(copy)
    stage_copies = {}
    for side in range(2):
        pos, device, view = ring(side)
        for copy in after[side][2:]:
            copy.wait_recv()
        mine[side, :, :, :LOW] = view(pos, low)[...] + left_low[side] + right_low[side]
        mine[side, :, :, LOW:] = view(pos, high_cols)[...] + left_high[side] + right_high[side]
        other, other_device, _ = ring(1 - side)
        stage_copies[side] = []
        for k in range(1, NY):
            peer = lax.rem(other + k, NY)
            copy = remote(
                mine.at[side, peer], mine_recv.at[side, k - 1],
                stage_ssem.at[side, k - 1], stage_rsem.at[side, k - 1], other_device(peer),
            )
            copy.start()
            stage_copies[side].append(copy)
    halves = []
    for side in range(2):
        other = ring(1 - side)[0]
        total = mine[side, other]
        for k in range(1, NY):
            stage_copies[side][k - 1].wait_recv()
            total = total + mine_recv[side, k - 1]
        halves.append(total)
    summed = jnp.concatenate(halves, axis=0)

    for j in range(8):
        spread[pl.ds(j, PR, stride=8), :] = summed[:, j * HD : (j + 1) * HD]
    msg[:, :PR, :] = spread[...].reshape(NF, PR, HD).astype(BF16)
    spread[...] = jnp.zeros_like(spread)
    spread[pl.ds(0, PR, stride=8), :] = summed[:, qcols:]
    msg[:, PR:, :] = spread[...].reshape(NF, PR, HD).astype(BF16)
    qkv[f] = msg[f]
    msg_copies = []
    for k in range(1, NF):
        peer = lax.rem(f + k, NF)
        copy = remote(
            msg.at[peer], qkv.at[f], msg_ssem.at[k - 1], msg_rsem.at[k - 1], (h, peer)
        )
        copy.start()
        msg_copies.append(copy)
    for side in range(2):
        for copy in after[side] + stage_copies[side]:
            copy.wait_send()
    for copy in msg_copies:
        copy.wait_recv()

    fresh_rows = []
    for i in range(2 * KV_HEADS):
        raw = qkv[i, PR:, :].astype(F32)
        cols = pl.ds((i % KV_HEADS) * HD, HD)
        if i < KV_HEADS:
            raw = rotate(raw, cosine, sine)
            kx[:PR, cols] = raw.astype(BF16)
        else:
            vx[:PR, cols] = raw.astype(BF16)
        fresh_rows.append(raw)

    rotated = [
        rotate(qkv[i, :PR, :].astype(F32), cosine, sine).astype(BF16) for i in range(NF)
    ]
    nothing = jnp.zeros((OWN, HD), BF16)
    queries = []
    for p in range(PAIRS):
        upper = jnp.concatenate(rotated[4 * p : 4 * p + 2], axis=0)
        lower = jnp.concatenate(rotated[4 * p + 2 : 4 * p + 4], axis=0)
        queries.append(
            jnp.concatenate(
                [
                    jnp.concatenate([upper, nothing], axis=1),
                    jnp.concatenate([nothing, lower], axis=1),
                ],
                axis=0,
            )
        )
    pair_rows, pair_cols = 2 * OWN, 2 * HD
    lane = lax.broadcasted_iota(jnp.int32, (pair_rows, HD), 1)
    step_row = lax.rem(lax.div(lax.broadcasted_iota(jnp.int32, (pair_rows, HD), 0), 8), 2)
    fresh_live = (lane == 0) | ((lane == 8) & (step_row == 1))
    nt = (((1,), (1,)), ((), ()))
    def attend(p):
        pair = pl.ds(p * pair_cols, pair_cols)
        rows_of = pl.ds(p * pair_rows, pair_rows)
        fresh = lax.dot_general(queries[p], kx[:, pair], nt, preferred_element_type=F32)
        fresh = jnp.where(fresh_live, fresh * SCALE, MASKED)

        def score_step(c, high):
            rows = pl.ds(pl.multiple_of(c * CHUNK, CHUNK), CHUNK)
            position = lax.broadcasted_iota(jnp.int32, (8, CHUNK), 1) + c * CHUNK
            cap = jnp.where(position < length, -MASKED, MASKED)
            cap = jnp.concatenate([cap] * (pair_rows // 8), axis=0)
            s = lax.dot_general(queries[p], k_v[rows, pair], nt, preferred_element_type=F32)
            s = jnp.minimum(s * SCALE, cap)
            scores[rows_of, rows] = s
            for t in range(CHUNK // HD):
                high = jnp.maximum(high, s[:, t * HD : (t + 1) * HD])
            return high

        high = lax.fori_loop(0, lmax // CHUNK, score_step, fresh)
        peak = jnp.broadcast_to(jnp.max(high, axis=1, keepdims=True), (pair_rows, HD))
        weights = jnp.exp2(fresh - peak).astype(BF16)
        weighted[p] = jnp.dot(weights, vx[:, pair], preferred_element_type=F32)

        def value_step(c, total):
            rows = pl.ds(pl.multiple_of(c * CHUNK, CHUNK), CHUNK)
            s = scores[rows_of, rows]
            pieces = []
            for t in range(CHUNK // HD):
                piece = jnp.exp2(s[:, t * HD : (t + 1) * HD] - peak).astype(BF16)
                total = total + piece.astype(F32)
                pieces.append(piece)
            weighted[p] += jnp.dot(
                jnp.concatenate(pieces, axis=1), v_v[rows, pair], preferred_element_type=F32
            )
            return total

        if p == 0:
            for copy in v_loads:
                copy.wait()
        total = lax.fori_loop(0, lmax // CHUNK, value_step, weights.astype(F32))
        weight_sum = jnp.sum(total, axis=1, keepdims=True)
        for i in range(2):
            rows = slice(i * OWN, (i + 1) * OWN)
            attended = weighted[p, rows, i * HD : (i + 1) * HD] / weight_sum[rows]
            attended = attended.astype(BF16)
            att_send[4 * p + 2 * i] = attended[:PR]
            att_send[4 * p + 2 * i + 1] = attended[PR:]

    odd = lax.rem(y + z, 2)
    slot = lax.rem(lax.div(y, 2) + lax.div(z, 2), 2)

    def send_attended(p):
        for m in range(4):
            peer = 4 * p + lax.rem(f + m, 4)
            landing = att_recv.at[odd, slot, f]

            @pl.when(peer == f)
            def _():
                pltpu.make_async_copy(
                    att_send.at[f], landing, att_rsem.at[odd, slot]
                ).start()

            for k in range(NY):
                chip = lax.rem(z + odd * k, NY) * NY + lax.rem(y + (1 - odd) * k, NY)
                copy = remote(
                    att_send.at[peer], landing, att_ssem.at[k], att_rsem.at[odd, slot],
                    (chip, peer),
                )
                if k == 0:
                    pl.when(peer != f)(copy.start)
                else:
                    copy.start()

    for copy in k_loads:
        copy.wait()
    for p in range(PAIRS):
        attend(p)
        send_attended(p)

    for i in range(2 * KV_HEADS):
        ne[0:1, i * HD : (i + 1) * HD] = fresh_rows[i][0:1]
        ne[1:2, i * HD : (i + 1) * HD] = fresh_rows[i][8:9]
    results[PR:, :, :] = ne[0:2, :].reshape(1, STEPS, ne.shape[1]).astype(BF16)

    line_copies = [[], []]
    for part_id in range(2):
        for side in range(2):
            whole = att_recv.at[side, part_id]
            pltpu.make_async_copy(whole, whole, att_rsem.at[side, part_id]).wait()
            pos = (z, y)[side]
            att_f32[...] = att_recv[side, part_id].astype(F32).reshape(NF * PR, HD)
            for j in range(8):
                rows_all[part_id, side, pos, :, j * HD : (j + 1) * HD] = att_f32[
                    pl.ds(j, PR, stride=8), :
                ].astype(BF16)
            mine_rows = rows_all.at[part_id, side, pos]
            for k in range(1, NY):
                q = lax.rem(pos + k, NY)
                device = (q * NY + y, f) if side == 0 else (z * NY + q, f)
                copy = remote(
                    mine_rows, mine_rows,
                    line_ssem.at[part_id, side, k - 1], line_rsem.at[part_id, side, k - 1],
                    device,
                )
                copy.start()
                line_copies[part_id].append(copy)
    wout_load.wait()
    for copy in msg_copies:
        copy.wait_send()
    for k in range(NY):
        sent = att_send.at[pl.ds(0, NF - 1)] if k == 0 else att_send
        pltpu.make_async_copy(sent, sent, att_ssem.at[k]).wait()

    def out_rows(index):
        return pl.ds(pl.multiple_of(index * OWN, OWN), OWN)

    sib_copies = [[], []]
    for part_id in range(2):
        for copy in line_copies[part_id]:
            copy.wait_recv()
        product = jnp.dot(
            rows_all[part_id].reshape(NH * PR // 2, wout_v.shape[0]),
            wout_v[...],
            preferred_element_type=F32,
        )
        for side in range(2):
            for q in range(NY):
                far = 2 * ((part_id + q // 2) % 2) + (q + side) % 2
                home = q * NY + far if side == 0 else far * NY + q
                first = (side * NY + q) * PR
                opart[home * PR : (home + 1) * PR, :] = product[first : first + PR]
        for e in range(2):
            x = 2 * lax.rem(1 + core + part_id, 2) + e
            copy = remote(
                opart.at[out_rows(2 * x + 1 - core)], sib_recv.at[part_id, e],
                sib_ssem.at[part_id, e], sib_rsem.at[part_id, e], (h, sib),
            )
            copy.start()
            sib_copies[part_id].append(copy)
    fin_copies = []
    for part_id in range(2):
        for copy in sib_copies[part_id]:
            copy.wait_recv()
        for e in range(2):
            x = 2 * lax.rem(core + part_id, 2) + e
            hop = lax.rem(x - cx + NX, NX)
            there = lax.rem(hop + NX - 1, NX)
            copy = remote(
                fin_send.at[part_id, e], fin_recv.at[there],
                fin_ssem.at[part_id, e], fin_rsem.at[there], (h, 2 * x + core),
            )
            fin_copies.append((hop, copy))

            @pl.when(hop != 0)
            def _():
                total = opart[out_rows(2 * x + core), :] + sib_recv[part_id, e]
                fin_send[part_id, e] = total.astype(BF16)
                copy.start()

    for copies in sib_copies + line_copies:
        for copy in copies:
            copy.wait_send()
    own_part = lax.rem(core + lax.div(cx, 2), 2)
    result = opart[out_rows(f), :] + sib_recv[own_part, lax.rem(cx, 2)]
    for k in range(1, NX):
        pltpu.make_async_copy(
            fin_recv.at[k - 1], fin_recv.at[k - 1], fin_rsem.at[k - 1]
        ).wait()
        result = result + fin_recv[k - 1].astype(F32)
    results[:PR, :, :] = result.reshape(PR, STEPS, result.shape[1]).astype(BF16)
    for hop, copy in fin_copies:
        pl.when(hop != 0)(copy.wait_send)


def hand_out(results, out, entries, sem):
    rows = out.shape[0]
    copies = [
        pltpu.make_async_copy(results.at[pl.ds(0, rows)], out, sem.at[0]),
        pltpu.make_async_copy(results.at[pl.ds(rows, 1)], entries, sem.at[1]),
    ]
    for copy in copies:
        copy.start()
    for copy in copies:
        copy.wait()


def body(tokens, norm_gain, query_weight, w_keyval, w_out, cache_keys, cache_values, lengths):
    width = tokens.shape[2]
    lmax = cache_keys.shape[1]
    qcols = query_weight.shape[1]
    kvcols = w_keyval.shape[1]
    halves = np.arange(HD // 2, dtype=np.float64) * (2.0 / HD)
    freq = (ROPE_BASE ** (-halves)).astype(np.float32)
    freq = jnp.asarray(np.tile(np.concatenate([freq, freq])[None, :], (PR, 1)))
    any_spec = pl.BlockSpec(memory_space=pl.ANY)
    hbm_spec = pl.BlockSpec(memory_space=pltpu.HBM)
    vmem_spec = pl.BlockSpec(memory_space=pltpu.VMEM)
    dma = pltpu.SemaphoreType.DMA
    rows = NH * PR
    results = pl.pallas_call(
        kernel,
        out_shape=pltpu.VMEM((PR + 1, STEPS, width), BF16),
        in_specs=[hbm_spec] * 9,
        out_specs=vmem_spec,
        scratch_shapes=[
            pltpu.SMEM(lengths.shape, jnp.int32),
            pltpu.VMEM(tokens.shape, BF16),
            pltpu.VMEM((OWN, width), BF16),
            pltpu.VMEM((PR, HD), F32),
            pltpu.VMEM((width,), BF16),
            pltpu.VMEM((width, qcols), BF16),
            pltpu.VMEM((width, kvcols), BF16),
            pltpu.VMEM((qcols, width), BF16),
            pltpu.VMEM((lmax, KV_HEADS * HD), BF16),
            pltpu.VMEM((lmax, KV_HEADS * HD), BF16),
            pltpu.VMEM((rows, width), BF16),
            pltpu.VMEM((rows // 2, width), BF16),
            pltpu.VMEM((8, HD), F32),
            pltpu.VMEM((NH - 1, 8, HD), F32),
            pltpu.VMEM((NF, 8, HD), F32),
            pltpu.VMEM((NY, NY, PR, qcols + kvcols), F32),
            pltpu.VMEM((2, NY, PR // 2, LOW), F32),
            pltpu.VMEM((2, NY, PR // 2, qcols + kvcols - LOW), F32),
            pltpu.VMEM((2, NY, PR // 2, LOW), F32),
            pltpu.VMEM((2, NY, PR // 2, qcols + kvcols - LOW), F32),
            pltpu.VMEM((2, NY, PR // 2, LOW), F32),
            pltpu.VMEM((2, NY, PR // 2, qcols + kvcols - LOW), F32),
            pltpu.VMEM((2, NY, PR // 2, qcols + kvcols), F32),
            pltpu.VMEM((2, NY - 1, PR // 2, qcols + kvcols), F32),
            pltpu.VMEM((NF * PR, HD), F32),
            pltpu.VMEM((NF, 2 * PR, HD), BF16),
            pltpu.VMEM((NF, 2 * PR, HD), BF16),
            pltpu.VMEM((HD, KV_HEADS * HD), BF16),
            pltpu.VMEM((HD, KV_HEADS * HD), BF16),
            pltpu.VMEM((8, 2 * KV_HEADS * HD), F32),
            pltpu.VMEM((KV_HEADS * OWN, lmax), F32),
            pltpu.VMEM((PAIRS, 2 * OWN, 2 * HD), F32),
            pltpu.VMEM((NF, PR, HD), BF16),
            pltpu.VMEM((2, 2, NF, PR, HD), BF16),
            pltpu.VMEM((NF * PR, HD), F32),
            pltpu.VMEM((2, 2, NY, PR, qcols), BF16),
            pltpu.VMEM((rows, width), F32),
            pltpu.VMEM((2, 2, OWN, width), F32),
            pltpu.VMEM((2, 2, OWN, width), BF16),
            pltpu.VMEM((NX - 1, OWN, width), BF16),
            dma((8,)),
            dma((CACHE_COPIES,)),
            dma((CACHE_COPIES,)),
            dma((NX - 1,)), dma((NX - 1,)),
            dma((NX,)), dma((NX,)),
            dma((NH - 1,)), dma((NH - 1,)),
            dma((NF - 1,)), dma((NF - 1,)),
            dma((2, 6)), dma((2, 6)),
            dma((2, NY - 1)), dma((2, NY - 1)),
            dma((NF - 1,)), dma((NF - 1,)),
            dma((NY,)), dma((2, 2)),
            dma((2, 2, NY - 1)), dma((2, 2, NY - 1)),
            dma((2, 2)), dma((2, 2)),
            dma((2, 2)), dma((NX - 1,)),
        ],
        compiler_params=pltpu.CompilerParams(
            collective_id=0, has_side_effects=True, vmem_limit_bytes=48 * 2**20
        ),
        name="decode_block",
    )(
        *[
            pltpu.with_memory_space_constraint(array, pltpu.HBM)
            for array in (
                lengths, freq, tokens, norm_gain, query_weight, w_keyval, w_out,
                cache_keys, cache_values,
            )
        ],
    )
    return pl.pallas_call(
        hand_out,
        out_shape=(
            jax.ShapeDtypeStruct(tokens.shape, BF16),
            jax.ShapeDtypeStruct((1, STEPS, 2 * KV_HEADS * HD), BF16),
        ),
        in_specs=[vmem_spec],
        out_specs=(any_spec, any_spec),
        scratch_shapes=[dma((2,))],
        name="hand_out",
    )(pltpu.with_memory_space_constraint(results, pltpu.VMEM))


def solution(mesh):
    in_specs = (
        P("ffn", None, "hid"),
        P("hid"),
        P("hid", "ffn"),
        P("hid", "ffn"),
        P("ffn", "hid"),
        P(("hid", "ffn"), None, None),
        P(("hid", "ffn"), None, None),
        P(),
    )
    out_specs = (P("ffn", None, "hid"), P(("hid", "ffn"), None, None))
    return jax.shard_map(body, mesh=mesh, in_specs=in_specs, out_specs=out_specs, check_vma=False)
```

```python
import functools

import jax
import jax.numpy as jnp
import numpy as np
from jax import lax
from jax.experimental import pallas as pl
from jax.experimental.pallas import tpu as pltpu
from jax.sharding import PartitionSpec as P

MESH = pl.DeviceIdType.MESH
F32 = jnp.float32
BF16 = jnp.bfloat16

HEADS = 64
KV_HEADS = 4
HD = 128
STEPS = 2
EPSILON = 1e-05
ROPE_BASE = 500000.0
SCALE = HD ** (-0.5) * 1.4426950408889634
MASKED = -1e30

NH = 16
NF = 8
NX = 4
NY = 4
GROUPS = (((0, 256), (256, 256)), ((512, 384), (896, 256)))
OWN = 32
PR = 16
CHUNK = 4096
CACHE_COPIES = 4
PAIRS = KV_HEADS // 2


def remote(src, dst, send_sem, recv_sem, device):
    return pltpu.make_async_remote_copy(
        src_ref=src,
        dst_ref=dst,
        send_sem=send_sem,
        recv_sem=recv_sem,
        device_id=device,
        device_id_type=MESH,
    )


def rotate(vectors, cosine, sine):
    return vectors * cosine + pltpu.roll(vectors, HD // 2, 1) * sine


def kernel(
    lengths_hbm, freq, tokens, gain, wq, wkv, wout, cache_k, cache_v,
    results,
    lengths, raw_v, tok_v, freq_v, gain_v, wq_v, wkv_v, wout_v, k_v, v_v,
    x_all, normed, ss_own, ss_recv, tot_all, part, relay, left, right, mine, mine_recv,
    spread, msg, qkv, kx, vx, ne, scores, weighted, att_send, att_recv, att_f32, rows_all,
    opart, sib_recv, fin_send, fin_recv,
    local_sem, k_sem, v_sem,
    tok_ssem, tok_rsem, fwd_ssem, fwd_rsem, ss_ssem, ss_rsem, tot_ssem, tot_rsem,
    ring_ssem, ring_rsem, stage_ssem, stage_rsem, msg_ssem, msg_rsem, att_ssem, att_rsem, line_ssem, line_rsem,
    sib_ssem, sib_rsem, fin_ssem, fin_rsem,
):
    h = lax.axis_index("hid")
    f = lax.axis_index("ffn")
    z = lax.div(h, NY)
    y = lax.rem(h, NY)
    cx = lax.div(f, 2)
    core = lax.rem(f, 2)
    sib = f + 1 - 2 * core
    lmax = cache_k.shape[1]

    barrier = pltpu.get_barrier_semaphore()
    tokens_load = pltpu.make_async_copy(tokens, raw_v, local_sem.at[0])
    tokens_load.start()

    def greet_hid(k, carry):
        pl.semaphore_signal(
            barrier, inc=1, device_id=(lax.rem(h + k, NH), f), device_id_type=MESH
        )
        return carry

    def greet_ffn(k, carry):
        pl.semaphore_signal(
            barrier, inc=1, device_id=(h, lax.rem(f + k, NF)), device_id_type=MESH
        )
        return carry

    lax.fori_loop(1, NF, greet_ffn, 0)
    lax.fori_loop(1, NH, greet_hid, 0)

    loads = []
    for i, (src, dst) in enumerate(
        [(gain, gain_v), (freq, freq_v), (wq, wq_v), (wkv, wkv_v), (lengths_hbm, lengths)]
    ):
        copy = pltpu.make_async_copy(src, dst, local_sem.at[1 + i])
        copy.start()
        loads.append(copy)
    span = lmax // CACHE_COPIES
    k_loads = []
    for i in range(CACHE_COPIES):
        copy = pltpu.make_async_copy(
            cache_k.at[0, pl.ds(i * span, span)], k_v.at[pl.ds(i * span, span)], k_sem.at[i]
        )
        copy.start()
        k_loads.append(copy)
    wout_load = pltpu.make_async_copy(wout, wout_v, local_sem.at[6])
    wout_load.start()

    tokens_load.wait()
    x_f32 = raw_v[...].astype(F32).reshape(tok_v.shape)
    x_own = x_f32.astype(BF16)
    tok_v[...] = x_own
    pl.semaphore_wait(barrier, NH + NF - 2)

    def block(index):
        return x_all.at[pl.ds(pl.multiple_of(index * OWN, OWN), OWN)]

    tok_copies = []
    for k in (1, 3, 2):
        peer = 2 * lax.rem(cx + k, NX) + core
        copy = remote(tok_v, block(f), tok_ssem.at[k - 1], tok_rsem.at[k - 1], (h, peer))
        copy.start()
        tok_copies.append((k, copy))
    fwd_copies = [remote(tok_v, block(f), fwd_ssem.at[0], fwd_rsem.at[0], (h, sib))]
    fwd_copies[0].start()

    sums = jnp.sum(x_f32 * x_f32, axis=1, keepdims=True)
    row_id = lax.broadcasted_iota(jnp.int32, (OWN, HD), 0)
    lane_id = lax.broadcasted_iota(jnp.int32, (OWN, HD), 1)
    diagonal = row_id == lane_id
    own_sums = jnp.sum(jnp.where(diagonal, sums, 0.0), axis=0, keepdims=True)
    ss_own[...] = jnp.broadcast_to(own_sums, (8, HD))

    def ss_copy(k):
        return remote(
            ss_own, ss_recv.at[k - 1], ss_ssem.at[k - 1], ss_rsem.at[k - 1],
            (lax.rem(h + k, NH), f),
        )

    def ss_start(k, carry):
        ss_copy(k).start()
        return carry

    lax.fori_loop(1, NH, ss_start, 0)
    x_all[pl.ds(pl.multiple_of(f * OWN, OWN), OWN), :] = x_own

    def ss_add(k, total):
        ss_copy(k).wait_recv()
        return total + ss_recv[k - 1]

    total = lax.fori_loop(1, NH, ss_add, ss_own[...])
    tot_all[f] = total
    tot_copies = []
    for k in range(1, NF):
        copy = remote(
            tot_all.at[f], tot_all.at[f], tot_ssem.at[k - 1], tot_rsem.at[k - 1],
            (h, lax.rem(f + k, NF)),
        )
        copy.start()
        tot_copies.append(copy)
    for k, tok_copy in tok_copies:
        tok_copy.wait_recv()
        came = 2 * lax.rem(cx + NX - k, NX) + core
        copy = remote(block(came), block(came), fwd_ssem.at[k], fwd_rsem.at[k], (h, sib))
        copy.start()
        fwd_copies.append(copy)

    loads[4].wait()
    length = lengths[h * NF + f]
    step_of = lax.div(lax.broadcasted_iota(jnp.int32, (PR, HD), 0), 8)
    loads[1].wait()
    angles = (step_of + length).astype(F32) * freq_v[...]
    cosine = jnp.cos(angles)
    sine = jnp.sin(angles)
    sine = jnp.where(
        lax.broadcasted_iota(jnp.int32, (PR, HD), 1) < HD // 2, -sine, sine
    )

    kx[...] = jnp.zeros_like(kx)
    vx[...] = jnp.zeros_like(vx)
    for copy in tot_copies:
        copy.wait_recv()
    loads[0].wait()
    width = x_all.shape[1]
    qcols = wq_v.shape[1]
    full = width * NH
    gain_row = gain_v[...].astype(F32).reshape(1, width)

    def project(parity):
        for x in range(NX):
            b = 2 * x + parity
            lane_sums = tot_all[b][0:1, :]
            row_sums = jnp.sum(jnp.where(diagonal, lane_sums, 0.0), axis=1, keepdims=True)
            inverse = lax.rsqrt(row_sums / full + EPSILON)
            normed[x * OWN : (x + 1) * OWN, :] = (
                block(b)[...].astype(F32) * inverse * gain_row
            ).astype(BF16)
        lhs = normed[...]
        for cols, weights in ((slice(0, qcols), wq_v), (slice(qcols, None), wkv_v)):
            product = jnp.dot(lhs, weights[...], preferred_element_type=F32)
            part[:, pl.ds(2 * parity, 2), :, cols] = product.reshape(NX, 2, PR, product.shape[1])

    loads[2].wait()
    loads[3].wait()
    project(core)
    for copy in fwd_copies:
        copy.wait_recv()
    project(1 - core)

    half = PR // 2

    def ring(side):
        pos = (y, z)[side]

        def device(q):
            return (z * NY + q, f) if side == 0 else (q * NY + y, f)

        def view(q, cols):
            if side == 0:
                return part.at[:, q, pl.ds(0, half), cols]
            return part.at[q, :, pl.ds(half, half), cols]

        return pos, device, view

    moves = {}
    for g, (low, high) in enumerate(GROUPS):
        for side in range(2):
            pos, device, view = ring(side)
            nxt, prv, far = lax.rem(pos + 1, NY), lax.rem(pos + 3, NY), lax.rem(pos + 2, NY)
            plan = [
                (far, low, relay, nxt),
                (far, high, relay, prv),
                (nxt, high, left, nxt),
                (prv, low, right, prv),
            ]
            moves[g, side] = [
                remote(
                    view(q, pl.ds(*cols)), dst.at[side, :, :, pl.ds(*cols)],
                    ring_ssem.at[g, side, i], ring_rsem.at[g, side, i], device(to),
                )
                for i, (q, cols, dst, to) in enumerate(plan)
            ]
    for first in (0, 2):
        for g in range(len(GROUPS)):
            for side in range(2):
                for copy in moves[g, side][first : first + 2]:
                    copy.start()
    v_loads = []
    for i in range(CACHE_COPIES):
        copy = pltpu.make_async_copy(
            cache_v.at[0, pl.ds(i * span, span)], v_v.at[pl.ds(i * span, span)], v_sem.at[i]
        )
        copy.start()
        v_loads.append(copy)

    def ss_sent(k, carry):
        ss_copy(k).wait_send()
        return carry

    lax.fori_loop(1, NH, ss_sent, 0)
    for copy in tot_copies + fwd_copies + [copy for _, copy in tok_copies]:
        copy.wait_send()
    for g, (low, high) in enumerate(GROUPS):
        for side in range(2):
            pos, device, view = ring(side)
            nxt, prv = lax.rem(pos + 1, NY), lax.rem(pos + 3, NY)
            for i, (to, cols, dst) in enumerate(((nxt, low, left), (prv, high, right))):
                cols = pl.ds(*cols)
                moves[g, side][i].wait_recv()
                passed = relay.at[side, :, :, cols]
                passed[...] = passed[...] + view(to, cols)[...]
                copy = remote(
                    passed, dst.at[side, :, :, cols],
                    ring_ssem.at[g, side, 4 + i], ring_rsem.at[g, side, 4 + i], device(to),
                )
                copy.start()
                moves[g, side].append(copy)
    stages = {}
    for g, (low, high) in enumerate(GROUPS):
        cols = pl.ds(low[0], low[1] + high[1])
        for side in range(2):
            pos, device, view = ring(side)
            for copy in moves[g, side][2:]:
                copy.wait_recv()
            mine[side, :, :, cols] = (
                view(pos, cols)[...] + left[side, :, :, cols] + right[side, :, :, cols]
            )
            other, other_device, _ = ring(1 - side)
            stages[g, side] = []
            for k in (1, 3, 2):
                peer = lax.rem(other + k, NY)
                copy = remote(
                    mine.at[side, peer, :, cols], mine_recv.at[side, k - 1, :, cols],
                    stage_ssem.at[g, side, k - 1], stage_rsem.at[g, side, k - 1],
                    other_device(peer),
                )
                copy.start()
                stages[g, side].append(copy)
    groups = []
    for g, (low, high) in enumerate(GROUPS):
        cols = pl.ds(low[0], low[1] + high[1])
        halves = []
        for side in range(2):
            other = ring(1 - side)[0]
            total = mine[side, other, :, cols]
            for copy in stages[g, side]:
                copy.wait_recv()
            for k in range(NY - 1):
                total = total + mine_recv[side, k, :, cols]
            halves.append(total)
        groups.append(jnp.concatenate(halves, axis=0))
    summed = jnp.concatenate(groups, axis=1)

    for j in range(8):
        spread[pl.ds(j, PR, stride=8), :] = summed[:, j * HD : (j + 1) * HD]
    msg[:, :PR, :] = spread[...].reshape(NF, PR, HD).astype(BF16)
    spread[...] = jnp.zeros_like(spread)
    spread[pl.ds(0, PR, stride=8), :] = summed[:, qcols:]
    msg[:, PR:, :] = spread[...].reshape(NF, PR, HD).astype(BF16)
    qkv[f] = msg[f]
    msg_copies = []
    for k in range(1, NF):
        peer = lax.rem(f + k, NF)
        copy = remote(
            msg.at[peer], qkv.at[f], msg_ssem.at[k - 1], msg_rsem.at[k - 1], (h, peer)
        )
        copy.start()
        msg_copies.append(copy)
    for key in moves:
        for copy in moves[key] + stages[key]:
            copy.wait_send()
    for copy in msg_copies:
        copy.wait_recv()

    fresh_rows = []
    for i in range(2 * KV_HEADS):
        raw = qkv[i, PR:, :].astype(F32)
        cols = pl.ds((i % KV_HEADS) * HD, HD)
        if i < KV_HEADS:
            raw = rotate(raw, cosine, sine)
            kx[:PR, cols] = raw.astype(BF16)
        else:
            vx[:PR, cols] = raw.astype(BF16)
        fresh_rows.append(raw)

    rotated = [
        rotate(qkv[i, :PR, :].astype(F32), cosine, sine).astype(BF16) for i in range(NF)
    ]
    nothing = jnp.zeros((OWN, HD), BF16)
    queries = []
    for p in range(PAIRS):
        upper = jnp.concatenate(rotated[4 * p : 4 * p + 2], axis=0)
        lower = jnp.concatenate(rotated[4 * p + 2 : 4 * p + 4], axis=0)
        queries.append(
            jnp.concatenate(
                [
                    jnp.concatenate([upper, nothing], axis=1),
                    jnp.concatenate([nothing, lower], axis=1),
                ],
                axis=0,
            )
        )
    pair_rows, pair_cols = 2 * OWN, 2 * HD
    lane = lax.broadcasted_iota(jnp.int32, (pair_rows, HD), 1)
    step_row = lax.rem(lax.div(lax.broadcasted_iota(jnp.int32, (pair_rows, HD), 0), 8), 2)
    fresh_live = (lane == 0) | ((lane == 8) & (step_row == 1))
    nt = (((1,), (1,)), ((), ()))
    def attend(p):
        pair = pl.ds(p * pair_cols, pair_cols)
        rows_of = pl.ds(p * pair_rows, pair_rows)
        fresh = lax.dot_general(queries[p], kx[:, pair], nt, preferred_element_type=F32)
        fresh = jnp.where(fresh_live, fresh * SCALE, MASKED)

        def score_step(c, high):
            rows = pl.ds(pl.multiple_of(c * CHUNK, CHUNK), CHUNK)
            position = lax.broadcasted_iota(jnp.int32, (8, CHUNK), 1) + c * CHUNK
            cap = jnp.where(position < length, -MASKED, MASKED)
            cap = jnp.concatenate([cap] * (pair_rows // 8), axis=0)
            s = lax.dot_general(queries[p], k_v[rows, pair], nt, preferred_element_type=F32)
            s = jnp.minimum(s * SCALE, cap)
            scores[rows_of, rows] = s
            for t in range(CHUNK // HD):
                high = jnp.maximum(high, s[:, t * HD : (t + 1) * HD])
            return high

        high = lax.fori_loop(0, lmax // CHUNK, score_step, fresh)
        peak = jnp.broadcast_to(jnp.max(high, axis=1, keepdims=True), (pair_rows, HD))
        weights = jnp.exp2(fresh - peak).astype(BF16)
        weighted[p] = jnp.dot(weights, vx[:, pair], preferred_element_type=F32)

        def value_step(c, total):
            rows = pl.ds(pl.multiple_of(c * CHUNK, CHUNK), CHUNK)
            s = scores[rows_of, rows]
            pieces = []
            for t in range(CHUNK // HD):
                piece = jnp.exp2(s[:, t * HD : (t + 1) * HD] - peak).astype(BF16)
                total = total + piece.astype(F32)
                pieces.append(piece)
            weighted[p] += jnp.dot(
                jnp.concatenate(pieces, axis=1), v_v[rows, pair], preferred_element_type=F32
            )
            return total

        if p == 0:
            for copy in v_loads:
                copy.wait()
        total = lax.fori_loop(0, lmax // CHUNK, value_step, weights.astype(F32))
        weight_sum = jnp.sum(total, axis=1, keepdims=True)
        for i in range(2):
            rows = slice(i * OWN, (i + 1) * OWN)
            attended = weighted[p, rows, i * HD : (i + 1) * HD] / weight_sum[rows]
            attended = attended.astype(BF16)
            att_send[4 * p + 2 * i] = attended[:PR]
            att_send[4 * p + 2 * i + 1] = attended[PR:]

    odd = lax.rem(y + z, 2)
    slot = lax.rem(lax.div(y, 2) + lax.div(z, 2), 2)

    def send_attended(p):
        for m in range(4):
            peer = 4 * p + lax.rem(f + m, 4)
            landing = att_recv.at[odd, slot, f]

            @pl.when(peer == f)
            def _():
                pltpu.make_async_copy(
                    att_send.at[f], landing, att_rsem.at[odd, slot]
                ).start()

            for k in range(NY):
                chip = lax.rem(z + odd * k, NY) * NY + lax.rem(y + (1 - odd) * k, NY)
                copy = remote(
                    att_send.at[peer], landing, att_ssem.at[k], att_rsem.at[odd, slot],
                    (chip, peer),
                )
                if k == 0:
                    pl.when(peer != f)(copy.start)
                else:
                    copy.start()

    for copy in k_loads:
        copy.wait()
    for p in range(PAIRS):
        attend(p)
        send_attended(p)

    for i in range(2 * KV_HEADS):
        ne[0:1, i * HD : (i + 1) * HD] = fresh_rows[i][0:1]
        ne[1:2, i * HD : (i + 1) * HD] = fresh_rows[i][8:9]
    results[PR:, :, :] = ne[0:2, :].reshape(1, STEPS, ne.shape[1]).astype(BF16)

    line_copies = [[], []]
    for part_id in range(2):
        for side in range(2):
            whole = att_recv.at[side, part_id]
            pltpu.make_async_copy(whole, whole, att_rsem.at[side, part_id]).wait()
            pos = (z, y)[side]
            att_f32[...] = att_recv[side, part_id].astype(F32).reshape(NF * PR, HD)
            for j in range(8):
                rows_all[part_id, side, pos, :, j * HD : (j + 1) * HD] = att_f32[
                    pl.ds(j, PR, stride=8), :
                ].astype(BF16)
            mine_rows = rows_all.at[part_id, side, pos]
            for k in range(1, NY):
                q = lax.rem(pos + k, NY)
                device = (q * NY + y, f) if side == 0 else (z * NY + q, f)
                copy = remote(
                    mine_rows, mine_rows,
                    line_ssem.at[part_id, side, k - 1], line_rsem.at[part_id, side, k - 1],
                    device,
                )
                copy.start()
                line_copies[part_id].append(copy)
    wout_load.wait()
    for copy in msg_copies:
        copy.wait_send()
    for k in range(NY):
        sent = att_send.at[pl.ds(0, NF - 1)] if k == 0 else att_send
        pltpu.make_async_copy(sent, sent, att_ssem.at[k]).wait()

    def out_rows(index):
        return pl.ds(pl.multiple_of(index * OWN, OWN), OWN)

    sib_copies = [[], []]
    for part_id in range(2):
        for copy in line_copies[part_id]:
            copy.wait_recv()
        product = jnp.dot(
            rows_all[part_id].reshape(NH * PR // 2, wout_v.shape[0]),
            wout_v[...],
            preferred_element_type=F32,
        )
        for side in range(2):
            for q in range(NY):
                far = 2 * ((part_id + q // 2) % 2) + (q + side) % 2
                home = q * NY + far if side == 0 else far * NY + q
                first = (side * NY + q) * PR
                opart[home * PR : (home + 1) * PR, :] = product[first : first + PR]
        for e in range(2):
            x = 2 * lax.rem(1 + core + part_id, 2) + e
            copy = remote(
                opart.at[out_rows(2 * x + 1 - core)], sib_recv.at[part_id, e],
                sib_ssem.at[part_id, e], sib_rsem.at[part_id, e], (h, sib),
            )
            copy.start()
            sib_copies[part_id].append(copy)
    fin_copies = []
    for part_id in range(2):
        for copy in sib_copies[part_id]:
            copy.wait_recv()
        for e in range(2):
            x = 2 * lax.rem(core + part_id, 2) + e
            hop = lax.rem(x - cx + NX, NX)
            there = lax.rem(hop + NX - 1, NX)
            copy = remote(
                fin_send.at[part_id, e], fin_recv.at[there],
                fin_ssem.at[part_id, e], fin_rsem.at[there], (h, 2 * x + core),
            )
            fin_copies.append((hop, copy))

            @pl.when(hop != 0)
            def _():
                total = opart[out_rows(2 * x + core), :] + sib_recv[part_id, e]
                fin_send[part_id, e] = total.astype(BF16)
                copy.start()

    for copies in sib_copies + line_copies:
        for copy in copies:
            copy.wait_send()
    own_part = lax.rem(core + lax.div(cx, 2), 2)
    result = opart[out_rows(f), :] + sib_recv[own_part, lax.rem(cx, 2)]
    for k in range(1, NX):
        pltpu.make_async_copy(
            fin_recv.at[k - 1], fin_recv.at[k - 1], fin_rsem.at[k - 1]
        ).wait()
        result = result + fin_recv[k - 1].astype(F32)
    results[:PR, :, :] = result.reshape(PR, STEPS, result.shape[1]).astype(BF16)
    for hop, copy in fin_copies:
        pl.when(hop != 0)(copy.wait_send)


def hand_out(results, out, entries, sem):
    rows = out.shape[0]
    copies = [
        pltpu.make_async_copy(results.at[pl.ds(0, rows)], out, sem.at[0]),
        pltpu.make_async_copy(results.at[pl.ds(rows, 1)], entries, sem.at[1]),
    ]
    for copy in copies:
        copy.start()
    for copy in copies:
        copy.wait()


def body(tokens, norm_gain, query_weight, w_keyval, w_out, cache_keys, cache_values, lengths):
    width = tokens.shape[2]
    lmax = cache_keys.shape[1]
    qcols = query_weight.shape[1]
    kvcols = w_keyval.shape[1]
    halves = np.arange(HD // 2, dtype=np.float64) * (2.0 / HD)
    freq = (ROPE_BASE ** (-halves)).astype(np.float32)
    freq = jnp.asarray(np.tile(np.concatenate([freq, freq])[None, :], (PR, 1)))
    any_spec = pl.BlockSpec(memory_space=pl.ANY)
    hbm_spec = pl.BlockSpec(memory_space=pltpu.HBM)
    vmem_spec = pl.BlockSpec(memory_space=pltpu.VMEM)
    dma = pltpu.SemaphoreType.DMA
    rows = NH * PR
    results = pl.pallas_call(
        kernel,
        out_shape=pltpu.VMEM((PR + 1, STEPS, width), BF16),
        in_specs=[hbm_spec] * 9,
        out_specs=vmem_spec,
        scratch_shapes=[
            pltpu.SMEM(lengths.shape, jnp.int32),
            pltpu.VMEM(tokens.shape, BF16),
            pltpu.VMEM((OWN, width), BF16),
            pltpu.VMEM((PR, HD), F32),
            pltpu.VMEM((width,), BF16),
            pltpu.VMEM((width, qcols), BF16),
            pltpu.VMEM((width, kvcols), BF16),
            pltpu.VMEM((qcols, width), BF16),
            pltpu.VMEM((lmax, KV_HEADS * HD), BF16),
            pltpu.VMEM((lmax, KV_HEADS * HD), BF16),
            pltpu.VMEM((rows, width), BF16),
            pltpu.VMEM((rows // 2, width), BF16),
            pltpu.VMEM((8, HD), F32),
            pltpu.VMEM((NH - 1, 8, HD), F32),
            pltpu.VMEM((NF, 8, HD), F32),
            pltpu.VMEM((NY, NY, PR, qcols + kvcols), F32),
            pltpu.VMEM((2, NY, PR // 2, qcols + kvcols), F32),
            pltpu.VMEM((2, NY, PR // 2, qcols + kvcols), F32),
            pltpu.VMEM((2, NY, PR // 2, qcols + kvcols), F32),
            pltpu.VMEM((2, NY, PR // 2, qcols + kvcols), F32),
            pltpu.VMEM((2, NY - 1, PR // 2, qcols + kvcols), F32),
            pltpu.VMEM((NF * PR, HD), F32),
            pltpu.VMEM((NF, 2 * PR, HD), BF16),
            pltpu.VMEM((NF, 2 * PR, HD), BF16),
            pltpu.VMEM((HD, KV_HEADS * HD), BF16),
            pltpu.VMEM((HD, KV_HEADS * HD), BF16),
            pltpu.VMEM((8, 2 * KV_HEADS * HD), F32),
            pltpu.VMEM((KV_HEADS * OWN, lmax), F32),
            pltpu.VMEM((PAIRS, 2 * OWN, 2 * HD), F32),
            pltpu.VMEM((NF, PR, HD), BF16),
            pltpu.VMEM((2, 2, NF, PR, HD), BF16),
            pltpu.VMEM((NF * PR, HD), F32),
            pltpu.VMEM((2, 2, NY, PR, qcols), BF16),
            pltpu.VMEM((rows, width), F32),
            pltpu.VMEM((2, 2, OWN, width), F32),
            pltpu.VMEM((2, 2, OWN, width), BF16),
            pltpu.VMEM((NX - 1, OWN, width), BF16),
            dma((8,)),
            dma((CACHE_COPIES,)),
            dma((CACHE_COPIES,)),
            dma((NX - 1,)), dma((NX - 1,)),
            dma((NX,)), dma((NX,)),
            dma((NH - 1,)), dma((NH - 1,)),
            dma((NF - 1,)), dma((NF - 1,)),
            dma((2, 2, 6)), dma((2, 2, 6)),
            dma((2, 2, NY - 1)), dma((2, 2, NY - 1)),
            dma((NF - 1,)), dma((NF - 1,)),
            dma((NY,)), dma((2, 2)),
            dma((2, 2, NY - 1)), dma((2, 2, NY - 1)),
            dma((2, 2)), dma((2, 2)),
            dma((2, 2)), dma((NX - 1,)),
        ],
        compiler_params=pltpu.CompilerParams(
            collective_id=0, has_side_effects=True, vmem_limit_bytes=48 * 2**20
        ),
        name="decode_block",
    )(
        *[
            pltpu.with_memory_space_constraint(array, pltpu.HBM)
            for array in (
                lengths, freq, tokens, norm_gain, query_weight, w_keyval, w_out,
                cache_keys, cache_values,
            )
        ],
    )
    return pl.pallas_call(
        hand_out,
        out_shape=(
            jax.ShapeDtypeStruct(tokens.shape, BF16),
            jax.ShapeDtypeStruct((1, STEPS, 2 * KV_HEADS * HD), BF16),
        ),
        in_specs=[vmem_spec],
        out_specs=(any_spec, any_spec),
        scratch_shapes=[dma((2,))],
        name="hand_out",
    )(pltpu.with_memory_space_constraint(results, pltpu.VMEM))


def solution(mesh):
    in_specs = (
        P("ffn", None, "hid"),
        P("hid"),
        P("hid", "ffn"),
        P("hid", "ffn"),
        P("ffn", "hid"),
        P(("hid", "ffn"), None, None),
        P(("hid", "ffn"), None, None),
        P(),
    )
    out_specs = (P("ffn", None, "hid"), P(("hid", "ffn"), None, None))
    return jax.shard_map(body, mesh=mesh, in_specs=in_specs, out_specs=out_specs, check_vma=False)
```

```python
import functools

import jax
import jax.numpy as jnp
import numpy as np
from jax import lax
from jax.experimental import pallas as pl
from jax.experimental.pallas import tpu as pltpu
from jax.sharding import PartitionSpec as P

MESH = pl.DeviceIdType.MESH
F32 = jnp.float32
BF16 = jnp.bfloat16

HEADS = 64
KV_HEADS = 4
HD = 128
STEPS = 2
EPSILON = 1e-05
ROPE_BASE = 500000.0
SCALE = HD ** (-0.5) * 1.4426950408889634
MASKED = -1e30

NH = 16
NF = 8
NX = 4
NY = 4
TURN = 512
GROUPS = (((0, 256), (256, 256)), ((512, 384), (896, 256)))
OWN = 32
PR = 16
CHUNK = 4096
CACHE_COPIES = 4
PAIRS = KV_HEADS // 2


def remote(src, dst, send_sem, recv_sem, device):
    return pltpu.make_async_remote_copy(
        src_ref=src,
        dst_ref=dst,
        send_sem=send_sem,
        recv_sem=recv_sem,
        device_id=device,
        device_id_type=MESH,
    )


def rotate(vectors, cosine, sine):
    return vectors * cosine + pltpu.roll(vectors, HD // 2, 1) * sine


def kernel(
    lengths_hbm, freq, tokens, gain, wq, wkv, wout, cache_k, cache_v,
    results,
    lengths, raw_v, tok_v, freq_v, gain_v, wq_v, wkv_v, wout_v, k_v, k_t, v_v,
    x_all, normed, ss_own, ss_recv, tot_all, part, relay, left, right, mine, mine_recv,
    spread, msg, qkv, kx, vx, ne, scores, weighted, att_send, att_recv, att_f32, rows_all,
    opart, sib_recv, fin_send, fin_recv,
    local_sem, k_sem, v_sem,
    tok_ssem, tok_rsem, fwd_ssem, fwd_rsem, ss_ssem, ss_rsem, tot_ssem, tot_rsem,
    ring_ssem, ring_rsem, stage_ssem, stage_rsem, msg_ssem, msg_rsem, att_ssem, att_rsem, line_ssem, line_rsem,
    sib_ssem, sib_rsem, fin_ssem, fin_rsem,
):
    h = lax.axis_index("hid")
    f = lax.axis_index("ffn")
    z = lax.div(h, NY)
    y = lax.rem(h, NY)
    cx = lax.div(f, 2)
    core = lax.rem(f, 2)
    sib = f + 1 - 2 * core
    lmax = cache_k.shape[1]

    barrier = pltpu.get_barrier_semaphore()
    tokens_load = pltpu.make_async_copy(tokens, raw_v, local_sem.at[0])
    tokens_load.start()

    def greet_hid(k, carry):
        pl.semaphore_signal(
            barrier, inc=1, device_id=(lax.rem(h + k, NH), f), device_id_type=MESH
        )
        return carry

    def greet_ffn(k, carry):
        pl.semaphore_signal(
            barrier, inc=1, device_id=(h, lax.rem(f + k, NF)), device_id_type=MESH
        )
        return carry

    lax.fori_loop(1, NF, greet_ffn, 0)
    lax.fori_loop(1, NH, greet_hid, 0)

    loads = []
    for i, (src, dst) in enumerate(
        [(gain, gain_v), (freq, freq_v), (wq, wq_v), (wkv, wkv_v), (lengths_hbm, lengths)]
    ):
        copy = pltpu.make_async_copy(src, dst, local_sem.at[1 + i])
        copy.start()
        loads.append(copy)
    span = lmax // CACHE_COPIES
    k_loads = []
    for i in range(CACHE_COPIES):
        copy = pltpu.make_async_copy(
            cache_k.at[0, pl.ds(i * span, span)], k_v.at[pl.ds(i * span, span)], k_sem.at[i]
        )
        copy.start()
        k_loads.append(copy)
    wout_load = pltpu.make_async_copy(wout, wout_v, local_sem.at[6])
    wout_load.start()

    def turn_keys(quarter):
        k_loads[quarter].wait()

        def turn(i, carry):
            rows = pl.ds(pl.multiple_of(quarter * span + i * TURN, TURN), TURN)
            k_t[:, rows] = k_v[rows, :].T
            return carry

        lax.fori_loop(0, span // TURN, turn, 0)

    tokens_load.wait()
    x_f32 = raw_v[...].astype(F32).reshape(tok_v.shape)
    x_own = x_f32.astype(BF16)
    tok_v[...] = x_own
    pl.semaphore_wait(barrier, NH + NF - 2)

    def block(index):
        return x_all.at[pl.ds(pl.multiple_of(index * OWN, OWN), OWN)]

    tok_copies = []
    for k in (1, 3, 2):
        peer = 2 * lax.rem(cx + k, NX) + core
        copy = remote(tok_v, block(f), tok_ssem.at[k - 1], tok_rsem.at[k - 1], (h, peer))
        copy.start()
        tok_copies.append((k, copy))
    fwd_copies = [remote(tok_v, block(f), fwd_ssem.at[0], fwd_rsem.at[0], (h, sib))]
    fwd_copies[0].start()

    sums = jnp.sum(x_f32 * x_f32, axis=1, keepdims=True)
    row_id = lax.broadcasted_iota(jnp.int32, (OWN, HD), 0)
    lane_id = lax.broadcasted_iota(jnp.int32, (OWN, HD), 1)
    diagonal = row_id == lane_id
    own_sums = jnp.sum(jnp.where(diagonal, sums, 0.0), axis=0, keepdims=True)
    ss_own[...] = jnp.broadcast_to(own_sums, (8, HD))

    def ss_copy(k):
        return remote(
            ss_own, ss_recv.at[k - 1], ss_ssem.at[k - 1], ss_rsem.at[k - 1],
            (lax.rem(h + k, NH), f),
        )

    def ss_start(k, carry):
        ss_copy(k).start()
        return carry

    lax.fori_loop(1, NH, ss_start, 0)
    x_all[pl.ds(pl.multiple_of(f * OWN, OWN), OWN), :] = x_own

    def ss_add(k, total):
        ss_copy(k).wait_recv()
        return total + ss_recv[k - 1]

    total = lax.fori_loop(1, NH, ss_add, ss_own[...])
    tot_all[f] = total
    tot_copies = []
    for k in range(1, NF):
        copy = remote(
            tot_all.at[f], tot_all.at[f], tot_ssem.at[k - 1], tot_rsem.at[k - 1],
            (h, lax.rem(f + k, NF)),
        )
        copy.start()
        tot_copies.append(copy)
    for k, tok_copy in tok_copies:
        tok_copy.wait_recv()
        came = 2 * lax.rem(cx + NX - k, NX) + core
        copy = remote(block(came), block(came), fwd_ssem.at[k], fwd_rsem.at[k], (h, sib))
        copy.start()
        fwd_copies.append(copy)

    loads[4].wait()
    length = lengths[h * NF + f]
    step_of = lax.div(lax.broadcasted_iota(jnp.int32, (PR, HD), 0), 8)
    loads[1].wait()
    angles = (step_of + length).astype(F32) * freq_v[...]
    cosine = jnp.cos(angles)
    sine = jnp.sin(angles)
    sine = jnp.where(
        lax.broadcasted_iota(jnp.int32, (PR, HD), 1) < HD // 2, -sine, sine
    )

    kx[...] = jnp.zeros_like(kx)
    vx[...] = jnp.zeros_like(vx)
    for copy in tot_copies:
        copy.wait_recv()
    loads[0].wait()
    width = x_all.shape[1]
    qcols = wq_v.shape[1]
    full = width * NH
    gain_row = gain_v[...].astype(F32).reshape(1, width)

    def project(parity):
        for x in range(NX):
            b = 2 * x + parity
            lane_sums = tot_all[b][0:1, :]
            row_sums = jnp.sum(jnp.where(diagonal, lane_sums, 0.0), axis=1, keepdims=True)
            inverse = lax.rsqrt(row_sums / full + EPSILON)
            normed[x * OWN : (x + 1) * OWN, :] = (
                block(b)[...].astype(F32) * inverse * gain_row
            ).astype(BF16)
        lhs = normed[...]
        for cols, weights in ((slice(0, qcols), wq_v), (slice(qcols, None), wkv_v)):
            product = jnp.dot(lhs, weights[...], preferred_element_type=F32)
            part[:, pl.ds(2 * parity, 2), :, cols] = product.reshape(NX, 2, PR, product.shape[1])

    loads[2].wait()
    loads[3].wait()
    project(core)
    for copy in fwd_copies:
        copy.wait_recv()
    project(1 - core)

    half = PR // 2

    def ring(side):
        pos = (y, z)[side]

        def device(q):
            return (z * NY + q, f) if side == 0 else (q * NY + y, f)

        def view(q, cols):
            if side == 0:
                return part.at[:, q, pl.ds(0, half), cols]
            return part.at[q, :, pl.ds(half, half), cols]

        return pos, device, view

    moves = {}
    for g, (low, high) in enumerate(GROUPS):
        for side in range(2):
            pos, device, view = ring(side)
            nxt, prv, far = lax.rem(pos + 1, NY), lax.rem(pos + 3, NY), lax.rem(pos + 2, NY)
            plan = [
                (far, low, relay, nxt),
                (far, high, relay, prv),
                (nxt, high, left, nxt),
                (prv, low, right, prv),
            ]
            moves[g, side] = [
                remote(
                    view(q, pl.ds(*cols)), dst.at[side, :, :, pl.ds(*cols)],
                    ring_ssem.at[g, side, i], ring_rsem.at[g, side, i], device(to),
                )
                for i, (q, cols, dst, to) in enumerate(plan)
            ]
    for first in (0, 2):
        for g in range(len(GROUPS)):
            for side in range(2):
                for copy in moves[g, side][first : first + 2]:
                    copy.start()
    v_loads = []
    for i in range(CACHE_COPIES):
        copy = pltpu.make_async_copy(
            cache_v.at[0, pl.ds(i * span, span)], v_v.at[pl.ds(i * span, span)], v_sem.at[i]
        )
        copy.start()
        v_loads.append(copy)

    def ss_sent(k, carry):
        ss_copy(k).wait_send()
        return carry

    lax.fori_loop(1, NH, ss_sent, 0)
    for copy in tot_copies + fwd_copies + [copy for _, copy in tok_copies]:
        copy.wait_send()
    turn_keys(0)
    for g, (low, high) in enumerate(GROUPS):
        for side in range(2):
            pos, device, view = ring(side)
            nxt, prv = lax.rem(pos + 1, NY), lax.rem(pos + 3, NY)
            for i, (to, cols, dst) in enumerate(((nxt, low, left), (prv, high, right))):
                cols = pl.ds(*cols)
                moves[g, side][i].wait_recv()
                passed = relay.at[side, :, :, cols]
                passed[...] = passed[...] + view(to, cols)[...]
                copy = remote(
                    passed, dst.at[side, :, :, cols],
                    ring_ssem.at[g, side, 4 + i], ring_rsem.at[g, side, 4 + i], device(to),
                )
                copy.start()
                moves[g, side].append(copy)
    turn_keys(1)
    stages = {}
    for g, (low, high) in enumerate(GROUPS):
        cols = pl.ds(low[0], low[1] + high[1])
        for side in range(2):
            pos, device, view = ring(side)
            for copy in moves[g, side][2:]:
                copy.wait_recv()
            mine[side, :, :, cols] = (
                view(pos, cols)[...] + left[side, :, :, cols] + right[side, :, :, cols]
            )
            other, other_device, _ = ring(1 - side)
            stages[g, side] = []
            for k in (1, 3, 2):
                peer = lax.rem(other + k, NY)
                copy = remote(
                    mine.at[side, peer, :, cols], mine_recv.at[side, k - 1, :, cols],
                    stage_ssem.at[g, side, k - 1], stage_rsem.at[g, side, k - 1],
                    other_device(peer),
                )
                copy.start()
                stages[g, side].append(copy)
    turn_keys(2)
    groups = []
    for g, (low, high) in enumerate(GROUPS):
        cols = pl.ds(low[0], low[1] + high[1])
        halves = []
        for side in range(2):
            other = ring(1 - side)[0]
            total = mine[side, other, :, cols]
            for copy in stages[g, side]:
                copy.wait_recv()
            for k in range(NY - 1):
                total = total + mine_recv[side, k, :, cols]
            halves.append(total)
        groups.append(jnp.concatenate(halves, axis=0))
    summed = jnp.concatenate(groups, axis=1)

    for j in range(8):
        spread[pl.ds(j, PR, stride=8), :] = summed[:, j * HD : (j + 1) * HD]
    msg[:, :PR, :] = spread[...].reshape(NF, PR, HD).astype(BF16)
    spread[...] = jnp.zeros_like(spread)
    spread[pl.ds(0, PR, stride=8), :] = summed[:, qcols:]
    msg[:, PR:, :] = spread[...].reshape(NF, PR, HD).astype(BF16)
    qkv[f] = msg[f]
    msg_copies = []
    for k in range(1, NF):
        peer = lax.rem(f + k, NF)
        copy = remote(
            msg.at[peer], qkv.at[f], msg_ssem.at[k - 1], msg_rsem.at[k - 1], (h, peer)
        )
        copy.start()
        msg_copies.append(copy)
    for key in moves:
        for copy in moves[key] + stages[key]:
            copy.wait_send()
    turn_keys(3)
    for copy in msg_copies:
        copy.wait_recv()

    fresh_rows = []
    for i in range(2 * KV_HEADS):
        raw = qkv[i, PR:, :].astype(F32)
        cols = pl.ds((i % KV_HEADS) * HD, HD)
        if i < KV_HEADS:
            raw = rotate(raw, cosine, sine)
            kx[:PR, cols] = raw.astype(BF16)
        else:
            vx[:PR, cols] = raw.astype(BF16)
        fresh_rows.append(raw)

    rotated = [
        rotate(qkv[i, :PR, :].astype(F32), cosine, sine).astype(BF16) for i in range(NF)
    ]
    nothing = jnp.zeros((OWN, HD), BF16)
    queries = []
    for p in range(PAIRS):
        upper = jnp.concatenate(rotated[4 * p : 4 * p + 2], axis=0)
        lower = jnp.concatenate(rotated[4 * p + 2 : 4 * p + 4], axis=0)
        queries.append(
            jnp.concatenate(
                [
                    jnp.concatenate([upper, nothing], axis=1),
                    jnp.concatenate([nothing, lower], axis=1),
                ],
                axis=0,
            )
        )
    pair_rows, pair_cols = 2 * OWN, 2 * HD
    lane = lax.broadcasted_iota(jnp.int32, (pair_rows, HD), 1)
    step_row = lax.rem(lax.div(lax.broadcasted_iota(jnp.int32, (pair_rows, HD), 0), 8), 2)
    fresh_live = (lane == 0) | ((lane == 8) & (step_row == 1))
    nt = (((1,), (1,)), ((), ()))
    def attend(p):
        pair = pl.ds(p * pair_cols, pair_cols)
        rows_of = pl.ds(p * pair_rows, pair_rows)
        fresh = lax.dot_general(queries[p], kx[:, pair], nt, preferred_element_type=F32)
        fresh = jnp.where(fresh_live, fresh * SCALE, MASKED)

        def score_step(c, high):
            rows = pl.ds(pl.multiple_of(c * CHUNK, CHUNK), CHUNK)
            position = lax.broadcasted_iota(jnp.int32, (8, CHUNK), 1) + c * CHUNK
            cap = jnp.where(position < length, -MASKED, MASKED)
            cap = jnp.concatenate([cap] * (pair_rows // 8), axis=0)
            s = jnp.dot(queries[p], k_t[pair, rows], preferred_element_type=F32)
            s = jnp.minimum(s * SCALE, cap)
            scores[rows_of, rows] = s
            for t in range(CHUNK // HD):
                high = jnp.maximum(high, s[:, t * HD : (t + 1) * HD])
            return high

        high = lax.fori_loop(0, lmax // CHUNK, score_step, fresh)
        peak = jnp.broadcast_to(jnp.max(high, axis=1, keepdims=True), (pair_rows, HD))
        weights = jnp.exp2(fresh - peak).astype(BF16)
        weighted[p] = jnp.dot(weights, vx[:, pair], preferred_element_type=F32)

        def value_step(c, total):
            rows = pl.ds(pl.multiple_of(c * CHUNK, CHUNK), CHUNK)
            s = scores[rows_of, rows]
            pieces = []
            for t in range(CHUNK // HD):
                piece = jnp.exp2(s[:, t * HD : (t + 1) * HD] - peak).astype(BF16)
                total = total + piece.astype(F32)
                pieces.append(piece)
            weighted[p] += jnp.dot(
                jnp.concatenate(pieces, axis=1), v_v[rows, pair], preferred_element_type=F32
            )
            return total

        if p == 0:
            for copy in v_loads:
                copy.wait()
        total = lax.fori_loop(0, lmax // CHUNK, value_step, weights.astype(F32))
        weight_sum = jnp.sum(total, axis=1, keepdims=True)
        for i in range(2):
            rows = slice(i * OWN, (i + 1) * OWN)
            attended = weighted[p, rows, i * HD : (i + 1) * HD] / weight_sum[rows]
            attended = attended.astype(BF16)
            att_send[4 * p + 2 * i] = attended[:PR]
            att_send[4 * p + 2 * i + 1] = attended[PR:]

    odd = lax.rem(y + z, 2)
    slot = lax.rem(lax.div(y, 2) + lax.div(z, 2), 2)

    def send_attended(p):
        for m in range(4):
            peer = 4 * p + lax.rem(f + m, 4)
            landing = att_recv.at[odd, slot, f]

            @pl.when(peer == f)
            def _():
                pltpu.make_async_copy(
                    att_send.at[f], landing, att_rsem.at[odd, slot]
                ).start()

            for k in range(NY):
                chip = lax.rem(z + odd * k, NY) * NY + lax.rem(y + (1 - odd) * k, NY)
                copy = remote(
                    att_send.at[peer], landing, att_ssem.at[k], att_rsem.at[odd, slot],
                    (chip, peer),
                )
                if k == 0:
                    pl.when(peer != f)(copy.start)
                else:
                    copy.start()

    for p in range(PAIRS):
        attend(p)
        send_attended(p)

    for i in range(2 * KV_HEADS):
        ne[0:1, i * HD : (i + 1) * HD] = fresh_rows[i][0:1]
        ne[1:2, i * HD : (i + 1) * HD] = fresh_rows[i][8:9]
    results[PR:, :, :] = ne[0:2, :].reshape(1, STEPS, ne.shape[1]).astype(BF16)

    line_copies = [[], []]
    for part_id in range(2):
        for side in range(2):
            whole = att_recv.at[side, part_id]
            pltpu.make_async_copy(whole, whole, att_rsem.at[side, part_id]).wait()
            pos = (z, y)[side]
            att_f32[...] = att_recv[side, part_id].astype(F32).reshape(NF * PR, HD)
            for j in range(8):
                rows_all[part_id, side, pos, :, j * HD : (j + 1) * HD] = att_f32[
                    pl.ds(j, PR, stride=8), :
                ].astype(BF16)
            mine_rows = rows_all.at[part_id, side, pos]
            for k in range(1, NY):
                q = lax.rem(pos + k, NY)
                device = (q * NY + y, f) if side == 0 else (z * NY + q, f)
                copy = remote(
                    mine_rows, mine_rows,
                    line_ssem.at[part_id, side, k - 1], line_rsem.at[part_id, side, k - 1],
                    device,
                )
                copy.start()
                line_copies[part_id].append(copy)
    wout_load.wait()
    for copy in msg_copies:
        copy.wait_send()
    for k in range(NY):
        sent = att_send.at[pl.ds(0, NF - 1)] if k == 0 else att_send
        pltpu.make_async_copy(sent, sent, att_ssem.at[k]).wait()

    def out_rows(index):
        return pl.ds(pl.multiple_of(index * OWN, OWN), OWN)

    sib_copies = [[], []]
    for part_id in range(2):
        for copy in line_copies[part_id]:
            copy.wait_recv()
        product = jnp.dot(
            rows_all[part_id].reshape(NH * PR // 2, wout_v.shape[0]),
            wout_v[...],
            preferred_element_type=F32,
        )
        for side in range(2):
            for q in range(NY):
                far = 2 * ((part_id + q // 2) % 2) + (q + side) % 2
                home = q * NY + far if side == 0 else far * NY + q
                first = (side * NY + q) * PR
                opart[home * PR : (home + 1) * PR, :] = product[first : first + PR]
        for e in range(2):
            x = 2 * lax.rem(1 + core + part_id, 2) + e
            copy = remote(
                opart.at[out_rows(2 * x + 1 - core)], sib_recv.at[part_id, e],
                sib_ssem.at[part_id, e], sib_rsem.at[part_id, e], (h, sib),
            )
            copy.start()
            sib_copies[part_id].append(copy)
    fin_copies = []
    for part_id in range(2):
        for copy in sib_copies[part_id]:
            copy.wait_recv()
        for e in range(2):
            x = 2 * lax.rem(core + part_id, 2) + e
            hop = lax.rem(x - cx + NX, NX)
            there = lax.rem(hop + NX - 1, NX)
            copy = remote(
                fin_send.at[part_id, e], fin_recv.at[there],
                fin_ssem.at[part_id, e], fin_rsem.at[there], (h, 2 * x + core),
            )
            fin_copies.append((hop, copy))

            @pl.when(hop != 0)
            def _():
                total = opart[out_rows(2 * x + core), :] + sib_recv[part_id, e]
                fin_send[part_id, e] = total.astype(BF16)
                copy.start()

    for copies in sib_copies + line_copies:
        for copy in copies:
            copy.wait_send()
    own_part = lax.rem(core + lax.div(cx, 2), 2)
    result = opart[out_rows(f), :] + sib_recv[own_part, lax.rem(cx, 2)]
    for k in range(1, NX):
        pltpu.make_async_copy(
            fin_recv.at[k - 1], fin_recv.at[k - 1], fin_rsem.at[k - 1]
        ).wait()
        result = result + fin_recv[k - 1].astype(F32)
    results[:PR, :, :] = result.reshape(PR, STEPS, result.shape[1]).astype(BF16)
    for hop, copy in fin_copies:
        pl.when(hop != 0)(copy.wait_send)


def hand_out(results, out, entries, sem):
    rows = out.shape[0]
    copies = [
        pltpu.make_async_copy(results.at[pl.ds(0, rows)], out, sem.at[0]),
        pltpu.make_async_copy(results.at[pl.ds(rows, 1)], entries, sem.at[1]),
    ]
    for copy in copies:
        copy.start()
    for copy in copies:
        copy.wait()


def body(tokens, norm_gain, query_weight, w_keyval, w_out, cache_keys, cache_values, lengths):
    width = tokens.shape[2]
    lmax = cache_keys.shape[1]
    qcols = query_weight.shape[1]
    kvcols = w_keyval.shape[1]
    halves = np.arange(HD // 2, dtype=np.float64) * (2.0 / HD)
    freq = (ROPE_BASE ** (-halves)).astype(np.float32)
    freq = jnp.asarray(np.tile(np.concatenate([freq, freq])[None, :], (PR, 1)))
    any_spec = pl.BlockSpec(memory_space=pl.ANY)
    hbm_spec = pl.BlockSpec(memory_space=pltpu.HBM)
    vmem_spec = pl.BlockSpec(memory_space=pltpu.VMEM)
    dma = pltpu.SemaphoreType.DMA
    rows = NH * PR
    results = pl.pallas_call(
        kernel,
        out_shape=pltpu.VMEM((PR + 1, STEPS, width), BF16),
        in_specs=[hbm_spec] * 9,
        out_specs=vmem_spec,
        scratch_shapes=[
            pltpu.SMEM(lengths.shape, jnp.int32),
            pltpu.VMEM(tokens.shape, BF16),
            pltpu.VMEM((OWN, width), BF16),
            pltpu.VMEM((PR, HD), F32),
            pltpu.VMEM((width,), BF16),
            pltpu.VMEM((width, qcols), BF16),
            pltpu.VMEM((width, kvcols), BF16),
            pltpu.VMEM((qcols, width), BF16),
            pltpu.VMEM((lmax, KV_HEADS * HD), BF16),
            pltpu.VMEM((KV_HEADS * HD, lmax), BF16),
            pltpu.VMEM((lmax, KV_HEADS * HD), BF16),
            pltpu.VMEM((rows, width), BF16),
            pltpu.VMEM((rows // 2, width), BF16),
            pltpu.VMEM((8, HD), F32),
            pltpu.VMEM((NH - 1, 8, HD), F32),
            pltpu.VMEM((NF, 8, HD), F32),
            pltpu.VMEM((NY, NY, PR, qcols + kvcols), F32),
            pltpu.VMEM((2, NY, PR // 2, qcols + kvcols), F32),
            pltpu.VMEM((2, NY, PR // 2, qcols + kvcols), F32),
            pltpu.VMEM((2, NY, PR // 2, qcols + kvcols), F32),
            pltpu.VMEM((2, NY, PR // 2, qcols + kvcols), F32),
            pltpu.VMEM((2, NY - 1, PR // 2, qcols + kvcols), F32),
            pltpu.VMEM((NF * PR, HD), F32),
            pltpu.VMEM((NF, 2 * PR, HD), BF16),
            pltpu.VMEM((NF, 2 * PR, HD), BF16),
            pltpu.VMEM((HD, KV_HEADS * HD), BF16),
            pltpu.VMEM((HD, KV_HEADS * HD), BF16),
            pltpu.VMEM((8, 2 * KV_HEADS * HD), F32),
            pltpu.VMEM((KV_HEADS * OWN, lmax), F32),
            pltpu.VMEM((PAIRS, 2 * OWN, 2 * HD), F32),
            pltpu.VMEM((NF, PR, HD), BF16),
            pltpu.VMEM((2, 2, NF, PR, HD), BF16),
            pltpu.VMEM((NF * PR, HD), F32),
            pltpu.VMEM((2, 2, NY, PR, qcols), BF16),
            pltpu.VMEM((rows, width), F32),
            pltpu.VMEM((2, 2, OWN, width), F32),
            pltpu.VMEM((2, 2, OWN, width), BF16),
            pltpu.VMEM((NX - 1, OWN, width), BF16),
            dma((8,)),
            dma((CACHE_COPIES,)),
            dma((CACHE_COPIES,)),
            dma((NX - 1,)), dma((NX - 1,)),
            dma((NX,)), dma((NX,)),
            dma((NH - 1,)), dma((NH - 1,)),
            dma((NF - 1,)), dma((NF - 1,)),
            dma((2, 2, 6)), dma((2, 2, 6)),
            dma((2, 2, NY - 1)), dma((2, 2, NY - 1)),
            dma((NF - 1,)), dma((NF - 1,)),
            dma((NY,)), dma((2, 2)),
            dma((2, 2, NY - 1)), dma((2, 2, NY - 1)),
            dma((2, 2)), dma((2, 2)),
            dma((2, 2)), dma((NX - 1,)),
        ],
        compiler_params=pltpu.CompilerParams(
            collective_id=0, has_side_effects=True, vmem_limit_bytes=48 * 2**20
        ),
        name="decode_block",
    )(
        *[
            pltpu.with_memory_space_constraint(array, pltpu.HBM)
            for array in (
                lengths, freq, tokens, norm_gain, query_weight, w_keyval, w_out,
                cache_keys, cache_values,
            )
        ],
    )
    return pl.pallas_call(
        hand_out,
        out_shape=(
            jax.ShapeDtypeStruct(tokens.shape, BF16),
            jax.ShapeDtypeStruct((1, STEPS, 2 * KV_HEADS * HD), BF16),
        ),
        in_specs=[vmem_spec],
        out_specs=(any_spec, any_spec),
        scratch_shapes=[dma((2,))],
        name="hand_out",
    )(pltpu.with_memory_space_constraint(results, pltpu.VMEM))


def solution(mesh):
    in_specs = (
        P("ffn", None, "hid"),
        P("hid"),
        P("hid", "ffn"),
        P("hid", "ffn"),
        P("ffn", "hid"),
        P(("hid", "ffn"), None, None),
        P(("hid", "ffn"), None, None),
        P(),
    )
    out_specs = (P("ffn", None, "hid"), P(("hid", "ffn"), None, None))
    return jax.shard_map(body, mesh=mesh, in_specs=in_specs, out_specs=out_specs, check_vma=False)
```

```python
import functools

import jax
import jax.numpy as jnp
import numpy as np
from jax import lax
from jax.experimental import pallas as pl
from jax.experimental.pallas import tpu as pltpu
from jax.sharding import PartitionSpec as P

MESH = pl.DeviceIdType.MESH
F32 = jnp.float32
BF16 = jnp.bfloat16

HEADS = 64
KV_HEADS = 4
HD = 128
STEPS = 2
EPSILON = 1e-05
ROPE_BASE = 500000.0
SCALE = HD ** (-0.5) * 1.4426950408889634
MASKED = -1e30

NH = 16
NF = 8
NX = 4
NY = 4
TURN = 512
OWN = 32
PR = 16
CHUNK = 4096
CACHE_COPIES = 4
PAIRS = KV_HEADS // 2


def remote(src, dst, send_sem, recv_sem, device):
    return pltpu.make_async_remote_copy(
        src_ref=src,
        dst_ref=dst,
        send_sem=send_sem,
        recv_sem=recv_sem,
        device_id=device,
        device_id_type=MESH,
    )


def rotate(vectors, cosine, sine):
    return vectors * cosine + pltpu.roll(vectors, HD // 2, 1) * sine


def kernel(
    lengths_hbm, freq, tokens, gain, wq, wkv, wout, cache_k, cache_v,
    results,
    lengths, raw_v, tok_v, freq_v, gain_v, wq_v, wkv_v, wout_v, k_v, k_t, v_v,
    x_all, normed, ss_own, ss_recv, tot_all, part, line_recv, mine, mine_recv,
    spread, msg, qkv, kx, vx, ne, scores, weighted, att_send, att_recv, att_f32, rows_all,
    opart, sib_recv, fin_send, fin_recv,
    local_sem, k_sem, v_sem,
    tok_ssem, tok_rsem, fwd_ssem, fwd_rsem, ss_ssem, ss_rsem, tot_ssem, tot_rsem,
    ring_ssem, ring_rsem, stage_ssem, stage_rsem, msg_ssem, msg_rsem, att_ssem, att_rsem, line_ssem, line_rsem,
    sib_ssem, sib_rsem, fin_ssem, fin_rsem,
):
    h = lax.axis_index("hid")
    f = lax.axis_index("ffn")
    z = lax.div(h, NY)
    y = lax.rem(h, NY)
    cx = lax.div(f, 2)
    core = lax.rem(f, 2)
    sib = f + 1 - 2 * core
    lmax = cache_k.shape[1]

    barrier = pltpu.get_barrier_semaphore()
    tokens_load = pltpu.make_async_copy(tokens, raw_v, local_sem.at[0])
    tokens_load.start()

    def greet_hid(k, carry):
        pl.semaphore_signal(
            barrier, inc=1, device_id=(lax.rem(h + k, NH), f), device_id_type=MESH
        )
        return carry

    def greet_ffn(k, carry):
        pl.semaphore_signal(
            barrier, inc=1, device_id=(h, lax.rem(f + k, NF)), device_id_type=MESH
        )
        return carry

    lax.fori_loop(1, NF, greet_ffn, 0)
    lax.fori_loop(1, NH, greet_hid, 0)

    loads = []
    for i, (src, dst) in enumerate(
        [(gain, gain_v), (freq, freq_v), (wq, wq_v), (wkv, wkv_v), (lengths_hbm, lengths)]
    ):
        copy = pltpu.make_async_copy(src, dst, local_sem.at[1 + i])
        copy.start()
        loads.append(copy)
    span = lmax // CACHE_COPIES
    k_loads = []
    for i in range(CACHE_COPIES):
        copy = pltpu.make_async_copy(
            cache_k.at[0, pl.ds(i * span, span)], k_v.at[pl.ds(i * span, span)], k_sem.at[i]
        )
        copy.start()
        k_loads.append(copy)
    wout_load = pltpu.make_async_copy(wout, wout_v, local_sem.at[6])
    wout_load.start()

    def turn_keys(quarter):
        k_loads[quarter].wait()

        def turn(i, carry):
            rows = pl.ds(pl.multiple_of(quarter * span + i * TURN, TURN), TURN)
            k_t[:, rows] = k_v[rows, :].T
            return carry

        lax.fori_loop(0, span // TURN, turn, 0)

    tokens_load.wait()
    x_f32 = raw_v[...].astype(F32).reshape(tok_v.shape)
    x_own = x_f32.astype(BF16)
    tok_v[...] = x_own
    pl.semaphore_wait(barrier, NH + NF - 2)

    def block(index):
        return x_all.at[pl.ds(pl.multiple_of(index * OWN, OWN), OWN)]

    tok_copies = []
    for k in (1, 3, 2):
        peer = 2 * lax.rem(cx + k, NX) + core
        copy = remote(tok_v, block(f), tok_ssem.at[k - 1], tok_rsem.at[k - 1], (h, peer))
        copy.start()
        tok_copies.append((k, copy))
    fwd_copies = [remote(tok_v, block(f), fwd_ssem.at[0], fwd_rsem.at[0], (h, sib))]
    fwd_copies[0].start()

    sums = jnp.sum(x_f32 * x_f32, axis=1, keepdims=True)
    row_id = lax.broadcasted_iota(jnp.int32, (OWN, HD), 0)
    lane_id = lax.broadcasted_iota(jnp.int32, (OWN, HD), 1)
    diagonal = row_id == lane_id
    own_sums = jnp.sum(jnp.where(diagonal, sums, 0.0), axis=0, keepdims=True)
    ss_own[...] = jnp.broadcast_to(own_sums, (8, HD))

    def ss_copy(k):
        return remote(
            ss_own, ss_recv.at[k - 1], ss_ssem.at[k - 1], ss_rsem.at[k - 1],
            (lax.rem(h + k, NH), f),
        )

    def ss_start(k, carry):
        ss_copy(k).start()
        return carry

    lax.fori_loop(1, NH, ss_start, 0)
    x_all[pl.ds(pl.multiple_of(f * OWN, OWN), OWN), :] = x_own

    def ss_add(k, total):
        ss_copy(k).wait_recv()
        return total + ss_recv[k - 1]

    total = lax.fori_loop(1, NH, ss_add, ss_own[...])
    tot_all[f] = total
    tot_copies = []
    for k in range(1, NF):
        copy = remote(
            tot_all.at[f], tot_all.at[f], tot_ssem.at[k - 1], tot_rsem.at[k - 1],
            (h, lax.rem(f + k, NF)),
        )
        copy.start()
        tot_copies.append(copy)
    turn_keys(0)
    for k, tok_copy in tok_copies:
        tok_copy.wait_recv()
        came = 2 * lax.rem(cx + NX - k, NX) + core
        copy = remote(block(came), block(came), fwd_ssem.at[k], fwd_rsem.at[k], (h, sib))
        copy.start()
        fwd_copies.append(copy)

    loads[4].wait()
    length = lengths[h * NF + f]
    step_of = lax.div(lax.broadcasted_iota(jnp.int32, (PR, HD), 0), 8)
    loads[1].wait()
    angles = (step_of + length).astype(F32) * freq_v[...]
    cosine = jnp.cos(angles)
    sine = jnp.sin(angles)
    sine = jnp.where(
        lax.broadcasted_iota(jnp.int32, (PR, HD), 1) < HD // 2, -sine, sine
    )

    kx[...] = jnp.zeros_like(kx)
    vx[...] = jnp.zeros_like(vx)
    for copy in tot_copies:
        copy.wait_recv()
    loads[0].wait()
    width = x_all.shape[1]
    qcols = wq_v.shape[1]
    full = width * NH
    gain_row = gain_v[...].astype(F32).reshape(1, width)

    def project(parity):
        for x in range(NX):
            b = 2 * x + parity
            lane_sums = tot_all[b][0:1, :]
            row_sums = jnp.sum(jnp.where(diagonal, lane_sums, 0.0), axis=1, keepdims=True)
            inverse = lax.rsqrt(row_sums / full + EPSILON)
            normed[x * OWN : (x + 1) * OWN, :] = (
                block(b)[...].astype(F32) * inverse * gain_row
            ).astype(BF16)
        lhs = normed[...]
        for cols, weights in ((slice(0, qcols), wq_v), (slice(qcols, None), wkv_v)):
            product = jnp.dot(lhs, weights[...], preferred_element_type=F32)
            part[:, pl.ds(2 * parity, 2), :, cols] = product.reshape(NX, 2, PR, product.shape[1])

    loads[2].wait()
    loads[3].wait()
    project(core)
    turn_keys(1)
    for copy in fwd_copies:
        copy.wait_recv()
    project(1 - core)

    half = PR // 2
    here = (y, z)

    def to_line(side, q):
        return (z * NY + q, f) if side == 0 else (q * NY + y, f)

    def view(side, q):
        return part.at[:, q, pl.ds(0, half)] if side == 0 else part.at[q, :, pl.ds(half, half)]

    moves = [[], []]
    for k in (2, 1, 3):
        for side in range(2):
            q = lax.rem(here[side] + k, NY)
            copy = remote(
                view(side, q), line_recv.at[side, k - 1],
                ring_ssem.at[side, k - 1], ring_rsem.at[side, k - 1], to_line(side, q),
            )
            copy.start()
            moves[side].append(copy)
    v_loads = []
    for i in range(CACHE_COPIES):
        copy = pltpu.make_async_copy(
            cache_v.at[0, pl.ds(i * span, span)], v_v.at[pl.ds(i * span, span)], v_sem.at[i]
        )
        copy.start()
        v_loads.append(copy)

    def ss_sent(k, carry):
        ss_copy(k).wait_send()
        return carry

    lax.fori_loop(1, NH, ss_sent, 0)
    for copy in tot_copies + fwd_copies + [copy for _, copy in tok_copies]:
        copy.wait_send()
    turn_keys(2)
    stages = [[], []]
    for side in range(2):
        for copy in moves[side]:
            copy.wait_recv()
        mine[side] = (
            view(side, here[side])[...]
            + line_recv[side, 0] + line_recv[side, 1] + line_recv[side, 2]
        )
        for k in (2, 1, 3):
            q = lax.rem(here[1 - side] + k, NY)
            copy = remote(
                mine.at[side, q], mine_recv.at[side, k - 1],
                stage_ssem.at[side, k - 1], stage_rsem.at[side, k - 1], to_line(1 - side, q),
            )
            copy.start()
            stages[side].append(copy)
    turn_keys(3)
    halves = []
    for side in range(2):
        total = mine[side, here[1 - side]]
        for copy in stages[side]:
            copy.wait_recv()
        for k in range(NY - 1):
            total = total + mine_recv[side, k]
        halves.append(total)
    summed = jnp.concatenate(halves, axis=0)

    for j in range(8):
        spread[pl.ds(j, PR, stride=8), :] = summed[:, j * HD : (j + 1) * HD]
    msg[:, :PR, :] = spread[...].reshape(NF, PR, HD).astype(BF16)
    spread[...] = jnp.zeros_like(spread)
    spread[pl.ds(0, PR, stride=8), :] = summed[:, qcols:]
    msg[:, PR:, :] = spread[...].reshape(NF, PR, HD).astype(BF16)
    qkv[f] = msg[f]
    msg_copies = []
    for k in range(1, NF):
        peer = lax.rem(f + k, NF)
        copy = remote(
            msg.at[peer], qkv.at[f], msg_ssem.at[k - 1], msg_rsem.at[k - 1], (h, peer)
        )
        copy.start()
        msg_copies.append(copy)
    for copy in moves[0] + moves[1] + stages[0] + stages[1]:
        copy.wait_send()
    for copy in msg_copies:
        copy.wait_recv()

    fresh_rows = []
    for i in range(2 * KV_HEADS):
        raw = qkv[i, PR:, :].astype(F32)
        cols = pl.ds((i % KV_HEADS) * HD, HD)
        if i < KV_HEADS:
            raw = rotate(raw, cosine, sine)
            kx[:PR, cols] = raw.astype(BF16)
        else:
            vx[:PR, cols] = raw.astype(BF16)
        fresh_rows.append(raw)

    rotated = [
        rotate(qkv[i, :PR, :].astype(F32), cosine, sine).astype(BF16) for i in range(NF)
    ]
    nothing = jnp.zeros((OWN, HD), BF16)
    queries = []
    for p in range(PAIRS):
        upper = jnp.concatenate(rotated[4 * p : 4 * p + 2], axis=0)
        lower = jnp.concatenate(rotated[4 * p + 2 : 4 * p + 4], axis=0)
        queries.append(
            jnp.concatenate(
                [
                    jnp.concatenate([upper, nothing], axis=1),
                    jnp.concatenate([nothing, lower], axis=1),
                ],
                axis=0,
            )
        )
    pair_rows, pair_cols = 2 * OWN, 2 * HD
    lane = lax.broadcasted_iota(jnp.int32, (pair_rows, HD), 1)
    step_row = lax.rem(lax.div(lax.broadcasted_iota(jnp.int32, (pair_rows, HD), 0), 8), 2)
    fresh_live = (lane == 0) | ((lane == 8) & (step_row == 1))
    nt = (((1,), (1,)), ((), ()))
    def attend(p):
        pair = pl.ds(p * pair_cols, pair_cols)
        rows_of = pl.ds(p * pair_rows, pair_rows)
        fresh = lax.dot_general(queries[p], kx[:, pair], nt, preferred_element_type=F32)
        fresh = jnp.where(fresh_live, fresh * SCALE, MASKED)

        def score_step(c, high):
            rows = pl.ds(pl.multiple_of(c * CHUNK, CHUNK), CHUNK)
            position = lax.broadcasted_iota(jnp.int32, (8, CHUNK), 1) + c * CHUNK
            cap = jnp.where(position < length, -MASKED, MASKED)
            cap = jnp.concatenate([cap] * (pair_rows // 8), axis=0)
            s = jnp.dot(queries[p], k_t[pair, rows], preferred_element_type=F32)
            s = jnp.minimum(s * SCALE, cap)
            scores[rows_of, rows] = s
            for t in range(CHUNK // HD):
                high = jnp.maximum(high, s[:, t * HD : (t + 1) * HD])
            return high

        high = lax.fori_loop(0, lmax // CHUNK, score_step, fresh)
        peak = jnp.broadcast_to(jnp.max(high, axis=1, keepdims=True), (pair_rows, HD))
        weights = jnp.exp2(fresh - peak).astype(BF16)
        weighted[p] = jnp.dot(weights, vx[:, pair], preferred_element_type=F32)

        def value_step(c, total):
            rows = pl.ds(pl.multiple_of(c * CHUNK, CHUNK), CHUNK)
            s = scores[rows_of, rows]
            pieces = []
            for t in range(CHUNK // HD):
                piece = jnp.exp2(s[:, t * HD : (t + 1) * HD] - peak).astype(BF16)
                total = total + piece.astype(F32)
                pieces.append(piece)
            weighted[p] += jnp.dot(
                jnp.concatenate(pieces, axis=1), v_v[rows, pair], preferred_element_type=F32
            )
            return total

        if p == 0:
            for copy in v_loads:
                copy.wait()
        total = lax.fori_loop(0, lmax // CHUNK, value_step, weights.astype(F32))
        weight_sum = jnp.sum(total, axis=1, keepdims=True)
        for i in range(2):
            rows = slice(i * OWN, (i + 1) * OWN)
            attended = weighted[p, rows, i * HD : (i + 1) * HD] / weight_sum[rows]
            attended = attended.astype(BF16)
            att_send[4 * p + 2 * i] = attended[:PR]
            att_send[4 * p + 2 * i + 1] = attended[PR:]

    odd = lax.rem(y + z, 2)
    slot = lax.rem(lax.div(y, 2) + lax.div(z, 2), 2)

    def send_attended(p):
        for m in range(4):
            peer = 4 * p + lax.rem(f + m, 4)
            landing = att_recv.at[odd, slot, f]

            @pl.when(peer == f)
            def _():
                pltpu.make_async_copy(
                    att_send.at[f], landing, att_rsem.at[odd, slot]
                ).start()

            for k in range(NY):
                chip = lax.rem(z + odd * k, NY) * NY + lax.rem(y + (1 - odd) * k, NY)
                copy = remote(
                    att_send.at[peer], landing, att_ssem.at[k], att_rsem.at[odd, slot],
                    (chip, peer),
                )
                if k == 0:
                    pl.when(peer != f)(copy.start)
                else:
                    copy.start()

    for p in range(PAIRS):
        attend(p)
        send_attended(p)

    for i in range(2 * KV_HEADS):
        ne[0:1, i * HD : (i + 1) * HD] = fresh_rows[i][0:1]
        ne[1:2, i * HD : (i + 1) * HD] = fresh_rows[i][8:9]
    results[PR:, :, :] = ne[0:2, :].reshape(1, STEPS, ne.shape[1]).astype(BF16)

    line_copies = [[], []]
    for part_id in range(2):
        for side in range(2):
            whole = att_recv.at[side, part_id]
            pltpu.make_async_copy(whole, whole, att_rsem.at[side, part_id]).wait()
            pos = (z, y)[side]
            att_f32[...] = att_recv[side, part_id].astype(F32).reshape(NF * PR, HD)
            for j in range(8):
                rows_all[part_id, side, pos, :, j * HD : (j + 1) * HD] = att_f32[
                    pl.ds(j, PR, stride=8), :
                ].astype(BF16)
            mine_rows = rows_all.at[part_id, side, pos]
            for k in range(1, NY):
                q = lax.rem(pos + k, NY)
                device = (q * NY + y, f) if side == 0 else (z * NY + q, f)
                copy = remote(
                    mine_rows, mine_rows,
                    line_ssem.at[part_id, side, k - 1], line_rsem.at[part_id, side, k - 1],
                    device,
                )
                copy.start()
                line_copies[part_id].append(copy)
    wout_load.wait()
    for copy in msg_copies:
        copy.wait_send()
    for k in range(NY):
        sent = att_send.at[pl.ds(0, NF - 1)] if k == 0 else att_send
        pltpu.make_async_copy(sent, sent, att_ssem.at[k]).wait()

    def out_rows(index):
        return pl.ds(pl.multiple_of(index * OWN, OWN), OWN)

    sib_copies = [[], []]
    for part_id in range(2):
        for copy in line_copies[part_id]:
            copy.wait_recv()
        product = jnp.dot(
            rows_all[part_id].reshape(NH * PR // 2, wout_v.shape[0]),
            wout_v[...],
            preferred_element_type=F32,
        )
        for side in range(2):
            for q in range(NY):
                far = 2 * ((part_id + q // 2) % 2) + (q + side) % 2
                home = q * NY + far if side == 0 else far * NY + q
                first = (side * NY + q) * PR
                opart[home * PR : (home + 1) * PR, :] = product[first : first + PR]
        for e in range(2):
            x = 2 * lax.rem(1 + core + part_id, 2) + e
            copy = remote(
                opart.at[out_rows(2 * x + 1 - core)], sib_recv.at[part_id, e],
                sib_ssem.at[part_id, e], sib_rsem.at[part_id, e], (h, sib),
            )
            copy.start()
            sib_copies[part_id].append(copy)
    fin_copies = []
    for part_id in range(2):
        for copy in sib_copies[part_id]:
            copy.wait_recv()
        for e in range(2):
            x = 2 * lax.rem(core + part_id, 2) + e
            hop = lax.rem(x - cx + NX, NX)
            there = lax.rem(hop + NX - 1, NX)
            copy = remote(
                fin_send.at[part_id, e], fin_recv.at[there],
                fin_ssem.at[part_id, e], fin_rsem.at[there], (h, 2 * x + core),
            )
            fin_copies.append((hop, copy))

            @pl.when(hop != 0)
            def _():
                total = opart[out_rows(2 * x + core), :] + sib_recv[part_id, e]
                fin_send[part_id, e] = total.astype(BF16)
                copy.start()

    for copies in sib_copies + line_copies:
        for copy in copies:
            copy.wait_send()
    own_part = lax.rem(core + lax.div(cx, 2), 2)
    result = opart[out_rows(f), :] + sib_recv[own_part, lax.rem(cx, 2)]
    for k in range(1, NX):
        pltpu.make_async_copy(
            fin_recv.at[k - 1], fin_recv.at[k - 1], fin_rsem.at[k - 1]
        ).wait()
        result = result + fin_recv[k - 1].astype(F32)
    results[:PR, :, :] = result.reshape(PR, STEPS, result.shape[1]).astype(BF16)
    for hop, copy in fin_copies:
        pl.when(hop != 0)(copy.wait_send)


def hand_out(results, out, entries, sem):
    rows = out.shape[0]
    copies = [
        pltpu.make_async_copy(results.at[pl.ds(0, rows)], out, sem.at[0]),
        pltpu.make_async_copy(results.at[pl.ds(rows, 1)], entries, sem.at[1]),
    ]
    for copy in copies:
        copy.start()
    for copy in copies:
        copy.wait()


def body(tokens, norm_gain, query_weight, w_keyval, w_out, cache_keys, cache_values, lengths):
    width = tokens.shape[2]
    lmax = cache_keys.shape[1]
    qcols = query_weight.shape[1]
    kvcols = w_keyval.shape[1]
    halves = np.arange(HD // 2, dtype=np.float64) * (2.0 / HD)
    freq = (ROPE_BASE ** (-halves)).astype(np.float32)
    freq = jnp.asarray(np.tile(np.concatenate([freq, freq])[None, :], (PR, 1)))
    any_spec = pl.BlockSpec(memory_space=pl.ANY)
    hbm_spec = pl.BlockSpec(memory_space=pltpu.HBM)
    vmem_spec = pl.BlockSpec(memory_space=pltpu.VMEM)
    dma = pltpu.SemaphoreType.DMA
    rows = NH * PR
    results = pl.pallas_call(
        kernel,
        out_shape=pltpu.VMEM((PR + 1, STEPS, width), BF16),
        in_specs=[hbm_spec] * 9,
        out_specs=vmem_spec,
        scratch_shapes=[
            pltpu.SMEM(lengths.shape, jnp.int32),
            pltpu.VMEM(tokens.shape, BF16),
            pltpu.VMEM((OWN, width), BF16),
            pltpu.VMEM((PR, HD), F32),
            pltpu.VMEM((width,), BF16),
            pltpu.VMEM((width, qcols), BF16),
            pltpu.VMEM((width, kvcols), BF16),
            pltpu.VMEM((qcols, width), BF16),
            pltpu.VMEM((lmax, KV_HEADS * HD), BF16),
            pltpu.VMEM((KV_HEADS * HD, lmax), BF16),
            pltpu.VMEM((lmax, KV_HEADS * HD), BF16),
            pltpu.VMEM((rows, width), BF16),
            pltpu.VMEM((rows // 2, width), BF16),
            pltpu.VMEM((8, HD), F32),
            pltpu.VMEM((NH - 1, 8, HD), F32),
            pltpu.VMEM((NF, 8, HD), F32),
            pltpu.VMEM((NY, NY, PR, qcols + kvcols), F32),
            pltpu.VMEM((2, NY - 1, NY, PR // 2, qcols + kvcols), F32),
            pltpu.VMEM((2, NY, PR // 2, qcols + kvcols), F32),
            pltpu.VMEM((2, NY - 1, PR // 2, qcols + kvcols), F32),
            pltpu.VMEM((NF * PR, HD), F32),
            pltpu.VMEM((NF, 2 * PR, HD), BF16),
            pltpu.VMEM((NF, 2 * PR, HD), BF16),
            pltpu.VMEM((HD, KV_HEADS * HD), BF16),
            pltpu.VMEM((HD, KV_HEADS * HD), BF16),
            pltpu.VMEM((8, 2 * KV_HEADS * HD), F32),
            pltpu.VMEM((KV_HEADS * OWN, lmax), F32),
            pltpu.VMEM((PAIRS, 2 * OWN, 2 * HD), F32),
            pltpu.VMEM((NF, PR, HD), BF16),
            pltpu.VMEM((2, 2, NF, PR, HD), BF16),
            pltpu.VMEM((NF * PR, HD), F32),
            pltpu.VMEM((2, 2, NY, PR, qcols), BF16),
            pltpu.VMEM((rows, width), F32),
            pltpu.VMEM((2, 2, OWN, width), F32),
            pltpu.VMEM((2, 2, OWN, width), BF16),
            pltpu.VMEM((NX - 1, OWN, width), BF16),
            dma((8,)),
            dma((CACHE_COPIES,)),
            dma((CACHE_COPIES,)),
            dma((NX - 1,)), dma((NX - 1,)),
            dma((NX,)), dma((NX,)),
            dma((NH - 1,)), dma((NH - 1,)),
            dma((NF - 1,)), dma((NF - 1,)),
            dma((2, NY - 1)), dma((2, NY - 1)),
            dma((2, NY - 1)), dma((2, NY - 1)),
            dma((NF - 1,)), dma((NF - 1,)),
            dma((NY,)), dma((2, 2)),
            dma((2, 2, NY - 1)), dma((2, 2, NY - 1)),
            dma((2, 2)), dma((2, 2)),
            dma((2, 2)), dma((NX - 1,)),
        ],
        compiler_params=pltpu.CompilerParams(
            collective_id=0, has_side_effects=True, vmem_limit_bytes=48 * 2**20
        ),
        name="decode_block",
    )(
        *[
            pltpu.with_memory_space_constraint(array, pltpu.HBM)
            for array in (
                lengths, freq, tokens, norm_gain, query_weight, w_keyval, w_out,
                cache_keys, cache_values,
            )
        ],
    )
    return pl.pallas_call(
        hand_out,
        out_shape=(
            jax.ShapeDtypeStruct(tokens.shape, BF16),
            jax.ShapeDtypeStruct((1, STEPS, 2 * KV_HEADS * HD), BF16),
        ),
        in_specs=[vmem_spec],
        out_specs=(any_spec, any_spec),
        scratch_shapes=[dma((2,))],
        name="hand_out",
    )(pltpu.with_memory_space_constraint(results, pltpu.VMEM))


def solution(mesh):
    in_specs = (
        P("ffn", None, "hid"),
        P("hid"),
        P("hid", "ffn"),
        P("hid", "ffn"),
        P("ffn", "hid"),
        P(("hid", "ffn"), None, None),
        P(("hid", "ffn"), None, None),
        P(),
    )
    out_specs = (P("ffn", None, "hid"), P(("hid", "ffn"), None, None))
    return jax.shard_map(body, mesh=mesh, in_specs=in_specs, out_specs=out_specs, check_vma=False)
```

```python
import functools

import jax
import jax.numpy as jnp
import numpy as np
from jax import lax
from jax.experimental import pallas as pl
from jax.experimental.pallas import tpu as pltpu
from jax.sharding import PartitionSpec as P

MESH = pl.DeviceIdType.MESH
F32 = jnp.float32
BF16 = jnp.bfloat16

HEADS = 64
KV_HEADS = 4
HD = 128
STEPS = 2
EPSILON = 1e-05
ROPE_BASE = 500000.0
SCALE = HD ** (-0.5) * 1.4426950408889634
MASKED = -1e30

NH = 16
NF = 8
NX = 4
NY = 4
TURN = 512
LOW = 512
OWN = 32
PR = 16
CHUNK = 4096
CACHE_COPIES = 4
PAIRS = KV_HEADS // 2


def remote(src, dst, send_sem, recv_sem, device):
    return pltpu.make_async_remote_copy(
        src_ref=src,
        dst_ref=dst,
        send_sem=send_sem,
        recv_sem=recv_sem,
        device_id=device,
        device_id_type=MESH,
    )


def rotate(vectors, cosine, sine):
    return vectors * cosine + pltpu.roll(vectors, HD // 2, 1) * sine


def kernel(
    lengths_hbm, freq, tokens, gain, wq, wkv, wout, cache_k, cache_v,
    results,
    lengths, raw_v, tok_v, freq_v, gain_v, wq_v, wkv_v, wout_v, k_v, k_t, v_v,
    x_all, normed, ss_own, ss_recv, tot_all, part, relay_low, relay_high, left_low, left_high,
    right_low, right_high, mine, mine_recv,
    spread, msg, qkv, kx, vx, ne, scores, weighted, att_send, att_recv, att_f32, rows_all,
    opart, sib_recv, fin_send, fin_recv,
    local_sem, k_sem, v_sem,
    tok_ssem, tok_rsem, fwd_ssem, fwd_rsem, ss_ssem, ss_rsem, tot_ssem, tot_rsem,
    ring_ssem, ring_rsem, stage_ssem, stage_rsem, msg_ssem, msg_rsem, att_ssem, att_rsem, line_ssem, line_rsem,
    sib_ssem, sib_rsem, fin_ssem, fin_rsem,
):
    h = lax.axis_index("hid")
    f = lax.axis_index("ffn")
    z = lax.div(h, NY)
    y = lax.rem(h, NY)
    cx = lax.div(f, 2)
    core = lax.rem(f, 2)
    sib = f + 1 - 2 * core
    lmax = cache_k.shape[1]

    barrier = pltpu.get_barrier_semaphore()
    tokens_load = pltpu.make_async_copy(tokens, raw_v, local_sem.at[0])
    tokens_load.start()

    def greet_hid(k, carry):
        pl.semaphore_signal(
            barrier, inc=1, device_id=(lax.rem(h + k, NH), f), device_id_type=MESH
        )
        return carry

    def greet_ffn(k, carry):
        pl.semaphore_signal(
            barrier, inc=1, device_id=(h, lax.rem(f + k, NF)), device_id_type=MESH
        )
        return carry

    lax.fori_loop(1, NF, greet_ffn, 0)
    lax.fori_loop(1, NH, greet_hid, 0)

    loads = []
    for i, (src, dst) in enumerate(
        [(gain, gain_v), (freq, freq_v), (wq, wq_v), (wkv, wkv_v), (lengths_hbm, lengths)]
    ):
        copy = pltpu.make_async_copy(src, dst, local_sem.at[1 + i])
        copy.start()
        loads.append(copy)
    span = lmax // CACHE_COPIES
    k_loads = []
    for i in range(CACHE_COPIES):
        copy = pltpu.make_async_copy(
            cache_k.at[0, pl.ds(i * span, span)], k_v.at[pl.ds(i * span, span)], k_sem.at[i]
        )
        copy.start()
        k_loads.append(copy)
    wout_load = pltpu.make_async_copy(wout, wout_v, local_sem.at[6])
    wout_load.start()

    def turn_keys(quarter):
        k_loads[quarter].wait()

        def turn(i, carry):
            rows = pl.ds(pl.multiple_of(quarter * span + i * TURN, TURN), TURN)
            k_t[:, rows] = k_v[rows, :].T
            return carry

        lax.fori_loop(0, span // TURN, turn, 0)

    tokens_load.wait()
    x_f32 = raw_v[...].astype(F32).reshape(tok_v.shape)
    x_own = x_f32.astype(BF16)
    tok_v[...] = x_own
    pl.semaphore_wait(barrier, NH + NF - 2)

    def block(index):
        return x_all.at[pl.ds(pl.multiple_of(index * OWN, OWN), OWN)]

    tok_copies = []
    for k in (1, 3, 2):
        peer = 2 * lax.rem(cx + k, NX) + core
        copy = remote(tok_v, block(f), tok_ssem.at[k - 1], tok_rsem.at[k - 1], (h, peer))
        copy.start()
        tok_copies.append((k, copy))
    fwd_copies = [remote(tok_v, block(f), fwd_ssem.at[0], fwd_rsem.at[0], (h, sib))]
    fwd_copies[0].start()

    sums = jnp.sum(x_f32 * x_f32, axis=1, keepdims=True)
    row_id = lax.broadcasted_iota(jnp.int32, (OWN, HD), 0)
    lane_id = lax.broadcasted_iota(jnp.int32, (OWN, HD), 1)
    diagonal = row_id == lane_id
    own_sums = jnp.sum(jnp.where(diagonal, sums, 0.0), axis=0, keepdims=True)
    ss_own[...] = jnp.broadcast_to(own_sums, (8, HD))

    def ss_copy(k):
        return remote(
            ss_own, ss_recv.at[k - 1], ss_ssem.at[k - 1], ss_rsem.at[k - 1],
            (lax.rem(h + k, NH), f),
        )

    def ss_start(k, carry):
        ss_copy(k).start()
        return carry

    lax.fori_loop(1, NH, ss_start, 0)
    x_all[pl.ds(pl.multiple_of(f * OWN, OWN), OWN), :] = x_own

    def ss_add(k, total):
        ss_copy(k).wait_recv()
        return total + ss_recv[k - 1]

    total = lax.fori_loop(1, NH, ss_add, ss_own[...])
    tot_all[f] = total
    tot_copies = []
    for k in range(1, NF):
        copy = remote(
            tot_all.at[f], tot_all.at[f], tot_ssem.at[k - 1], tot_rsem.at[k - 1],
            (h, lax.rem(f + k, NF)),
        )
        copy.start()
        tot_copies.append(copy)
    turn_keys(0)
    for k, tok_copy in tok_copies:
        tok_copy.wait_recv()
        came = 2 * lax.rem(cx + NX - k, NX) + core
        copy = remote(block(came), block(came), fwd_ssem.at[k], fwd_rsem.at[k], (h, sib))
        copy.start()
        fwd_copies.append(copy)

    loads[4].wait()
    length = lengths[h * NF + f]
    step_of = lax.div(lax.broadcasted_iota(jnp.int32, (PR, HD), 0), 8)
    loads[1].wait()
    angles = (step_of + length).astype(F32) * freq_v[...]
    cosine = jnp.cos(angles)
    sine = jnp.sin(angles)
    sine = jnp.where(
        lax.broadcasted_iota(jnp.int32, (PR, HD), 1) < HD // 2, -sine, sine
    )

    kx[...] = jnp.zeros_like(kx)
    vx[...] = jnp.zeros_like(vx)
    for copy in tot_copies:
        copy.wait_recv()
    loads[0].wait()
    width = x_all.shape[1]
    qcols = wq_v.shape[1]
    full = width * NH
    gain_row = gain_v[...].astype(F32).reshape(1, width)

    def project(parity):
        for x in range(NX):
            b = 2 * x + parity
            lane_sums = tot_all[b][0:1, :]
            row_sums = jnp.sum(jnp.where(diagonal, lane_sums, 0.0), axis=1, keepdims=True)
            inverse = lax.rsqrt(row_sums / full + EPSILON)
            normed[x * OWN : (x + 1) * OWN, :] = (
                block(b)[...].astype(F32) * inverse * gain_row
            ).astype(BF16)
        lhs = normed[...]
        for cols, weights in ((slice(0, qcols), wq_v), (slice(qcols, None), wkv_v)):
            product = jnp.dot(lhs, weights[...], preferred_element_type=F32)
            part[:, pl.ds(2 * parity, 2), :, cols] = product.reshape(NX, 2, PR, product.shape[1])

    loads[2].wait()
    loads[3].wait()
    project(core)
    turn_keys(1)
    for copy in fwd_copies:
        copy.wait_recv()
    project(1 - core)

    half = PR // 2
    low, high_cols = pl.ds(0, LOW), pl.ds(LOW, part.shape[3] - LOW)

    def ring(side):
        pos = (y, z)[side]

        def device(q):
            return (z * NY + q, f) if side == 0 else (q * NY + y, f)

        def view(q, cols):
            if side == 0:
                return part.at[:, q, pl.ds(0, half), cols]
            return part.at[q, :, pl.ds(half, half), cols]

        return pos, device, view

    after = {}
    for side in range(2):
        pos, device, view = ring(side)
        nxt, prv, far = lax.rem(pos + 1, NY), lax.rem(pos + 3, NY), lax.rem(pos + 2, NY)
        plan = [
            (view(far, low), relay_low, nxt),
            (view(far, high_cols), relay_high, prv),
            (view(nxt, high_cols), left_high, nxt),
            (view(prv, low), right_low, prv),
        ]
        copies = [
            remote(
                src, dst.at[side], ring_ssem.at[side, i], ring_rsem.at[side, i], device(to)
            )
            for i, (src, dst, to) in enumerate(plan)
        ]
        after[side] = copies
    for first in (0, 2):
        for side in range(2):
            for copy in after[side][first : first + 2]:
                copy.start()
    v_loads = []
    for i in range(CACHE_COPIES):
        copy = pltpu.make_async_copy(
            cache_v.at[0, pl.ds(i * span, span)], v_v.at[pl.ds(i * span, span)], v_sem.at[i]
        )
        copy.start()
        v_loads.append(copy)

    def ss_sent(k, carry):
        ss_copy(k).wait_send()
        return carry

    lax.fori_loop(1, NH, ss_sent, 0)
    for copy in tot_copies + fwd_copies + [copy for _, copy in tok_copies]:
        copy.wait_send()
    turn_keys(2)
    for side in range(2):
        pos, device, view = ring(side)
        nxt, prv = lax.rem(pos + 1, NY), lax.rem(pos + 3, NY)
        plan = [
            (view(nxt, low), relay_low, left_low, nxt),
            (view(prv, high_cols), relay_high, right_high, prv),
        ]
        for i, (own, relay, dst, to) in enumerate(plan):
            after[side][i].wait_recv()
            relay[side] = relay[side] + own[...]
            copy = remote(
                relay.at[side], dst.at[side],
                ring_ssem.at[side, 4 + i], ring_rsem.at[side, 4 + i], device(to),
            )
            copy.start()
            after[side].append(copy)
    turn_keys(3)
    stage_copies = {}
    for side in range(2):
        pos, device, view = ring(side)
        for copy in after[side][2:]:
            copy.wait_recv()
        mine[side, :, :, :LOW] = view(pos, low)[...] + left_low[side] + right_low[side]
        mine[side, :, :, LOW:] = view(pos, high_cols)[...] + left_high[side] + right_high[side]
        other, other_device, _ = ring(1 - side)
        stage_copies[side] = []
        for k in range(1, NY):
            peer = lax.rem(other + k, NY)
            copy = remote(
                mine.at[side, peer], mine_recv.at[side, k - 1],
                stage_ssem.at[side, k - 1], stage_rsem.at[side, k - 1], other_device(peer),
            )
            copy.start()
            stage_copies[side].append(copy)
    halves = []
    for side in range(2):
        other = ring(1 - side)[0]
        total = mine[side, other]
        for k in range(1, NY):
            stage_copies[side][k - 1].wait_recv()
            total = total + mine_recv[side, k - 1]
        halves.append(total)
    summed = jnp.concatenate(halves, axis=0)

    for j in range(8):
        spread[pl.ds(j, PR, stride=8), :] = summed[:, j * HD : (j + 1) * HD]
    msg[:, :PR, :] = spread[...].reshape(NF, PR, HD).astype(BF16)
    spread[...] = jnp.zeros_like(spread)
    spread[pl.ds(0, PR, stride=8), :] = summed[:, qcols:]
    msg[:, PR:, :] = spread[...].reshape(NF, PR, HD).astype(BF16)
    qkv[f] = msg[f]
    msg_copies = []
    for k in range(1, NF):
        peer = lax.rem(f + k, NF)
        copy = remote(
            msg.at[peer], qkv.at[f], msg_ssem.at[k - 1], msg_rsem.at[k - 1], (h, peer)
        )
        copy.start()
        msg_copies.append(copy)
    for side in range(2):
        for copy in after[side] + stage_copies[side]:
            copy.wait_send()
    for copy in msg_copies:
        copy.wait_recv()

    fresh_rows = []
    for i in range(2 * KV_HEADS):
        raw = qkv[i, PR:, :].astype(F32)
        cols = pl.ds((i % KV_HEADS) * HD, HD)
        if i < KV_HEADS:
            raw = rotate(raw, cosine, sine)
            kx[:PR, cols] = raw.astype(BF16)
        else:
            vx[:PR, cols] = raw.astype(BF16)
        fresh_rows.append(raw)

    rotated = [
        rotate(qkv[i, :PR, :].astype(F32), cosine, sine).astype(BF16) for i in range(NF)
    ]
    nothing = jnp.zeros((OWN, HD), BF16)
    queries = []
    for p in range(PAIRS):
        upper = jnp.concatenate(rotated[4 * p : 4 * p + 2], axis=0)
        lower = jnp.concatenate(rotated[4 * p + 2 : 4 * p + 4], axis=0)
        queries.append(
            jnp.concatenate(
                [
                    jnp.concatenate([upper, nothing], axis=1),
                    jnp.concatenate([nothing, lower], axis=1),
                ],
                axis=0,
            )
        )
    pair_rows, pair_cols = 2 * OWN, 2 * HD
    lane = lax.broadcasted_iota(jnp.int32, (pair_rows, HD), 1)
    step_row = lax.rem(lax.div(lax.broadcasted_iota(jnp.int32, (pair_rows, HD), 0), 8), 2)
    fresh_live = (lane == 0) | ((lane == 8) & (step_row == 1))
    nt = (((1,), (1,)), ((), ()))
    def attend(p):
        pair = pl.ds(p * pair_cols, pair_cols)
        rows_of = pl.ds(p * pair_rows, pair_rows)
        fresh = lax.dot_general(queries[p], kx[:, pair], nt, preferred_element_type=F32)
        fresh = jnp.where(fresh_live, fresh * SCALE, MASKED)

        def score_step(c, high):
            rows = pl.ds(pl.multiple_of(c * CHUNK, CHUNK), CHUNK)
            position = lax.broadcasted_iota(jnp.int32, (8, CHUNK), 1) + c * CHUNK
            cap = jnp.where(position < length, -MASKED, MASKED)
            cap = jnp.concatenate([cap] * (pair_rows // 8), axis=0)
            s = jnp.dot(queries[p], k_t[pair, rows], preferred_element_type=F32)
            s = jnp.minimum(s * SCALE, cap)
            scores[rows_of, rows] = s
            for t in range(CHUNK // HD):
                high = jnp.maximum(high, s[:, t * HD : (t + 1) * HD])
            return high

        high = lax.fori_loop(0, lmax // CHUNK, score_step, fresh)
        peak = jnp.broadcast_to(jnp.max(high, axis=1, keepdims=True), (pair_rows, HD))
        weights = jnp.exp2(fresh - peak).astype(BF16)
        weighted[p] = jnp.dot(weights, vx[:, pair], preferred_element_type=F32)

        def value_step(c, total):
            rows = pl.ds(pl.multiple_of(c * CHUNK, CHUNK), CHUNK)
            s = scores[rows_of, rows]
            pieces = []
            for t in range(CHUNK // HD):
                piece = jnp.exp2(s[:, t * HD : (t + 1) * HD] - peak).astype(BF16)
                total = total + piece.astype(F32)
                pieces.append(piece)
            weighted[p] += jnp.dot(
                jnp.concatenate(pieces, axis=1), v_v[rows, pair], preferred_element_type=F32
            )
            return total

        if p == 0:
            for copy in v_loads:
                copy.wait()
        total = lax.fori_loop(0, lmax // CHUNK, value_step, weights.astype(F32))
        weight_sum = jnp.sum(total, axis=1, keepdims=True)
        for i in range(2):
            rows = slice(i * OWN, (i + 1) * OWN)
            attended = weighted[p, rows, i * HD : (i + 1) * HD] / weight_sum[rows]
            attended = attended.astype(BF16)
            att_send[4 * p + 2 * i] = attended[:PR]
            att_send[4 * p + 2 * i + 1] = attended[PR:]

    odd = lax.rem(y + z, 2)
    slot = lax.rem(lax.div(y, 2) + lax.div(z, 2), 2)

    def send_attended(p):
        for m in range(4):
            peer = 4 * p + lax.rem(f + m, 4)
            landing = att_recv.at[odd, slot, f]

            @pl.when(peer == f)
            def _():
                pltpu.make_async_copy(
                    att_send.at[f], landing, att_rsem.at[odd, slot]
                ).start()

            for k in range(NY):
                chip = lax.rem(z + odd * k, NY) * NY + lax.rem(y + (1 - odd) * k, NY)
                copy = remote(
                    att_send.at[peer], landing, att_ssem.at[k], att_rsem.at[odd, slot],
                    (chip, peer),
                )
                if k == 0:
                    pl.when(peer != f)(copy.start)
                else:
                    copy.start()

    for p in range(PAIRS):
        attend(p)
        send_attended(p)

    for i in range(2 * KV_HEADS):
        ne[0:1, i * HD : (i + 1) * HD] = fresh_rows[i][0:1]
        ne[1:2, i * HD : (i + 1) * HD] = fresh_rows[i][8:9]
    results[PR:, :, :] = ne[0:2, :].reshape(1, STEPS, ne.shape[1]).astype(BF16)

    line_copies = [[], []]
    for part_id in range(2):
        for side in range(2):
            whole = att_recv.at[side, part_id]
            pltpu.make_async_copy(whole, whole, att_rsem.at[side, part_id]).wait()
            pos = (z, y)[side]
            att_f32[...] = att_recv[side, part_id].astype(F32).reshape(NF * PR, HD)
            for j in range(8):
                rows_all[part_id, side, pos, :, j * HD : (j + 1) * HD] = att_f32[
                    pl.ds(j, PR, stride=8), :
                ].astype(BF16)
            mine_rows = rows_all.at[part_id, side, pos]
            for k in range(1, NY):
                q = lax.rem(pos + k, NY)
                device = (q * NY + y, f) if side == 0 else (z * NY + q, f)
                copy = remote(
                    mine_rows, mine_rows,
                    line_ssem.at[part_id, side, k - 1], line_rsem.at[part_id, side, k - 1],
                    device,
                )
                copy.start()
                line_copies[part_id].append(copy)
    wout_load.wait()
    for copy in msg_copies:
        copy.wait_send()
    for k in range(NY):
        sent = att_send.at[pl.ds(0, NF - 1)] if k == 0 else att_send
        pltpu.make_async_copy(sent, sent, att_ssem.at[k]).wait()

    def out_rows(index):
        return pl.ds(pl.multiple_of(index * OWN, OWN), OWN)

    sib_copies = [[], []]
    for part_id in range(2):
        for copy in line_copies[part_id]:
            copy.wait_recv()
        product = jnp.dot(
            rows_all[part_id].reshape(NH * PR // 2, wout_v.shape[0]),
            wout_v[...],
            preferred_element_type=F32,
        )
        for side in range(2):
            for q in range(NY):
                far = 2 * ((part_id + q // 2) % 2) + (q + side) % 2
                home = q * NY + far if side == 0 else far * NY + q
                first = (side * NY + q) * PR
                opart[home * PR : (home + 1) * PR, :] = product[first : first + PR]
        for e in range(2):
            x = 2 * lax.rem(1 + core + part_id, 2) + e
            copy = remote(
                opart.at[out_rows(2 * x + 1 - core)], sib_recv.at[part_id, e],
                sib_ssem.at[part_id, e], sib_rsem.at[part_id, e], (h, sib),
            )
            copy.start()
            sib_copies[part_id].append(copy)
    fin_copies = []
    for part_id in range(2):
        for copy in sib_copies[part_id]:
            copy.wait_recv()
        for e in range(2):
            x = 2 * lax.rem(core + part_id, 2) + e
            hop = lax.rem(x - cx + NX, NX)
            there = lax.rem(hop + NX - 1, NX)
            copy = remote(
                fin_send.at[part_id, e], fin_recv.at[there],
                fin_ssem.at[part_id, e], fin_rsem.at[there], (h, 2 * x + core),
            )
            fin_copies.append((hop, copy))

            @pl.when(hop != 0)
            def _():
                total = opart[out_rows(2 * x + core), :] + sib_recv[part_id, e]
                fin_send[part_id, e] = total.astype(BF16)
                copy.start()

    for copies in sib_copies + line_copies:
        for copy in copies:
            copy.wait_send()
    own_part = lax.rem(core + lax.div(cx, 2), 2)
    result = opart[out_rows(f), :] + sib_recv[own_part, lax.rem(cx, 2)]
    for k in range(1, NX):
        pltpu.make_async_copy(
            fin_recv.at[k - 1], fin_recv.at[k - 1], fin_rsem.at[k - 1]
        ).wait()
        result = result + fin_recv[k - 1].astype(F32)
    results[:PR, :, :] = result.reshape(PR, STEPS, result.shape[1]).astype(BF16)
    for hop, copy in fin_copies:
        pl.when(hop != 0)(copy.wait_send)


def hand_out(results, out, entries, sem):
    rows = out.shape[0]
    copies = [
        pltpu.make_async_copy(results.at[pl.ds(0, rows)], out, sem.at[0]),
        pltpu.make_async_copy(results.at[pl.ds(rows, 1)], entries, sem.at[1]),
    ]
    for copy in copies:
        copy.start()
    for copy in copies:
        copy.wait()


def body(tokens, norm_gain, query_weight, w_keyval, w_out, cache_keys, cache_values, lengths):
    width = tokens.shape[2]
    lmax = cache_keys.shape[1]
    qcols = query_weight.shape[1]
    kvcols = w_keyval.shape[1]
    halves = np.arange(HD // 2, dtype=np.float64) * (2.0 / HD)
    freq = (ROPE_BASE ** (-halves)).astype(np.float32)
    freq = jnp.asarray(np.tile(np.concatenate([freq, freq])[None, :], (PR, 1)))
    any_spec = pl.BlockSpec(memory_space=pl.ANY)
    hbm_spec = pl.BlockSpec(memory_space=pltpu.HBM)
    vmem_spec = pl.BlockSpec(memory_space=pltpu.VMEM)
    dma = pltpu.SemaphoreType.DMA
    rows = NH * PR
    results = pl.pallas_call(
        kernel,
        out_shape=pltpu.VMEM((PR + 1, STEPS, width), BF16),
        in_specs=[hbm_spec] * 9,
        out_specs=vmem_spec,
        scratch_shapes=[
            pltpu.SMEM(lengths.shape, jnp.int32),
            pltpu.VMEM(tokens.shape, BF16),
            pltpu.VMEM((OWN, width), BF16),
            pltpu.VMEM((PR, HD), F32),
            pltpu.VMEM((width,), BF16),
            pltpu.VMEM((width, qcols), BF16),
            pltpu.VMEM((width, kvcols), BF16),
            pltpu.VMEM((qcols, width), BF16),
            pltpu.VMEM((lmax, KV_HEADS * HD), BF16),
            pltpu.VMEM((KV_HEADS * HD, lmax), BF16),
            pltpu.VMEM((lmax, KV_HEADS * HD), BF16),
            pltpu.VMEM((rows, width), BF16),
            pltpu.VMEM((rows // 2, width), BF16),
            pltpu.VMEM((8, HD), F32),
            pltpu.VMEM((NH - 1, 8, HD), F32),
            pltpu.VMEM((NF, 8, HD), F32),
            pltpu.VMEM((NY, NY, PR, qcols + kvcols), F32),
            pltpu.VMEM((2, NY, PR // 2, LOW), F32),
            pltpu.VMEM((2, NY, PR // 2, qcols + kvcols - LOW), F32),
            pltpu.VMEM((2, NY, PR // 2, LOW), F32),
            pltpu.VMEM((2, NY, PR // 2, qcols + kvcols - LOW), F32),
            pltpu.VMEM((2, NY, PR // 2, LOW), F32),
            pltpu.VMEM((2, NY, PR // 2, qcols + kvcols - LOW), F32),
            pltpu.VMEM((2, NY, PR // 2, qcols + kvcols), F32),
            pltpu.VMEM((2, NY - 1, PR // 2, qcols + kvcols), F32),
            pltpu.VMEM((NF * PR, HD), F32),
            pltpu.VMEM((NF, 2 * PR, HD), BF16),
            pltpu.VMEM((NF, 2 * PR, HD), BF16),
            pltpu.VMEM((HD, KV_HEADS * HD), BF16),
            pltpu.VMEM((HD, KV_HEADS * HD), BF16),
            pltpu.VMEM((8, 2 * KV_HEADS * HD), F32),
            pltpu.VMEM((KV_HEADS * OWN, lmax), F32),
            pltpu.VMEM((PAIRS, 2 * OWN, 2 * HD), F32),
            pltpu.VMEM((NF, PR, HD), BF16),
            pltpu.VMEM((2, 2, NF, PR, HD), BF16),
            pltpu.VMEM((NF * PR, HD), F32),
            pltpu.VMEM((2, 2, NY, PR, qcols), BF16),
            pltpu.VMEM((rows, width), F32),
            pltpu.VMEM((2, 2, OWN, width), F32),
            pltpu.VMEM((2, 2, OWN, width), BF16),
            pltpu.VMEM((NX - 1, OWN, width), BF16),
            dma((8,)),
            dma((CACHE_COPIES,)),
            dma((CACHE_COPIES,)),
            dma((NX - 1,)), dma((NX - 1,)),
            dma((NX,)), dma((NX,)),
            dma((NH - 1,)), dma((NH - 1,)),
            dma((NF - 1,)), dma((NF - 1,)),
            dma((2, 6)), dma((2, 6)),
            dma((2, NY - 1)), dma((2, NY - 1)),
            dma((NF - 1,)), dma((NF - 1,)),
            dma((NY,)), dma((2, 2)),
            dma((2, 2, NY - 1)), dma((2, 2, NY - 1)),
            dma((2, 2)), dma((2, 2)),
            dma((2, 2)), dma((NX - 1,)),
        ],
        compiler_params=pltpu.CompilerParams(
            collective_id=0, has_side_effects=True, vmem_limit_bytes=48 * 2**20
        ),
        name="decode_block",
    )(
        *[
            pltpu.with_memory_space_constraint(array, pltpu.HBM)
            for array in (
                lengths, freq, tokens, norm_gain, query_weight, w_keyval, w_out,
                cache_keys, cache_values,
            )
        ],
    )
    return pl.pallas_call(
        hand_out,
        out_shape=(
            jax.ShapeDtypeStruct(tokens.shape, BF16),
            jax.ShapeDtypeStruct((1, STEPS, 2 * KV_HEADS * HD), BF16),
        ),
        in_specs=[vmem_spec],
        out_specs=(any_spec, any_spec),
        scratch_shapes=[dma((2,))],
        name="hand_out",
    )(pltpu.with_memory_space_constraint(results, pltpu.VMEM))


def solution(mesh):
    in_specs = (
        P("ffn", None, "hid"),
        P("hid"),
        P("hid", "ffn"),
        P("hid", "ffn"),
        P("ffn", "hid"),
        P(("hid", "ffn"), None, None),
        P(("hid", "ffn"), None, None),
        P(),
    )
    out_specs = (P("ffn", None, "hid"), P(("hid", "ffn"), None, None))
    return jax.shard_map(body, mesh=mesh, in_specs=in_specs, out_specs=out_specs, check_vma=False)
```

```python
import functools

import jax
import jax.numpy as jnp
import numpy as np
from jax import lax
from jax.experimental import pallas as pl
from jax.experimental.pallas import tpu as pltpu
from jax.sharding import PartitionSpec as P

MESH = pl.DeviceIdType.MESH
F32 = jnp.float32
BF16 = jnp.bfloat16

HEADS = 64
KV_HEADS = 4
HD = 128
STEPS = 2
EPSILON = 1e-05
ROPE_BASE = 500000.0
SCALE = HD ** (-0.5) * 1.4426950408889634
MASKED = -1e30

NH = 16
NF = 8
NX = 4
NY = 4
LOW = 512
OWN = 32
PR = 16
CHUNK = 2048
VCHUNK = 4096
CACHE_COPIES = 4
PAIRS = KV_HEADS // 2


def remote(src, dst, send_sem, recv_sem, device):
    return pltpu.make_async_remote_copy(
        src_ref=src,
        dst_ref=dst,
        send_sem=send_sem,
        recv_sem=recv_sem,
        device_id=device,
        device_id_type=MESH,
    )


def rotate(vectors, cosine, sine):
    return vectors * cosine + pltpu.roll(vectors, HD // 2, 1) * sine


def kernel(
    lengths_hbm, freq, tokens, gain, wq, wkv, wout, cache_k, cache_v,
    results,
    lengths, raw_v, tok_v, freq_v, gain_v, wq_v, wkv_v, wout_v, k_v, q_t, v_v,
    x_all, normed, ss_own, ss_recv, tot_all, part, relay_low, relay_high, left_low, left_high,
    right_low, right_high, mine, mine_recv,
    spread, msg, qkv, kx, vx, ne, scores, weighted, att_send, att_recv, att_f32, rows_all,
    opart, sib_recv, fin_send, fin_recv,
    local_sem, k_sem, v_sem,
    tok_ssem, tok_rsem, fwd_ssem, fwd_rsem, ss_ssem, ss_rsem, tot_ssem, tot_rsem,
    ring_ssem, ring_rsem, stage_ssem, stage_rsem, msg_ssem, msg_rsem, att_ssem, att_rsem, line_ssem, line_rsem,
    sib_ssem, sib_rsem, fin_ssem, fin_rsem,
):
    h = lax.axis_index("hid")
    f = lax.axis_index("ffn")
    z = lax.div(h, NY)
    y = lax.rem(h, NY)
    cx = lax.div(f, 2)
    core = lax.rem(f, 2)
    sib = f + 1 - 2 * core
    lmax = cache_k.shape[1]

    barrier = pltpu.get_barrier_semaphore()
    tokens_load = pltpu.make_async_copy(tokens, raw_v, local_sem.at[0])
    tokens_load.start()

    def greet_hid(k, carry):
        pl.semaphore_signal(
            barrier, inc=1, device_id=(lax.rem(h + k, NH), f), device_id_type=MESH
        )
        return carry

    def greet_ffn(k, carry):
        pl.semaphore_signal(
            barrier, inc=1, device_id=(h, lax.rem(f + k, NF)), device_id_type=MESH
        )
        return carry

    lax.fori_loop(1, NF, greet_ffn, 0)
    lax.fori_loop(1, NH, greet_hid, 0)

    loads = []
    for i, (src, dst) in enumerate(
        [(gain, gain_v), (freq, freq_v), (wq, wq_v), (wkv, wkv_v), (lengths_hbm, lengths)]
    ):
        copy = pltpu.make_async_copy(src, dst, local_sem.at[1 + i])
        copy.start()
        loads.append(copy)
    span = lmax // CACHE_COPIES
    k_loads = []
    for i in range(CACHE_COPIES):
        copy = pltpu.make_async_copy(
            cache_k.at[0, pl.ds(i * span, span)], k_v.at[pl.ds(i * span, span)], k_sem.at[i]
        )
        copy.start()
        k_loads.append(copy)
    wout_load = pltpu.make_async_copy(wout, wout_v, local_sem.at[6])
    wout_load.start()

    tokens_load.wait()
    x_f32 = raw_v[...].astype(F32).reshape(tok_v.shape)
    x_own = x_f32.astype(BF16)
    tok_v[...] = x_own
    pl.semaphore_wait(barrier, NH + NF - 2)

    def block(index):
        return x_all.at[pl.ds(pl.multiple_of(index * OWN, OWN), OWN)]

    tok_copies = []
    for k in (1, 3, 2):
        peer = 2 * lax.rem(cx + k, NX) + core
        copy = remote(tok_v, block(f), tok_ssem.at[k - 1], tok_rsem.at[k - 1], (h, peer))
        copy.start()
        tok_copies.append((k, copy))
    fwd_copies = [remote(tok_v, block(f), fwd_ssem.at[0], fwd_rsem.at[0], (h, sib))]
    fwd_copies[0].start()

    sums = jnp.sum(x_f32 * x_f32, axis=1, keepdims=True)
    row_id = lax.broadcasted_iota(jnp.int32, (OWN, HD), 0)
    lane_id = lax.broadcasted_iota(jnp.int32, (OWN, HD), 1)
    diagonal = row_id == lane_id
    own_sums = jnp.sum(jnp.where(diagonal, sums, 0.0), axis=0, keepdims=True)
    ss_own[...] = jnp.broadcast_to(own_sums, (8, HD))

    def ss_copy(k):
        return remote(
            ss_own, ss_recv.at[k - 1], ss_ssem.at[k - 1], ss_rsem.at[k - 1],
            (lax.rem(h + k, NH), f),
        )

    def ss_start(k, carry):
        ss_copy(k).start()
        return carry

    lax.fori_loop(1, NH, ss_start, 0)
    x_all[pl.ds(pl.multiple_of(f * OWN, OWN), OWN), :] = x_own

    def ss_add(k, total):
        ss_copy(k).wait_recv()
        return total + ss_recv[k - 1]

    total = lax.fori_loop(1, NH, ss_add, ss_own[...])
    tot_all[f] = total
    tot_copies = []
    for k in range(1, NF):
        copy = remote(
            tot_all.at[f], tot_all.at[f], tot_ssem.at[k - 1], tot_rsem.at[k - 1],
            (h, lax.rem(f + k, NF)),
        )
        copy.start()
        tot_copies.append(copy)
    for k, tok_copy in tok_copies:
        tok_copy.wait_recv()
        came = 2 * lax.rem(cx + NX - k, NX) + core
        copy = remote(block(came), block(came), fwd_ssem.at[k], fwd_rsem.at[k], (h, sib))
        copy.start()
        fwd_copies.append(copy)

    loads[4].wait()
    length = lengths[h * NF + f]
    step_of = lax.div(lax.broadcasted_iota(jnp.int32, (PR, HD), 0), 8)
    loads[1].wait()
    angles = (step_of + length).astype(F32) * freq_v[...]
    cosine = jnp.cos(angles)
    sine = jnp.sin(angles)
    sine = jnp.where(
        lax.broadcasted_iota(jnp.int32, (PR, HD), 1) < HD // 2, -sine, sine
    )

    kx[...] = jnp.zeros_like(kx)
    vx[...] = jnp.zeros_like(vx)
    for copy in tot_copies:
        copy.wait_recv()
    loads[0].wait()
    width = x_all.shape[1]
    qcols = wq_v.shape[1]
    full = width * NH
    gain_row = gain_v[...].astype(F32).reshape(1, width)

    def project(parity):
        for x in range(NX):
            b = 2 * x + parity
            lane_sums = tot_all[b][0:1, :]
            row_sums = jnp.sum(jnp.where(diagonal, lane_sums, 0.0), axis=1, keepdims=True)
            inverse = lax.rsqrt(row_sums / full + EPSILON)
            normed[x * OWN : (x + 1) * OWN, :] = (
                block(b)[...].astype(F32) * inverse * gain_row
            ).astype(BF16)
        lhs = normed[...]
        for cols, weights in ((slice(0, qcols), wq_v), (slice(qcols, None), wkv_v)):
            product = jnp.dot(lhs, weights[...], preferred_element_type=F32)
            part[:, pl.ds(2 * parity, 2), :, cols] = product.reshape(NX, 2, PR, product.shape[1])

    loads[2].wait()
    loads[3].wait()
    project(core)
    for copy in fwd_copies:
        copy.wait_recv()
    project(1 - core)

    half = PR // 2
    low, high_cols = pl.ds(0, LOW), pl.ds(LOW, part.shape[3] - LOW)

    def ring(side):
        pos = (y, z)[side]

        def device(q):
            return (z * NY + q, f) if side == 0 else (q * NY + y, f)

        def view(q, cols):
            if side == 0:
                return part.at[:, q, pl.ds(0, half), cols]
            return part.at[q, :, pl.ds(half, half), cols]

        return pos, device, view

    after = {}
    for side in range(2):
        pos, device, view = ring(side)
        nxt, prv, far = lax.rem(pos + 1, NY), lax.rem(pos + 3, NY), lax.rem(pos + 2, NY)
        plan = [
            (view(far, low), relay_low, nxt),
            (view(far, high_cols), relay_high, prv),
            (view(nxt, high_cols), left_high, nxt),
            (view(prv, low), right_low, prv),
        ]
        copies = [
            remote(
                src, dst.at[side], ring_ssem.at[side, i], ring_rsem.at[side, i], device(to)
            )
            for i, (src, dst, to) in enumerate(plan)
        ]
        after[side] = copies
    for first in (0, 2):
        for side in range(2):
            for copy in after[side][first : first + 2]:
                copy.start()
    v_loads = []
    for i in range(CACHE_COPIES):
        copy = pltpu.make_async_copy(
            cache_v.at[0, pl.ds(i * span, span)], v_v.at[pl.ds(i * span, span)], v_sem.at[i]
        )
        copy.start()
        v_loads.append(copy)

    def ss_sent(k, carry):
        ss_copy(k).wait_send()
        return carry

    lax.fori_loop(1, NH, ss_sent, 0)
    for copy in tot_copies + fwd_copies + [copy for _, copy in tok_copies]:
        copy.wait_send()
    for side in range(2):
        pos, device, view = ring(side)
        nxt, prv = lax.rem(pos + 1, NY), lax.rem(pos + 3, NY)
        plan = [
            (view(nxt, low), relay_low, left_low, nxt),
            (view(prv, high_cols), relay_high, right_high, prv),
        ]
        for i, (own, relay, dst, to) in enumerate(plan):
            after[side][i].wait_recv()
            relay[side] = relay[side] + own[...]
            copy = remote(
                relay.at[side], dst.at[side],
                ring_ssem.at[side, 4 + i], ring_rsem.at[side, 4 + i], device(to),
            )
            copy.start()
            after[side].append(copy)
    stage_copies = {}
    for side in range(2):
        pos, device, view = ring(side)
        for copy in after[side][2:]:
            copy.wait_recv()
        mine[side, :, :, :LOW] = view(pos, low)[...] + left_low[side] + right_low[side]
        mine[side, :, :, LOW:] = view(pos, high_cols)[...] + left_high[side] + right_high[side]
        other, other_device, _ = ring(1 - side)
        stage_copies[side] = []
        for k in range(1, NY):
            peer = lax.rem(other + k, NY)
            copy = remote(
                mine.at[side, peer], mine_recv.at[side, k - 1],
                stage_ssem.at[side, k - 1], stage_rsem.at[side, k - 1], other_device(peer),
            )
            copy.start()
            stage_copies[side].append(copy)
    halves = []
    for side in range(2):
        other = ring(1 - side)[0]
        total = mine[side, other]
        for k in range(1, NY):
            stage_copies[side][k - 1].wait_recv()
            total = total + mine_recv[side, k - 1]
        halves.append(total)
    summed = jnp.concatenate(halves, axis=0)

    for j in range(8):
        spread[pl.ds(j, PR, stride=8), :] = summed[:, j * HD : (j + 1) * HD]
    msg[:, :PR, :] = spread[...].reshape(NF, PR, HD).astype(BF16)
    spread[...] = jnp.zeros_like(spread)
    spread[pl.ds(0, PR, stride=8), :] = summed[:, qcols:]
    msg[:, PR:, :] = spread[...].reshape(NF, PR, HD).astype(BF16)
    qkv[f] = msg[f]
    msg_copies = []
    for k in range(1, NF):
        peer = lax.rem(f + k, NF)
        copy = remote(
            msg.at[peer], qkv.at[f], msg_ssem.at[k - 1], msg_rsem.at[k - 1], (h, peer)
        )
        copy.start()
        msg_copies.append(copy)
    for side in range(2):
        for copy in after[side] + stage_copies[side]:
            copy.wait_send()
    for copy in msg_copies:
        copy.wait_recv()

    fresh_rows = []
    for i in range(2 * KV_HEADS):
        raw = qkv[i, PR:, :].astype(F32)
        cols = pl.ds((i % KV_HEADS) * HD, HD)
        if i < KV_HEADS:
            raw = rotate(raw, cosine, sine)
            kx[:PR, cols] = raw.astype(BF16)
        else:
            vx[:PR, cols] = raw.astype(BF16)
        fresh_rows.append(raw)

    nothing = jnp.zeros((OWN, HD), BF16)
    query_rows = []
    for g in range(KV_HEADS):
        pair = [
            rotate(qkv[2 * g + i, :PR, :].astype(F32), cosine, sine).astype(BF16)
            for i in range(2)
        ]
        rotated = jnp.concatenate(pair, axis=0)
        query_rows.append(
            jnp.concatenate([nothing] * g + [rotated] + [nothing] * (KV_HEADS - 1 - g), axis=1)
        )
    queries = jnp.concatenate(query_rows, axis=0)
    q_t[...] = queries.T
    all_rows = KV_HEADS * OWN
    lane = lax.broadcasted_iota(jnp.int32, (all_rows, HD), 1)
    step_row = lax.rem(lax.div(lax.broadcasted_iota(jnp.int32, (all_rows, HD), 0), 8), 2)
    fresh_live = (lane == 0) | ((lane == 8) & (step_row == 1))
    fresh = lax.dot_general(
        queries, kx[...], (((1,), (1,)), ((), ())), preferred_element_type=F32
    )
    fresh = jnp.where(fresh_live, fresh * SCALE, MASKED)
    for copy in k_loads:
        copy.wait()

    def score_step(c, high):
        rows = pl.ds(pl.multiple_of(c * CHUNK, CHUNK), CHUNK)
        position = lax.broadcasted_iota(jnp.int32, (8, CHUNK), 1) + c * CHUNK
        cap = jnp.where(position < length, -MASKED, MASKED)
        cap = jnp.concatenate([cap] * (all_rows // 8), axis=0)
        s = jnp.dot(k_v[rows, :], q_t[...], preferred_element_type=F32).T
        s = jnp.minimum(s * SCALE, cap)
        scores[:, rows] = s
        for t in range(CHUNK // HD):
            high = jnp.maximum(high, s[:, t * HD : (t + 1) * HD])
        return high

    high = lax.fori_loop(0, lmax // CHUNK, score_step, fresh)
    peaks = jnp.broadcast_to(jnp.max(high, axis=1, keepdims=True), (all_rows, HD))
    for copy in v_loads:
        copy.wait()
    pair_rows, pair_cols = 2 * OWN, 2 * HD

    def attend(p):
        pair = pl.ds(p * pair_cols, pair_cols)
        rows_of = pl.ds(p * pair_rows, pair_rows)
        peak = peaks[p * pair_rows : (p + 1) * pair_rows]
        weights = jnp.exp2(fresh[p * pair_rows : (p + 1) * pair_rows] - peak).astype(BF16)
        weighted[p] = jnp.dot(weights, vx[:, pair], preferred_element_type=F32)

        def value_step(c, total):
            rows = pl.ds(pl.multiple_of(c * VCHUNK, VCHUNK), VCHUNK)
            s = scores[rows_of, rows]
            pieces = []
            for t in range(VCHUNK // HD):
                piece = jnp.exp2(s[:, t * HD : (t + 1) * HD] - peak).astype(BF16)
                total = total + piece.astype(F32)
                pieces.append(piece)
            weighted[p] += jnp.dot(
                jnp.concatenate(pieces, axis=1), v_v[rows, pair], preferred_element_type=F32
            )
            return total

        total = lax.fori_loop(0, lmax // VCHUNK, value_step, weights.astype(F32))
        weight_sum = jnp.sum(total, axis=1, keepdims=True)
        for i in range(2):
            rows = slice(i * OWN, (i + 1) * OWN)
            attended = weighted[p, rows, i * HD : (i + 1) * HD] / weight_sum[rows]
            attended = attended.astype(BF16)
            att_send[4 * p + 2 * i] = attended[:PR]
            att_send[4 * p + 2 * i + 1] = attended[PR:]

    odd = lax.rem(y + z, 2)
    slot = lax.rem(lax.div(y, 2) + lax.div(z, 2), 2)

    def send_attended(p):
        for m in range(4):
            peer = 4 * p + lax.rem(f + m, 4)
            landing = att_recv.at[odd, slot, f]

            @pl.when(peer == f)
            def _():
                pltpu.make_async_copy(
                    att_send.at[f], landing, att_rsem.at[odd, slot]
                ).start()

            for k in range(NY):
                chip = lax.rem(z + odd * k, NY) * NY + lax.rem(y + (1 - odd) * k, NY)
                copy = remote(
                    att_send.at[peer], landing, att_ssem.at[k], att_rsem.at[odd, slot],
                    (chip, peer),
                )
                if k == 0:
                    pl.when(peer != f)(copy.start)
                else:
                    copy.start()

    for p in range(PAIRS):
        attend(p)
        send_attended(p)

    for i in range(2 * KV_HEADS):
        ne[0:1, i * HD : (i + 1) * HD] = fresh_rows[i][0:1]
        ne[1:2, i * HD : (i + 1) * HD] = fresh_rows[i][8:9]
    results[PR:, :, :] = ne[0:2, :].reshape(1, STEPS, ne.shape[1]).astype(BF16)

    line_copies = [[], []]
    for part_id in range(2):
        for side in range(2):
            whole = att_recv.at[side, part_id]
            pltpu.make_async_copy(whole, whole, att_rsem.at[side, part_id]).wait()
            pos = (z, y)[side]
            att_f32[...] = att_recv[side, part_id].astype(F32).reshape(NF * PR, HD)
            for j in range(8):
                rows_all[part_id, side, pos, :, j * HD : (j + 1) * HD] = att_f32[
                    pl.ds(j, PR, stride=8), :
                ].astype(BF16)
            mine_rows = rows_all.at[part_id, side, pos]
            for k in range(1, NY):
                q = lax.rem(pos + k, NY)
                device = (q * NY + y, f) if side == 0 else (z * NY + q, f)
                copy = remote(
                    mine_rows, mine_rows,
                    line_ssem.at[part_id, side, k - 1], line_rsem.at[part_id, side, k - 1],
                    device,
                )
                copy.start()
                line_copies[part_id].append(copy)
    wout_load.wait()
    for copy in msg_copies:
        copy.wait_send()
    for k in range(NY):
        sent = att_send.at[pl.ds(0, NF - 1)] if k == 0 else att_send
        pltpu.make_async_copy(sent, sent, att_ssem.at[k]).wait()

    def out_rows(index):
        return pl.ds(pl.multiple_of(index * OWN, OWN), OWN)

    sib_copies = [[], []]
    for part_id in range(2):
        for copy in line_copies[part_id]:
            copy.wait_recv()
        product = jnp.dot(
            rows_all[part_id].reshape(NH * PR // 2, wout_v.shape[0]),
            wout_v[...],
            preferred_element_type=F32,
        )
        for side in range(2):
            for q in range(NY):
                far = 2 * ((part_id + q // 2) % 2) + (q + side) % 2
                home = q * NY + far if side == 0 else far * NY + q
                first = (side * NY + q) * PR
                opart[home * PR : (home + 1) * PR, :] = product[first : first + PR]
        for e in range(2):
            x = 2 * lax.rem(1 + core + part_id, 2) + e
            copy = remote(
                opart.at[out_rows(2 * x + 1 - core)], sib_recv.at[part_id, e],
                sib_ssem.at[part_id, e], sib_rsem.at[part_id, e], (h, sib),
            )
            copy.start()
            sib_copies[part_id].append(copy)
    fin_copies = []
    for part_id in range(2):
        for copy in sib_copies[part_id]:
            copy.wait_recv()
        for e in range(2):
            x = 2 * lax.rem(core + part_id, 2) + e
            hop = lax.rem(x - cx + NX, NX)
            there = lax.rem(hop + NX - 1, NX)
            copy = remote(
                fin_send.at[part_id, e], fin_recv.at[there],
                fin_ssem.at[part_id, e], fin_rsem.at[there], (h, 2 * x + core),
            )
            fin_copies.append((hop, copy))

            @pl.when(hop != 0)
            def _():
                total = opart[out_rows(2 * x + core), :] + sib_recv[part_id, e]
                fin_send[part_id, e] = total.astype(BF16)
                copy.start()

    for copies in sib_copies + line_copies:
        for copy in copies:
            copy.wait_send()
    own_part = lax.rem(core + lax.div(cx, 2), 2)
    result = opart[out_rows(f), :] + sib_recv[own_part, lax.rem(cx, 2)]
    for k in range(1, NX):
        pltpu.make_async_copy(
            fin_recv.at[k - 1], fin_recv.at[k - 1], fin_rsem.at[k - 1]
        ).wait()
        result = result + fin_recv[k - 1].astype(F32)
    results[:PR, :, :] = result.reshape(PR, STEPS, result.shape[1]).astype(BF16)
    for hop, copy in fin_copies:
        pl.when(hop != 0)(copy.wait_send)


def hand_out(results, out, entries, sem):
    rows = out.shape[0]
    copies = [
        pltpu.make_async_copy(results.at[pl.ds(0, rows)], out, sem.at[0]),
        pltpu.make_async_copy(results.at[pl.ds(rows, 1)], entries, sem.at[1]),
    ]
    for copy in copies:
        copy.start()
    for copy in copies:
        copy.wait()


def body(tokens, norm_gain, query_weight, w_keyval, w_out, cache_keys, cache_values, lengths):
    width = tokens.shape[2]
    lmax = cache_keys.shape[1]
    qcols = query_weight.shape[1]
    kvcols = w_keyval.shape[1]
    halves = np.arange(HD // 2, dtype=np.float64) * (2.0 / HD)
    freq = (ROPE_BASE ** (-halves)).astype(np.float32)
    freq = jnp.asarray(np.tile(np.concatenate([freq, freq])[None, :], (PR, 1)))
    any_spec = pl.BlockSpec(memory_space=pl.ANY)
    hbm_spec = pl.BlockSpec(memory_space=pltpu.HBM)
    vmem_spec = pl.BlockSpec(memory_space=pltpu.VMEM)
    dma = pltpu.SemaphoreType.DMA
    rows = NH * PR
    results = pl.pallas_call(
        kernel,
        out_shape=pltpu.VMEM((PR + 1, STEPS, width), BF16),
        in_specs=[hbm_spec] * 9,
        out_specs=vmem_spec,
        scratch_shapes=[
            pltpu.SMEM(lengths.shape, jnp.int32),
            pltpu.VMEM(tokens.shape, BF16),
            pltpu.VMEM((OWN, width), BF16),
            pltpu.VMEM((PR, HD), F32),
            pltpu.VMEM((width,), BF16),
            pltpu.VMEM((width, qcols), BF16),
            pltpu.VMEM((width, kvcols), BF16),
            pltpu.VMEM((qcols, width), BF16),
            pltpu.VMEM((lmax, KV_HEADS * HD), BF16),
            pltpu.VMEM((KV_HEADS * HD, HD), BF16),
            pltpu.VMEM((lmax, KV_HEADS * HD), BF16),
            pltpu.VMEM((rows, width), BF16),
            pltpu.VMEM((rows // 2, width), BF16),
            pltpu.VMEM((8, HD), F32),
            pltpu.VMEM((NH - 1, 8, HD), F32),
            pltpu.VMEM((NF, 8, HD), F32),
            pltpu.VMEM((NY, NY, PR, qcols + kvcols), F32),
            pltpu.VMEM((2, NY, PR // 2, LOW), F32),
            pltpu.VMEM((2, NY, PR // 2, qcols + kvcols - LOW), F32),
            pltpu.VMEM((2, NY, PR // 2, LOW), F32),
            pltpu.VMEM((2, NY, PR // 2, qcols + kvcols - LOW), F32),
            pltpu.VMEM((2, NY, PR // 2, LOW), F32),
            pltpu.VMEM((2, NY, PR // 2, qcols + kvcols - LOW), F32),
            pltpu.VMEM((2, NY, PR // 2, qcols + kvcols), F32),
            pltpu.VMEM((2, NY - 1, PR // 2, qcols + kvcols), F32),
            pltpu.VMEM((NF * PR, HD), F32),
            pltpu.VMEM((NF, 2 * PR, HD), BF16),
            pltpu.VMEM((NF, 2 * PR, HD), BF16),
            pltpu.VMEM((HD, KV_HEADS * HD), BF16),
            pltpu.VMEM((HD, KV_HEADS * HD), BF16),
            pltpu.VMEM((8, 2 * KV_HEADS * HD), F32),
            pltpu.VMEM((KV_HEADS * OWN, lmax), F32),
            pltpu.VMEM((PAIRS, 2 * OWN, 2 * HD), F32),
            pltpu.VMEM((NF, PR, HD), BF16),
            pltpu.VMEM((2, 2, NF, PR, HD), BF16),
            pltpu.VMEM((NF * PR, HD), F32),
            pltpu.VMEM((2, 2, NY, PR, qcols), BF16),
            pltpu.VMEM((rows, width), F32),
            pltpu.VMEM((2, 2, OWN, width), F32),
            pltpu.VMEM((2, 2, OWN, width), BF16),
            pltpu.VMEM((NX - 1, OWN, width), BF16),
            dma((8,)),
            dma((CACHE_COPIES,)),
            dma((CACHE_COPIES,)),
            dma((NX - 1,)), dma((NX - 1,)),
            dma((NX,)), dma((NX,)),
            dma((NH - 1,)), dma((NH - 1,)),
            dma((NF - 1,)), dma((NF - 1,)),
            dma((2, 6)), dma((2, 6)),
            dma((2, NY - 1)), dma((2, NY - 1)),
            dma((NF - 1,)), dma((NF - 1,)),
            dma((NY,)), dma((2, 2)),
            dma((2, 2, NY - 1)), dma((2, 2, NY - 1)),
            dma((2, 2)), dma((2, 2)),
            dma((2, 2)), dma((NX - 1,)),
        ],
        compiler_params=pltpu.CompilerParams(
            collective_id=0, has_side_effects=True, vmem_limit_bytes=48 * 2**20
        ),
        name="decode_block",
    )(
        *[
            pltpu.with_memory_space_constraint(array, pltpu.HBM)
            for array in (
                lengths, freq, tokens, norm_gain, query_weight, w_keyval, w_out,
                cache_keys, cache_values,
            )
        ],
    )
    return pl.pallas_call(
        hand_out,
        out_shape=(
            jax.ShapeDtypeStruct(tokens.shape, BF16),
            jax.ShapeDtypeStruct((1, STEPS, 2 * KV_HEADS * HD), BF16),
        ),
        in_specs=[vmem_spec],
        out_specs=(any_spec, any_spec),
        scratch_shapes=[dma((2,))],
        name="hand_out",
    )(pltpu.with_memory_space_constraint(results, pltpu.VMEM))


def solution(mesh):
    in_specs = (
        P("ffn", None, "hid"),
        P("hid"),
        P("hid", "ffn"),
        P("hid", "ffn"),
        P("ffn", "hid"),
        P(("hid", "ffn"), None, None),
        P(("hid", "ffn"), None, None),
        P(),
    )
    out_specs = (P("ffn", None, "hid"), P(("hid", "ffn"), None, None))
    return jax.shard_map(body, mesh=mesh, in_specs=in_specs, out_specs=out_specs, check_vma=False)
```

```python
import functools

import jax
import jax.numpy as jnp
import numpy as np
from jax import lax
from jax.experimental import pallas as pl
from jax.experimental.pallas import tpu as pltpu
from jax.sharding import PartitionSpec as P

MESH = pl.DeviceIdType.MESH
F32 = jnp.float32
BF16 = jnp.bfloat16

HEADS = 64
KV_HEADS = 4
HD = 128
STEPS = 2
EPSILON = 1e-05
ROPE_BASE = 500000.0
SCALE = HD ** (-0.5) * 1.4426950408889634
MASKED = -1e30

NH = 16
NF = 8
NX = 4
NY = 4
TURN = 512
GROUPS = (((0, 256), (256, 256)), ((512, 384), (896, 256)))
OWN = 32
PR = 16
CHUNK = 4096
CACHE_COPIES = 4
PAIRS = KV_HEADS // 2


def remote(src, dst, send_sem, recv_sem, device):
    return pltpu.make_async_remote_copy(
        src_ref=src,
        dst_ref=dst,
        send_sem=send_sem,
        recv_sem=recv_sem,
        device_id=device,
        device_id_type=MESH,
    )


def rotate(vectors, cosine, sine):
    return vectors * cosine + pltpu.roll(vectors, HD // 2, 1) * sine


def kernel(
    lengths_hbm, freq, tokens, gain, wq, wkv, wout, cache_k, cache_v,
    results,
    lengths, raw_v, tok_v, freq_v, gain_v, wq_v, wkv_v, wout_v, k_v, k_t, v_v,
    x_all, normed, ss_own, ss_recv, tot_all, part, relay, left, right, mine, mine_recv,
    spread, msg, qkv, kx, vx, ne, scores, weighted, att_send, att_recv, att_f32, rows_all,
    opart, sib_recv, fin_send, fin_recv,
    local_sem, k_sem, v_sem,
    tok_ssem, tok_rsem, fwd_ssem, fwd_rsem, ss_ssem, ss_rsem, tot_ssem, tot_rsem,
    ring_ssem, ring_rsem, stage_ssem, stage_rsem, msg_ssem, msg_rsem, att_ssem, att_rsem, line_ssem, line_rsem,
    sib_ssem, sib_rsem, fin_ssem, fin_rsem,
):
    h = lax.axis_index("hid")
    f = lax.axis_index("ffn")
    z = lax.div(h, NY)
    y = lax.rem(h, NY)
    cx = lax.div(f, 2)
    core = lax.rem(f, 2)
    sib = f + 1 - 2 * core
    lmax = cache_k.shape[1]

    barrier = pltpu.get_barrier_semaphore()
    tokens_load = pltpu.make_async_copy(tokens, raw_v, local_sem.at[0])
    tokens_load.start()

    def greet_hid(k, carry):
        pl.semaphore_signal(
            barrier, inc=1, device_id=(lax.rem(h + k, NH), f), device_id_type=MESH
        )
        return carry

    def greet_ffn(k, carry):
        pl.semaphore_signal(
            barrier, inc=1, device_id=(h, lax.rem(f + k, NF)), device_id_type=MESH
        )
        return carry

    lax.fori_loop(1, NF, greet_ffn, 0)
    lax.fori_loop(1, NH, greet_hid, 0)

    loads = []
    for i, (src, dst) in enumerate(
        [(gain, gain_v), (freq, freq_v), (wq, wq_v), (wkv, wkv_v), (lengths_hbm, lengths)]
    ):
        copy = pltpu.make_async_copy(src, dst, local_sem.at[1 + i])
        copy.start()
        loads.append(copy)
    span = lmax // CACHE_COPIES
    k_loads = []
    for i in range(CACHE_COPIES):
        copy = pltpu.make_async_copy(
            cache_k.at[0, pl.ds(i * span, span)], k_v.at[pl.ds(i * span, span)], k_sem.at[i]
        )
        copy.start()
        k_loads.append(copy)
    wout_load = pltpu.make_async_copy(wout, wout_v, local_sem.at[6])
    wout_load.start()

    def turn_keys(quarter):
        k_loads[quarter].wait()

        def turn(i, carry):
            rows = pl.ds(pl.multiple_of(quarter * span + i * TURN, TURN), TURN)
            k_t[:, rows] = k_v[rows, :].T
            return carry

        lax.fori_loop(0, span // TURN, turn, 0)

    tokens_load.wait()
    x_f32 = raw_v[...].astype(F32).reshape(tok_v.shape)
    x_own = x_f32.astype(BF16)
    tok_v[...] = x_own
    pl.semaphore_wait(barrier, NH + NF - 2)

    def block(index):
        return x_all.at[pl.ds(pl.multiple_of(index * OWN, OWN), OWN)]

    tok_copies = []
    for k in (1, 3, 2):
        peer = 2 * lax.rem(cx + k, NX) + core
        copy = remote(tok_v, block(f), tok_ssem.at[k - 1], tok_rsem.at[k - 1], (h, peer))
        copy.start()
        tok_copies.append((k, copy))
    fwd_copies = [remote(tok_v, block(f), fwd_ssem.at[0], fwd_rsem.at[0], (h, sib))]
    fwd_copies[0].start()

    sums = jnp.sum(x_f32 * x_f32, axis=1, keepdims=True)
    row_id = lax.broadcasted_iota(jnp.int32, (OWN, HD), 0)
    lane_id = lax.broadcasted_iota(jnp.int32, (OWN, HD), 1)
    diagonal = row_id == lane_id
    own_sums = jnp.sum(jnp.where(diagonal, sums, 0.0), axis=0, keepdims=True)
    ss_own[...] = jnp.broadcast_to(own_sums, (8, HD))

    def ss_copy(k):
        return remote(
            ss_own, ss_recv.at[k - 1], ss_ssem.at[k - 1], ss_rsem.at[k - 1],
            (lax.rem(h + k, NH), f),
        )

    def ss_start(k, carry):
        ss_copy(k).start()
        return carry

    lax.fori_loop(1, NH, ss_start, 0)
    x_all[pl.ds(pl.multiple_of(f * OWN, OWN), OWN), :] = x_own

    def ss_add(k, total):
        ss_copy(k).wait_recv()
        return total + ss_recv[k - 1]

    total = lax.fori_loop(1, NH, ss_add, ss_own[...])
    tot_all[f] = total
    tot_copies = []
    for k in range(1, NF):
        copy = remote(
            tot_all.at[f], tot_all.at[f], tot_ssem.at[k - 1], tot_rsem.at[k - 1],
            (h, lax.rem(f + k, NF)),
        )
        copy.start()
        tot_copies.append(copy)
    for k, tok_copy in tok_copies:
        tok_copy.wait_recv()
        came = 2 * lax.rem(cx + NX - k, NX) + core
        copy = remote(block(came), block(came), fwd_ssem.at[k], fwd_rsem.at[k], (h, sib))
        copy.start()
        fwd_copies.append(copy)

    for copy in tot_copies:
        copy.wait_recv()
    loads[0].wait()
    width = x_all.shape[1]
    qcols = wq_v.shape[1]
    full = width * NH
    gain_row = gain_v[...].astype(F32).reshape(1, width)

    def project(parity):
        for x in range(NX):
            b = 2 * x + parity
            lane_sums = tot_all[b][0:1, :]
            row_sums = jnp.sum(jnp.where(diagonal, lane_sums, 0.0), axis=1, keepdims=True)
            inverse = lax.rsqrt(row_sums / full + EPSILON)
            normed[x * OWN : (x + 1) * OWN, :] = (
                block(b)[...].astype(F32) * inverse * gain_row
            ).astype(BF16)
        lhs = normed[...]
        for cols, weights in ((slice(0, qcols), wq_v), (slice(qcols, None), wkv_v)):
            product = jnp.dot(lhs, weights[...], preferred_element_type=F32)
            part[:, pl.ds(2 * parity, 2), :, cols] = product.reshape(NX, 2, PR, product.shape[1])

    loads[2].wait()
    loads[3].wait()
    project(core)

    loads[4].wait()
    length = lengths[h * NF + f]
    step_of = lax.div(lax.broadcasted_iota(jnp.int32, (PR, HD), 0), 8)
    loads[1].wait()
    angles = (step_of + length).astype(F32) * freq_v[...]
    cosine = jnp.cos(angles)
    sine = jnp.sin(angles)
    sine = jnp.where(
        lax.broadcasted_iota(jnp.int32, (PR, HD), 1) < HD // 2, -sine, sine
    )
    kx[...] = jnp.zeros_like(kx)
    vx[...] = jnp.zeros_like(vx)

    for copy in fwd_copies:
        copy.wait_recv()
    project(1 - core)

    half = PR // 2

    def ring(side):
        pos = (y, z)[side]

        def device(q):
            return (z * NY + q, f) if side == 0 else (q * NY + y, f)

        def view(q, cols):
            if side == 0:
                return part.at[:, q, pl.ds(0, half), cols]
            return part.at[q, :, pl.ds(half, half), cols]

        return pos, device, view

    moves = {}
    for g, (low, high) in enumerate(GROUPS):
        for side in range(2):
            pos, device, view = ring(side)
            nxt, prv, far = lax.rem(pos + 1, NY), lax.rem(pos + 3, NY), lax.rem(pos + 2, NY)
            plan = [
                (far, low, relay, nxt),
                (far, high, relay, prv),
                (nxt, high, left, nxt),
                (prv, low, right, prv),
            ]
            moves[g, side] = [
                remote(
                    view(q, pl.ds(*cols)), dst.at[side, :, :, pl.ds(*cols)],
                    ring_ssem.at[g, side, i], ring_rsem.at[g, side, i], device(to),
                )
                for i, (q, cols, dst, to) in enumerate(plan)
            ]
    for first in (0, 2):
        for g in range(len(GROUPS)):
            for side in range(2):
                for copy in moves[g, side][first : first + 2]:
                    copy.start()
    v_loads = []
    for i in range(CACHE_COPIES):
        copy = pltpu.make_async_copy(
            cache_v.at[0, pl.ds(i * span, span)], v_v.at[pl.ds(i * span, span)], v_sem.at[i]
        )
        copy.start()
        v_loads.append(copy)

    def ss_sent(k, carry):
        ss_copy(k).wait_send()
        return carry

    lax.fori_loop(1, NH, ss_sent, 0)
    for copy in tot_copies + fwd_copies + [copy for _, copy in tok_copies]:
        copy.wait_send()
    turn_keys(0)
    for g, (low, high) in enumerate(GROUPS):
        for side in range(2):
            pos, device, view = ring(side)
            nxt, prv = lax.rem(pos + 1, NY), lax.rem(pos + 3, NY)
            for i, (to, cols, dst) in enumerate(((nxt, low, left), (prv, high, right))):
                cols = pl.ds(*cols)
                moves[g, side][i].wait_recv()
                passed = relay.at[side, :, :, cols]
                passed[...] = passed[...] + view(to, cols)[...]
                copy = remote(
                    passed, dst.at[side, :, :, cols],
                    ring_ssem.at[g, side, 4 + i], ring_rsem.at[g, side, 4 + i], device(to),
                )
                copy.start()
                moves[g, side].append(copy)
    turn_keys(1)
    stages = {}
    for g, (low, high) in enumerate(GROUPS):
        cols = pl.ds(low[0], low[1] + high[1])
        for side in range(2):
            pos, device, view = ring(side)
            for copy in moves[g, side][2:]:
                copy.wait_recv()
            mine[side, :, :, cols] = (
                view(pos, cols)[...] + left[side, :, :, cols] + right[side, :, :, cols]
            )
            other, other_device, _ = ring(1 - side)
            stages[g, side] = []
            for k in (1, 3, 2):
                peer = lax.rem(other + k, NY)
                copy = remote(
                    mine.at[side, peer, :, cols], mine_recv.at[side, k - 1, :, cols],
                    stage_ssem.at[g, side, k - 1], stage_rsem.at[g, side, k - 1],
                    other_device(peer),
                )
                copy.start()
                stages[g, side].append(copy)
    turn_keys(2)
    groups = []
    for g, (low, high) in enumerate(GROUPS):
        cols = pl.ds(low[0], low[1] + high[1])
        halves = []
        for side in range(2):
            other = ring(1 - side)[0]
            total = mine[side, other, :, cols]
            for copy in stages[g, side]:
                copy.wait_recv()
            for k in range(NY - 1):
                total = total + mine_recv[side, k, :, cols]
            halves.append(total)
        groups.append(jnp.concatenate(halves, axis=0))
    summed = jnp.concatenate(groups, axis=1)

    for j in range(8):
        spread[pl.ds(j, PR, stride=8), :] = summed[:, j * HD : (j + 1) * HD]
    msg[:, :PR, :] = spread[...].reshape(NF, PR, HD).astype(BF16)
    spread[...] = jnp.zeros_like(spread)
    spread[pl.ds(0, PR, stride=8), :] = summed[:, qcols:]
    msg[:, PR:, :] = spread[...].reshape(NF, PR, HD).astype(BF16)
    qkv[f] = msg[f]
    msg_copies = []
    for k in range(1, NF):
        peer = lax.rem(f + k, NF)
        copy = remote(
            msg.at[peer], qkv.at[f], msg_ssem.at[k - 1], msg_rsem.at[k - 1], (h, peer)
        )
        copy.start()
        msg_copies.append(copy)
    for key in moves:
        for copy in moves[key] + stages[key]:
            copy.wait_send()
    turn_keys(3)
    for copy in msg_copies:
        copy.wait_recv()

    fresh_rows = []
    for i in range(2 * KV_HEADS):
        raw = qkv[i, PR:, :].astype(F32)
        cols = pl.ds((i % KV_HEADS) * HD, HD)
        if i < KV_HEADS:
            raw = rotate(raw, cosine, sine)
            kx[:PR, cols] = raw.astype(BF16)
        else:
            vx[:PR, cols] = raw.astype(BF16)
        fresh_rows.append(raw)

    rotated = [
        rotate(qkv[i, :PR, :].astype(F32), cosine, sine).astype(BF16) for i in range(NF)
    ]
    nothing = jnp.zeros((OWN, HD), BF16)
    queries = []
    for p in range(PAIRS):
        upper = jnp.concatenate(rotated[4 * p : 4 * p + 2], axis=0)
        lower = jnp.concatenate(rotated[4 * p + 2 : 4 * p + 4], axis=0)
        queries.append(
            jnp.concatenate(
                [
                    jnp.concatenate([upper, nothing], axis=1),
                    jnp.concatenate([nothing, lower], axis=1),
                ],
                axis=0,
            )
        )
    pair_rows, pair_cols = 2 * OWN, 2 * HD
    lane = lax.broadcasted_iota(jnp.int32, (pair_rows, HD), 1)
    step_row = lax.rem(lax.div(lax.broadcasted_iota(jnp.int32, (pair_rows, HD), 0), 8), 2)
    fresh_live = (lane == 0) | ((lane == 8) & (step_row == 1))
    nt = (((1,), (1,)), ((), ()))
    def attend(p):
        pair = pl.ds(p * pair_cols, pair_cols)
        rows_of = pl.ds(p * pair_rows, pair_rows)
        fresh = lax.dot_general(queries[p], kx[:, pair], nt, preferred_element_type=F32)
        fresh = jnp.where(fresh_live, fresh * SCALE, MASKED)

        def score_step(c, high):
            rows = pl.ds(pl.multiple_of(c * CHUNK, CHUNK), CHUNK)
            position = lax.broadcasted_iota(jnp.int32, (8, CHUNK), 1) + c * CHUNK
            cap = jnp.where(position < length, -MASKED, MASKED)
            cap = jnp.concatenate([cap] * (pair_rows // 8), axis=0)
            s = jnp.dot(queries[p], k_t[pair, rows], preferred_element_type=F32)
            s = jnp.minimum(s * SCALE, cap)
            scores[rows_of, rows] = s
            for t in range(CHUNK // HD):
                high = jnp.maximum(high, s[:, t * HD : (t + 1) * HD])
            return high

        high = lax.fori_loop(0, lmax // CHUNK, score_step, fresh)
        peak = jnp.broadcast_to(jnp.max(high, axis=1, keepdims=True), (pair_rows, HD))
        weights = jnp.exp2(fresh - peak).astype(BF16)
        weighted[p] = jnp.dot(weights, vx[:, pair], preferred_element_type=F32)

        def value_step(c, total):
            rows = pl.ds(pl.multiple_of(c * CHUNK, CHUNK), CHUNK)
            s = scores[rows_of, rows]
            pieces = []
            for t in range(CHUNK // HD):
                piece = jnp.exp2(s[:, t * HD : (t + 1) * HD] - peak).astype(BF16)
                total = total + piece.astype(F32)
                pieces.append(piece)
            weighted[p] += jnp.dot(
                jnp.concatenate(pieces, axis=1), v_v[rows, pair], preferred_element_type=F32
            )
            return total

        if p == 0:
            for copy in v_loads:
                copy.wait()
        total = lax.fori_loop(0, lmax // CHUNK, value_step, weights.astype(F32))
        weight_sum = jnp.sum(total, axis=1, keepdims=True)
        for i in range(2):
            rows = slice(i * OWN, (i + 1) * OWN)
            attended = weighted[p, rows, i * HD : (i + 1) * HD] / weight_sum[rows]
            attended = attended.astype(BF16)
            att_send[4 * p + 2 * i] = attended[:PR]
            att_send[4 * p + 2 * i + 1] = attended[PR:]

    odd = lax.rem(y + z, 2)
    slot = lax.rem(lax.div(y, 2) + lax.div(z, 2), 2)

    def send_attended(p):
        for m in range(4):
            peer = 4 * p + lax.rem(f + m, 4)
            landing = att_recv.at[odd, slot, f]

            @pl.when(peer == f)
            def _():
                pltpu.make_async_copy(
                    att_send.at[f], landing, att_rsem.at[odd, slot]
                ).start()

            for k in range(NY):
                chip = lax.rem(z + odd * k, NY) * NY + lax.rem(y + (1 - odd) * k, NY)
                copy = remote(
                    att_send.at[peer], landing, att_ssem.at[k], att_rsem.at[odd, slot],
                    (chip, peer),
                )
                if k == 0:
                    pl.when(peer != f)(copy.start)
                else:
                    copy.start()

    for p in range(PAIRS):
        attend(p)
        send_attended(p)

    for i in range(2 * KV_HEADS):
        ne[0:1, i * HD : (i + 1) * HD] = fresh_rows[i][0:1]
        ne[1:2, i * HD : (i + 1) * HD] = fresh_rows[i][8:9]
    results[PR:, :, :] = ne[0:2, :].reshape(1, STEPS, ne.shape[1]).astype(BF16)

    line_copies = [[], []]
    for part_id in range(2):
        for side in range(2):
            whole = att_recv.at[side, part_id]
            pltpu.make_async_copy(whole, whole, att_rsem.at[side, part_id]).wait()
            pos = (z, y)[side]
            att_f32[...] = att_recv[side, part_id].astype(F32).reshape(NF * PR, HD)
            for j in range(8):
                rows_all[part_id, side, pos, :, j * HD : (j + 1) * HD] = att_f32[
                    pl.ds(j, PR, stride=8), :
                ].astype(BF16)
            mine_rows = rows_all.at[part_id, side, pos]
            for k in range(1, NY):
                q = lax.rem(pos + k, NY)
                device = (q * NY + y, f) if side == 0 else (z * NY + q, f)
                copy = remote(
                    mine_rows, mine_rows,
                    line_ssem.at[part_id, side, k - 1], line_rsem.at[part_id, side, k - 1],
                    device,
                )
                copy.start()
                line_copies[part_id].append(copy)
    wout_load.wait()
    for copy in msg_copies:
        copy.wait_send()
    for k in range(NY):
        sent = att_send.at[pl.ds(0, NF - 1)] if k == 0 else att_send
        pltpu.make_async_copy(sent, sent, att_ssem.at[k]).wait()

    def out_rows(index):
        return pl.ds(pl.multiple_of(index * OWN, OWN), OWN)

    sib_copies = [[], []]
    for part_id in range(2):
        for copy in line_copies[part_id]:
            copy.wait_recv()
        product = jnp.dot(
            rows_all[part_id].reshape(NH * PR // 2, wout_v.shape[0]),
            wout_v[...],
            preferred_element_type=F32,
        )
        for side in range(2):
            for q in range(NY):
                far = 2 * ((part_id + q // 2) % 2) + (q + side) % 2
                home = q * NY + far if side == 0 else far * NY + q
                first = (side * NY + q) * PR
                opart[home * PR : (home + 1) * PR, :] = product[first : first + PR]
        for e in range(2):
            x = 2 * lax.rem(1 + core + part_id, 2) + e
            copy = remote(
                opart.at[out_rows(2 * x + 1 - core)], sib_recv.at[part_id, e],
                sib_ssem.at[part_id, e], sib_rsem.at[part_id, e], (h, sib),
            )
            copy.start()
            sib_copies[part_id].append(copy)
    fin_copies = []
    for part_id in range(2):
        for copy in sib_copies[part_id]:
            copy.wait_recv()
        for e in range(2):
            x = 2 * lax.rem(core + part_id, 2) + e
            hop = lax.rem(x - cx + NX, NX)
            there = lax.rem(hop + NX - 1, NX)
            copy = remote(
                fin_send.at[part_id, e], fin_recv.at[there],
                fin_ssem.at[part_id, e], fin_rsem.at[there], (h, 2 * x + core),
            )
            fin_copies.append((hop, copy))

            @pl.when(hop != 0)
            def _():
                total = opart[out_rows(2 * x + core), :] + sib_recv[part_id, e]
                fin_send[part_id, e] = total.astype(BF16)
                copy.start()

    for copies in sib_copies + line_copies:
        for copy in copies:
            copy.wait_send()
    own_part = lax.rem(core + lax.div(cx, 2), 2)
    result = opart[out_rows(f), :] + sib_recv[own_part, lax.rem(cx, 2)]
    for k in range(1, NX):
        pltpu.make_async_copy(
            fin_recv.at[k - 1], fin_recv.at[k - 1], fin_rsem.at[k - 1]
        ).wait()
        result = result + fin_recv[k - 1].astype(F32)
    results[:PR, :, :] = result.reshape(PR, STEPS, result.shape[1]).astype(BF16)
    for hop, copy in fin_copies:
        pl.when(hop != 0)(copy.wait_send)


def hand_out(results, out, entries, sem):
    rows = out.shape[0]
    copies = [
        pltpu.make_async_copy(results.at[pl.ds(0, rows)], out, sem.at[0]),
        pltpu.make_async_copy(results.at[pl.ds(rows, 1)], entries, sem.at[1]),
    ]
    for copy in copies:
        copy.start()
    for copy in copies:
        copy.wait()


def body(tokens, norm_gain, query_weight, w_keyval, w_out, cache_keys, cache_values, lengths):
    width = tokens.shape[2]
    lmax = cache_keys.shape[1]
    qcols = query_weight.shape[1]
    kvcols = w_keyval.shape[1]
    halves = np.arange(HD // 2, dtype=np.float64) * (2.0 / HD)
    freq = (ROPE_BASE ** (-halves)).astype(np.float32)
    freq = jnp.asarray(np.tile(np.concatenate([freq, freq])[None, :], (PR, 1)))
    any_spec = pl.BlockSpec(memory_space=pl.ANY)
    hbm_spec = pl.BlockSpec(memory_space=pltpu.HBM)
    vmem_spec = pl.BlockSpec(memory_space=pltpu.VMEM)
    dma = pltpu.SemaphoreType.DMA
    rows = NH * PR
    results = pl.pallas_call(
        kernel,
        out_shape=pltpu.VMEM((PR + 1, STEPS, width), BF16),
        in_specs=[hbm_spec] * 9,
        out_specs=vmem_spec,
        scratch_shapes=[
            pltpu.SMEM(lengths.shape, jnp.int32),
            pltpu.VMEM(tokens.shape, BF16),
            pltpu.VMEM((OWN, width), BF16),
            pltpu.VMEM((PR, HD), F32),
            pltpu.VMEM((width,), BF16),
            pltpu.VMEM((width, qcols), BF16),
            pltpu.VMEM((width, kvcols), BF16),
            pltpu.VMEM((qcols, width), BF16),
            pltpu.VMEM((lmax, KV_HEADS * HD), BF16),
            pltpu.VMEM((KV_HEADS * HD, lmax), BF16),
            pltpu.VMEM((lmax, KV_HEADS * HD), BF16),
            pltpu.VMEM((rows, width), BF16),
            pltpu.VMEM((rows // 2, width), BF16),
            pltpu.VMEM((8, HD), F32),
            pltpu.VMEM((NH - 1, 8, HD), F32),
            pltpu.VMEM((NF, 8, HD), F32),
            pltpu.VMEM((NY, NY, PR, qcols + kvcols), F32),
            pltpu.VMEM((2, NY, PR // 2, qcols + kvcols), F32),
            pltpu.VMEM((2, NY, PR // 2, qcols + kvcols), F32),
            pltpu.VMEM((2, NY, PR // 2, qcols + kvcols), F32),
            pltpu.VMEM((2, NY, PR // 2, qcols + kvcols), F32),
            pltpu.VMEM((2, NY - 1, PR // 2, qcols + kvcols), F32),
            pltpu.VMEM((NF * PR, HD), F32),
            pltpu.VMEM((NF, 2 * PR, HD), BF16),
            pltpu.VMEM((NF, 2 * PR, HD), BF16),
            pltpu.VMEM((HD, KV_HEADS * HD), BF16),
            pltpu.VMEM((HD, KV_HEADS * HD), BF16),
            pltpu.VMEM((8, 2 * KV_HEADS * HD), F32),
            pltpu.VMEM((KV_HEADS * OWN, lmax), F32),
            pltpu.VMEM((PAIRS, 2 * OWN, 2 * HD), F32),
            pltpu.VMEM((NF, PR, HD), BF16),
            pltpu.VMEM((2, 2, NF, PR, HD), BF16),
            pltpu.VMEM((NF * PR, HD), F32),
            pltpu.VMEM((2, 2, NY, PR, qcols), BF16),
            pltpu.VMEM((rows, width), F32),
            pltpu.VMEM((2, 2, OWN, width), F32),
            pltpu.VMEM((2, 2, OWN, width), BF16),
            pltpu.VMEM((NX - 1, OWN, width), BF16),
            dma((8,)),
            dma((CACHE_COPIES,)),
            dma((CACHE_COPIES,)),
            dma((NX - 1,)), dma((NX - 1,)),
            dma((NX,)), dma((NX,)),
            dma((NH - 1,)), dma((NH - 1,)),
            dma((NF - 1,)), dma((NF - 1,)),
            dma((2, 2, 6)), dma((2, 2, 6)),
            dma((2, 2, NY - 1)), dma((2, 2, NY - 1)),
            dma((NF - 1,)), dma((NF - 1,)),
            dma((NY,)), dma((2, 2)),
            dma((2, 2, NY - 1)), dma((2, 2, NY - 1)),
            dma((2, 2)), dma((2, 2)),
            dma((2, 2)), dma((NX - 1,)),
        ],
        compiler_params=pltpu.CompilerParams(
            collective_id=0, has_side_effects=True, vmem_limit_bytes=48 * 2**20
        ),
        name="decode_block",
    )(
        *[
            pltpu.with_memory_space_constraint(array, pltpu.HBM)
            for array in (
                lengths, freq, tokens, norm_gain, query_weight, w_keyval, w_out,
                cache_keys, cache_values,
            )
        ],
    )
    return pl.pallas_call(
        hand_out,
        out_shape=(
            jax.ShapeDtypeStruct(tokens.shape, BF16),
            jax.ShapeDtypeStruct((1, STEPS, 2 * KV_HEADS * HD), BF16),
        ),
        in_specs=[vmem_spec],
        out_specs=(any_spec, any_spec),
        scratch_shapes=[dma((2,))],
        name="hand_out",
    )(pltpu.with_memory_space_constraint(results, pltpu.VMEM))


def solution(mesh):
    in_specs = (
        P("ffn", None, "hid"),
        P("hid"),
        P("hid", "ffn"),
        P("hid", "ffn"),
        P("ffn", "hid"),
        P(("hid", "ffn"), None, None),
        P(("hid", "ffn"), None, None),
        P(),
    )
    out_specs = (P("ffn", None, "hid"), P(("hid", "ffn"), None, None))
    return jax.shard_map(body, mesh=mesh, in_specs=in_specs, out_specs=out_specs, check_vma=False)
```

```python
import functools

import jax
import jax.numpy as jnp
import numpy as np
from jax import lax
from jax.experimental import pallas as pl
from jax.experimental.pallas import tpu as pltpu
from jax.sharding import PartitionSpec as P

MESH = pl.DeviceIdType.MESH
F32 = jnp.float32
BF16 = jnp.bfloat16

HEADS = 64
KV_HEADS = 4
HD = 128
STEPS = 2
EPSILON = 1e-05
ROPE_BASE = 500000.0
SCALE = HD ** (-0.5) * 1.4426950408889634
MASKED = -1e30

NH = 16
NF = 8
NX = 4
NY = 4
TURN = 512
GROUPS = (((0, 256), (256, 256)), ((512, 384), (896, 256)))
OWN = 32
PR = 16
CHUNK = 1024
CACHE_COPIES = 4
PAIRS = KV_HEADS // 2


def remote(src, dst, send_sem, recv_sem, device):
    return pltpu.make_async_remote_copy(
        src_ref=src,
        dst_ref=dst,
        send_sem=send_sem,
        recv_sem=recv_sem,
        device_id=device,
        device_id_type=MESH,
    )


def rotate(vectors, cosine, sine):
    return vectors * cosine + pltpu.roll(vectors, HD // 2, 1) * sine


def kernel(
    lengths_hbm, freq, tokens, gain, wq, wkv, wout, cache_k, cache_v,
    results,
    lengths, raw_v, tok_v, freq_v, gain_v, wq_v, wkv_v, wout_v, k_v, k_t, v_v,
    x_all, normed, ss_own, ss_recv, tot_all, part, relay, left, right, mine, mine_recv,
    spread, msg, qkv, kx, vx, ne, scores, weighted, att_send, att_recv, att_f32, rows_all,
    opart, sib_recv, fin_send, fin_recv,
    local_sem, k_sem, v_sem,
    tok_ssem, tok_rsem, fwd_ssem, fwd_rsem, ss_ssem, ss_rsem, tot_ssem, tot_rsem,
    ring_ssem, ring_rsem, stage_ssem, stage_rsem, msg_ssem, msg_rsem, att_ssem, att_rsem, line_ssem, line_rsem,
    sib_ssem, sib_rsem, fin_ssem, fin_rsem,
):
    h = lax.axis_index("hid")
    f = lax.axis_index("ffn")
    z = lax.div(h, NY)
    y = lax.rem(h, NY)
    cx = lax.div(f, 2)
    core = lax.rem(f, 2)
    sib = f + 1 - 2 * core
    lmax = cache_k.shape[1]

    barrier = pltpu.get_barrier_semaphore()
    tokens_load = pltpu.make_async_copy(tokens, raw_v, local_sem.at[0])
    tokens_load.start()

    def greet_hid(k, carry):
        pl.semaphore_signal(
            barrier, inc=1, device_id=(lax.rem(h + k, NH), f), device_id_type=MESH
        )
        return carry

    def greet_ffn(k, carry):
        pl.semaphore_signal(
            barrier, inc=1, device_id=(h, lax.rem(f + k, NF)), device_id_type=MESH
        )
        return carry

    lax.fori_loop(1, NF, greet_ffn, 0)
    lax.fori_loop(1, NH, greet_hid, 0)

    loads = []
    for i, (src, dst) in enumerate(
        [(gain, gain_v), (freq, freq_v), (wq, wq_v), (wkv, wkv_v), (lengths_hbm, lengths)]
    ):
        copy = pltpu.make_async_copy(src, dst, local_sem.at[1 + i])
        copy.start()
        loads.append(copy)
    span = lmax // CACHE_COPIES
    k_loads = []
    for i in range(CACHE_COPIES):
        copy = pltpu.make_async_copy(
            cache_k.at[0, pl.ds(i * span, span)], k_v.at[pl.ds(i * span, span)], k_sem.at[i]
        )
        copy.start()
        k_loads.append(copy)
    wout_load = pltpu.make_async_copy(wout, wout_v, local_sem.at[6])
    wout_load.start()

    def turn_keys(quarter):
        k_loads[quarter].wait()

        def turn(i, carry):
            rows = pl.ds(pl.multiple_of(quarter * span + i * TURN, TURN), TURN)
            k_t[:, rows] = k_v[rows, :].T
            return carry

        lax.fori_loop(0, span // TURN, turn, 0)

    tokens_load.wait()
    x_f32 = raw_v[...].astype(F32).reshape(tok_v.shape)
    x_own = x_f32.astype(BF16)
    tok_v[...] = x_own
    pl.semaphore_wait(barrier, NH + NF - 2)

    def block(index):
        return x_all.at[pl.ds(pl.multiple_of(index * OWN, OWN), OWN)]

    tok_copies = []
    for k in (1, 3, 2):
        peer = 2 * lax.rem(cx + k, NX) + core
        copy = remote(tok_v, block(f), tok_ssem.at[k - 1], tok_rsem.at[k - 1], (h, peer))
        copy.start()
        tok_copies.append((k, copy))
    fwd_copies = [remote(tok_v, block(f), fwd_ssem.at[0], fwd_rsem.at[0], (h, sib))]
    fwd_copies[0].start()

    sums = jnp.sum(x_f32 * x_f32, axis=1, keepdims=True)
    row_id = lax.broadcasted_iota(jnp.int32, (OWN, HD), 0)
    lane_id = lax.broadcasted_iota(jnp.int32, (OWN, HD), 1)
    diagonal = row_id == lane_id
    own_sums = jnp.sum(jnp.where(diagonal, sums, 0.0), axis=0, keepdims=True)
    ss_own[...] = jnp.broadcast_to(own_sums, (8, HD))

    def ss_copy(k):
        return remote(
            ss_own, ss_recv.at[k - 1], ss_ssem.at[k - 1], ss_rsem.at[k - 1],
            (lax.rem(h + k, NH), f),
        )

    def ss_start(k, carry):
        ss_copy(k).start()
        return carry

    lax.fori_loop(1, NH, ss_start, 0)
    x_all[pl.ds(pl.multiple_of(f * OWN, OWN), OWN), :] = x_own

    def ss_add(k, total):
        ss_copy(k).wait_recv()
        return total + ss_recv[k - 1]

    total = lax.fori_loop(1, NH, ss_add, ss_own[...])
    tot_all[f] = total
    tot_copies = []
    for k in range(1, NF):
        copy = remote(
            tot_all.at[f], tot_all.at[f], tot_ssem.at[k - 1], tot_rsem.at[k - 1],
            (h, lax.rem(f + k, NF)),
        )
        copy.start()
        tot_copies.append(copy)
    for k, tok_copy in tok_copies:
        tok_copy.wait_recv()
        came = 2 * lax.rem(cx + NX - k, NX) + core
        copy = remote(block(came), block(came), fwd_ssem.at[k], fwd_rsem.at[k], (h, sib))
        copy.start()
        fwd_copies.append(copy)

    for copy in tot_copies:
        copy.wait_recv()
    loads[0].wait()
    width = x_all.shape[1]
    qcols = wq_v.shape[1]
    full = width * NH
    gain_row = gain_v[...].astype(F32).reshape(1, width)

    def project(parity):
        for x in range(NX):
            b = 2 * x + parity
            lane_sums = tot_all[b][0:1, :]
            row_sums = jnp.sum(jnp.where(diagonal, lane_sums, 0.0), axis=1, keepdims=True)
            inverse = lax.rsqrt(row_sums / full + EPSILON)
            normed[x * OWN : (x + 1) * OWN, :] = (
                block(b)[...].astype(F32) * inverse * gain_row
            ).astype(BF16)
        lhs = normed[...]
        for cols, weights in ((slice(0, qcols), wq_v), (slice(qcols, None), wkv_v)):
            product = jnp.dot(lhs, weights[...], preferred_element_type=F32)
            part[:, pl.ds(2 * parity, 2), :, cols] = product.reshape(NX, 2, PR, product.shape[1])

    loads[2].wait()
    loads[3].wait()
    project(core)

    loads[4].wait()
    length = lengths[h * NF + f]
    step_of = lax.div(lax.broadcasted_iota(jnp.int32, (PR, HD), 0), 8)
    loads[1].wait()
    angles = (step_of + length).astype(F32) * freq_v[...]
    cosine = jnp.cos(angles)
    sine = jnp.sin(angles)
    sine = jnp.where(
        lax.broadcasted_iota(jnp.int32, (PR, HD), 1) < HD // 2, -sine, sine
    )
    kx[...] = jnp.zeros_like(kx)
    vx[...] = jnp.zeros_like(vx)

    for copy in fwd_copies:
        copy.wait_recv()
    project(1 - core)

    half = PR // 2

    def ring(side):
        pos = (y, z)[side]

        def device(q):
            return (z * NY + q, f) if side == 0 else (q * NY + y, f)

        def view(q, cols):
            if side == 0:
                return part.at[:, q, pl.ds(0, half), cols]
            return part.at[q, :, pl.ds(half, half), cols]

        return pos, device, view

    moves = {}
    for g, (low, high) in enumerate(GROUPS):
        for side in range(2):
            pos, device, view = ring(side)
            nxt, prv, far = lax.rem(pos + 1, NY), lax.rem(pos + 3, NY), lax.rem(pos + 2, NY)
            plan = [
                (far, low, relay, nxt),
                (far, high, relay, prv),
                (nxt, high, left, nxt),
                (prv, low, right, prv),
            ]
            moves[g, side] = [
                remote(
                    view(q, pl.ds(*cols)), dst.at[side, :, :, pl.ds(*cols)],
                    ring_ssem.at[g, side, i], ring_rsem.at[g, side, i], device(to),
                )
                for i, (q, cols, dst, to) in enumerate(plan)
            ]
    for first in (0, 2):
        for g in range(len(GROUPS)):
            for side in range(2):
                for copy in moves[g, side][first : first + 2]:
                    copy.start()
    v_loads = []
    for i in range(CACHE_COPIES):
        copy = pltpu.make_async_copy(
            cache_v.at[0, pl.ds(i * span, span)], v_v.at[pl.ds(i * span, span)], v_sem.at[i]
        )
        copy.start()
        v_loads.append(copy)

    def ss_sent(k, carry):
        ss_copy(k).wait_send()
        return carry

    lax.fori_loop(1, NH, ss_sent, 0)
    for copy in tot_copies + fwd_copies + [copy for _, copy in tok_copies]:
        copy.wait_send()
    turn_keys(0)
    for g, (low, high) in enumerate(GROUPS):
        for side in range(2):
            pos, device, view = ring(side)
            nxt, prv = lax.rem(pos + 1, NY), lax.rem(pos + 3, NY)
            for i, (to, cols, dst) in enumerate(((nxt, low, left), (prv, high, right))):
                cols = pl.ds(*cols)
                moves[g, side][i].wait_recv()
                passed = relay.at[side, :, :, cols]
                passed[...] = passed[...] + view(to, cols)[...]
                copy = remote(
                    passed, dst.at[side, :, :, cols],
                    ring_ssem.at[g, side, 4 + i], ring_rsem.at[g, side, 4 + i], device(to),
                )
                copy.start()
                moves[g, side].append(copy)
    turn_keys(1)
    stages = {}
    for g, (low, high) in enumerate(GROUPS):
        cols = pl.ds(low[0], low[1] + high[1])
        for side in range(2):
            pos, device, view = ring(side)
            for copy in moves[g, side][2:]:
                copy.wait_recv()
            mine[side, :, :, cols] = (
                view(pos, cols)[...] + left[side, :, :, cols] + right[side, :, :, cols]
            )
            other, other_device, _ = ring(1 - side)
            stages[g, side] = []
            for k in (1, 3, 2):
                peer = lax.rem(other + k, NY)
                copy = remote(
                    mine.at[side, peer, :, cols], mine_recv.at[side, k - 1, :, cols],
                    stage_ssem.at[g, side, k - 1], stage_rsem.at[g, side, k - 1],
                    other_device(peer),
                )
                copy.start()
                stages[g, side].append(copy)
    turn_keys(2)
    groups = []
    for g, (low, high) in enumerate(GROUPS):
        cols = pl.ds(low[0], low[1] + high[1])
        halves = []
        for side in range(2):
            other = ring(1 - side)[0]
            total = mine[side, other, :, cols]
            for copy in stages[g, side]:
                copy.wait_recv()
            for k in range(NY - 1):
                total = total + mine_recv[side, k, :, cols]
            halves.append(total)
        groups.append(jnp.concatenate(halves, axis=0))
    summed = jnp.concatenate(groups, axis=1)

    for j in range(8):
        spread[pl.ds(j, PR, stride=8), :] = summed[:, j * HD : (j + 1) * HD]
    msg[:, :PR, :] = spread[...].reshape(NF, PR, HD).astype(BF16)
    spread[...] = jnp.zeros_like(spread)
    spread[pl.ds(0, PR, stride=8), :] = summed[:, qcols:]
    msg[:, PR:, :] = spread[...].reshape(NF, PR, HD).astype(BF16)
    qkv[f] = msg[f]
    msg_copies = []
    for k in range(1, NF):
        peer = lax.rem(f + k, NF)
        copy = remote(
            msg.at[peer], qkv.at[f], msg_ssem.at[k - 1], msg_rsem.at[k - 1], (h, peer)
        )
        copy.start()
        msg_copies.append(copy)
    for key in moves:
        for copy in moves[key] + stages[key]:
            copy.wait_send()
    turn_keys(3)
    for copy in msg_copies:
        copy.wait_recv()

    fresh_rows = []
    for i in range(2 * KV_HEADS):
        raw = qkv[i, PR:, :].astype(F32)
        cols = pl.ds((i % KV_HEADS) * HD, HD)
        if i < KV_HEADS:
            raw = rotate(raw, cosine, sine)
            kx[:PR, cols] = raw.astype(BF16)
        else:
            vx[:PR, cols] = raw.astype(BF16)
        fresh_rows.append(raw)

    rotated = [
        rotate(qkv[i, :PR, :].astype(F32), cosine, sine).astype(BF16) for i in range(NF)
    ]
    nothing = jnp.zeros((OWN, HD), BF16)
    queries = []
    for p in range(PAIRS):
        upper = jnp.concatenate(rotated[4 * p : 4 * p + 2], axis=0)
        lower = jnp.concatenate(rotated[4 * p + 2 : 4 * p + 4], axis=0)
        queries.append(
            jnp.concatenate(
                [
                    jnp.concatenate([upper, nothing], axis=1),
                    jnp.concatenate([nothing, lower], axis=1),
                ],
                axis=0,
            )
        )
    pair_rows, pair_cols = 2 * OWN, 2 * HD
    lane = lax.broadcasted_iota(jnp.int32, (pair_rows, HD), 1)
    step_row = lax.rem(lax.div(lax.broadcasted_iota(jnp.int32, (pair_rows, HD), 0), 8), 2)
    fresh_live = (lane == 0) | ((lane == 8) & (step_row == 1))
    nt = (((1,), (1,)), ((), ()))
    def attend(p):
        pair = pl.ds(p * pair_cols, pair_cols)
        rows_of = pl.ds(p * pair_rows, pair_rows)
        fresh = lax.dot_general(queries[p], kx[:, pair], nt, preferred_element_type=F32)
        fresh = jnp.where(fresh_live, fresh * SCALE, MASKED)

        def score_step(c, high):
            rows = pl.ds(pl.multiple_of(c * CHUNK, CHUNK), CHUNK)
            position = lax.broadcasted_iota(jnp.int32, (8, CHUNK), 1) + c * CHUNK
            cap = jnp.where(position < length, -MASKED, MASKED)
            cap = jnp.concatenate([cap] * (pair_rows // 8), axis=0)
            s = jnp.dot(queries[p], k_t[pair, rows], preferred_element_type=F32)
            s = jnp.minimum(s * SCALE, cap)
            scores[rows_of, rows] = s
            for t in range(CHUNK // HD):
                high = jnp.maximum(high, s[:, t * HD : (t + 1) * HD])
            return high

        high = lax.fori_loop(0, lmax // CHUNK, score_step, fresh)
        peak = jnp.broadcast_to(jnp.max(high, axis=1, keepdims=True), (pair_rows, HD))
        weights = jnp.exp2(fresh - peak).astype(BF16)
        weighted[p] = jnp.dot(weights, vx[:, pair], preferred_element_type=F32)

        def value_step(c, total):
            rows = pl.ds(pl.multiple_of(c * CHUNK, CHUNK), CHUNK)
            s = scores[rows_of, rows]
            pieces = []
            for t in range(CHUNK // HD):
                piece = jnp.exp2(s[:, t * HD : (t + 1) * HD] - peak).astype(BF16)
                total = total + piece.astype(F32)
                pieces.append(piece)
            weighted[p] += jnp.dot(
                jnp.concatenate(pieces, axis=1), v_v[rows, pair], preferred_element_type=F32
            )
            return total

        if p == 0:
            for copy in v_loads:
                copy.wait()
        total = lax.fori_loop(0, lmax // CHUNK, value_step, weights.astype(F32))
        weight_sum = jnp.sum(total, axis=1, keepdims=True)
        for i in range(2):
            rows = slice(i * OWN, (i + 1) * OWN)
            attended = weighted[p, rows, i * HD : (i + 1) * HD] / weight_sum[rows]
            attended = attended.astype(BF16)
            att_send[4 * p + 2 * i] = attended[:PR]
            att_send[4 * p + 2 * i + 1] = attended[PR:]

    odd = lax.rem(y + z, 2)
    slot = lax.rem(lax.div(y, 2) + lax.div(z, 2), 2)

    def send_attended(p):
        for m in range(4):
            peer = 4 * p + lax.rem(f + m, 4)
            landing = att_recv.at[odd, slot, f]

            @pl.when(peer == f)
            def _():
                pltpu.make_async_copy(
                    att_send.at[f], landing, att_rsem.at[odd, slot]
                ).start()

            for k in range(NY):
                chip = lax.rem(z + odd * k, NY) * NY + lax.rem(y + (1 - odd) * k, NY)
                copy = remote(
                    att_send.at[peer], landing, att_ssem.at[k], att_rsem.at[odd, slot],
                    (chip, peer),
                )
                if k == 0:
                    pl.when(peer != f)(copy.start)
                else:
                    copy.start()

    for p in range(PAIRS):
        attend(p)
        send_attended(p)

    for i in range(2 * KV_HEADS):
        ne[0:1, i * HD : (i + 1) * HD] = fresh_rows[i][0:1]
        ne[1:2, i * HD : (i + 1) * HD] = fresh_rows[i][8:9]
    results[PR:, :, :] = ne[0:2, :].reshape(1, STEPS, ne.shape[1]).astype(BF16)

    line_copies = [[], []]
    for part_id in range(2):
        for side in range(2):
            whole = att_recv.at[side, part_id]
            pltpu.make_async_copy(whole, whole, att_rsem.at[side, part_id]).wait()
            pos = (z, y)[side]
            att_f32[...] = att_recv[side, part_id].astype(F32).reshape(NF * PR, HD)
            for j in range(8):
                rows_all[part_id, side, pos, :, j * HD : (j + 1) * HD] = att_f32[
                    pl.ds(j, PR, stride=8), :
                ].astype(BF16)
            mine_rows = rows_all.at[part_id, side, pos]
            for k in range(1, NY):
                q = lax.rem(pos + k, NY)
                device = (q * NY + y, f) if side == 0 else (z * NY + q, f)
                copy = remote(
                    mine_rows, mine_rows,
                    line_ssem.at[part_id, side, k - 1], line_rsem.at[part_id, side, k - 1],
                    device,
                )
                copy.start()
                line_copies[part_id].append(copy)
    wout_load.wait()
    for copy in msg_copies:
        copy.wait_send()
    for k in range(NY):
        sent = att_send.at[pl.ds(0, NF - 1)] if k == 0 else att_send
        pltpu.make_async_copy(sent, sent, att_ssem.at[k]).wait()

    def out_rows(index):
        return pl.ds(pl.multiple_of(index * OWN, OWN), OWN)

    sib_copies = [[], []]
    for part_id in range(2):
        for copy in line_copies[part_id]:
            copy.wait_recv()
        product = jnp.dot(
            rows_all[part_id].reshape(NH * PR // 2, wout_v.shape[0]),
            wout_v[...],
            preferred_element_type=F32,
        )
        for side in range(2):
            for q in range(NY):
                far = 2 * ((part_id + q // 2) % 2) + (q + side) % 2
                home = q * NY + far if side == 0 else far * NY + q
                first = (side * NY + q) * PR
                opart[home * PR : (home + 1) * PR, :] = product[first : first + PR]
        for e in range(2):
            x = 2 * lax.rem(1 + core + part_id, 2) + e
            copy = remote(
                opart.at[out_rows(2 * x + 1 - core)], sib_recv.at[part_id, e],
                sib_ssem.at[part_id, e], sib_rsem.at[part_id, e], (h, sib),
            )
            copy.start()
            sib_copies[part_id].append(copy)
    fin_copies = []
    for part_id in range(2):
        for copy in sib_copies[part_id]:
            copy.wait_recv()
        for e in range(2):
            x = 2 * lax.rem(core + part_id, 2) + e
            hop = lax.rem(x - cx + NX, NX)
            there = lax.rem(hop + NX - 1, NX)
            copy = remote(
                fin_send.at[part_id, e], fin_recv.at[there],
                fin_ssem.at[part_id, e], fin_rsem.at[there], (h, 2 * x + core),
            )
            fin_copies.append((hop, copy))

            @pl.when(hop != 0)
            def _():
                total = opart[out_rows(2 * x + core), :] + sib_recv[part_id, e]
                fin_send[part_id, e] = total.astype(BF16)
                copy.start()

    for copies in sib_copies + line_copies:
        for copy in copies:
            copy.wait_send()
    own_part = lax.rem(core + lax.div(cx, 2), 2)
    result = opart[out_rows(f), :] + sib_recv[own_part, lax.rem(cx, 2)]
    for k in range(1, NX):
        pltpu.make_async_copy(
            fin_recv.at[k - 1], fin_recv.at[k - 1], fin_rsem.at[k - 1]
        ).wait()
        result = result + fin_recv[k - 1].astype(F32)
    results[:PR, :, :] = result.reshape(PR, STEPS, result.shape[1]).astype(BF16)
    for hop, copy in fin_copies:
        pl.when(hop != 0)(copy.wait_send)


def hand_out(results, out, entries, sem):
    rows = out.shape[0]
    copies = [
        pltpu.make_async_copy(results.at[pl.ds(0, rows)], out, sem.at[0]),
        pltpu.make_async_copy(results.at[pl.ds(rows, 1)], entries, sem.at[1]),
    ]
    for copy in copies:
        copy.start()
    for copy in copies:
        copy.wait()


def body(tokens, norm_gain, query_weight, w_keyval, w_out, cache_keys, cache_values, lengths):
    width = tokens.shape[2]
    lmax = cache_keys.shape[1]
    qcols = query_weight.shape[1]
    kvcols = w_keyval.shape[1]
    halves = np.arange(HD // 2, dtype=np.float64) * (2.0 / HD)
    freq = (ROPE_BASE ** (-halves)).astype(np.float32)
    freq = jnp.asarray(np.tile(np.concatenate([freq, freq])[None, :], (PR, 1)))
    any_spec = pl.BlockSpec(memory_space=pl.ANY)
    hbm_spec = pl.BlockSpec(memory_space=pltpu.HBM)
    vmem_spec = pl.BlockSpec(memory_space=pltpu.VMEM)
    dma = pltpu.SemaphoreType.DMA
    rows = NH * PR
    results = pl.pallas_call(
        kernel,
        out_shape=pltpu.VMEM((PR + 1, STEPS, width), BF16),
        in_specs=[hbm_spec] * 9,
        out_specs=vmem_spec,
        scratch_shapes=[
            pltpu.SMEM(lengths.shape, jnp.int32),
            pltpu.VMEM(tokens.shape, BF16),
            pltpu.VMEM((OWN, width), BF16),
            pltpu.VMEM((PR, HD), F32),
            pltpu.VMEM((width,), BF16),
            pltpu.VMEM((width, qcols), BF16),
            pltpu.VMEM((width, kvcols), BF16),
            pltpu.VMEM((qcols, width), BF16),
            pltpu.VMEM((lmax, KV_HEADS * HD), BF16),
            pltpu.VMEM((KV_HEADS * HD, lmax), BF16),
            pltpu.VMEM((lmax, KV_HEADS * HD), BF16),
            pltpu.VMEM((rows, width), BF16),
            pltpu.VMEM((rows // 2, width), BF16),
            pltpu.VMEM((8, HD), F32),
            pltpu.VMEM((NH - 1, 8, HD), F32),
            pltpu.VMEM((NF, 8, HD), F32),
            pltpu.VMEM((NY, NY, PR, qcols + kvcols), F32),
            pltpu.VMEM((2, NY, PR // 2, qcols + kvcols), F32),
            pltpu.VMEM((2, NY, PR // 2, qcols + kvcols), F32),
            pltpu.VMEM((2, NY, PR // 2, qcols + kvcols), F32),
            pltpu.VMEM((2, NY, PR // 2, qcols + kvcols), F32),
            pltpu.VMEM((2, NY - 1, PR // 2, qcols + kvcols), F32),
            pltpu.VMEM((NF * PR, HD), F32),
            pltpu.VMEM((NF, 2 * PR, HD), BF16),
            pltpu.VMEM((NF, 2 * PR, HD), BF16),
            pltpu.VMEM((HD, KV_HEADS * HD), BF16),
            pltpu.VMEM((HD, KV_HEADS * HD), BF16),
            pltpu.VMEM((8, 2 * KV_HEADS * HD), F32),
            pltpu.VMEM((KV_HEADS * OWN, lmax), F32),
            pltpu.VMEM((PAIRS, 2 * OWN, 2 * HD), F32),
            pltpu.VMEM((NF, PR, HD), BF16),
            pltpu.VMEM((2, 2, NF, PR, HD), BF16),
            pltpu.VMEM((NF * PR, HD), F32),
            pltpu.VMEM((2, 2, NY, PR, qcols), BF16),
            pltpu.VMEM((rows, width), F32),
            pltpu.VMEM((2, 2, OWN, width), F32),
            pltpu.VMEM((2, 2, OWN, width), BF16),
            pltpu.VMEM((NX - 1, OWN, width), BF16),
            dma((8,)),
            dma((CACHE_COPIES,)),
            dma((CACHE_COPIES,)),
            dma((NX - 1,)), dma((NX - 1,)),
            dma((NX,)), dma((NX,)),
            dma((NH - 1,)), dma((NH - 1,)),
            dma((NF - 1,)), dma((NF - 1,)),
            dma((2, 2, 6)), dma((2, 2, 6)),
            dma((2, 2, NY - 1)), dma((2, 2, NY - 1)),
            dma((NF - 1,)), dma((NF - 1,)),
            dma((NY,)), dma((2, 2)),
            dma((2, 2, NY - 1)), dma((2, 2, NY - 1)),
            dma((2, 2)), dma((2, 2)),
            dma((2, 2)), dma((NX - 1,)),
        ],
        compiler_params=pltpu.CompilerParams(
            collective_id=0, has_side_effects=True, vmem_limit_bytes=48 * 2**20
        ),
        name="decode_block",
    )(
        *[
            pltpu.with_memory_space_constraint(array, pltpu.HBM)
            for array in (
                lengths, freq, tokens, norm_gain, query_weight, w_keyval, w_out,
                cache_keys, cache_values,
            )
        ],
    )
    return pl.pallas_call(
        hand_out,
        out_shape=(
            jax.ShapeDtypeStruct(tokens.shape, BF16),
            jax.ShapeDtypeStruct((1, STEPS, 2 * KV_HEADS * HD), BF16),
        ),
        in_specs=[vmem_spec],
        out_specs=(any_spec, any_spec),
        scratch_shapes=[dma((2,))],
        name="hand_out",
    )(pltpu.with_memory_space_constraint(results, pltpu.VMEM))


def solution(mesh):
    in_specs = (
        P("ffn", None, "hid"),
        P("hid"),
        P("hid", "ffn"),
        P("hid", "ffn"),
        P("ffn", "hid"),
        P(("hid", "ffn"), None, None),
        P(("hid", "ffn"), None, None),
        P(),
    )
    out_specs = (P("ffn", None, "hid"), P(("hid", "ffn"), None, None))
    return jax.shard_map(body, mesh=mesh, in_specs=in_specs, out_specs=out_specs, check_vma=False)
```

```python
import functools

import jax
import jax.numpy as jnp
import numpy as np
from jax import lax
from jax.experimental import pallas as pl
from jax.experimental.pallas import tpu as pltpu
from jax.sharding import PartitionSpec as P

MESH = pl.DeviceIdType.MESH
F32 = jnp.float32
BF16 = jnp.bfloat16

HEADS = 64
KV_HEADS = 4
HD = 128
STEPS = 2
EPSILON = 1e-05
ROPE_BASE = 500000.0
SCALE = HD ** (-0.5) * 1.4426950408889634
MASKED = -1e30

NH = 16
NF = 8
NX = 4
NY = 4
TURN = 1024
GROUPS = (((0, 256), (256, 256)), ((512, 384), (896, 256)))
OWN = 32
PR = 16
CHUNK = 2048
CACHE_COPIES = 4
PAIRS = KV_HEADS // 2


def remote(src, dst, send_sem, recv_sem, device):
    return pltpu.make_async_remote_copy(
        src_ref=src,
        dst_ref=dst,
        send_sem=send_sem,
        recv_sem=recv_sem,
        device_id=device,
        device_id_type=MESH,
    )


def rotate(vectors, cosine, sine):
    return vectors * cosine + pltpu.roll(vectors, HD // 2, 1) * sine


def kernel(
    lengths_hbm, freq, tokens, gain, wq, wkv, wout, cache_k, cache_v,
    results,
    lengths, raw_v, tok_v, freq_v, gain_v, wq_v, wkv_v, wout_v, k_v, k_t, v_v,
    x_all, normed, ss_own, ss_recv, tot_all, part, relay, left, right, mine, mine_recv,
    spread, msg, qkv, kx, vx, ne, scores, att_send, att_recv, att_f32, rows_all,
    opart, sib_recv, fin_send, fin_recv,
    local_sem, k_sem, v_sem,
    tok_ssem, tok_rsem, fwd_ssem, fwd_rsem, ss_ssem, ss_rsem, tot_ssem, tot_rsem,
    ring_ssem, ring_rsem, stage_ssem, stage_rsem, msg_ssem, msg_rsem, att_ssem, att_rsem, line_ssem, line_rsem,
    sib_ssem, sib_rsem, fin_ssem, fin_rsem,
):
    h = lax.axis_index("hid")
    f = lax.axis_index("ffn")
    z = lax.div(h, NY)
    y = lax.rem(h, NY)
    cx = lax.div(f, 2)
    core = lax.rem(f, 2)
    sib = f + 1 - 2 * core
    lmax = cache_k.shape[1]

    barrier = pltpu.get_barrier_semaphore()
    tokens_load = pltpu.make_async_copy(tokens, raw_v, local_sem.at[0])
    tokens_load.start()

    for k in range(1, NF):
        pl.semaphore_signal(
            barrier, inc=1, device_id=(h, lax.rem(f + k, NF)), device_id_type=MESH
        )
    for k in range(1, NH):
        pl.semaphore_signal(
            barrier, inc=1, device_id=(lax.rem(h + k, NH), f), device_id_type=MESH
        )

    loads = []
    for i, (src, dst) in enumerate(
        [(gain, gain_v), (freq, freq_v), (wq, wq_v), (wkv, wkv_v), (lengths_hbm, lengths)]
    ):
        copy = pltpu.make_async_copy(src, dst, local_sem.at[1 + i])
        copy.start()
        loads.append(copy)
    span = lmax // CACHE_COPIES
    k_loads = []
    for i in range(CACHE_COPIES):
        copy = pltpu.make_async_copy(
            cache_k.at[0, pl.ds(i * span, span)], k_v.at[pl.ds(i * span, span)], k_sem.at[i]
        )
        copy.start()
        k_loads.append(copy)
    wout_load = pltpu.make_async_copy(wout, wout_v, local_sem.at[6])
    wout_load.start()

    def turn_keys(quarter):
        k_loads[quarter].wait()

        def turn(i, carry):
            rows = pl.ds(pl.multiple_of(quarter * span + i * TURN, TURN), TURN)
            k_t[:, rows] = k_v[rows, :].T
            return carry

        lax.fori_loop(0, span // TURN, turn, 0)

    tokens_load.wait()
    x_f32 = raw_v[...].astype(F32).reshape(tok_v.shape)
    x_own = x_f32.astype(BF16)
    tok_v[...] = x_own
    pl.semaphore_wait(barrier, NH + NF - 2)

    def block(index):
        return x_all.at[pl.ds(pl.multiple_of(index * OWN, OWN), OWN)]

    tok_copies = []
    for k in (1, 3, 2):
        peer = 2 * lax.rem(cx + k, NX) + core
        copy = remote(tok_v, block(f), tok_ssem.at[k - 1], tok_rsem.at[k - 1], (h, peer))
        copy.start()
        tok_copies.append((k, copy))
    fwd_copies = [remote(tok_v, block(f), fwd_ssem.at[0], fwd_rsem.at[0], (h, sib))]
    fwd_copies[0].start()

    sums = jnp.sum(x_f32 * x_f32, axis=1, keepdims=True)
    row_id = lax.broadcasted_iota(jnp.int32, (OWN, HD), 0)
    lane_id = lax.broadcasted_iota(jnp.int32, (OWN, HD), 1)
    diagonal = row_id == lane_id
    own_sums = jnp.sum(jnp.where(diagonal, sums, 0.0), axis=0, keepdims=True)
    ss_own[...] = jnp.broadcast_to(own_sums, (8, HD))

    def ss_copy(k):
        return remote(
            ss_own, ss_recv.at[k - 1], ss_ssem.at[k - 1], ss_rsem.at[k - 1],
            (lax.rem(h + k, NH), f),
        )

    for k in range(1, NH):
        ss_copy(k).start()
    x_all[pl.ds(pl.multiple_of(f * OWN, OWN), OWN), :] = x_own

    total = ss_own[...]
    for k in range(1, NH):
        ss_copy(k).wait_recv()
        total = total + ss_recv[k - 1]
    tot_all[f] = total
    tot_copies = []
    for k in range(1, NF):
        copy = remote(
            tot_all.at[f], tot_all.at[f], tot_ssem.at[k - 1], tot_rsem.at[k - 1],
            (h, lax.rem(f + k, NF)),
        )
        copy.start()
        tot_copies.append(copy)
    for k, tok_copy in tok_copies:
        tok_copy.wait_recv()
        came = 2 * lax.rem(cx + NX - k, NX) + core
        copy = remote(block(came), block(came), fwd_ssem.at[k], fwd_rsem.at[k], (h, sib))
        copy.start()
        fwd_copies.append(copy)

    for copy in tot_copies:
        copy.wait_recv()
    loads[0].wait()
    width = x_all.shape[1]
    qcols = wq_v.shape[1]
    full = width * NH
    gain_row = gain_v[...].astype(F32).reshape(1, width)

    def project(parity):
        for x in range(NX):
            b = 2 * x + parity
            lane_sums = tot_all[b][0:1, :]
            row_sums = jnp.sum(jnp.where(diagonal, lane_sums, 0.0), axis=1, keepdims=True)
            inverse = lax.rsqrt(row_sums / full + EPSILON)
            normed[x * OWN : (x + 1) * OWN, :] = (
                block(b)[...].astype(F32) * inverse * gain_row
            ).astype(BF16)
        lhs = normed[...]
        for cols, weights in ((slice(0, qcols), wq_v), (slice(qcols, None), wkv_v)):
            product = jnp.dot(lhs, weights[...], preferred_element_type=F32)
            part[:, pl.ds(2 * parity, 2), :, cols] = product.reshape(NX, 2, PR, product.shape[1])

    loads[2].wait()
    loads[3].wait()
    project(core)

    loads[4].wait()
    length = lengths[h * NF + f]
    step_of = lax.div(lax.broadcasted_iota(jnp.int32, (PR, HD), 0), 8)
    loads[1].wait()
    angles = (step_of + length).astype(F32) * freq_v[...]
    cosine = jnp.cos(angles)
    sine = jnp.sin(angles)
    sine = jnp.where(
        lax.broadcasted_iota(jnp.int32, (PR, HD), 1) < HD // 2, -sine, sine
    )
    kx[...] = jnp.zeros_like(kx)
    vx[...] = jnp.zeros_like(vx)

    for copy in fwd_copies:
        copy.wait_recv()
    project(1 - core)

    half = PR // 2

    def ring(side):
        pos = (y, z)[side]

        def device(q):
            return (z * NY + q, f) if side == 0 else (q * NY + y, f)

        def view(q, cols):
            if side == 0:
                return part.at[:, q, pl.ds(0, half), cols]
            return part.at[q, :, pl.ds(half, half), cols]

        return pos, device, view

    moves = {}
    for g, (low, high) in enumerate(GROUPS):
        for side in range(2):
            pos, device, view = ring(side)
            nxt, prv, far = lax.rem(pos + 1, NY), lax.rem(pos + 3, NY), lax.rem(pos + 2, NY)
            plan = [
                (far, low, relay, nxt),
                (far, high, relay, prv),
                (nxt, high, left, nxt),
                (prv, low, right, prv),
            ]
            moves[g, side] = [
                remote(
                    view(q, pl.ds(*cols)), dst.at[side, :, :, pl.ds(*cols)],
                    ring_ssem.at[g, side, i], ring_rsem.at[g, side, i], device(to),
                )
                for i, (q, cols, dst, to) in enumerate(plan)
            ]
    for first in (0, 2):
        for g in range(len(GROUPS)):
            for side in range(2):
                for copy in moves[g, side][first : first + 2]:
                    copy.start()
    v_loads = []
    for i in range(CACHE_COPIES):
        copy = pltpu.make_async_copy(
            cache_v.at[0, pl.ds(i * span, span)], v_v.at[pl.ds(i * span, span)], v_sem.at[i]
        )
        copy.start()
        v_loads.append(copy)

    for k in range(1, NH):
        ss_copy(k).wait_send()
    for copy in tot_copies + fwd_copies + [copy for _, copy in tok_copies]:
        copy.wait_send()
    turn_keys(0)
    for g, (low, high) in enumerate(GROUPS):
        for side in range(2):
            pos, device, view = ring(side)
            nxt, prv = lax.rem(pos + 1, NY), lax.rem(pos + 3, NY)
            for i, (to, cols, dst) in enumerate(((nxt, low, left), (prv, high, right))):
                cols = pl.ds(*cols)
                moves[g, side][i].wait_recv()
                passed = relay.at[side, :, :, cols]
                passed[...] = passed[...] + view(to, cols)[...]
                copy = remote(
                    passed, dst.at[side, :, :, cols],
                    ring_ssem.at[g, side, 4 + i], ring_rsem.at[g, side, 4 + i], device(to),
                )
                copy.start()
                moves[g, side].append(copy)
    turn_keys(1)
    stages = {}
    for g, (low, high) in enumerate(GROUPS):
        cols = pl.ds(low[0], low[1] + high[1])
        for side in range(2):
            pos, device, view = ring(side)
            for copy in moves[g, side][2:]:
                copy.wait_recv()
            mine[side, :, :, cols] = (
                view(pos, cols)[...] + left[side, :, :, cols] + right[side, :, :, cols]
            )
            other, other_device, _ = ring(1 - side)
            stages[g, side] = []
            for k in (1, 3, 2):
                peer = lax.rem(other + k, NY)
                copy = remote(
                    mine.at[side, peer, :, cols], mine_recv.at[side, k - 1, :, cols],
                    stage_ssem.at[g, side, k - 1], stage_rsem.at[g, side, k - 1],
                    other_device(peer),
                )
                copy.start()
                stages[g, side].append(copy)
    turn_keys(2)
    groups = []
    for g, (low, high) in enumerate(GROUPS):
        cols = pl.ds(low[0], low[1] + high[1])
        halves = []
        for side in range(2):
            other = ring(1 - side)[0]
            total = mine[side, other, :, cols]
            for copy in stages[g, side]:
                copy.wait_recv()
            for k in range(NY - 1):
                total = total + mine_recv[side, k, :, cols]
            halves.append(total)
        groups.append(jnp.concatenate(halves, axis=0))
    summed = jnp.concatenate(groups, axis=1)

    for j in range(8):
        spread[pl.ds(j, PR, stride=8), :] = summed[:, j * HD : (j + 1) * HD]
    msg[:, :PR, :] = spread[...].reshape(NF, PR, HD).astype(BF16)
    spread[...] = jnp.zeros_like(spread)
    spread[pl.ds(0, PR, stride=8), :] = summed[:, qcols:]
    msg[:, PR:, :] = spread[...].reshape(NF, PR, HD).astype(BF16)
    qkv[f] = msg[f]
    msg_copies = []
    for k in range(1, NF):
        peer = lax.rem(f + k, NF)
        copy = remote(
            msg.at[peer], qkv.at[f], msg_ssem.at[k - 1], msg_rsem.at[k - 1], (h, peer)
        )
        copy.start()
        msg_copies.append(copy)
    for key in moves:
        for copy in moves[key] + stages[key]:
            copy.wait_send()
    turn_keys(3)
    for copy in msg_copies:
        copy.wait_recv()

    fresh_rows = []
    for i in range(2 * KV_HEADS):
        raw = qkv[i, PR:, :].astype(F32)
        cols = pl.ds((i % KV_HEADS) * HD, HD)
        if i < KV_HEADS:
            raw = rotate(raw, cosine, sine)
            kx[:PR, cols] = raw.astype(BF16)
        else:
            vx[:PR, cols] = raw.astype(BF16)
        fresh_rows.append(raw)

    rotated = [
        rotate(qkv[i, :PR, :].astype(F32), cosine, sine).astype(BF16) for i in range(NF)
    ]
    nothing = jnp.zeros((OWN, HD), BF16)
    queries = []
    for p in range(PAIRS):
        upper = jnp.concatenate(rotated[4 * p : 4 * p + 2], axis=0)
        lower = jnp.concatenate(rotated[4 * p + 2 : 4 * p + 4], axis=0)
        queries.append(
            jnp.concatenate(
                [
                    jnp.concatenate([upper, nothing], axis=1),
                    jnp.concatenate([nothing, lower], axis=1),
                ],
                axis=0,
            )
        )
    pair_rows, pair_cols = 2 * OWN, 2 * HD
    lane = lax.broadcasted_iota(jnp.int32, (pair_rows, HD), 1)
    step_row = lax.rem(lax.div(lax.broadcasted_iota(jnp.int32, (pair_rows, HD), 0), 8), 2)
    fresh_live = (lane == 0) | ((lane == 8) & (step_row == 1))
    nt = (((1,), (1,)), ((), ()))
    for copy in v_loads:
        copy.wait()

    def score(p):
        pair = pl.ds(p * pair_cols, pair_cols)
        fresh = lax.dot_general(queries[p], kx[:, pair], nt, preferred_element_type=F32)
        fresh = jnp.where(fresh_live, fresh * SCALE, MASKED)
        high = fresh
        for c in range(lmax // CHUNK):
            rows = pl.ds(c * CHUNK, CHUNK)
            s = jnp.dot(queries[p], k_t[pair, rows], preferred_element_type=F32) * SCALE
            if (c + 1) * CHUNK > lmax // 4:
                position = lax.broadcasted_iota(jnp.int32, (8, CHUNK), 1) + c * CHUNK
                cap = jnp.where(position < length, -MASKED, MASKED)
                s = jnp.minimum(s, jnp.concatenate([cap] * (pair_rows // 8), axis=0))
            scores[pl.ds(p * pair_rows, pair_rows), rows] = s
            for t in range(CHUNK // HD):
                high = jnp.maximum(high, s[:, t * HD : (t + 1) * HD])
        peak = jnp.broadcast_to(jnp.max(high, axis=1, keepdims=True), (pair_rows, HD))
        return fresh, peak

    def attend(p, fresh, peak):
        pair = pl.ds(p * pair_cols, pair_cols)
        weights = jnp.exp2(fresh - peak).astype(BF16)
        total = weights.astype(F32)
        acc = jnp.dot(weights, vx[:, pair], preferred_element_type=F32)
        for c in range(lmax // CHUNK):
            rows = pl.ds(c * CHUNK, CHUNK)
            s = scores[pl.ds(p * pair_rows, pair_rows), rows]
            pieces = []
            for t in range(CHUNK // HD):
                piece = jnp.exp2(s[:, t * HD : (t + 1) * HD] - peak).astype(BF16)
                total = total + piece.astype(F32)
                pieces.append(piece)
            acc = acc + jnp.dot(
                jnp.concatenate(pieces, axis=1), v_v[rows, pair], preferred_element_type=F32
            )
        weight_sum = jnp.sum(total, axis=1, keepdims=True)
        for i in range(2):
            rows = slice(i * OWN, (i + 1) * OWN)
            attended = acc[rows, i * HD : (i + 1) * HD] / weight_sum[rows]
            attended = attended.astype(BF16)
            att_send[4 * p + 2 * i] = attended[:PR]
            att_send[4 * p + 2 * i + 1] = attended[PR:]

    odd = lax.rem(y + z, 2)
    slot = lax.rem(lax.div(y, 2) + lax.div(z, 2), 2)

    def send_attended(p):
        for m in range(4):
            peer = 4 * p + lax.rem(f + m, 4)
            landing = att_recv.at[odd, slot, f]

            @pl.when(peer == f)
            def _():
                pltpu.make_async_copy(
                    att_send.at[f], landing, att_rsem.at[odd, slot]
                ).start()

            for k in range(NY):
                chip = lax.rem(z + odd * k, NY) * NY + lax.rem(y + (1 - odd) * k, NY)
                copy = remote(
                    att_send.at[peer], landing, att_ssem.at[k], att_rsem.at[odd, slot],
                    (chip, peer),
                )
                if k == 0:
                    pl.when(peer != f)(copy.start)
                else:
                    copy.start()

    scored = [score(p) for p in range(PAIRS)]
    for p in range(PAIRS):
        attend(p, *scored[p])
        send_attended(p)

    for i in range(2 * KV_HEADS):
        ne[0:1, i * HD : (i + 1) * HD] = fresh_rows[i][0:1]
        ne[1:2, i * HD : (i + 1) * HD] = fresh_rows[i][8:9]
    results[PR:, :, :] = ne[0:2, :].reshape(1, STEPS, ne.shape[1]).astype(BF16)

    line_copies = [[], []]
    for part_id in range(2):
        for side in range(2):
            whole = att_recv.at[side, part_id]
            pltpu.make_async_copy(whole, whole, att_rsem.at[side, part_id]).wait()
            pos = (z, y)[side]
            att_f32[...] = att_recv[side, part_id].astype(F32).reshape(NF * PR, HD)
            for j in range(8):
                rows_all[part_id, side, pos, :, j * HD : (j + 1) * HD] = att_f32[
                    pl.ds(j, PR, stride=8), :
                ].astype(BF16)
            mine_rows = rows_all.at[part_id, side, pos]
            for k in range(1, NY):
                q = lax.rem(pos + k, NY)
                device = (q * NY + y, f) if side == 0 else (z * NY + q, f)
                copy = remote(
                    mine_rows, mine_rows,
                    line_ssem.at[part_id, side, k - 1], line_rsem.at[part_id, side, k - 1],
                    device,
                )
                copy.start()
                line_copies[part_id].append(copy)
    wout_load.wait()
    for copy in msg_copies:
        copy.wait_send()
    for k in range(NY):
        sent = att_send.at[pl.ds(0, NF - 1)] if k == 0 else att_send
        pltpu.make_async_copy(sent, sent, att_ssem.at[k]).wait()

    def out_rows(index):
        return pl.ds(pl.multiple_of(index * OWN, OWN), OWN)

    sib_copies = [[], []]
    for part_id in range(2):
        for copy in line_copies[part_id]:
            copy.wait_recv()
        product = jnp.dot(
            rows_all[part_id].reshape(NH * PR // 2, wout_v.shape[0]),
            wout_v[...],
            preferred_element_type=F32,
        )
        for side in range(2):
            for q in range(NY):
                far = 2 * ((part_id + q // 2) % 2) + (q + side) % 2
                home = q * NY + far if side == 0 else far * NY + q
                first = (side * NY + q) * PR
                opart[home * PR : (home + 1) * PR, :] = product[first : first + PR]
        for e in range(2):
            x = 2 * lax.rem(1 + core + part_id, 2) + e
            copy = remote(
                opart.at[out_rows(2 * x + 1 - core)], sib_recv.at[part_id, e],
                sib_ssem.at[part_id, e], sib_rsem.at[part_id, e], (h, sib),
            )
            copy.start()
            sib_copies[part_id].append(copy)
    fin_copies = []
    for part_id in range(2):
        for copy in sib_copies[part_id]:
            copy.wait_recv()
        for e in range(2):
            x = 2 * lax.rem(core + part_id, 2) + e
            hop = lax.rem(x - cx + NX, NX)
            there = lax.rem(hop + NX - 1, NX)
            copy = remote(
                fin_send.at[part_id, e], fin_recv.at[there],
                fin_ssem.at[part_id, e], fin_rsem.at[there], (h, 2 * x + core),
            )
            fin_copies.append((hop, copy))

            @pl.when(hop != 0)
            def _():
                total = opart[out_rows(2 * x + core), :] + sib_recv[part_id, e]
                fin_send[part_id, e] = total.astype(BF16)
                copy.start()

    for copies in sib_copies + line_copies:
        for copy in copies:
            copy.wait_send()
    own_part = lax.rem(core + lax.div(cx, 2), 2)
    result = opart[out_rows(f), :] + sib_recv[own_part, lax.rem(cx, 2)]
    for k in range(1, NX):
        pltpu.make_async_copy(
            fin_recv.at[k - 1], fin_recv.at[k - 1], fin_rsem.at[k - 1]
        ).wait()
        result = result + fin_recv[k - 1].astype(F32)
    results[:PR, :, :] = result.reshape(PR, STEPS, result.shape[1]).astype(BF16)
    for hop, copy in fin_copies:
        pl.when(hop != 0)(copy.wait_send)


def hand_out(results, out, entries, sem):
    rows = out.shape[0]
    copies = [
        pltpu.make_async_copy(results.at[pl.ds(0, rows)], out, sem.at[0]),
        pltpu.make_async_copy(results.at[pl.ds(rows, 1)], entries, sem.at[1]),
    ]
    for copy in copies:
        copy.start()
    for copy in copies:
        copy.wait()


def body(tokens, norm_gain, query_weight, w_keyval, w_out, cache_keys, cache_values, lengths):
    width = tokens.shape[2]
    lmax = cache_keys.shape[1]
    qcols = query_weight.shape[1]
    kvcols = w_keyval.shape[1]
    halves = np.arange(HD // 2, dtype=np.float64) * (2.0 / HD)
    freq = (ROPE_BASE ** (-halves)).astype(np.float32)
    freq = jnp.asarray(np.tile(np.concatenate([freq, freq])[None, :], (PR, 1)))
    any_spec = pl.BlockSpec(memory_space=pl.ANY)
    hbm_spec = pl.BlockSpec(memory_space=pltpu.HBM)
    vmem_spec = pl.BlockSpec(memory_space=pltpu.VMEM)
    dma = pltpu.SemaphoreType.DMA
    rows = NH * PR
    results = pl.pallas_call(
        kernel,
        out_shape=pltpu.VMEM((PR + 1, STEPS, width), BF16),
        in_specs=[hbm_spec] * 9,
        out_specs=vmem_spec,
        scratch_shapes=[
            pltpu.SMEM(lengths.shape, jnp.int32),
            pltpu.VMEM(tokens.shape, BF16),
            pltpu.VMEM((OWN, width), BF16),
            pltpu.VMEM((PR, HD), F32),
            pltpu.VMEM((width,), BF16),
            pltpu.VMEM((width, qcols), BF16),
            pltpu.VMEM((width, kvcols), BF16),
            pltpu.VMEM((qcols, width), BF16),
            pltpu.VMEM((lmax, KV_HEADS * HD), BF16),
            pltpu.VMEM((KV_HEADS * HD, lmax), BF16),
            pltpu.VMEM((lmax, KV_HEADS * HD), BF16),
            pltpu.VMEM((rows, width), BF16),
            pltpu.VMEM((rows // 2, width), BF16),
            pltpu.VMEM((8, HD), F32),
            pltpu.VMEM((NH - 1, 8, HD), F32),
            pltpu.VMEM((NF, 8, HD), F32),
            pltpu.VMEM((NY, NY, PR, qcols + kvcols), F32),
            pltpu.VMEM((2, NY, PR // 2, qcols + kvcols), F32),
            pltpu.VMEM((2, NY, PR // 2, qcols + kvcols), F32),
            pltpu.VMEM((2, NY, PR // 2, qcols + kvcols), F32),
            pltpu.VMEM((2, NY, PR // 2, qcols + kvcols), F32),
            pltpu.VMEM((2, NY - 1, PR // 2, qcols + kvcols), F32),
            pltpu.VMEM((NF * PR, HD), F32),
            pltpu.VMEM((NF, 2 * PR, HD), BF16),
            pltpu.VMEM((NF, 2 * PR, HD), BF16),
            pltpu.VMEM((HD, KV_HEADS * HD), BF16),
            pltpu.VMEM((HD, KV_HEADS * HD), BF16),
            pltpu.VMEM((8, 2 * KV_HEADS * HD), F32),
            pltpu.VMEM((KV_HEADS * OWN, lmax), F32),
            pltpu.VMEM((NF, PR, HD), BF16),
            pltpu.VMEM((2, 2, NF, PR, HD), BF16),
            pltpu.VMEM((NF * PR, HD), F32),
            pltpu.VMEM((2, 2, NY, PR, qcols), BF16),
            pltpu.VMEM((rows, width), F32),
            pltpu.VMEM((2, 2, OWN, width), F32),
            pltpu.VMEM((2, 2, OWN, width), BF16),
            pltpu.VMEM((NX - 1, OWN, width), BF16),
            dma((8,)),
            dma((CACHE_COPIES,)),
            dma((CACHE_COPIES,)),
            dma((NX - 1,)), dma((NX - 1,)),
            dma((NX,)), dma((NX,)),
            dma((NH - 1,)), dma((NH - 1,)),
            dma((NF - 1,)), dma((NF - 1,)),
            dma((2, 2, 6)), dma((2, 2, 6)),
            dma((2, 2, NY - 1)), dma((2, 2, NY - 1)),
            dma((NF - 1,)), dma((NF - 1,)),
            dma((NY,)), dma((2, 2)),
            dma((2, 2, NY - 1)), dma((2, 2, NY - 1)),
            dma((2, 2)), dma((2, 2)),
            dma((2, 2)), dma((NX - 1,)),
        ],
        compiler_params=pltpu.CompilerParams(
            collective_id=0, has_side_effects=True, vmem_limit_bytes=48 * 2**20
        ),
        name="decode_block",
    )(
        *[
            pltpu.with_memory_space_constraint(array, pltpu.HBM)
            for array in (
                lengths, freq, tokens, norm_gain, query_weight, w_keyval, w_out,
                cache_keys, cache_values,
            )
        ],
    )
    return pl.pallas_call(
        hand_out,
        out_shape=(
            jax.ShapeDtypeStruct(tokens.shape, BF16),
            jax.ShapeDtypeStruct((1, STEPS, 2 * KV_HEADS * HD), BF16),
        ),
        in_specs=[vmem_spec],
        out_specs=(any_spec, any_spec),
        scratch_shapes=[dma((2,))],
        name="hand_out",
    )(pltpu.with_memory_space_constraint(results, pltpu.VMEM))


def solution(mesh):
    in_specs = (
        P("ffn", None, "hid"),
        P("hid"),
        P("hid", "ffn"),
        P("hid", "ffn"),
        P("ffn", "hid"),
        P(("hid", "ffn"), None, None),
        P(("hid", "ffn"), None, None),
        P(),
    )
    out_specs = (P("ffn", None, "hid"), P(("hid", "ffn"), None, None))
    return jax.shard_map(body, mesh=mesh, in_specs=in_specs, out_specs=out_specs, check_vma=False)
```

```python
import functools

import jax
import jax.numpy as jnp
import numpy as np
from jax import lax
from jax.experimental import pallas as pl
from jax.experimental.pallas import tpu as pltpu
from jax.sharding import PartitionSpec as P

MESH = pl.DeviceIdType.MESH
F32 = jnp.float32
BF16 = jnp.bfloat16

HEADS = 64
KV_HEADS = 4
HD = 128
STEPS = 2
EPSILON = 1e-05
ROPE_BASE = 500000.0
SCALE = HD ** (-0.5) * 1.4426950408889634
MASKED = -1e30

NH = 16
NF = 8
NX = 4
NY = 4
TURN = 1024
GROUPS = (((0, 256), (256, 256)), ((512, 384), (896, 256)))
OWN = 32
PR = 16
CHUNK = 2048
CACHE_COPIES = 4
PAIRS = KV_HEADS // 2


def remote(src, dst, send_sem, recv_sem, device):
    return pltpu.make_async_remote_copy(
        src_ref=src,
        dst_ref=dst,
        send_sem=send_sem,
        recv_sem=recv_sem,
        device_id=device,
        device_id_type=MESH,
    )


def rotate(vectors, cosine, sine):
    return vectors * cosine + pltpu.roll(vectors, HD // 2, 1) * sine


def kernel(
    lengths_hbm, freq, tokens, gain, wq, wkv, wout, cache_k, cache_v,
    results,
    lengths, raw_v, tok_v, freq_v, gain_v, wq_v, wkv_v, wout_v, k_v, k_t, v_v,
    x_all, normed, ss_own, ss_recv, tot_all, part, relay, left, right, mine, mine_recv,
    spread, msg, qkv, kx, vx, ne, scores, att_send, att_recv, att_f32, rows_all,
    opart, fin_send, fin_recv,
    local_sem, k_sem, v_sem,
    tok_ssem, tok_rsem, fwd_ssem, fwd_rsem, ss_ssem, ss_rsem, tot_ssem, tot_rsem,
    ring_ssem, ring_rsem, stage_ssem, stage_rsem, msg_ssem, msg_rsem, att_ssem, att_rsem, line_ssem, line_rsem,
    fin_ssem, fin_rsem,
):
    h = lax.axis_index("hid")
    f = lax.axis_index("ffn")
    z = lax.div(h, NY)
    y = lax.rem(h, NY)
    cx = lax.div(f, 2)
    core = lax.rem(f, 2)
    sib = f + 1 - 2 * core
    lmax = cache_k.shape[1]

    barrier = pltpu.get_barrier_semaphore()
    tokens_load = pltpu.make_async_copy(tokens, raw_v, local_sem.at[0])
    tokens_load.start()

    for k in range(1, NF):
        pl.semaphore_signal(
            barrier, inc=1, device_id=(h, lax.rem(f + k, NF)), device_id_type=MESH
        )
    for k in range(1, NH):
        pl.semaphore_signal(
            barrier, inc=1, device_id=(lax.rem(h + k, NH), f), device_id_type=MESH
        )

    loads = []
    for i, (src, dst) in enumerate(
        [(gain, gain_v), (freq, freq_v), (wq, wq_v), (wkv, wkv_v), (lengths_hbm, lengths)]
    ):
        copy = pltpu.make_async_copy(src, dst, local_sem.at[1 + i])
        copy.start()
        loads.append(copy)
    span = lmax // CACHE_COPIES
    k_loads = []
    for i in range(CACHE_COPIES):
        copy = pltpu.make_async_copy(
            cache_k.at[0, pl.ds(i * span, span)], k_v.at[pl.ds(i * span, span)], k_sem.at[i]
        )
        copy.start()
        k_loads.append(copy)
    wout_load = pltpu.make_async_copy(wout, wout_v, local_sem.at[6])
    wout_load.start()

    def turn_keys(quarter):
        k_loads[quarter].wait()

        def turn(i, carry):
            rows = pl.ds(pl.multiple_of(quarter * span + i * TURN, TURN), TURN)
            k_t[:, rows] = k_v[rows, :].T
            return carry

        lax.fori_loop(0, span // TURN, turn, 0)

    tokens_load.wait()
    x_f32 = raw_v[...].astype(F32).reshape(tok_v.shape)
    x_own = x_f32.astype(BF16)
    tok_v[...] = x_own
    pl.semaphore_wait(barrier, NH + NF - 2)

    def block(index):
        return x_all.at[pl.ds(pl.multiple_of(index * OWN, OWN), OWN)]

    tok_copies = []
    for k in (1, 3, 2):
        peer = 2 * lax.rem(cx + k, NX) + core
        copy = remote(tok_v, block(f), tok_ssem.at[k - 1], tok_rsem.at[k - 1], (h, peer))
        copy.start()
        tok_copies.append((k, copy))
    opposite = 2 * lax.rem(cx + 2, NX) + 1 - core
    fwd_copies = [
        remote(tok_v, block(f), fwd_ssem.at[0], fwd_rsem.at[0], (h, sib)),
        remote(tok_v, block(f), fwd_ssem.at[2], fwd_rsem.at[2], (h, opposite)),
    ]
    for copy in fwd_copies:
        copy.start()

    sums = jnp.sum(x_f32 * x_f32, axis=1, keepdims=True)
    row_id = lax.broadcasted_iota(jnp.int32, (OWN, HD), 0)
    lane_id = lax.broadcasted_iota(jnp.int32, (OWN, HD), 1)
    diagonal = row_id == lane_id
    own_sums = jnp.sum(jnp.where(diagonal, sums, 0.0), axis=0, keepdims=True)
    ss_own[...] = jnp.broadcast_to(own_sums, (8, HD))

    def ss_copy(k):
        return remote(
            ss_own, ss_recv.at[k - 1], ss_ssem.at[k - 1], ss_rsem.at[k - 1],
            (lax.rem(h + k, NH), f),
        )

    for k in range(1, NH):
        ss_copy(k).start()
    x_all[pl.ds(pl.multiple_of(f * OWN, OWN), OWN), :] = x_own

    total = ss_own[...]
    for k in range(1, NH):
        ss_copy(k).wait_recv()
        total = total + ss_recv[k - 1]
    tot_all[f] = total
    tot_copies = []
    for k in range(1, NF):
        copy = remote(
            tot_all.at[f], tot_all.at[f], tot_ssem.at[k - 1], tot_rsem.at[k - 1],
            (h, lax.rem(f + k, NF)),
        )
        copy.start()
        tot_copies.append(copy)
    for k, tok_copy in tok_copies:
        tok_copy.wait_recv()
        if k != 2:
            came = 2 * lax.rem(cx + NX - k, NX) + core
            copy = remote(block(came), block(came), fwd_ssem.at[k], fwd_rsem.at[k], (h, sib))
            copy.start()
            fwd_copies.append(copy)

    for copy in tot_copies:
        copy.wait_recv()
    loads[0].wait()
    width = x_all.shape[1]
    qcols = wq_v.shape[1]
    full = width * NH
    gain_row = gain_v[...].astype(F32).reshape(1, width)

    def project(parity):
        for x in range(NX):
            b = 2 * x + parity
            lane_sums = tot_all[b][0:1, :]
            row_sums = jnp.sum(jnp.where(diagonal, lane_sums, 0.0), axis=1, keepdims=True)
            inverse = lax.rsqrt(row_sums / full + EPSILON)
            normed[x * OWN : (x + 1) * OWN, :] = (
                block(b)[...].astype(F32) * inverse * gain_row
            ).astype(BF16)
        lhs = normed[...]
        for cols, weights in ((slice(0, qcols), wq_v), (slice(qcols, None), wkv_v)):
            product = jnp.dot(lhs, weights[...], preferred_element_type=F32)
            part[:, pl.ds(2 * parity, 2), :, cols] = product.reshape(NX, 2, PR, product.shape[1])

    loads[2].wait()
    loads[3].wait()
    project(core)

    loads[4].wait()
    length = lengths[h * NF + f]
    step_of = lax.div(lax.broadcasted_iota(jnp.int32, (PR, HD), 0), 8)
    loads[1].wait()
    angles = (step_of + length).astype(F32) * freq_v[...]
    cosine = jnp.cos(angles)
    sine = jnp.sin(angles)
    sine = jnp.where(
        lax.broadcasted_iota(jnp.int32, (PR, HD), 1) < HD // 2, -sine, sine
    )
    kx[...] = jnp.zeros_like(kx)
    vx[...] = jnp.zeros_like(vx)

    for copy in fwd_copies:
        copy.wait_recv()
    project(1 - core)

    half = PR // 2

    def ring(side):
        pos = (y, z)[side]

        def device(q):
            return (z * NY + q, f) if side == 0 else (q * NY + y, f)

        def view(q, cols):
            if side == 0:
                return part.at[:, q, pl.ds(0, half), cols]
            return part.at[q, :, pl.ds(half, half), cols]

        return pos, device, view

    moves = {}
    for g, (low, high) in enumerate(GROUPS):
        for side in range(2):
            pos, device, view = ring(side)
            nxt, prv, far = lax.rem(pos + 1, NY), lax.rem(pos + 3, NY), lax.rem(pos + 2, NY)
            plan = [
                (far, low, relay, nxt),
                (far, high, relay, prv),
                (nxt, high, left, nxt),
                (prv, low, right, prv),
            ]
            moves[g, side] = [
                remote(
                    view(q, pl.ds(*cols)), dst.at[side, :, :, pl.ds(*cols)],
                    ring_ssem.at[g, side, i], ring_rsem.at[g, side, i], device(to),
                )
                for i, (q, cols, dst, to) in enumerate(plan)
            ]
    for first in (0, 2):
        for g in range(len(GROUPS)):
            for side in range(2):
                for copy in moves[g, side][first : first + 2]:
                    copy.start()
    v_loads = []
    for i in range(CACHE_COPIES):
        copy = pltpu.make_async_copy(
            cache_v.at[0, pl.ds(i * span, span)], v_v.at[pl.ds(i * span, span)], v_sem.at[i]
        )
        copy.start()
        v_loads.append(copy)

    for k in range(1, NH):
        ss_copy(k).wait_send()
    for copy in tot_copies + fwd_copies + [copy for _, copy in tok_copies]:
        copy.wait_send()
    turn_keys(0)
    for g, (low, high) in enumerate(GROUPS):
        for side in range(2):
            pos, device, view = ring(side)
            nxt, prv = lax.rem(pos + 1, NY), lax.rem(pos + 3, NY)
            for i, (to, cols, dst) in enumerate(((nxt, low, left), (prv, high, right))):
                cols = pl.ds(*cols)
                moves[g, side][i].wait_recv()
                passed = relay.at[side, :, :, cols]
                passed[...] = passed[...] + view(to, cols)[...]
                copy = remote(
                    passed, dst.at[side, :, :, cols],
                    ring_ssem.at[g, side, 4 + i], ring_rsem.at[g, side, 4 + i], device(to),
                )
                copy.start()
                moves[g, side].append(copy)
    turn_keys(1)
    stages = {}
    for g, (low, high) in enumerate(GROUPS):
        cols = pl.ds(low[0], low[1] + high[1])
        for side in range(2):
            pos, device, view = ring(side)
            for copy in moves[g, side][2:]:
                copy.wait_recv()
            mine[side, :, :, cols] = (
                view(pos, cols)[...] + left[side, :, :, cols] + right[side, :, :, cols]
            )
            other, other_device, _ = ring(1 - side)
            stages[g, side] = []
            for k in (1, 3, 2):
                peer = lax.rem(other + k, NY)
                copy = remote(
                    mine.at[side, peer, :, cols], mine_recv.at[side, k - 1, :, cols],
                    stage_ssem.at[g, side, k - 1], stage_rsem.at[g, side, k - 1],
                    other_device(peer),
                )
                copy.start()
                stages[g, side].append(copy)
    turn_keys(2)
    groups = []
    for g, (low, high) in enumerate(GROUPS):
        cols = pl.ds(low[0], low[1] + high[1])
        halves = []
        for side in range(2):
            other = ring(1 - side)[0]
            total = mine[side, other, :, cols]
            for copy in stages[g, side]:
                copy.wait_recv()
            for k in range(NY - 1):
                total = total + mine_recv[side, k, :, cols]
            halves.append(total)
        groups.append(jnp.concatenate(halves, axis=0))
    summed = jnp.concatenate(groups, axis=1)

    for j in range(8):
        spread[pl.ds(j, PR, stride=8), :] = summed[:, j * HD : (j + 1) * HD]
    msg[:, :PR, :] = spread[...].reshape(NF, PR, HD).astype(BF16)
    spread[...] = jnp.zeros_like(spread)
    spread[pl.ds(0, PR, stride=8), :] = summed[:, qcols:]
    msg[:, PR:, :] = spread[...].reshape(NF, PR, HD).astype(BF16)
    qkv[f] = msg[f]
    msg_copies = []
    for k in range(1, NF):
        peer = lax.rem(f + k, NF)
        copy = remote(
            msg.at[peer], qkv.at[f], msg_ssem.at[k - 1], msg_rsem.at[k - 1], (h, peer)
        )
        copy.start()
        msg_copies.append(copy)
    for key in moves:
        for copy in moves[key] + stages[key]:
            copy.wait_send()
    turn_keys(3)
    for copy in msg_copies:
        copy.wait_recv()

    fresh_rows = []
    for i in range(2 * KV_HEADS):
        raw = qkv[i, PR:, :].astype(F32)
        cols = pl.ds((i % KV_HEADS) * HD, HD)
        if i < KV_HEADS:
            raw = rotate(raw, cosine, sine)
            kx[:PR, cols] = raw.astype(BF16)
        else:
            vx[:PR, cols] = raw.astype(BF16)
        fresh_rows.append(raw)

    rotated = [
        rotate(qkv[i, :PR, :].astype(F32), cosine, sine).astype(BF16) for i in range(NF)
    ]
    nothing = jnp.zeros((OWN, HD), BF16)
    queries = []
    for p in range(PAIRS):
        upper = jnp.concatenate(rotated[4 * p : 4 * p + 2], axis=0)
        lower = jnp.concatenate(rotated[4 * p + 2 : 4 * p + 4], axis=0)
        queries.append(
            jnp.concatenate(
                [
                    jnp.concatenate([upper, nothing], axis=1),
                    jnp.concatenate([nothing, lower], axis=1),
                ],
                axis=0,
            )
        )
    pair_rows, pair_cols = 2 * OWN, 2 * HD
    lane = lax.broadcasted_iota(jnp.int32, (pair_rows, HD), 1)
    step_row = lax.rem(lax.div(lax.broadcasted_iota(jnp.int32, (pair_rows, HD), 0), 8), 2)
    fresh_live = (lane == 0) | ((lane == 8) & (step_row == 1))
    nt = (((1,), (1,)), ((), ()))
    for copy in v_loads:
        copy.wait()

    def score(p):
        pair = pl.ds(p * pair_cols, pair_cols)
        fresh = lax.dot_general(queries[p], kx[:, pair], nt, preferred_element_type=F32)
        fresh = jnp.where(fresh_live, fresh * SCALE, MASKED)
        high = fresh
        for c in range(lmax // CHUNK):
            rows = pl.ds(c * CHUNK, CHUNK)
            s = jnp.dot(queries[p], k_t[pair, rows], preferred_element_type=F32) * SCALE
            if (c + 1) * CHUNK > lmax // 4:
                position = lax.broadcasted_iota(jnp.int32, (8, CHUNK), 1) + c * CHUNK
                cap = jnp.where(position < length, -MASKED, MASKED)
                s = jnp.minimum(s, jnp.concatenate([cap] * (pair_rows // 8), axis=0))
            scores[pl.ds(p * pair_rows, pair_rows), rows] = s
            for t in range(CHUNK // HD):
                high = jnp.maximum(high, s[:, t * HD : (t + 1) * HD])
        peak = jnp.broadcast_to(jnp.max(high, axis=1, keepdims=True), (pair_rows, HD))
        return fresh, peak

    def attend(p, fresh, peak):
        pair = pl.ds(p * pair_cols, pair_cols)
        weights = jnp.exp2(fresh - peak).astype(BF16)
        total = weights.astype(F32)
        acc = jnp.dot(weights, vx[:, pair], preferred_element_type=F32)
        for c in range(lmax // CHUNK):
            rows = pl.ds(c * CHUNK, CHUNK)
            s = scores[pl.ds(p * pair_rows, pair_rows), rows]
            pieces = []
            for t in range(CHUNK // HD):
                piece = jnp.exp2(s[:, t * HD : (t + 1) * HD] - peak).astype(BF16)
                total = total + piece.astype(F32)
                pieces.append(piece)
            acc = acc + jnp.dot(
                jnp.concatenate(pieces, axis=1), v_v[rows, pair], preferred_element_type=F32
            )
        weight_sum = jnp.sum(total, axis=1, keepdims=True)
        for i in range(2):
            rows = slice(i * OWN, (i + 1) * OWN)
            attended = acc[rows, i * HD : (i + 1) * HD] / weight_sum[rows]
            attended = attended.astype(BF16)
            att_send[4 * p + 2 * i] = attended[:PR]
            att_send[4 * p + 2 * i + 1] = attended[PR:]

    odd = lax.rem(y + z, 2)
    slot = lax.rem(lax.div(y, 2) + lax.div(z, 2), 2)

    def send_attended(p):
        for m in range(4):
            peer = 4 * p + lax.rem(f + m, 4)
            landing = att_recv.at[odd, slot, f]

            @pl.when(peer == f)
            def _():
                pltpu.make_async_copy(
                    att_send.at[f], landing, att_rsem.at[odd, slot]
                ).start()

            for k in range(NY):
                chip = lax.rem(z + odd * k, NY) * NY + lax.rem(y + (1 - odd) * k, NY)
                copy = remote(
                    att_send.at[peer], landing, att_ssem.at[k], att_rsem.at[odd, slot],
                    (chip, peer),
                )
                if k == 0:
                    pl.when(peer != f)(copy.start)
                else:
                    copy.start()

    scored = [score(p) for p in range(PAIRS)]
    for p in range(PAIRS):
        attend(p, *scored[p])
        send_attended(p)

    for i in range(2 * KV_HEADS):
        ne[0:1, i * HD : (i + 1) * HD] = fresh_rows[i][0:1]
        ne[1:2, i * HD : (i + 1) * HD] = fresh_rows[i][8:9]
    results[PR:, :, :] = ne[0:2, :].reshape(1, STEPS, ne.shape[1]).astype(BF16)

    line_copies = [[], []]
    for part_id in range(2):
        for side in range(2):
            whole = att_recv.at[side, part_id]
            pltpu.make_async_copy(whole, whole, att_rsem.at[side, part_id]).wait()
            pos = (z, y)[side]
            att_f32[...] = att_recv[side, part_id].astype(F32).reshape(NF * PR, HD)
            for j in range(8):
                rows_all[part_id, side, pos, :, j * HD : (j + 1) * HD] = att_f32[
                    pl.ds(j, PR, stride=8), :
                ].astype(BF16)
            mine_rows = rows_all.at[part_id, side, pos]
            for k in range(1, NY):
                q = lax.rem(pos + k, NY)
                device = (q * NY + y, f) if side == 0 else (z * NY + q, f)
                copy = remote(
                    mine_rows, mine_rows,
                    line_ssem.at[part_id, side, k - 1], line_rsem.at[part_id, side, k - 1],
                    device,
                )
                copy.start()
                line_copies[part_id].append(copy)
    wout_load.wait()
    for copy in msg_copies:
        copy.wait_send()
    for k in range(NY):
        sent = att_send.at[pl.ds(0, NF - 1)] if k == 0 else att_send
        pltpu.make_async_copy(sent, sent, att_ssem.at[k]).wait()

    def out_rows(index):
        return pl.ds(pl.multiple_of(index * OWN, OWN), OWN)

    fin_copies = []
    for part_id in range(2):
        for copy in line_copies[part_id]:
            copy.wait_recv()
        product = jnp.dot(
            rows_all[part_id].reshape(NH * PR // 2, wout_v.shape[0]),
            wout_v[...],
            preferred_element_type=F32,
        )
        for side in range(2):
            for q in range(NY):
                far = 2 * ((part_id + q // 2) % 2) + (q + side) % 2
                home = q * NY + far if side == 0 else far * NY + q
                first = (side * NY + q) * PR
                opart[home * PR : (home + 1) * PR, :] = product[first : first + PR]
        for k in (2, 1, 3, 0):
            x = lax.rem(cx + k, NX)
            peer = 2 * x + lax.rem(part_id + lax.div(x, 2), 2)
            hop = lax.rem(peer - f + NF, NF)
            there = lax.rem(hop + NF - 1, NF)
            fin_send[part_id, k] = opart[out_rows(peer), :].astype(BF16)
            copy = remote(
                fin_send.at[part_id, k], fin_recv.at[there],
                fin_ssem.at[part_id, k], fin_rsem.at[there], (h, peer),
            )
            fin_copies.append((k, hop, copy))
            if k == 0:
                pl.when(hop != 0)(copy.start)
            else:
                copy.start()
    for copies in line_copies:
        for copy in copies:
            copy.wait_send()
    result = opart[out_rows(f), :]
    for k in range(1, NF):
        pltpu.make_async_copy(
            fin_recv.at[k - 1], fin_recv.at[k - 1], fin_rsem.at[k - 1]
        ).wait()
        result = result + fin_recv[k - 1].astype(F32)
    results[:PR, :, :] = result.reshape(PR, STEPS, result.shape[1]).astype(BF16)
    for k, hop, copy in fin_copies:
        if k == 0:
            pl.when(hop != 0)(copy.wait_send)
        else:
            copy.wait_send()


def hand_out(results, out, entries, sem):
    rows = out.shape[0]
    copies = [
        pltpu.make_async_copy(results.at[pl.ds(0, rows)], out, sem.at[0]),
        pltpu.make_async_copy(results.at[pl.ds(rows, 1)], entries, sem.at[1]),
    ]
    for copy in copies:
        copy.start()
    for copy in copies:
        copy.wait()


def body(tokens, norm_gain, query_weight, w_keyval, w_out, cache_keys, cache_values, lengths):
    width = tokens.shape[2]
    lmax = cache_keys.shape[1]
    qcols = query_weight.shape[1]
    kvcols = w_keyval.shape[1]
    halves = np.arange(HD // 2, dtype=np.float64) * (2.0 / HD)
    freq = (ROPE_BASE ** (-halves)).astype(np.float32)
    freq = jnp.asarray(np.tile(np.concatenate([freq, freq])[None, :], (PR, 1)))
    any_spec = pl.BlockSpec(memory_space=pl.ANY)
    hbm_spec = pl.BlockSpec(memory_space=pltpu.HBM)
    vmem_spec = pl.BlockSpec(memory_space=pltpu.VMEM)
    dma = pltpu.SemaphoreType.DMA
    rows = NH * PR
    results = pl.pallas_call(
        kernel,
        out_shape=pltpu.VMEM((PR + 1, STEPS, width), BF16),
        in_specs=[hbm_spec] * 9,
        out_specs=vmem_spec,
        scratch_shapes=[
            pltpu.SMEM(lengths.shape, jnp.int32),
            pltpu.VMEM(tokens.shape, BF16),
            pltpu.VMEM((OWN, width), BF16),
            pltpu.VMEM((PR, HD), F32),
            pltpu.VMEM((width,), BF16),
            pltpu.VMEM((width, qcols), BF16),
            pltpu.VMEM((width, kvcols), BF16),
            pltpu.VMEM((qcols, width), BF16),
            pltpu.VMEM((lmax, KV_HEADS * HD), BF16),
            pltpu.VMEM((KV_HEADS * HD, lmax), BF16),
            pltpu.VMEM((lmax, KV_HEADS * HD), BF16),
            pltpu.VMEM((rows, width), BF16),
            pltpu.VMEM((rows // 2, width), BF16),
            pltpu.VMEM((8, HD), F32),
            pltpu.VMEM((NH - 1, 8, HD), F32),
            pltpu.VMEM((NF, 8, HD), F32),
            pltpu.VMEM((NY, NY, PR, qcols + kvcols), F32),
            pltpu.VMEM((2, NY, PR // 2, qcols + kvcols), F32),
            pltpu.VMEM((2, NY, PR // 2, qcols + kvcols), F32),
            pltpu.VMEM((2, NY, PR // 2, qcols + kvcols), F32),
            pltpu.VMEM((2, NY, PR // 2, qcols + kvcols), F32),
            pltpu.VMEM((2, NY - 1, PR // 2, qcols + kvcols), F32),
            pltpu.VMEM((NF * PR, HD), F32),
            pltpu.VMEM((NF, 2 * PR, HD), BF16),
            pltpu.VMEM((NF, 2 * PR, HD), BF16),
            pltpu.VMEM((HD, KV_HEADS * HD), BF16),
            pltpu.VMEM((HD, KV_HEADS * HD), BF16),
            pltpu.VMEM((8, 2 * KV_HEADS * HD), F32),
            pltpu.VMEM((KV_HEADS * OWN, lmax), F32),
            pltpu.VMEM((NF, PR, HD), BF16),
            pltpu.VMEM((2, 2, NF, PR, HD), BF16),
            pltpu.VMEM((NF * PR, HD), F32),
            pltpu.VMEM((2, 2, NY, PR, qcols), BF16),
            pltpu.VMEM((rows, width), F32),
            pltpu.VMEM((2, NX, OWN, width), BF16),
            pltpu.VMEM((NF - 1, OWN, width), BF16),
            dma((8,)),
            dma((CACHE_COPIES,)),
            dma((CACHE_COPIES,)),
            dma((NX - 1,)), dma((NX - 1,)),
            dma((NX,)), dma((NX,)),
            dma((NH - 1,)), dma((NH - 1,)),
            dma((NF - 1,)), dma((NF - 1,)),
            dma((2, 2, 6)), dma((2, 2, 6)),
            dma((2, 2, NY - 1)), dma((2, 2, NY - 1)),
            dma((NF - 1,)), dma((NF - 1,)),
            dma((NY,)), dma((2, 2)),
            dma((2, 2, NY - 1)), dma((2, 2, NY - 1)),
            dma((2, NX)), dma((NF - 1,)),
        ],
        compiler_params=pltpu.CompilerParams(
            collective_id=0, has_side_effects=True, vmem_limit_bytes=48 * 2**20
        ),
        name="decode_block",
    )(
        *[
            pltpu.with_memory_space_constraint(array, pltpu.HBM)
            for array in (
                lengths, freq, tokens, norm_gain, query_weight, w_keyval, w_out,
                cache_keys, cache_values,
            )
        ],
    )
    return pl.pallas_call(
        hand_out,
        out_shape=(
            jax.ShapeDtypeStruct(tokens.shape, BF16),
            jax.ShapeDtypeStruct((1, STEPS, 2 * KV_HEADS * HD), BF16),
        ),
        in_specs=[vmem_spec],
        out_specs=(any_spec, any_spec),
        scratch_shapes=[dma((2,))],
        name="hand_out",
    )(pltpu.with_memory_space_constraint(results, pltpu.VMEM))


def solution(mesh):
    in_specs = (
        P("ffn", None, "hid"),
        P("hid"),
        P("hid", "ffn"),
        P("hid", "ffn"),
        P("ffn", "hid"),
        P(("hid", "ffn"), None, None),
        P(("hid", "ffn"), None, None),
        P(),
    )
    out_specs = (P("ffn", None, "hid"), P(("hid", "ffn"), None, None))
    return jax.shard_map(body, mesh=mesh, in_specs=in_specs, out_specs=out_specs, check_vma=False)
```

```python
import functools

import jax
import jax.numpy as jnp
import numpy as np
from jax import lax
from jax.experimental import pallas as pl
from jax.experimental.pallas import tpu as pltpu
from jax.sharding import PartitionSpec as P

MESH = pl.DeviceIdType.MESH
F32 = jnp.float32
BF16 = jnp.bfloat16

HEADS = 64
KV_HEADS = 4
HD = 128
STEPS = 2
EPSILON = 1e-05
ROPE_BASE = 500000.0
SCALE = HD ** (-0.5) * 1.4426950408889634
MASKED = -1e30

NH = 16
NF = 8
NX = 4
NY = 4
TURN = 1024
GROUPS = (((0, 256), (256, 256)), ((512, 384), (896, 256)))
OWN = 32
PR = 16
CHUNK = 2048
CACHE_COPIES = 8
PAIRS = KV_HEADS // 2


def remote(src, dst, send_sem, recv_sem, device):
    return pltpu.make_async_remote_copy(
        src_ref=src,
        dst_ref=dst,
        send_sem=send_sem,
        recv_sem=recv_sem,
        device_id=device,
        device_id_type=MESH,
    )


def rotate(vectors, cosine, sine):
    return vectors * cosine + pltpu.roll(vectors, HD // 2, 1) * sine


def kernel(
    lengths_hbm, freq, tokens, gain, wq, wkv, wout, cache_k, cache_v,
    results,
    lengths, raw_v, tok_v, freq_v, gain_v, wq_v, wkv_v, wout_v, k_v, k_t, v_v,
    x_all, normed, ss_own, ss_recv, tot_all, part, relay, left, right, mine, mine_recv,
    spread, msg, qkv, kx, vx, ne, scores, att_send, att_recv, att_f32, rows_all,
    opart, fin_send, fin_recv,
    local_sem, k_sem, v_sem,
    tok_ssem, tok_rsem, fwd_ssem, fwd_rsem, ss_ssem, ss_rsem, tot_ssem, tot_rsem,
    ring_ssem, ring_rsem, stage_ssem, stage_rsem, msg_ssem, msg_rsem, att_ssem, att_rsem, line_ssem, line_rsem,
    fin_ssem, fin_rsem,
):
    h = lax.axis_index("hid")
    f = lax.axis_index("ffn")
    z = lax.div(h, NY)
    y = lax.rem(h, NY)
    cx = lax.div(f, 2)
    core = lax.rem(f, 2)
    sib = f + 1 - 2 * core
    lmax = cache_k.shape[1]

    barrier = pltpu.get_barrier_semaphore()
    tokens_load = pltpu.make_async_copy(tokens, raw_v, local_sem.at[0])
    tokens_load.start()

    for k in range(1, NF):
        pl.semaphore_signal(
            barrier, inc=1, device_id=(h, lax.rem(f + k, NF)), device_id_type=MESH
        )
    for k in range(1, NH):
        pl.semaphore_signal(
            barrier, inc=1, device_id=(lax.rem(h + k, NH), f), device_id_type=MESH
        )

    loads = []
    for i, (src, dst) in enumerate(
        [(gain, gain_v), (freq, freq_v), (wq, wq_v), (wkv, wkv_v), (lengths_hbm, lengths)]
    ):
        copy = pltpu.make_async_copy(src, dst, local_sem.at[1 + i])
        copy.start()
        loads.append(copy)
    span = lmax // CACHE_COPIES
    k_loads = []
    for i in range(CACHE_COPIES):
        copy = pltpu.make_async_copy(
            cache_k.at[0, pl.ds(i * span, span)], k_v.at[pl.ds(i * span, span)], k_sem.at[i]
        )
        copy.start()
        k_loads.append(copy)
    v_loads = []
    for i in range(CACHE_COPIES):
        copy = pltpu.make_async_copy(
            cache_v.at[0, pl.ds(i * span, span)], v_v.at[pl.ds(i * span, span)], v_sem.at[i]
        )
        copy.start()
        v_loads.append(copy)
    wout_load = pltpu.make_async_copy(wout, wout_v, local_sem.at[6])
    wout_load.start()

    def turn_keys(quarter):
        for copy in k_loads[2 * quarter : 2 * quarter + 2]:
            copy.wait()

        def turn(i, carry):
            rows = pl.ds(pl.multiple_of(quarter * 2 * span + i * TURN, TURN), TURN)
            k_t[:, rows] = k_v[rows, :].T
            return carry

        lax.fori_loop(0, 2 * span // TURN, turn, 0)

    tokens_load.wait()
    x_f32 = raw_v[...].astype(F32).reshape(tok_v.shape)
    x_own = x_f32.astype(BF16)
    tok_v[...] = x_own
    pl.semaphore_wait(barrier, NH + NF - 2)

    def block(index):
        return x_all.at[pl.ds(pl.multiple_of(index * OWN, OWN), OWN)]

    tok_copies = []
    for k in (1, 3, 2):
        peer = 2 * lax.rem(cx + k, NX) + core
        copy = remote(tok_v, block(f), tok_ssem.at[k - 1], tok_rsem.at[k - 1], (h, peer))
        copy.start()
        tok_copies.append((k, copy))
    opposite = 2 * lax.rem(cx + 2, NX) + 1 - core
    fwd_copies = [
        remote(tok_v, block(f), fwd_ssem.at[0], fwd_rsem.at[0], (h, sib)),
        remote(tok_v, block(f), fwd_ssem.at[2], fwd_rsem.at[2], (h, opposite)),
    ]
    for copy in fwd_copies:
        copy.start()

    sums = jnp.sum(x_f32 * x_f32, axis=1, keepdims=True)
    row_id = lax.broadcasted_iota(jnp.int32, (OWN, HD), 0)
    lane_id = lax.broadcasted_iota(jnp.int32, (OWN, HD), 1)
    diagonal = row_id == lane_id
    own_sums = jnp.sum(jnp.where(diagonal, sums, 0.0), axis=0, keepdims=True)
    ss_own[...] = jnp.broadcast_to(own_sums, (8, HD))

    def ss_copy(k):
        return remote(
            ss_own, ss_recv.at[k - 1], ss_ssem.at[k - 1], ss_rsem.at[k - 1],
            (lax.rem(h + k, NH), f),
        )

    for k in range(1, NH):
        ss_copy(k).start()
    x_all[pl.ds(pl.multiple_of(f * OWN, OWN), OWN), :] = x_own

    total = ss_own[...]
    for k in range(1, NH):
        ss_copy(k).wait_recv()
        total = total + ss_recv[k - 1]
    tot_all[f] = total
    tot_copies = []
    for k in range(1, NF):
        copy = remote(
            tot_all.at[f], tot_all.at[f], tot_ssem.at[k - 1], tot_rsem.at[k - 1],
            (h, lax.rem(f + k, NF)),
        )
        copy.start()
        tot_copies.append(copy)
    for k, tok_copy in tok_copies:
        tok_copy.wait_recv()
        if k != 2:
            came = 2 * lax.rem(cx + NX - k, NX) + core
            copy = remote(block(came), block(came), fwd_ssem.at[k], fwd_rsem.at[k], (h, sib))
            copy.start()
            fwd_copies.append(copy)

    for copy in tot_copies:
        copy.wait_recv()
    loads[0].wait()
    width = x_all.shape[1]
    qcols = wq_v.shape[1]
    full = width * NH
    gain_row = gain_v[...].astype(F32).reshape(1, width)

    def project(parity):
        for x in range(NX):
            b = 2 * x + parity
            lane_sums = tot_all[b][0:1, :]
            row_sums = jnp.sum(jnp.where(diagonal, lane_sums, 0.0), axis=1, keepdims=True)
            inverse = lax.rsqrt(row_sums / full + EPSILON)
            normed[x * OWN : (x + 1) * OWN, :] = (
                block(b)[...].astype(F32) * inverse * gain_row
            ).astype(BF16)
        lhs = normed[...]
        for cols, weights in ((slice(0, qcols), wq_v), (slice(qcols, None), wkv_v)):
            product = jnp.dot(lhs, weights[...], preferred_element_type=F32)
            part[:, pl.ds(2 * parity, 2), :, cols] = product.reshape(NX, 2, PR, product.shape[1])

    loads[2].wait()
    loads[3].wait()
    project(core)

    loads[4].wait()
    length = lengths[h * NF + f]
    step_of = lax.div(lax.broadcasted_iota(jnp.int32, (PR, HD), 0), 8)
    loads[1].wait()
    angles = (step_of + length).astype(F32) * freq_v[...]
    cosine = jnp.cos(angles)
    sine = jnp.sin(angles)
    sine = jnp.where(
        lax.broadcasted_iota(jnp.int32, (PR, HD), 1) < HD // 2, -sine, sine
    )
    kx[...] = jnp.zeros_like(kx)
    vx[...] = jnp.zeros_like(vx)

    for copy in fwd_copies:
        copy.wait_recv()
    project(1 - core)

    half = PR // 2

    def ring(side):
        pos = (y, z)[side]

        def device(q):
            return (z * NY + q, f) if side == 0 else (q * NY + y, f)

        def view(q, cols):
            if side == 0:
                return part.at[:, q, pl.ds(0, half), cols]
            return part.at[q, :, pl.ds(half, half), cols]

        return pos, device, view

    moves = {}
    for g, (low, high) in enumerate(GROUPS):
        for side in range(2):
            pos, device, view = ring(side)
            nxt, prv, far = lax.rem(pos + 1, NY), lax.rem(pos + 3, NY), lax.rem(pos + 2, NY)
            plan = [
                (far, low, relay, nxt),
                (far, high, relay, prv),
                (nxt, high, left, nxt),
                (prv, low, right, prv),
            ]
            moves[g, side] = [
                remote(
                    view(q, pl.ds(*cols)), dst.at[side, :, :, pl.ds(*cols)],
                    ring_ssem.at[g, side, i], ring_rsem.at[g, side, i], device(to),
                )
                for i, (q, cols, dst, to) in enumerate(plan)
            ]
    for first in (0, 2):
        for g in range(len(GROUPS)):
            for side in range(2):
                for copy in moves[g, side][first : first + 2]:
                    copy.start()
    for k in range(1, NH):
        ss_copy(k).wait_send()
    for copy in tot_copies + fwd_copies + [copy for _, copy in tok_copies]:
        copy.wait_send()
    turn_keys(0)
    for g, (low, high) in enumerate(GROUPS):
        for side in range(2):
            pos, device, view = ring(side)
            nxt, prv = lax.rem(pos + 1, NY), lax.rem(pos + 3, NY)
            for i, (to, cols, dst) in enumerate(((nxt, low, left), (prv, high, right))):
                cols = pl.ds(*cols)
                moves[g, side][i].wait_recv()
                passed = relay.at[side, :, :, cols]
                passed[...] = passed[...] + view(to, cols)[...]
                copy = remote(
                    passed, dst.at[side, :, :, cols],
                    ring_ssem.at[g, side, 4 + i], ring_rsem.at[g, side, 4 + i], device(to),
                )
                copy.start()
                moves[g, side].append(copy)
    turn_keys(1)
    stages = {}
    for g, (low, high) in enumerate(GROUPS):
        cols = pl.ds(low[0], low[1] + high[1])
        for side in range(2):
            pos, device, view = ring(side)
            for copy in moves[g, side][2:]:
                copy.wait_recv()
            mine[side, :, :, cols] = (
                view(pos, cols)[...] + left[side, :, :, cols] + right[side, :, :, cols]
            )
            other, other_device, _ = ring(1 - side)
            stages[g, side] = []
            for k in (1, 3, 2):
                peer = lax.rem(other + k, NY)
                copy = remote(
                    mine.at[side, peer, :, cols], mine_recv.at[side, k - 1, :, cols],
                    stage_ssem.at[g, side, k - 1], stage_rsem.at[g, side, k - 1],
                    other_device(peer),
                )
                copy.start()
                stages[g, side].append(copy)
    turn_keys(2)
    groups = []
    for g, (low, high) in enumerate(GROUPS):
        cols = pl.ds(low[0], low[1] + high[1])
        halves = []
        for side in range(2):
            other = ring(1 - side)[0]
            total = mine[side, other, :, cols]
            for copy in stages[g, side]:
                copy.wait_recv()
            for k in range(NY - 1):
                total = total + mine_recv[side, k, :, cols]
            halves.append(total)
        groups.append(jnp.concatenate(halves, axis=0))
    summed = jnp.concatenate(groups, axis=1)

    for j in range(8):
        spread[pl.ds(j, PR, stride=8), :] = summed[:, j * HD : (j + 1) * HD]
    msg[:, :PR, :] = spread[...].reshape(NF, PR, HD).astype(BF16)
    spread[...] = jnp.zeros_like(spread)
    spread[pl.ds(0, PR, stride=8), :] = summed[:, qcols:]
    msg[:, PR:, :] = spread[...].reshape(NF, PR, HD).astype(BF16)
    qkv[f] = msg[f]
    msg_copies = []
    for k in range(1, NF):
        peer = lax.rem(f + k, NF)
        copy = remote(
            msg.at[peer], qkv.at[f], msg_ssem.at[k - 1], msg_rsem.at[k - 1], (h, peer)
        )
        copy.start()
        msg_copies.append(copy)
    for key in moves:
        for copy in moves[key] + stages[key]:
            copy.wait_send()
    turn_keys(3)
    for copy in msg_copies:
        copy.wait_recv()

    fresh_rows = []
    for i in range(2 * KV_HEADS):
        raw = qkv[i, PR:, :].astype(F32)
        cols = pl.ds((i % KV_HEADS) * HD, HD)
        if i < KV_HEADS:
            raw = rotate(raw, cosine, sine)
            kx[:PR, cols] = raw.astype(BF16)
        else:
            vx[:PR, cols] = raw.astype(BF16)
        fresh_rows.append(raw)

    rotated = [
        rotate(qkv[i, :PR, :].astype(F32), cosine, sine).astype(BF16) for i in range(NF)
    ]
    nothing = jnp.zeros((OWN, HD), BF16)
    queries = []
    for p in range(PAIRS):
        upper = jnp.concatenate(rotated[4 * p : 4 * p + 2], axis=0)
        lower = jnp.concatenate(rotated[4 * p + 2 : 4 * p + 4], axis=0)
        queries.append(
            jnp.concatenate(
                [
                    jnp.concatenate([upper, nothing], axis=1),
                    jnp.concatenate([nothing, lower], axis=1),
                ],
                axis=0,
            )
        )
    pair_rows, pair_cols = 2 * OWN, 2 * HD
    lane = lax.broadcasted_iota(jnp.int32, (pair_rows, HD), 1)
    step_row = lax.rem(lax.div(lax.broadcasted_iota(jnp.int32, (pair_rows, HD), 0), 8), 2)
    fresh_live = (lane == 0) | ((lane == 8) & (step_row == 1))
    nt = (((1,), (1,)), ((), ()))
    for copy in v_loads:
        copy.wait()

    def score(p):
        pair = pl.ds(p * pair_cols, pair_cols)
        fresh = lax.dot_general(queries[p], kx[:, pair], nt, preferred_element_type=F32)
        fresh = jnp.where(fresh_live, fresh * SCALE, MASKED)
        high = fresh
        for c in range(lmax // CHUNK):
            rows = pl.ds(c * CHUNK, CHUNK)
            s = jnp.dot(queries[p], k_t[pair, rows], preferred_element_type=F32) * SCALE
            if (c + 1) * CHUNK > lmax // 4:
                position = lax.broadcasted_iota(jnp.int32, (8, CHUNK), 1) + c * CHUNK
                cap = jnp.where(position < length, -MASKED, MASKED)
                s = jnp.minimum(s, jnp.concatenate([cap] * (pair_rows // 8), axis=0))
            scores[pl.ds(p * pair_rows, pair_rows), rows] = s
            for t in range(CHUNK // HD):
                high = jnp.maximum(high, s[:, t * HD : (t + 1) * HD])
        peak = jnp.broadcast_to(jnp.max(high, axis=1, keepdims=True), (pair_rows, HD))
        return fresh, peak

    def attend(p, fresh, peak):
        pair = pl.ds(p * pair_cols, pair_cols)
        weights = jnp.exp2(fresh - peak).astype(BF16)
        total = weights.astype(F32)
        acc = jnp.dot(weights, vx[:, pair], preferred_element_type=F32)
        for c in range(lmax // CHUNK):
            rows = pl.ds(c * CHUNK, CHUNK)
            s = scores[pl.ds(p * pair_rows, pair_rows), rows]
            pieces = []
            for t in range(CHUNK // HD):
                piece = jnp.exp2(s[:, t * HD : (t + 1) * HD] - peak).astype(BF16)
                total = total + piece.astype(F32)
                pieces.append(piece)
            acc = acc + jnp.dot(
                jnp.concatenate(pieces, axis=1), v_v[rows, pair], preferred_element_type=F32
            )
        weight_sum = jnp.sum(total, axis=1, keepdims=True)
        for i in range(2):
            rows = slice(i * OWN, (i + 1) * OWN)
            attended = acc[rows, i * HD : (i + 1) * HD] / weight_sum[rows]
            attended = attended.astype(BF16)
            att_send[4 * p + 2 * i] = attended[:PR]
            att_send[4 * p + 2 * i + 1] = attended[PR:]

    odd = lax.rem(y + z, 2)
    slot = lax.rem(lax.div(y, 2) + lax.div(z, 2), 2)

    def send_attended(p):
        for m in range(4):
            peer = 4 * p + lax.rem(f + m, 4)
            landing = att_recv.at[odd, slot, f]

            @pl.when(peer == f)
            def _():
                pltpu.make_async_copy(
                    att_send.at[f], landing, att_rsem.at[odd, slot]
                ).start()

            for k in range(NY):
                chip = lax.rem(z + odd * k, NY) * NY + lax.rem(y + (1 - odd) * k, NY)
                copy = remote(
                    att_send.at[peer], landing, att_ssem.at[k], att_rsem.at[odd, slot],
                    (chip, peer),
                )
                if k == 0:
                    pl.when(peer != f)(copy.start)
                else:
                    copy.start()

    scored = [score(p) for p in range(PAIRS)]
    for p in range(PAIRS):
        attend(p, *scored[p])
        send_attended(p)

    for i in range(2 * KV_HEADS):
        ne[0:1, i * HD : (i + 1) * HD] = fresh_rows[i][0:1]
        ne[1:2, i * HD : (i + 1) * HD] = fresh_rows[i][8:9]
    results[PR:, :, :] = ne[0:2, :].reshape(1, STEPS, ne.shape[1]).astype(BF16)

    line_copies = [[], []]
    for part_id in range(2):
        for side in range(2):
            whole = att_recv.at[side, part_id]
            pltpu.make_async_copy(whole, whole, att_rsem.at[side, part_id]).wait()
            pos = (z, y)[side]
            att_f32[...] = att_recv[side, part_id].astype(F32).reshape(NF * PR, HD)
            for j in range(8):
                rows_all[part_id, side, pos, :, j * HD : (j + 1) * HD] = att_f32[
                    pl.ds(j, PR, stride=8), :
                ].astype(BF16)
            mine_rows = rows_all.at[part_id, side, pos]
            for k in range(1, NY):
                q = lax.rem(pos + k, NY)
                device = (q * NY + y, f) if side == 0 else (z * NY + q, f)
                copy = remote(
                    mine_rows, mine_rows,
                    line_ssem.at[part_id, side, k - 1], line_rsem.at[part_id, side, k - 1],
                    device,
                )
                copy.start()
                line_copies[part_id].append(copy)
    wout_load.wait()
    for copy in msg_copies:
        copy.wait_send()
    for k in range(NY):
        sent = att_send.at[pl.ds(0, NF - 1)] if k == 0 else att_send
        pltpu.make_async_copy(sent, sent, att_ssem.at[k]).wait()

    def out_rows(index):
        return pl.ds(pl.multiple_of(index * OWN, OWN), OWN)

    fin_copies = []
    for part_id in range(2):
        for copy in line_copies[part_id]:
            copy.wait_recv()
        product = jnp.dot(
            rows_all[part_id].reshape(NH * PR // 2, wout_v.shape[0]),
            wout_v[...],
            preferred_element_type=F32,
        )
        for side in range(2):
            for q in range(NY):
                far = 2 * ((part_id + q // 2) % 2) + (q + side) % 2
                home = q * NY + far if side == 0 else far * NY + q
                first = (side * NY + q) * PR
                opart[home * PR : (home + 1) * PR, :] = product[first : first + PR]
        for k in (2, 1, 3, 0):
            x = lax.rem(cx + k, NX)
            peer = 2 * x + lax.rem(part_id + lax.div(x, 2), 2)
            hop = lax.rem(peer - f + NF, NF)
            there = lax.rem(hop + NF - 1, NF)
            fin_send[part_id, k] = opart[out_rows(peer), :].astype(BF16)
            copy = remote(
                fin_send.at[part_id, k], fin_recv.at[there],
                fin_ssem.at[part_id, k], fin_rsem.at[there], (h, peer),
            )
            fin_copies.append((k, hop, copy))
            if k == 0:
                pl.when(hop != 0)(copy.start)
            else:
                copy.start()
    for copies in line_copies:
        for copy in copies:
            copy.wait_send()
    result = opart[out_rows(f), :]
    for k in range(1, NF):
        pltpu.make_async_copy(
            fin_recv.at[k - 1], fin_recv.at[k - 1], fin_rsem.at[k - 1]
        ).wait()
        result = result + fin_recv[k - 1].astype(F32)
    results[:PR, :, :] = result.reshape(PR, STEPS, result.shape[1]).astype(BF16)
    for k, hop, copy in fin_copies:
        if k == 0:
            pl.when(hop != 0)(copy.wait_send)
        else:
            copy.wait_send()


def hand_out(results, out, entries, sem):
    rows = out.shape[0]
    copies = [
        pltpu.make_async_copy(results.at[pl.ds(0, rows)], out, sem.at[0]),
        pltpu.make_async_copy(results.at[pl.ds(rows, 1)], entries, sem.at[1]),
    ]
    for copy in copies:
        copy.start()
    for copy in copies:
        copy.wait()


def body(tokens, norm_gain, query_weight, w_keyval, w_out, cache_keys, cache_values, lengths):
    width = tokens.shape[2]
    lmax = cache_keys.shape[1]
    qcols = query_weight.shape[1]
    kvcols = w_keyval.shape[1]
    halves = np.arange(HD // 2, dtype=np.float64) * (2.0 / HD)
    freq = (ROPE_BASE ** (-halves)).astype(np.float32)
    freq = jnp.asarray(np.tile(np.concatenate([freq, freq])[None, :], (PR, 1)))
    any_spec = pl.BlockSpec(memory_space=pl.ANY)
    hbm_spec = pl.BlockSpec(memory_space=pltpu.HBM)
    vmem_spec = pl.BlockSpec(memory_space=pltpu.VMEM)
    dma = pltpu.SemaphoreType.DMA
    rows = NH * PR
    results = pl.pallas_call(
        kernel,
        out_shape=pltpu.VMEM((PR + 1, STEPS, width), BF16),
        in_specs=[hbm_spec] * 9,
        out_specs=vmem_spec,
        scratch_shapes=[
            pltpu.SMEM(lengths.shape, jnp.int32),
            pltpu.VMEM(tokens.shape, BF16),
            pltpu.VMEM((OWN, width), BF16),
            pltpu.VMEM((PR, HD), F32),
            pltpu.VMEM((width,), BF16),
            pltpu.VMEM((width, qcols), BF16),
            pltpu.VMEM((width, kvcols), BF16),
            pltpu.VMEM((qcols, width), BF16),
            pltpu.VMEM((lmax, KV_HEADS * HD), BF16),
            pltpu.VMEM((KV_HEADS * HD, lmax), BF16),
            pltpu.VMEM((lmax, KV_HEADS * HD), BF16),
            pltpu.VMEM((rows, width), BF16),
            pltpu.VMEM((rows // 2, width), BF16),
            pltpu.VMEM((8, HD), F32),
            pltpu.VMEM((NH - 1, 8, HD), F32),
            pltpu.VMEM((NF, 8, HD), F32),
            pltpu.VMEM((NY, NY, PR, qcols + kvcols), F32),
            pltpu.VMEM((2, NY, PR // 2, qcols + kvcols), F32),
            pltpu.VMEM((2, NY, PR // 2, qcols + kvcols), F32),
            pltpu.VMEM((2, NY, PR // 2, qcols + kvcols), F32),
            pltpu.VMEM((2, NY, PR // 2, qcols + kvcols), F32),
            pltpu.VMEM((2, NY - 1, PR // 2, qcols + kvcols), F32),
            pltpu.VMEM((NF * PR, HD), F32),
            pltpu.VMEM((NF, 2 * PR, HD), BF16),
            pltpu.VMEM((NF, 2 * PR, HD), BF16),
            pltpu.VMEM((HD, KV_HEADS * HD), BF16),
            pltpu.VMEM((HD, KV_HEADS * HD), BF16),
            pltpu.VMEM((8, 2 * KV_HEADS * HD), F32),
            pltpu.VMEM((KV_HEADS * OWN, lmax), F32),
            pltpu.VMEM((NF, PR, HD), BF16),
            pltpu.VMEM((2, 2, NF, PR, HD), BF16),
            pltpu.VMEM((NF * PR, HD), F32),
            pltpu.VMEM((2, 2, NY, PR, qcols), BF16),
            pltpu.VMEM((rows, width), F32),
            pltpu.VMEM((2, NX, OWN, width), BF16),
            pltpu.VMEM((NF - 1, OWN, width), BF16),
            dma((8,)),
            dma((CACHE_COPIES,)),
            dma((CACHE_COPIES,)),
            dma((NX - 1,)), dma((NX - 1,)),
            dma((NX,)), dma((NX,)),
            dma((NH - 1,)), dma((NH - 1,)),
            dma((NF - 1,)), dma((NF - 1,)),
            dma((2, 2, 6)), dma((2, 2, 6)),
            dma((2, 2, NY - 1)), dma((2, 2, NY - 1)),
            dma((NF - 1,)), dma((NF - 1,)),
            dma((NY,)), dma((2, 2)),
            dma((2, 2, NY - 1)), dma((2, 2, NY - 1)),
            dma((2, NX)), dma((NF - 1,)),
        ],
        compiler_params=pltpu.CompilerParams(
            collective_id=0, has_side_effects=True, vmem_limit_bytes=48 * 2**20
        ),
        name="decode_block",
    )(
        *[
            pltpu.with_memory_space_constraint(array, pltpu.HBM)
            for array in (
                lengths, freq, tokens, norm_gain, query_weight, w_keyval, w_out,
                cache_keys, cache_values,
            )
        ],
    )
    return pl.pallas_call(
        hand_out,
        out_shape=(
            jax.ShapeDtypeStruct(tokens.shape, BF16),
            jax.ShapeDtypeStruct((1, STEPS, 2 * KV_HEADS * HD), BF16),
        ),
        in_specs=[vmem_spec],
        out_specs=(any_spec, any_spec),
        scratch_shapes=[dma((2,))],
        name="hand_out",
    )(pltpu.with_memory_space_constraint(results, pltpu.VMEM))


def solution(mesh):
    in_specs = (
        P("ffn", None, "hid"),
        P("hid"),
        P("hid", "ffn"),
        P("hid", "ffn"),
        P("ffn", "hid"),
        P(("hid", "ffn"), None, None),
        P(("hid", "ffn"), None, None),
        P(),
    )
    out_specs = (P("ffn", None, "hid"), P(("hid", "ffn"), None, None))
    return jax.shard_map(body, mesh=mesh, in_specs=in_specs, out_specs=out_specs, check_vma=False)
```

```python
import functools

import jax
import jax.numpy as jnp
import numpy as np
from jax import lax
from jax.experimental import pallas as pl
from jax.experimental.pallas import tpu as pltpu
from jax.sharding import PartitionSpec as P

MESH = pl.DeviceIdType.MESH
F32 = jnp.float32
BF16 = jnp.bfloat16

HEADS = 64
KV_HEADS = 4
HD = 128
STEPS = 2
EPSILON = 1e-05
ROPE_BASE = 500000.0
SCALE = HD ** (-0.5) * 1.4426950408889634
MASKED = -1e30

NH = 16
NF = 8
NX = 4
NY = 4
TURN = 1024
GROUPS = (((0, 256), (256, 256)), ((512, 384), (896, 256)))
OWN = 32
PR = 16
CHUNK = 2048
CACHE_COPIES = 8
PAIRS = KV_HEADS // 2


def remote(src, dst, send_sem, recv_sem, device):
    return pltpu.make_async_remote_copy(
        src_ref=src,
        dst_ref=dst,
        send_sem=send_sem,
        recv_sem=recv_sem,
        device_id=device,
        device_id_type=MESH,
    )


def rotate(vectors, cosine, sine):
    return vectors * cosine + pltpu.roll(vectors, HD // 2, 1) * sine


def kernel(
    lengths_hbm, freq, tokens, gain, wq, wkv, wout, cache_k, cache_v,
    results,
    lengths, raw_v, tok_v, freq_v, gain_v, wq_v, wkv_v, wout_v, k_v, k_t, v_v,
    x_all, normed, ss_own, ss_recv, tot_all, part, relay, left, right, mine, mine_recv,
    spread, msg, qkv, kx, vx, ne, scores, att_send, att_recv, att_f32, rows_all,
    opart, fin_send, fin_recv,
    local_sem, k_sem, v_sem,
    tok_ssem, tok_rsem, fwd_ssem, fwd_rsem, ss_ssem, ss_rsem, tot_ssem, tot_rsem,
    ring_ssem, ring_rsem, stage_ssem, stage_rsem, msg_ssem, msg_rsem, att_ssem, att_rsem, line_ssem, line_rsem,
    fin_ssem, fin_rsem,
):
    h = lax.axis_index("hid")
    f = lax.axis_index("ffn")
    z = lax.div(h, NY)
    y = lax.rem(h, NY)
    cx = lax.div(f, 2)
    core = lax.rem(f, 2)
    sib = f + 1 - 2 * core
    lmax = cache_k.shape[1]

    barrier = pltpu.get_barrier_semaphore()
    tokens_load = pltpu.make_async_copy(tokens, raw_v, local_sem.at[0])
    tokens_load.start()

    for k in range(1, NF):
        pl.semaphore_signal(
            barrier, inc=1, device_id=(h, lax.rem(f + k, NF)), device_id_type=MESH
        )
    for k in range(1, NH):
        pl.semaphore_signal(
            barrier, inc=1, device_id=(lax.rem(h + k, NH), f), device_id_type=MESH
        )

    loads = []
    for i, (src, dst) in enumerate(
        [(gain, gain_v), (freq, freq_v), (wq, wq_v), (wkv, wkv_v), (lengths_hbm, lengths)]
    ):
        copy = pltpu.make_async_copy(src, dst, local_sem.at[1 + i])
        copy.start()
        loads.append(copy)
    span = lmax // CACHE_COPIES
    k_loads = []
    for i in range(CACHE_COPIES):
        copy = pltpu.make_async_copy(
            cache_k.at[0, pl.ds(i * span, span)], k_v.at[pl.ds(i * span, span)], k_sem.at[i]
        )
        copy.start()
        k_loads.append(copy)
    v_loads = []
    for i in range(CACHE_COPIES):
        copy = pltpu.make_async_copy(
            cache_v.at[0, pl.ds(i * span, span)], v_v.at[pl.ds(i * span, span)], v_sem.at[i]
        )
        copy.start()
        v_loads.append(copy)
    wout_load = pltpu.make_async_copy(wout, wout_v, local_sem.at[6])

    def turn_keys(quarter):
        for copy in k_loads[2 * quarter : 2 * quarter + 2]:
            copy.wait()

        def turn(i, carry):
            rows = pl.ds(pl.multiple_of(quarter * 2 * span + i * TURN, TURN), TURN)
            k_t[:, rows] = k_v[rows, :].T
            return carry

        lax.fori_loop(0, 2 * span // TURN, turn, 0)

    tokens_load.wait()
    x_f32 = raw_v[...].astype(F32).reshape(tok_v.shape)
    x_own = x_f32.astype(BF16)
    tok_v[...] = x_own
    pl.semaphore_wait(barrier, NH + NF - 2)

    def block(index):
        return x_all.at[pl.ds(pl.multiple_of(index * OWN, OWN), OWN)]

    tok_copies = []
    for k in (1, 3, 2):
        peer = 2 * lax.rem(cx + k, NX) + core
        copy = remote(tok_v, block(f), tok_ssem.at[k - 1], tok_rsem.at[k - 1], (h, peer))
        copy.start()
        tok_copies.append((k, copy))
    opposite = 2 * lax.rem(cx + 2, NX) + 1 - core
    fwd_copies = [
        remote(tok_v, block(f), fwd_ssem.at[0], fwd_rsem.at[0], (h, sib)),
        remote(tok_v, block(f), fwd_ssem.at[2], fwd_rsem.at[2], (h, opposite)),
    ]
    for copy in fwd_copies:
        copy.start()

    sums = jnp.sum(x_f32 * x_f32, axis=1, keepdims=True)
    row_id = lax.broadcasted_iota(jnp.int32, (OWN, HD), 0)
    lane_id = lax.broadcasted_iota(jnp.int32, (OWN, HD), 1)
    diagonal = row_id == lane_id
    own_sums = jnp.sum(jnp.where(diagonal, sums, 0.0), axis=0, keepdims=True)
    ss_own[...] = jnp.broadcast_to(own_sums, (8, HD))

    def ss_copy(k):
        return remote(
            ss_own, ss_recv.at[k - 1], ss_ssem.at[k - 1], ss_rsem.at[k - 1],
            (lax.rem(h + k, NH), f),
        )

    for k in range(1, NH):
        ss_copy(k).start()
    x_all[pl.ds(pl.multiple_of(f * OWN, OWN), OWN), :] = x_own

    total = ss_own[...]
    for k in range(1, NH):
        ss_copy(k).wait_recv()
        total = total + ss_recv[k - 1]
    tot_all[f] = total
    tot_copies = []
    for k in range(1, NF):
        copy = remote(
            tot_all.at[f], tot_all.at[f], tot_ssem.at[k - 1], tot_rsem.at[k - 1],
            (h, lax.rem(f + k, NF)),
        )
        copy.start()
        tot_copies.append(copy)
    for k, tok_copy in tok_copies:
        tok_copy.wait_recv()
        if k != 2:
            came = 2 * lax.rem(cx + NX - k, NX) + core
            copy = remote(block(came), block(came), fwd_ssem.at[k], fwd_rsem.at[k], (h, sib))
            copy.start()
            fwd_copies.append(copy)

    for copy in tot_copies:
        copy.wait_recv()
    loads[0].wait()
    width = x_all.shape[1]
    qcols = wq_v.shape[1]
    full = width * NH
    gain_row = gain_v[...].astype(F32).reshape(1, width)

    def project(parity):
        for x in range(NX):
            b = 2 * x + parity
            lane_sums = tot_all[b][0:1, :]
            row_sums = jnp.sum(jnp.where(diagonal, lane_sums, 0.0), axis=1, keepdims=True)
            inverse = lax.rsqrt(row_sums / full + EPSILON)
            normed[x * OWN : (x + 1) * OWN, :] = (
                block(b)[...].astype(F32) * inverse * gain_row
            ).astype(BF16)
        lhs = normed[...]
        for cols, weights in ((slice(0, qcols), wq_v), (slice(qcols, None), wkv_v)):
            product = jnp.dot(lhs, weights[...], preferred_element_type=F32)
            part[:, pl.ds(2 * parity, 2), :, cols] = product.reshape(NX, 2, PR, product.shape[1])

    loads[2].wait()
    loads[3].wait()
    project(core)

    loads[4].wait()
    length = lengths[h * NF + f]
    step_of = lax.div(lax.broadcasted_iota(jnp.int32, (PR, HD), 0), 8)
    loads[1].wait()
    angles = (step_of + length).astype(F32) * freq_v[...]
    cosine = jnp.cos(angles)
    sine = jnp.sin(angles)
    sine = jnp.where(
        lax.broadcasted_iota(jnp.int32, (PR, HD), 1) < HD // 2, -sine, sine
    )
    kx[...] = jnp.zeros_like(kx)
    vx[...] = jnp.zeros_like(vx)

    for copy in fwd_copies:
        copy.wait_recv()
    project(1 - core)

    half = PR // 2

    def ring(side):
        pos = (y, z)[side]

        def device(q):
            return (z * NY + q, f) if side == 0 else (q * NY + y, f)

        def view(q, cols):
            if side == 0:
                return part.at[:, q, pl.ds(0, half), cols]
            return part.at[q, :, pl.ds(half, half), cols]

        return pos, device, view

    moves = {}
    for g, (low, high) in enumerate(GROUPS):
        for side in range(2):
            pos, device, view = ring(side)
            nxt, prv, far = lax.rem(pos + 1, NY), lax.rem(pos + 3, NY), lax.rem(pos + 2, NY)
            plan = [
                (far, low, relay, nxt),
                (far, high, relay, prv),
                (nxt, high, left, nxt),
                (prv, low, right, prv),
            ]
            moves[g, side] = [
                remote(
                    view(q, pl.ds(*cols)), dst.at[side, :, :, pl.ds(*cols)],
                    ring_ssem.at[g, side, i], ring_rsem.at[g, side, i], device(to),
                )
                for i, (q, cols, dst, to) in enumerate(plan)
            ]
    for first in (0, 2):
        for g in range(len(GROUPS)):
            for side in range(2):
                for copy in moves[g, side][first : first + 2]:
                    copy.start()
    for k in range(1, NH):
        ss_copy(k).wait_send()
    for copy in tot_copies + fwd_copies + [copy for _, copy in tok_copies]:
        copy.wait_send()
    turn_keys(0)
    for g, (low, high) in enumerate(GROUPS):
        for side in range(2):
            pos, device, view = ring(side)
            nxt, prv = lax.rem(pos + 1, NY), lax.rem(pos + 3, NY)
            for i, (to, cols, dst) in enumerate(((nxt, low, left), (prv, high, right))):
                cols = pl.ds(*cols)
                moves[g, side][i].wait_recv()
                passed = relay.at[side, :, :, cols]
                passed[...] = passed[...] + view(to, cols)[...]
                copy = remote(
                    passed, dst.at[side, :, :, cols],
                    ring_ssem.at[g, side, 4 + i], ring_rsem.at[g, side, 4 + i], device(to),
                )
                copy.start()
                moves[g, side].append(copy)
    turn_keys(1)
    stages = {}
    for g, (low, high) in enumerate(GROUPS):
        cols = pl.ds(low[0], low[1] + high[1])
        for side in range(2):
            pos, device, view = ring(side)
            for copy in moves[g, side][2:]:
                copy.wait_recv()
            mine[side, :, :, cols] = (
                view(pos, cols)[...] + left[side, :, :, cols] + right[side, :, :, cols]
            )
            other, other_device, _ = ring(1 - side)
            stages[g, side] = []
            for k in (1, 3, 2):
                peer = lax.rem(other + k, NY)
                copy = remote(
                    mine.at[side, peer, :, cols], mine_recv.at[side, k - 1, :, cols],
                    stage_ssem.at[g, side, k - 1], stage_rsem.at[g, side, k - 1],
                    other_device(peer),
                )
                copy.start()
                stages[g, side].append(copy)
    turn_keys(2)
    groups = []
    for g, (low, high) in enumerate(GROUPS):
        cols = pl.ds(low[0], low[1] + high[1])
        halves = []
        for side in range(2):
            other = ring(1 - side)[0]
            total = mine[side, other, :, cols]
            for copy in stages[g, side]:
                copy.wait_recv()
            for k in range(NY - 1):
                total = total + mine_recv[side, k, :, cols]
            halves.append(total)
        groups.append(jnp.concatenate(halves, axis=0))
    summed = jnp.concatenate(groups, axis=1)

    for j in range(8):
        spread[pl.ds(j, PR, stride=8), :] = summed[:, j * HD : (j + 1) * HD]
    msg[:, :PR, :] = spread[...].reshape(NF, PR, HD).astype(BF16)
    spread[...] = jnp.zeros_like(spread)
    spread[pl.ds(0, PR, stride=8), :] = summed[:, qcols:]
    msg[:, PR:, :] = spread[...].reshape(NF, PR, HD).astype(BF16)
    qkv[f] = msg[f]
    msg_copies = []
    for k in range(1, NF):
        peer = lax.rem(f + k, NF)
        copy = remote(
            msg.at[peer], qkv.at[f], msg_ssem.at[k - 1], msg_rsem.at[k - 1], (h, peer)
        )
        copy.start()
        msg_copies.append(copy)
    for key in moves:
        for copy in moves[key] + stages[key]:
            copy.wait_send()
    wout_load.start()
    turn_keys(3)
    for copy in msg_copies:
        copy.wait_recv()

    fresh_rows = []
    for i in range(2 * KV_HEADS):
        raw = qkv[i, PR:, :].astype(F32)
        cols = pl.ds((i % KV_HEADS) * HD, HD)
        if i < KV_HEADS:
            raw = rotate(raw, cosine, sine)
            kx[:PR, cols] = raw.astype(BF16)
        else:
            vx[:PR, cols] = raw.astype(BF16)
        fresh_rows.append(raw)

    rotated = [
        rotate(qkv[i, :PR, :].astype(F32), cosine, sine).astype(BF16) for i in range(NF)
    ]
    nothing = jnp.zeros((OWN, HD), BF16)
    queries = []
    for p in range(PAIRS):
        upper = jnp.concatenate(rotated[4 * p : 4 * p + 2], axis=0)
        lower = jnp.concatenate(rotated[4 * p + 2 : 4 * p + 4], axis=0)
        queries.append(
            jnp.concatenate(
                [
                    jnp.concatenate([upper, nothing], axis=1),
                    jnp.concatenate([nothing, lower], axis=1),
                ],
                axis=0,
            )
        )
    pair_rows, pair_cols = 2 * OWN, 2 * HD
    lane = lax.broadcasted_iota(jnp.int32, (pair_rows, HD), 1)
    step_row = lax.rem(lax.div(lax.broadcasted_iota(jnp.int32, (pair_rows, HD), 0), 8), 2)
    fresh_live = (lane == 0) | ((lane == 8) & (step_row == 1))
    nt = (((1,), (1,)), ((), ()))
    for copy in v_loads:
        copy.wait()

    def score(p):
        pair = pl.ds(p * pair_cols, pair_cols)
        fresh = lax.dot_general(queries[p], kx[:, pair], nt, preferred_element_type=F32)
        fresh = jnp.where(fresh_live, fresh * SCALE, MASKED)
        high = fresh
        for c in range(lmax // CHUNK):
            rows = pl.ds(c * CHUNK, CHUNK)
            s = jnp.dot(queries[p], k_t[pair, rows], preferred_element_type=F32) * SCALE
            if (c + 1) * CHUNK > lmax // 4:
                position = lax.broadcasted_iota(jnp.int32, (8, CHUNK), 1) + c * CHUNK
                cap = jnp.where(position < length, -MASKED, MASKED)
                s = jnp.minimum(s, jnp.concatenate([cap] * (pair_rows // 8), axis=0))
            scores[pl.ds(p * pair_rows, pair_rows), rows] = s
            for t in range(CHUNK // HD):
                high = jnp.maximum(high, s[:, t * HD : (t + 1) * HD])
        peak = jnp.broadcast_to(jnp.max(high, axis=1, keepdims=True), (pair_rows, HD))
        return fresh, peak

    def attend(p, fresh, peak):
        pair = pl.ds(p * pair_cols, pair_cols)
        weights = jnp.exp2(fresh - peak).astype(BF16)
        total = weights.astype(F32)
        acc = jnp.dot(weights, vx[:, pair], preferred_element_type=F32)
        for c in range(lmax // CHUNK):
            rows = pl.ds(c * CHUNK, CHUNK)
            s = scores[pl.ds(p * pair_rows, pair_rows), rows]
            pieces = []
            for t in range(CHUNK // HD):
                piece = jnp.exp2(s[:, t * HD : (t + 1) * HD] - peak).astype(BF16)
                total = total + piece.astype(F32)
                pieces.append(piece)
            acc = acc + jnp.dot(
                jnp.concatenate(pieces, axis=1), v_v[rows, pair], preferred_element_type=F32
            )
        weight_sum = jnp.sum(total, axis=1, keepdims=True)
        for i in range(2):
            rows = slice(i * OWN, (i + 1) * OWN)
            attended = acc[rows, i * HD : (i + 1) * HD] / weight_sum[rows]
            attended = attended.astype(BF16)
            att_send[4 * p + 2 * i] = attended[:PR]
            att_send[4 * p + 2 * i + 1] = attended[PR:]

    odd = lax.rem(y + z, 2)
    slot = lax.rem(lax.div(y, 2) + lax.div(z, 2), 2)

    def send_attended(p):
        for m in range(4):
            peer = 4 * p + lax.rem(f + m, 4)
            landing = att_recv.at[odd, slot, f]

            @pl.when(peer == f)
            def _():
                pltpu.make_async_copy(
                    att_send.at[f], landing, att_rsem.at[odd, slot]
                ).start()

            for k in range(NY):
                chip = lax.rem(z + odd * k, NY) * NY + lax.rem(y + (1 - odd) * k, NY)
                copy = remote(
                    att_send.at[peer], landing, att_ssem.at[k], att_rsem.at[odd, slot],
                    (chip, peer),
                )
                if k == 0:
                    pl.when(peer != f)(copy.start)
                else:
                    copy.start()

    scored = [score(p) for p in range(PAIRS)]
    for p in range(PAIRS):
        attend(p, *scored[p])
        send_attended(p)

    for i in range(2 * KV_HEADS):
        ne[0:1, i * HD : (i + 1) * HD] = fresh_rows[i][0:1]
        ne[1:2, i * HD : (i + 1) * HD] = fresh_rows[i][8:9]
    results[PR:, :, :] = ne[0:2, :].reshape(1, STEPS, ne.shape[1]).astype(BF16)

    line_copies = [[], []]
    for part_id in range(2):
        for side in range(2):
            whole = att_recv.at[side, part_id]
            pltpu.make_async_copy(whole, whole, att_rsem.at[side, part_id]).wait()
            pos = (z, y)[side]
            att_f32[...] = att_recv[side, part_id].astype(F32).reshape(NF * PR, HD)
            for j in range(8):
                rows_all[part_id, side, pos, :, j * HD : (j + 1) * HD] = att_f32[
                    pl.ds(j, PR, stride=8), :
                ].astype(BF16)
            mine_rows = rows_all.at[part_id, side, pos]
            for k in range(1, NY):
                q = lax.rem(pos + k, NY)
                device = (q * NY + y, f) if side == 0 else (z * NY + q, f)
                copy = remote(
                    mine_rows, mine_rows,
                    line_ssem.at[part_id, side, k - 1], line_rsem.at[part_id, side, k - 1],
                    device,
                )
                copy.start()
                line_copies[part_id].append(copy)
    wout_load.wait()
    for copy in msg_copies:
        copy.wait_send()
    for k in range(NY):
        sent = att_send.at[pl.ds(0, NF - 1)] if k == 0 else att_send
        pltpu.make_async_copy(sent, sent, att_ssem.at[k]).wait()

    def out_rows(index):
        return pl.ds(pl.multiple_of(index * OWN, OWN), OWN)

    fin_copies = []
    for part_id in range(2):
        for copy in line_copies[part_id]:
            copy.wait_recv()
        product = jnp.dot(
            rows_all[part_id].reshape(NH * PR // 2, wout_v.shape[0]),
            wout_v[...],
            preferred_element_type=F32,
        )
        for side in range(2):
            for q in range(NY):
                far = 2 * ((part_id + q // 2) % 2) + (q + side) % 2
                home = q * NY + far if side == 0 else far * NY + q
                first = (side * NY + q) * PR
                opart[home * PR : (home + 1) * PR, :] = product[first : first + PR]
        for k in (2, 1, 3, 0):
            x = lax.rem(cx + k, NX)
            peer = 2 * x + lax.rem(part_id + lax.div(x, 2), 2)
            hop = lax.rem(peer - f + NF, NF)
            there = lax.rem(hop + NF - 1, NF)
            fin_send[part_id, k] = opart[out_rows(peer), :].astype(BF16)
            copy = remote(
                fin_send.at[part_id, k], fin_recv.at[there],
                fin_ssem.at[part_id, k], fin_rsem.at[there], (h, peer),
            )
            fin_copies.append((k, hop, copy))
            if k == 0:
                pl.when(hop != 0)(copy.start)
            else:
                copy.start()
    for copies in line_copies:
        for copy in copies:
            copy.wait_send()
    result = opart[out_rows(f), :]
    for k in range(1, NF):
        pltpu.make_async_copy(
            fin_recv.at[k - 1], fin_recv.at[k - 1], fin_rsem.at[k - 1]
        ).wait()
        result = result + fin_recv[k - 1].astype(F32)
    results[:PR, :, :] = result.reshape(PR, STEPS, result.shape[1]).astype(BF16)
    for k, hop, copy in fin_copies:
        if k == 0:
            pl.when(hop != 0)(copy.wait_send)
        else:
            copy.wait_send()


def hand_out(results, out, entries, sem):
    rows = out.shape[0]
    copies = [
        pltpu.make_async_copy(results.at[pl.ds(0, rows)], out, sem.at[0]),
        pltpu.make_async_copy(results.at[pl.ds(rows, 1)], entries, sem.at[1]),
    ]
    for copy in copies:
        copy.start()
    for copy in copies:
        copy.wait()


def body(tokens, norm_gain, query_weight, w_keyval, w_out, cache_keys, cache_values, lengths):
    width = tokens.shape[2]
    lmax = cache_keys.shape[1]
    qcols = query_weight.shape[1]
    kvcols = w_keyval.shape[1]
    halves = np.arange(HD // 2, dtype=np.float64) * (2.0 / HD)
    freq = (ROPE_BASE ** (-halves)).astype(np.float32)
    freq = jnp.asarray(np.tile(np.concatenate([freq, freq])[None, :], (PR, 1)))
    any_spec = pl.BlockSpec(memory_space=pl.ANY)
    hbm_spec = pl.BlockSpec(memory_space=pltpu.HBM)
    vmem_spec = pl.BlockSpec(memory_space=pltpu.VMEM)
    dma = pltpu.SemaphoreType.DMA
    rows = NH * PR
    results = pl.pallas_call(
        kernel,
        out_shape=pltpu.VMEM((PR + 1, STEPS, width), BF16),
        in_specs=[hbm_spec] * 9,
        out_specs=vmem_spec,
        scratch_shapes=[
            pltpu.SMEM(lengths.shape, jnp.int32),
            pltpu.VMEM(tokens.shape, BF16),
            pltpu.VMEM((OWN, width), BF16),
            pltpu.VMEM((PR, HD), F32),
            pltpu.VMEM((width,), BF16),
            pltpu.VMEM((width, qcols), BF16),
            pltpu.VMEM((width, kvcols), BF16),
            pltpu.VMEM((qcols, width), BF16),
            pltpu.VMEM((lmax, KV_HEADS * HD), BF16),
            pltpu.VMEM((KV_HEADS * HD, lmax), BF16),
            pltpu.VMEM((lmax, KV_HEADS * HD), BF16),
            pltpu.VMEM((rows, width), BF16),
            pltpu.VMEM((rows // 2, width), BF16),
            pltpu.VMEM((8, HD), F32),
            pltpu.VMEM((NH - 1, 8, HD), F32),
            pltpu.VMEM((NF, 8, HD), F32),
            pltpu.VMEM((NY, NY, PR, qcols + kvcols), F32),
            pltpu.VMEM((2, NY, PR // 2, qcols + kvcols), F32),
            pltpu.VMEM((2, NY, PR // 2, qcols + kvcols), F32),
            pltpu.VMEM((2, NY, PR // 2, qcols + kvcols), F32),
            pltpu.VMEM((2, NY, PR // 2, qcols + kvcols), F32),
            pltpu.VMEM((2, NY - 1, PR // 2, qcols + kvcols), F32),
            pltpu.VMEM((NF * PR, HD), F32),
            pltpu.VMEM((NF, 2 * PR, HD), BF16),
            pltpu.VMEM((NF, 2 * PR, HD), BF16),
            pltpu.VMEM((HD, KV_HEADS * HD), BF16),
            pltpu.VMEM((HD, KV_HEADS * HD), BF16),
            pltpu.VMEM((8, 2 * KV_HEADS * HD), F32),
            pltpu.VMEM((KV_HEADS * OWN, lmax), F32),
            pltpu.VMEM((NF, PR, HD), BF16),
            pltpu.VMEM((2, 2, NF, PR, HD), BF16),
            pltpu.VMEM((NF * PR, HD), F32),
            pltpu.VMEM((2, 2, NY, PR, qcols), BF16),
            pltpu.VMEM((rows, width), F32),
            pltpu.VMEM((2, NX, OWN, width), BF16),
            pltpu.VMEM((NF - 1, OWN, width), BF16),
            dma((8,)),
            dma((CACHE_COPIES,)),
            dma((CACHE_COPIES,)),
            dma((NX - 1,)), dma((NX - 1,)),
            dma((NX,)), dma((NX,)),
            dma((NH - 1,)), dma((NH - 1,)),
            dma((NF - 1,)), dma((NF - 1,)),
            dma((2, 2, 6)), dma((2, 2, 6)),
            dma((2, 2, NY - 1)), dma((2, 2, NY - 1)),
            dma((NF - 1,)), dma((NF - 1,)),
            dma((NY,)), dma((2, 2)),
            dma((2, 2, NY - 1)), dma((2, 2, NY - 1)),
            dma((2, NX)), dma((NF - 1,)),
        ],
        compiler_params=pltpu.CompilerParams(
            collective_id=0, has_side_effects=True, vmem_limit_bytes=48 * 2**20
        ),
        name="decode_block",
    )(
        *[
            pltpu.with_memory_space_constraint(array, pltpu.HBM)
            for array in (
                lengths, freq, tokens, norm_gain, query_weight, w_keyval, w_out,
                cache_keys, cache_values,
            )
        ],
    )
    return pl.pallas_call(
        hand_out,
        out_shape=(
            jax.ShapeDtypeStruct(tokens.shape, BF16),
            jax.ShapeDtypeStruct((1, STEPS, 2 * KV_HEADS * HD), BF16),
        ),
        in_specs=[vmem_spec],
        out_specs=(any_spec, any_spec),
        scratch_shapes=[dma((2,))],
        name="hand_out",
    )(pltpu.with_memory_space_constraint(results, pltpu.VMEM))


def solution(mesh):
    in_specs = (
        P("ffn", None, "hid"),
        P("hid"),
        P("hid", "ffn"),
        P("hid", "ffn"),
        P("ffn", "hid"),
        P(("hid", "ffn"), None, None),
        P(("hid", "ffn"), None, None),
        P(),
    )
    out_specs = (P("ffn", None, "hid"), P(("hid", "ffn"), None, None))
    return jax.shard_map(body, mesh=mesh, in_specs=in_specs, out_specs=out_specs, check_vma=False)
```

```python
import functools

import jax
import jax.numpy as jnp
import numpy as np
from jax import lax
from jax.experimental import pallas as pl
from jax.experimental.pallas import tpu as pltpu
from jax.sharding import PartitionSpec as P

MESH = pl.DeviceIdType.MESH
F32 = jnp.float32
BF16 = jnp.bfloat16

HEADS = 64
KV_HEADS = 4
HD = 128
STEPS = 2
EPSILON = 1e-05
ROPE_BASE = 500000.0
SCALE = HD ** (-0.5) * 1.4426950408889634
MASKED = -1e30

NH = 16
NF = 8
NX = 4
NY = 4
TURN = 1024
OWN = 32
PR = 16
CHUNK = 2048
CACHE_COPIES = 8
PAIRS = KV_HEADS // 2


def remote(src, dst, send_sem, recv_sem, device):
    return pltpu.make_async_remote_copy(
        src_ref=src,
        dst_ref=dst,
        send_sem=send_sem,
        recv_sem=recv_sem,
        device_id=device,
        device_id_type=MESH,
    )


def rotate(vectors, cosine, sine):
    return vectors * cosine + pltpu.roll(vectors, HD // 2, 1) * sine


def kernel(
    lengths_hbm, freq, tokens, gain, wq, wkv, wout, cache_k, cache_v,
    results,
    lengths, raw_v, tok_v, freq_v, gain_v, wq_v, wkv_v, wout_v, k_v, k_t, v_v,
    x_all, normed, ss_own, ss_recv, tot_all, part, line_recv, mine, mine_recv,
    spread, msg, qkv, kx, vx, ne, scores, att_send, att_recv, att_f32, rows_all,
    opart, fin_send, fin_recv,
    local_sem, k_sem, v_sem,
    tok_ssem, tok_rsem, fwd_ssem, fwd_rsem, ss_ssem, ss_rsem, tot_ssem, tot_rsem,
    ring_ssem, ring_rsem, stage_ssem, stage_rsem, msg_ssem, msg_rsem, att_ssem, att_rsem, line_ssem, line_rsem,
    fin_ssem, fin_rsem,
):
    h = lax.axis_index("hid")
    f = lax.axis_index("ffn")
    z = lax.div(h, NY)
    y = lax.rem(h, NY)
    cx = lax.div(f, 2)
    core = lax.rem(f, 2)
    sib = f + 1 - 2 * core
    lmax = cache_k.shape[1]

    barrier = pltpu.get_barrier_semaphore()
    tokens_load = pltpu.make_async_copy(tokens, raw_v, local_sem.at[0])
    tokens_load.start()

    for k in range(1, NF):
        pl.semaphore_signal(
            barrier, inc=1, device_id=(h, lax.rem(f + k, NF)), device_id_type=MESH
        )
    for k in range(1, NH):
        pl.semaphore_signal(
            barrier, inc=1, device_id=(lax.rem(h + k, NH), f), device_id_type=MESH
        )

    loads = []
    for i, (src, dst) in enumerate(
        [(gain, gain_v), (freq, freq_v), (wq, wq_v), (wkv, wkv_v), (lengths_hbm, lengths)]
    ):
        copy = pltpu.make_async_copy(src, dst, local_sem.at[1 + i])
        copy.start()
        loads.append(copy)
    span = lmax // CACHE_COPIES
    k_loads = []
    for i in range(CACHE_COPIES):
        copy = pltpu.make_async_copy(
            cache_k.at[0, pl.ds(i * span, span)], k_v.at[pl.ds(i * span, span)], k_sem.at[i]
        )
        copy.start()
        k_loads.append(copy)
    v_loads = []
    for i in range(CACHE_COPIES):
        copy = pltpu.make_async_copy(
            cache_v.at[0, pl.ds(i * span, span)], v_v.at[pl.ds(i * span, span)], v_sem.at[i]
        )
        copy.start()
        v_loads.append(copy)
    wout_load = pltpu.make_async_copy(wout, wout_v, local_sem.at[6])

    def turn_keys(quarter):
        for copy in k_loads[2 * quarter : 2 * quarter + 2]:
            copy.wait()

        def turn(i, carry):
            rows = pl.ds(pl.multiple_of(quarter * 2 * span + i * TURN, TURN), TURN)
            k_t[:, rows] = k_v[rows, :].T
            return carry

        lax.fori_loop(0, 2 * span // TURN, turn, 0)

    tokens_load.wait()
    x_f32 = raw_v[...].astype(F32).reshape(tok_v.shape)
    x_own = x_f32.astype(BF16)
    tok_v[...] = x_own
    pl.semaphore_wait(barrier, NH + NF - 2)

    def block(index):
        return x_all.at[pl.ds(pl.multiple_of(index * OWN, OWN), OWN)]

    tok_copies = []
    for k in (1, 3, 2):
        peer = 2 * lax.rem(cx + k, NX) + core
        copy = remote(tok_v, block(f), tok_ssem.at[k - 1], tok_rsem.at[k - 1], (h, peer))
        copy.start()
        tok_copies.append((k, copy))
    opposite = 2 * lax.rem(cx + 2, NX) + 1 - core
    fwd_copies = [
        remote(tok_v, block(f), fwd_ssem.at[0], fwd_rsem.at[0], (h, sib)),
        remote(tok_v, block(f), fwd_ssem.at[2], fwd_rsem.at[2], (h, opposite)),
    ]
    for copy in fwd_copies:
        copy.start()

    sums = jnp.sum(x_f32 * x_f32, axis=1, keepdims=True)
    row_id = lax.broadcasted_iota(jnp.int32, (OWN, HD), 0)
    lane_id = lax.broadcasted_iota(jnp.int32, (OWN, HD), 1)
    diagonal = row_id == lane_id
    own_sums = jnp.sum(jnp.where(diagonal, sums, 0.0), axis=0, keepdims=True)
    ss_own[...] = jnp.broadcast_to(own_sums, (8, HD))

    def ss_copy(k):
        return remote(
            ss_own, ss_recv.at[k - 1], ss_ssem.at[k - 1], ss_rsem.at[k - 1],
            (lax.rem(h + k, NH), f),
        )

    for k in range(1, NH):
        ss_copy(k).start()
    x_all[pl.ds(pl.multiple_of(f * OWN, OWN), OWN), :] = x_own

    total = ss_own[...]
    for k in range(1, NH):
        ss_copy(k).wait_recv()
        total = total + ss_recv[k - 1]
    tot_all[f] = total
    tot_copies = []
    for k in range(1, NF):
        copy = remote(
            tot_all.at[f], tot_all.at[f], tot_ssem.at[k - 1], tot_rsem.at[k - 1],
            (h, lax.rem(f + k, NF)),
        )
        copy.start()
        tot_copies.append(copy)
    for k, tok_copy in tok_copies:
        tok_copy.wait_recv()
        if k != 2:
            came = 2 * lax.rem(cx + NX - k, NX) + core
            copy = remote(block(came), block(came), fwd_ssem.at[k], fwd_rsem.at[k], (h, sib))
            copy.start()
            fwd_copies.append(copy)

    for copy in tot_copies:
        copy.wait_recv()
    loads[0].wait()
    width = x_all.shape[1]
    qcols = wq_v.shape[1]
    full = width * NH
    gain_row = gain_v[...].astype(F32).reshape(1, width)

    def project(parity):
        for x in range(NX):
            b = 2 * x + parity
            lane_sums = tot_all[b][0:1, :]
            row_sums = jnp.sum(jnp.where(diagonal, lane_sums, 0.0), axis=1, keepdims=True)
            inverse = lax.rsqrt(row_sums / full + EPSILON)
            normed[x * OWN : (x + 1) * OWN, :] = (
                block(b)[...].astype(F32) * inverse * gain_row
            ).astype(BF16)
        lhs = normed[...]
        for cols, weights in ((slice(0, qcols), wq_v), (slice(qcols, None), wkv_v)):
            product = jnp.dot(lhs, weights[...], preferred_element_type=F32)
            part[:, pl.ds(2 * parity, 2), :, cols] = product.reshape(NX, 2, PR, product.shape[1])

    loads[2].wait()
    loads[3].wait()
    project(core)

    loads[4].wait()
    length = lengths[h * NF + f]
    step_of = lax.div(lax.broadcasted_iota(jnp.int32, (PR, HD), 0), 8)
    loads[1].wait()
    angles = (step_of + length).astype(F32) * freq_v[...]
    cosine = jnp.cos(angles)
    sine = jnp.sin(angles)
    sine = jnp.where(
        lax.broadcasted_iota(jnp.int32, (PR, HD), 1) < HD // 2, -sine, sine
    )
    kx[...] = jnp.zeros_like(kx)
    vx[...] = jnp.zeros_like(vx)

    for copy in fwd_copies:
        copy.wait_recv()
    project(1 - core)

    half = PR // 2
    here = (y, z)

    def to_line(side, q):
        return (z * NY + q, f) if side == 0 else (q * NY + y, f)

    def view(side, q):
        return part.at[:, q, pl.ds(0, half)] if side == 0 else part.at[q, :, pl.ds(half, half)]

    moves = [[], []]
    for k in (2, 1, 3):
        for side in range(2):
            q = lax.rem(here[side] + k, NY)
            copy = remote(
                view(side, q), line_recv.at[side, k - 1],
                ring_ssem.at[side, k - 1], ring_rsem.at[side, k - 1], to_line(side, q),
            )
            copy.start()
            moves[side].append(copy)
    for k in range(1, NH):
        ss_copy(k).wait_send()
    for copy in tot_copies + fwd_copies + [copy for _, copy in tok_copies]:
        copy.wait_send()
    turn_keys(0)
    turn_keys(1)
    turn_keys(2)
    stages = [[], []]
    for side in range(2):
        for copy in moves[side]:
            copy.wait_recv()
        mine[side] = (
            view(side, here[side])[...]
            + line_recv[side, 0] + line_recv[side, 1] + line_recv[side, 2]
        )
        for k in (2, 1, 3):
            q = lax.rem(here[1 - side] + k, NY)
            copy = remote(
                mine.at[side, q], mine_recv.at[side, k - 1],
                stage_ssem.at[side, k - 1], stage_rsem.at[side, k - 1], to_line(1 - side, q),
            )
            copy.start()
            stages[side].append(copy)
    turn_keys(3)
    halves = []
    for side in range(2):
        total = mine[side, here[1 - side]]
        for copy in stages[side]:
            copy.wait_recv()
        for k in range(NY - 1):
            total = total + mine_recv[side, k]
        halves.append(total)
    summed = jnp.concatenate(halves, axis=0)

    for j in range(8):
        spread[pl.ds(j, PR, stride=8), :] = summed[:, j * HD : (j + 1) * HD]
    msg[:, :PR, :] = spread[...].reshape(NF, PR, HD).astype(BF16)
    spread[...] = jnp.zeros_like(spread)
    spread[pl.ds(0, PR, stride=8), :] = summed[:, qcols:]
    msg[:, PR:, :] = spread[...].reshape(NF, PR, HD).astype(BF16)
    qkv[f] = msg[f]
    msg_copies = []
    for k in range(1, NF):
        peer = lax.rem(f + k, NF)
        copy = remote(
            msg.at[peer], qkv.at[f], msg_ssem.at[k - 1], msg_rsem.at[k - 1], (h, peer)
        )
        copy.start()
        msg_copies.append(copy)
    for copy in moves[0] + moves[1] + stages[0] + stages[1]:
        copy.wait_send()
    wout_load.start()
    for copy in msg_copies:
        copy.wait_recv()

    fresh_rows = []
    for i in range(2 * KV_HEADS):
        raw = qkv[i, PR:, :].astype(F32)
        cols = pl.ds((i % KV_HEADS) * HD, HD)
        if i < KV_HEADS:
            raw = rotate(raw, cosine, sine)
            kx[:PR, cols] = raw.astype(BF16)
        else:
            vx[:PR, cols] = raw.astype(BF16)
        fresh_rows.append(raw)

    rotated = [
        rotate(qkv[i, :PR, :].astype(F32), cosine, sine).astype(BF16) for i in range(NF)
    ]
    nothing = jnp.zeros((OWN, HD), BF16)
    queries = []
    for p in range(PAIRS):
        upper = jnp.concatenate(rotated[4 * p : 4 * p + 2], axis=0)
        lower = jnp.concatenate(rotated[4 * p + 2 : 4 * p + 4], axis=0)
        queries.append(
            jnp.concatenate(
                [
                    jnp.concatenate([upper, nothing], axis=1),
                    jnp.concatenate([nothing, lower], axis=1),
                ],
                axis=0,
            )
        )
    pair_rows, pair_cols = 2 * OWN, 2 * HD
    lane = lax.broadcasted_iota(jnp.int32, (pair_rows, HD), 1)
    step_row = lax.rem(lax.div(lax.broadcasted_iota(jnp.int32, (pair_rows, HD), 0), 8), 2)
    fresh_live = (lane == 0) | ((lane == 8) & (step_row == 1))
    nt = (((1,), (1,)), ((), ()))
    for copy in v_loads:
        copy.wait()

    def score(p):
        pair = pl.ds(p * pair_cols, pair_cols)
        fresh = lax.dot_general(queries[p], kx[:, pair], nt, preferred_element_type=F32)
        fresh = jnp.where(fresh_live, fresh * SCALE, MASKED)
        high = fresh
        for c in range(lmax // CHUNK):
            rows = pl.ds(c * CHUNK, CHUNK)
            s = jnp.dot(queries[p], k_t[pair, rows], preferred_element_type=F32) * SCALE
            if (c + 1) * CHUNK > lmax // 4:
                position = lax.broadcasted_iota(jnp.int32, (8, CHUNK), 1) + c * CHUNK
                cap = jnp.where(position < length, -MASKED, MASKED)
                s = jnp.minimum(s, jnp.concatenate([cap] * (pair_rows // 8), axis=0))
            scores[pl.ds(p * pair_rows, pair_rows), rows] = s
            for t in range(CHUNK // HD):
                high = jnp.maximum(high, s[:, t * HD : (t + 1) * HD])
        peak = jnp.broadcast_to(jnp.max(high, axis=1, keepdims=True), (pair_rows, HD))
        return fresh, peak

    def attend(p, fresh, peak):
        pair = pl.ds(p * pair_cols, pair_cols)
        weights = jnp.exp2(fresh - peak).astype(BF16)
        total = weights.astype(F32)
        acc = jnp.dot(weights, vx[:, pair], preferred_element_type=F32)
        for c in range(lmax // CHUNK):
            rows = pl.ds(c * CHUNK, CHUNK)
            s = scores[pl.ds(p * pair_rows, pair_rows), rows]
            pieces = []
            for t in range(CHUNK // HD):
                piece = jnp.exp2(s[:, t * HD : (t + 1) * HD] - peak).astype(BF16)
                total = total + piece.astype(F32)
                pieces.append(piece)
            acc = acc + jnp.dot(
                jnp.concatenate(pieces, axis=1), v_v[rows, pair], preferred_element_type=F32
            )
        weight_sum = jnp.sum(total, axis=1, keepdims=True)
        for i in range(2):
            rows = slice(i * OWN, (i + 1) * OWN)
            attended = acc[rows, i * HD : (i + 1) * HD] / weight_sum[rows]
            attended = attended.astype(BF16)
            att_send[4 * p + 2 * i] = attended[:PR]
            att_send[4 * p + 2 * i + 1] = attended[PR:]

    odd = lax.rem(y + z, 2)
    slot = lax.rem(lax.div(y, 2) + lax.div(z, 2), 2)

    def send_attended(p):
        for m in range(4):
            peer = 4 * p + lax.rem(f + m, 4)
            landing = att_recv.at[odd, slot, f]

            @pl.when(peer == f)
            def _():
                pltpu.make_async_copy(
                    att_send.at[f], landing, att_rsem.at[odd, slot]
                ).start()

            for k in range(NY):
                chip = lax.rem(z + odd * k, NY) * NY + lax.rem(y + (1 - odd) * k, NY)
                copy = remote(
                    att_send.at[peer], landing, att_ssem.at[k], att_rsem.at[odd, slot],
                    (chip, peer),
                )
                if k == 0:
                    pl.when(peer != f)(copy.start)
                else:
                    copy.start()

    scored = [score(p) for p in range(PAIRS)]
    for p in range(PAIRS):
        attend(p, *scored[p])
        send_attended(p)

    for i in range(2 * KV_HEADS):
        ne[0:1, i * HD : (i + 1) * HD] = fresh_rows[i][0:1]
        ne[1:2, i * HD : (i + 1) * HD] = fresh_rows[i][8:9]
    results[PR:, :, :] = ne[0:2, :].reshape(1, STEPS, ne.shape[1]).astype(BF16)

    line_copies = [[], []]
    for part_id in range(2):
        for side in range(2):
            whole = att_recv.at[side, part_id]
            pltpu.make_async_copy(whole, whole, att_rsem.at[side, part_id]).wait()
            pos = (z, y)[side]
            att_f32[...] = att_recv[side, part_id].astype(F32).reshape(NF * PR, HD)
            for j in range(8):
                rows_all[part_id, side, pos, :, j * HD : (j + 1) * HD] = att_f32[
                    pl.ds(j, PR, stride=8), :
                ].astype(BF16)
            mine_rows = rows_all.at[part_id, side, pos]
            for k in range(1, NY):
                q = lax.rem(pos + k, NY)
                device = (q * NY + y, f) if side == 0 else (z * NY + q, f)
                copy = remote(
                    mine_rows, mine_rows,
                    line_ssem.at[part_id, side, k - 1], line_rsem.at[part_id, side, k - 1],
                    device,
                )
                copy.start()
                line_copies[part_id].append(copy)
    wout_load.wait()
    for copy in msg_copies:
        copy.wait_send()
    for k in range(NY):
        sent = att_send.at[pl.ds(0, NF - 1)] if k == 0 else att_send
        pltpu.make_async_copy(sent, sent, att_ssem.at[k]).wait()

    def out_rows(index):
        return pl.ds(pl.multiple_of(index * OWN, OWN), OWN)

    fin_copies = []
    for part_id in range(2):
        for copy in line_copies[part_id]:
            copy.wait_recv()
        product = jnp.dot(
            rows_all[part_id].reshape(NH * PR // 2, wout_v.shape[0]),
            wout_v[...],
            preferred_element_type=F32,
        )
        for side in range(2):
            for q in range(NY):
                far = 2 * ((part_id + q // 2) % 2) + (q + side) % 2
                home = q * NY + far if side == 0 else far * NY + q
                first = (side * NY + q) * PR
                opart[home * PR : (home + 1) * PR, :] = product[first : first + PR]
        for k in (2, 1, 3, 0):
            x = lax.rem(cx + k, NX)
            peer = 2 * x + lax.rem(part_id + lax.div(x, 2), 2)
            hop = lax.rem(peer - f + NF, NF)
            there = lax.rem(hop + NF - 1, NF)
            fin_send[part_id, k] = opart[out_rows(peer), :].astype(BF16)
            copy = remote(
                fin_send.at[part_id, k], fin_recv.at[there],
                fin_ssem.at[part_id, k], fin_rsem.at[there], (h, peer),
            )
            fin_copies.append((k, hop, copy))
            if k == 0:
                pl.when(hop != 0)(copy.start)
            else:
                copy.start()
    for copies in line_copies:
        for copy in copies:
            copy.wait_send()
    result = opart[out_rows(f), :]
    for k in range(1, NF):
        pltpu.make_async_copy(
            fin_recv.at[k - 1], fin_recv.at[k - 1], fin_rsem.at[k - 1]
        ).wait()
        result = result + fin_recv[k - 1].astype(F32)
    results[:PR, :, :] = result.reshape(PR, STEPS, result.shape[1]).astype(BF16)
    for k, hop, copy in fin_copies:
        if k == 0:
            pl.when(hop != 0)(copy.wait_send)
        else:
            copy.wait_send()


def hand_out(results, out, entries, sem):
    rows = out.shape[0]
    copies = [
        pltpu.make_async_copy(results.at[pl.ds(0, rows)], out, sem.at[0]),
        pltpu.make_async_copy(results.at[pl.ds(rows, 1)], entries, sem.at[1]),
    ]
    for copy in copies:
        copy.start()
    for copy in copies:
        copy.wait()


def body(tokens, norm_gain, query_weight, w_keyval, w_out, cache_keys, cache_values, lengths):
    width = tokens.shape[2]
    lmax = cache_keys.shape[1]
    qcols = query_weight.shape[1]
    kvcols = w_keyval.shape[1]
    halves = np.arange(HD // 2, dtype=np.float64) * (2.0 / HD)
    freq = (ROPE_BASE ** (-halves)).astype(np.float32)
    freq = jnp.asarray(np.tile(np.concatenate([freq, freq])[None, :], (PR, 1)))
    any_spec = pl.BlockSpec(memory_space=pl.ANY)
    hbm_spec = pl.BlockSpec(memory_space=pltpu.HBM)
    vmem_spec = pl.BlockSpec(memory_space=pltpu.VMEM)
    dma = pltpu.SemaphoreType.DMA
    rows = NH * PR
    results = pl.pallas_call(
        kernel,
        out_shape=pltpu.VMEM((PR + 1, STEPS, width), BF16),
        in_specs=[hbm_spec] * 9,
        out_specs=vmem_spec,
        scratch_shapes=[
            pltpu.SMEM(lengths.shape, jnp.int32),
            pltpu.VMEM(tokens.shape, BF16),
            pltpu.VMEM((OWN, width), BF16),
            pltpu.VMEM((PR, HD), F32),
            pltpu.VMEM((width,), BF16),
            pltpu.VMEM((width, qcols), BF16),
            pltpu.VMEM((width, kvcols), BF16),
            pltpu.VMEM((qcols, width), BF16),
            pltpu.VMEM((lmax, KV_HEADS * HD), BF16),
            pltpu.VMEM((KV_HEADS * HD, lmax), BF16),
            pltpu.VMEM((lmax, KV_HEADS * HD), BF16),
            pltpu.VMEM((rows, width), BF16),
            pltpu.VMEM((rows // 2, width), BF16),
            pltpu.VMEM((8, HD), F32),
            pltpu.VMEM((NH - 1, 8, HD), F32),
            pltpu.VMEM((NF, 8, HD), F32),
            pltpu.VMEM((NY, NY, PR, qcols + kvcols), F32),
            pltpu.VMEM((2, NY - 1, NY, PR // 2, qcols + kvcols), F32),
            pltpu.VMEM((2, NY, PR // 2, qcols + kvcols), F32),
            pltpu.VMEM((2, NY - 1, PR // 2, qcols + kvcols), F32),
            pltpu.VMEM((NF * PR, HD), F32),
            pltpu.VMEM((NF, 2 * PR, HD), BF16),
            pltpu.VMEM((NF, 2 * PR, HD), BF16),
            pltpu.VMEM((HD, KV_HEADS * HD), BF16),
            pltpu.VMEM((HD, KV_HEADS * HD), BF16),
            pltpu.VMEM((8, 2 * KV_HEADS * HD), F32),
            pltpu.VMEM((KV_HEADS * OWN, lmax), F32),
            pltpu.VMEM((NF, PR, HD), BF16),
            pltpu.VMEM((2, 2, NF, PR, HD), BF16),
            pltpu.VMEM((NF * PR, HD), F32),
            pltpu.VMEM((2, 2, NY, PR, qcols), BF16),
            pltpu.VMEM((rows, width), F32),
            pltpu.VMEM((2, NX, OWN, width), BF16),
            pltpu.VMEM((NF - 1, OWN, width), BF16),
            dma((8,)),
            dma((CACHE_COPIES,)),
            dma((CACHE_COPIES,)),
            dma((NX - 1,)), dma((NX - 1,)),
            dma((NX,)), dma((NX,)),
            dma((NH - 1,)), dma((NH - 1,)),
            dma((NF - 1,)), dma((NF - 1,)),
            dma((2, NY - 1)), dma((2, NY - 1)),
            dma((2, NY - 1)), dma((2, NY - 1)),
            dma((NF - 1,)), dma((NF - 1,)),
            dma((NY,)), dma((2, 2)),
            dma((2, 2, NY - 1)), dma((2, 2, NY - 1)),
            dma((2, NX)), dma((NF - 1,)),
        ],
        compiler_params=pltpu.CompilerParams(
            collective_id=0, has_side_effects=True, vmem_limit_bytes=48 * 2**20
        ),
        name="decode_block",
    )(
        *[
            pltpu.with_memory_space_constraint(array, pltpu.HBM)
            for array in (
                lengths, freq, tokens, norm_gain, query_weight, w_keyval, w_out,
                cache_keys, cache_values,
            )
        ],
    )
    return pl.pallas_call(
        hand_out,
        out_shape=(
            jax.ShapeDtypeStruct(tokens.shape, BF16),
            jax.ShapeDtypeStruct((1, STEPS, 2 * KV_HEADS * HD), BF16),
        ),
        in_specs=[vmem_spec],
        out_specs=(any_spec, any_spec),
        scratch_shapes=[dma((2,))],
        name="hand_out",
    )(pltpu.with_memory_space_constraint(results, pltpu.VMEM))


def solution(mesh):
    in_specs = (
        P("ffn", None, "hid"),
        P("hid"),
        P("hid", "ffn"),
        P("hid", "ffn"),
        P("ffn", "hid"),
        P(("hid", "ffn"), None, None),
        P(("hid", "ffn"), None, None),
        P(),
    )
    out_specs = (P("ffn", None, "hid"), P(("hid", "ffn"), None, None))
    return jax.shard_map(body, mesh=mesh, in_specs=in_specs, out_specs=out_specs, check_vma=False)
```

```python
import functools

import jax
import jax.numpy as jnp
import numpy as np
from jax import lax
from jax.experimental import pallas as pl
from jax.experimental.pallas import tpu as pltpu
from jax.sharding import PartitionSpec as P

MESH = pl.DeviceIdType.MESH
F32 = jnp.float32
BF16 = jnp.bfloat16

HEADS = 64
KV_HEADS = 4
HD = 128
STEPS = 2
EPSILON = 1e-05
ROPE_BASE = 500000.0
SCALE = HD ** (-0.5) * 1.4426950408889634
MASKED = -1e30

NH = 16
NF = 8
NX = 4
NY = 4
TURN = 1024
GROUPS = (((0, 256), (256, 256)), ((512, 384), (896, 256)))
OWN = 32
PR = 16
CHUNK = 2048
CACHE_COPIES = 8
PAIRS = KV_HEADS // 2


def remote(src, dst, send_sem, recv_sem, device):
    return pltpu.make_async_remote_copy(
        src_ref=src,
        dst_ref=dst,
        send_sem=send_sem,
        recv_sem=recv_sem,
        device_id=device,
        device_id_type=MESH,
    )


def rotate(vectors, cosine, sine):
    return vectors * cosine + pltpu.roll(vectors, HD // 2, 1) * sine


def kernel(
    lengths_hbm, freq, tokens, gain, wq, wkv, wout, cache_k, cache_v,
    results,
    lengths, raw_v, tok_v, freq_v, gain_v, wq_v, wkv_v, wout_v, k_v, k_t, v_v,
    x_all, normed, ss_own, ss_recv, tot_all, part, relay, left, right, mine, mine_recv,
    spread, msg, qkv, kx, vx, ne, scores, att_send, att_recv, att_f32, rows_all,
    opart, fin_send, fin_recv,
    local_sem, k_sem, v_sem,
    tok_ssem, tok_rsem, fwd_ssem, fwd_rsem, ss_ssem, ss_rsem, tot_ssem, tot_rsem,
    ring_ssem, ring_rsem, stage_ssem, stage_rsem, msg_ssem, msg_rsem, att_ssem, att_rsem, line_ssem, line_rsem,
    fin_ssem, fin_rsem,
):
    h = lax.axis_index("hid")
    f = lax.axis_index("ffn")
    z = lax.div(h, NY)
    y = lax.rem(h, NY)
    cx = lax.div(f, 2)
    core = lax.rem(f, 2)
    sib = f + 1 - 2 * core
    lmax = cache_k.shape[1]

    barrier = pltpu.get_barrier_semaphore()
    tokens_load = pltpu.make_async_copy(tokens, raw_v, local_sem.at[0])
    tokens_load.start()

    for k in range(1, NF):
        pl.semaphore_signal(
            barrier, inc=1, device_id=(h, lax.rem(f + k, NF)), device_id_type=MESH
        )
    for k in range(1, NH):
        pl.semaphore_signal(
            barrier, inc=1, device_id=(lax.rem(h + k, NH), f), device_id_type=MESH
        )

    loads = []
    for i, (src, dst) in enumerate(
        [(gain, gain_v), (freq, freq_v), (wq, wq_v), (wkv, wkv_v), (lengths_hbm, lengths)]
    ):
        copy = pltpu.make_async_copy(src, dst, local_sem.at[1 + i])
        copy.start()
        loads.append(copy)
    span = lmax // CACHE_COPIES
    k_loads = []
    for i in range(CACHE_COPIES):
        copy = pltpu.make_async_copy(
            cache_k.at[0, pl.ds(i * span, span)], k_v.at[pl.ds(i * span, span)], k_sem.at[i]
        )
        copy.start()
        k_loads.append(copy)
    v_loads = []
    for i in range(CACHE_COPIES):
        copy = pltpu.make_async_copy(
            cache_v.at[0, pl.ds(i * span, span)], v_v.at[pl.ds(i * span, span)], v_sem.at[i]
        )
        copy.start()
        v_loads.append(copy)
    wout_load = pltpu.make_async_copy(wout, wout_v, local_sem.at[6])

    def turn_keys(quarter):
        for copy in k_loads[2 * quarter : 2 * quarter + 2]:
            copy.wait()

        def turn(i, carry):
            rows = pl.ds(pl.multiple_of(quarter * 2 * span + i * TURN, TURN), TURN)
            k_t[:, rows] = k_v[rows, :].T
            return carry

        lax.fori_loop(0, 2 * span // TURN, turn, 0)

    tokens_load.wait()
    x_f32 = raw_v[...].astype(F32).reshape(tok_v.shape)
    x_own = x_f32.astype(BF16)
    tok_v[...] = x_own
    pl.semaphore_wait(barrier, NH + NF - 2)

    def block(index):
        return x_all.at[pl.ds(pl.multiple_of(index * OWN, OWN), OWN)]

    tok_copies = []
    for k in (1, 3, 2):
        peer = 2 * lax.rem(cx + k, NX) + core
        copy = remote(tok_v, block(f), tok_ssem.at[k - 1], tok_rsem.at[k - 1], (h, peer))
        copy.start()
        tok_copies.append((k, copy))
    opposite = 2 * lax.rem(cx + 2, NX) + 1 - core
    fwd_copies = [
        remote(tok_v, block(f), fwd_ssem.at[0], fwd_rsem.at[0], (h, sib)),
        remote(tok_v, block(f), fwd_ssem.at[2], fwd_rsem.at[2], (h, opposite)),
    ]
    for copy in fwd_copies:
        copy.start()

    sums = jnp.sum(x_f32 * x_f32, axis=1, keepdims=True)
    row_id = lax.broadcasted_iota(jnp.int32, (OWN, HD), 0)
    lane_id = lax.broadcasted_iota(jnp.int32, (OWN, HD), 1)
    diagonal = row_id == lane_id
    own_sums = jnp.sum(jnp.where(diagonal, sums, 0.0), axis=0, keepdims=True)
    ss_own[...] = jnp.broadcast_to(own_sums, (8, HD))

    def ss_copy(k):
        return remote(
            ss_own, ss_recv.at[k - 1], ss_ssem.at[k - 1], ss_rsem.at[k - 1],
            (lax.rem(h + k, NH), f),
        )

    for k in range(1, NH):
        ss_copy(k).start()
    x_all[pl.ds(pl.multiple_of(f * OWN, OWN), OWN), :] = x_own

    total = ss_own[...]
    for k in range(1, NH):
        ss_copy(k).wait_recv()
        total = total + ss_recv[k - 1]
    tot_all[f] = total
    tot_copies = []
    for k in range(1, NF):
        copy = remote(
            tot_all.at[f], tot_all.at[f], tot_ssem.at[k - 1], tot_rsem.at[k - 1],
            (h, lax.rem(f + k, NF)),
        )
        copy.start()
        tot_copies.append(copy)
    for k, tok_copy in tok_copies:
        tok_copy.wait_recv()
        if k != 2:
            came = 2 * lax.rem(cx + NX - k, NX) + core
            copy = remote(block(came), block(came), fwd_ssem.at[k], fwd_rsem.at[k], (h, sib))
            copy.start()
            fwd_copies.append(copy)

    for copy in tot_copies:
        copy.wait_recv()
    loads[0].wait()
    width = x_all.shape[1]
    qcols = wq_v.shape[1]
    full = width * NH
    gain_row = gain_v[...].astype(F32).reshape(1, width)

    def project(parity):
        for x in range(NX):
            b = 2 * x + parity
            lane_sums = tot_all[b][0:1, :]
            row_sums = jnp.sum(jnp.where(diagonal, lane_sums, 0.0), axis=1, keepdims=True)
            inverse = lax.rsqrt(row_sums / full + EPSILON)
            normed[x * OWN : (x + 1) * OWN, :] = (
                block(b)[...].astype(F32) * inverse * gain_row
            ).astype(BF16)
        lhs = normed[...]
        for cols, weights in ((slice(0, qcols), wq_v), (slice(qcols, None), wkv_v)):
            product = jnp.dot(lhs, weights[...], preferred_element_type=F32)
            part[:, pl.ds(2 * parity, 2), :, cols] = product.reshape(NX, 2, PR, product.shape[1])

    loads[2].wait()
    loads[3].wait()
    project(core)

    loads[4].wait()
    length = lengths[h * NF + f]
    step_of = lax.div(lax.broadcasted_iota(jnp.int32, (PR, HD), 0), 8)
    loads[1].wait()
    angles = (step_of + length).astype(F32) * freq_v[...]
    cosine = jnp.cos(angles)
    sine = jnp.sin(angles)
    sine = jnp.where(
        lax.broadcasted_iota(jnp.int32, (PR, HD), 1) < HD // 2, -sine, sine
    )
    kx[...] = jnp.zeros_like(kx)
    vx[...] = jnp.zeros_like(vx)

    for copy in fwd_copies:
        copy.wait_recv()
    project(1 - core)

    half = PR // 2

    def ring(side):
        pos = (y, z)[side]

        def device(q):
            return (z * NY + q, f) if side == 0 else (q * NY + y, f)

        def view(q, cols):
            if side == 0:
                return part.at[:, q, pl.ds(0, half), cols]
            return part.at[q, :, pl.ds(half, half), cols]

        return pos, device, view

    moves = {}
    for g, (low, high) in enumerate(GROUPS):
        for side in range(2):
            pos, device, view = ring(side)
            nxt, prv, far = lax.rem(pos + 1, NY), lax.rem(pos + 3, NY), lax.rem(pos + 2, NY)
            plan = [
                (far, low, relay, nxt),
                (far, high, relay, prv),
                (nxt, high, left, nxt),
                (prv, low, right, prv),
            ]
            moves[g, side] = [
                remote(
                    view(q, pl.ds(*cols)), dst.at[side, :, :, pl.ds(*cols)],
                    ring_ssem.at[g, side, i], ring_rsem.at[g, side, i], device(to),
                )
                for i, (q, cols, dst, to) in enumerate(plan)
            ]
    for first in (0, 2):
        for g in range(len(GROUPS)):
            for side in range(2):
                for copy in moves[g, side][first : first + 2]:
                    copy.start()
    for k in range(1, NH):
        ss_copy(k).wait_send()
    for copy in tot_copies + fwd_copies + [copy for _, copy in tok_copies]:
        copy.wait_send()
    turn_keys(0)
    for g, (low, high) in enumerate(GROUPS):
        for side in range(2):
            pos, device, view = ring(side)
            nxt, prv = lax.rem(pos + 1, NY), lax.rem(pos + 3, NY)
            for i, (to, cols, dst) in enumerate(((nxt, low, left), (prv, high, right))):
                cols = pl.ds(*cols)
                moves[g, side][i].wait_recv()
                passed = relay.at[side, :, :, cols]
                passed[...] = passed[...] + view(to, cols)[...]
                copy = remote(
                    passed, dst.at[side, :, :, cols],
                    ring_ssem.at[g, side, 4 + i], ring_rsem.at[g, side, 4 + i], device(to),
                )
                copy.start()
                moves[g, side].append(copy)
    turn_keys(1)
    stages = {}
    for g, (low, high) in enumerate(GROUPS):
        cols = pl.ds(low[0], low[1] + high[1])
        for side in range(2):
            pos, device, view = ring(side)
            for copy in moves[g, side][2:]:
                copy.wait_recv()
            mine[side, :, :, cols] = (
                view(pos, cols)[...] + left[side, :, :, cols] + right[side, :, :, cols]
            )
            other, other_device, _ = ring(1 - side)
            stages[g, side] = []
            for k in (1, 3, 2):
                peer = lax.rem(other + k, NY)
                copy = remote(
                    mine.at[side, peer, :, cols], mine_recv.at[side, k - 1, :, cols],
                    stage_ssem.at[g, side, k - 1], stage_rsem.at[g, side, k - 1],
                    other_device(peer),
                )
                copy.start()
                stages[g, side].append(copy)
    turn_keys(2)
    groups = []
    for g, (low, high) in enumerate(GROUPS):
        cols = pl.ds(low[0], low[1] + high[1])
        halves = []
        for side in range(2):
            other = ring(1 - side)[0]
            total = mine[side, other, :, cols]
            for copy in stages[g, side]:
                copy.wait_recv()
            for k in range(NY - 1):
                total = total + mine_recv[side, k, :, cols]
            halves.append(total)
        groups.append(jnp.concatenate(halves, axis=0))
    summed = jnp.concatenate(groups, axis=1)

    for j in range(8):
        spread[pl.ds(j, PR, stride=8), :] = summed[:, j * HD : (j + 1) * HD]
    msg[:, :PR, :] = spread[...].reshape(NF, PR, HD).astype(BF16)
    spread[...] = jnp.zeros_like(spread)
    spread[pl.ds(0, PR, stride=8), :] = summed[:, qcols:]
    msg[:, PR:, :] = spread[...].reshape(NF, PR, HD).astype(BF16)
    qkv[f] = msg[f]
    msg_copies = []
    for k in range(1, NF):
        peer = lax.rem(f + k, NF)
        copy = remote(
            msg.at[peer], qkv.at[f], msg_ssem.at[k - 1], msg_rsem.at[k - 1], (h, peer)
        )
        copy.start()
        msg_copies.append(copy)
    for key in moves:
        for copy in moves[key] + stages[key]:
            copy.wait_send()
    wout_load.start()
    turn_keys(3)
    for copy in msg_copies:
        copy.wait_recv()

    fresh_rows = []
    for i in range(2 * KV_HEADS):
        raw = qkv[i, PR:, :].astype(F32)
        cols = pl.ds((i % KV_HEADS) * HD, HD)
        if i < KV_HEADS:
            raw = rotate(raw, cosine, sine)
            kx[:PR, cols] = raw.astype(BF16)
        else:
            vx[:PR, cols] = raw.astype(BF16)
        fresh_rows.append(raw)

    rotated = [
        rotate(qkv[i, :PR, :].astype(F32), cosine, sine).astype(BF16) for i in range(NF)
    ]
    nothing = jnp.zeros((OWN, HD), BF16)
    queries = []
    for p in range(PAIRS):
        upper = jnp.concatenate(rotated[4 * p : 4 * p + 2], axis=0)
        lower = jnp.concatenate(rotated[4 * p + 2 : 4 * p + 4], axis=0)
        queries.append(
            jnp.concatenate(
                [
                    jnp.concatenate([upper, nothing], axis=1),
                    jnp.concatenate([nothing, lower], axis=1),
                ],
                axis=0,
            )
        )
    pair_rows, pair_cols = 2 * OWN, 2 * HD
    lane = lax.broadcasted_iota(jnp.int32, (pair_rows, HD), 1)
    step_row = lax.rem(lax.div(lax.broadcasted_iota(jnp.int32, (pair_rows, HD), 0), 8), 2)
    fresh_live = (lane == 0) | ((lane == 8) & (step_row == 1))
    nt = (((1,), (1,)), ((), ()))
    for copy in v_loads:
        copy.wait()

    def score(p):
        pair = pl.ds(p * pair_cols, pair_cols)
        fresh = lax.dot_general(queries[p], kx[:, pair], nt, preferred_element_type=F32)
        fresh = jnp.where(fresh_live, fresh * SCALE, MASKED)
        high = fresh
        for c in range(lmax // CHUNK):
            rows = pl.ds(c * CHUNK, CHUNK)
            s = jnp.dot(queries[p], k_t[pair, rows], preferred_element_type=F32) * SCALE
            if (c + 1) * CHUNK > lmax // 4:
                position = lax.broadcasted_iota(jnp.int32, (8, CHUNK), 1) + c * CHUNK
                cap = jnp.where(position < length, -MASKED, MASKED)
                s = jnp.minimum(s, jnp.concatenate([cap] * (pair_rows // 8), axis=0))
            scores[pl.ds(p * pair_rows, pair_rows), rows] = s
            for t in range(CHUNK // HD):
                high = jnp.maximum(high, s[:, t * HD : (t + 1) * HD])
        peak = jnp.broadcast_to(jnp.max(high, axis=1, keepdims=True), (pair_rows, HD))
        return fresh, peak

    def attend(p, fresh, peak):
        pair = pl.ds(p * pair_cols, pair_cols)
        weights = jnp.exp2(fresh - peak).astype(BF16)
        total = weights.astype(F32)
        acc = jnp.dot(weights, vx[:, pair], preferred_element_type=F32)
        for c in range(lmax // CHUNK):
            rows = pl.ds(c * CHUNK, CHUNK)
            s = scores[pl.ds(p * pair_rows, pair_rows), rows]
            pieces = []
            for t in range(CHUNK // HD):
                piece = jnp.exp2(s[:, t * HD : (t + 1) * HD] - peak).astype(BF16)
                total = total + piece.astype(F32)
                pieces.append(piece)
            acc = acc + jnp.dot(
                jnp.concatenate(pieces, axis=1), v_v[rows, pair], preferred_element_type=F32
            )
        weight_sum = jnp.sum(total, axis=1, keepdims=True)
        for i in range(2):
            rows = slice(i * OWN, (i + 1) * OWN)
            attended = acc[rows, i * HD : (i + 1) * HD] / weight_sum[rows]
            attended = attended.astype(BF16)
            att_send[4 * p + 2 * i] = attended[:PR]
            att_send[4 * p + 2 * i + 1] = attended[PR:]

    odd = lax.rem(y + z, 2)
    slot = lax.rem(lax.div(y, 2) + lax.div(z, 2), 2)

    def send_attended(p):
        for m in range(4):
            peer = 4 * p + lax.rem(f + m, 4)
            landing = att_recv.at[odd, slot, f]

            @pl.when(peer == f)
            def _():
                pltpu.make_async_copy(
                    att_send.at[f], landing, att_rsem.at[odd, slot]
                ).start()

            for k in range(NY):
                chip = lax.rem(z + odd * k, NY) * NY + lax.rem(y + (1 - odd) * k, NY)
                copy = remote(
                    att_send.at[peer], landing, att_ssem.at[k], att_rsem.at[odd, slot],
                    (chip, peer),
                )
                if k == 0:
                    pl.when(peer != f)(copy.start)
                else:
                    copy.start()

    for p in range(PAIRS):
        attend(p, *score(p))
        send_attended(p)

    for i in range(2 * KV_HEADS):
        ne[0:1, i * HD : (i + 1) * HD] = fresh_rows[i][0:1]
        ne[1:2, i * HD : (i + 1) * HD] = fresh_rows[i][8:9]
    results[PR:, :, :] = ne[0:2, :].reshape(1, STEPS, ne.shape[1]).astype(BF16)

    line_copies = [[], []]
    for part_id in range(2):
        for side in range(2):
            whole = att_recv.at[side, part_id]
            pltpu.make_async_copy(whole, whole, att_rsem.at[side, part_id]).wait()
            pos = (z, y)[side]
            att_f32[...] = att_recv[side, part_id].astype(F32).reshape(NF * PR, HD)
            for j in range(8):
                rows_all[part_id, side, pos, :, j * HD : (j + 1) * HD] = att_f32[
                    pl.ds(j, PR, stride=8), :
                ].astype(BF16)
            mine_rows = rows_all.at[part_id, side, pos]
            for k in range(1, NY):
                q = lax.rem(pos + k, NY)
                device = (q * NY + y, f) if side == 0 else (z * NY + q, f)
                copy = remote(
                    mine_rows, mine_rows,
                    line_ssem.at[part_id, side, k - 1], line_rsem.at[part_id, side, k - 1],
                    device,
                )
                copy.start()
                line_copies[part_id].append(copy)
    wout_load.wait()
    for copy in msg_copies:
        copy.wait_send()
    for k in range(NY):
        sent = att_send.at[pl.ds(0, NF - 1)] if k == 0 else att_send
        pltpu.make_async_copy(sent, sent, att_ssem.at[k]).wait()

    def out_rows(index):
        return pl.ds(pl.multiple_of(index * OWN, OWN), OWN)

    fin_copies = []
    for part_id in range(2):
        for copy in line_copies[part_id]:
            copy.wait_recv()
        product = jnp.dot(
            rows_all[part_id].reshape(NH * PR // 2, wout_v.shape[0]),
            wout_v[...],
            preferred_element_type=F32,
        )
        for side in range(2):
            for q in range(NY):
                far = 2 * ((part_id + q // 2) % 2) + (q + side) % 2
                home = q * NY + far if side == 0 else far * NY + q
                first = (side * NY + q) * PR
                opart[home * PR : (home + 1) * PR, :] = product[first : first + PR]
        for k in (2, 1, 3, 0):
            x = lax.rem(cx + k, NX)
            peer = 2 * x + lax.rem(part_id + lax.div(x, 2), 2)
            hop = lax.rem(peer - f + NF, NF)
            there = lax.rem(hop + NF - 1, NF)
            fin_send[part_id, k] = opart[out_rows(peer), :].astype(BF16)
            copy = remote(
                fin_send.at[part_id, k], fin_recv.at[there],
                fin_ssem.at[part_id, k], fin_rsem.at[there], (h, peer),
            )
            fin_copies.append((k, hop, copy))
            if k == 0:
                pl.when(hop != 0)(copy.start)
            else:
                copy.start()
    for copies in line_copies:
        for copy in copies:
            copy.wait_send()
    result = opart[out_rows(f), :]
    for k in range(1, NF):
        pltpu.make_async_copy(
            fin_recv.at[k - 1], fin_recv.at[k - 1], fin_rsem.at[k - 1]
        ).wait()
        result = result + fin_recv[k - 1].astype(F32)
    results[:PR, :, :] = result.reshape(PR, STEPS, result.shape[1]).astype(BF16)
    for k, hop, copy in fin_copies:
        if k == 0:
            pl.when(hop != 0)(copy.wait_send)
        else:
            copy.wait_send()


def hand_out(results, out, entries, sem):
    rows = out.shape[0]
    copies = [
        pltpu.make_async_copy(results.at[pl.ds(0, rows)], out, sem.at[0]),
        pltpu.make_async_copy(results.at[pl.ds(rows, 1)], entries, sem.at[1]),
    ]
    for copy in copies:
        copy.start()
    for copy in copies:
        copy.wait()


def body(tokens, norm_gain, query_weight, w_keyval, w_out, cache_keys, cache_values, lengths):
    width = tokens.shape[2]
    lmax = cache_keys.shape[1]
    qcols = query_weight.shape[1]
    kvcols = w_keyval.shape[1]
    halves = np.arange(HD // 2, dtype=np.float64) * (2.0 / HD)
    freq = (ROPE_BASE ** (-halves)).astype(np.float32)
    freq = jnp.asarray(np.tile(np.concatenate([freq, freq])[None, :], (PR, 1)))
    any_spec = pl.BlockSpec(memory_space=pl.ANY)
    hbm_spec = pl.BlockSpec(memory_space=pltpu.HBM)
    vmem_spec = pl.BlockSpec(memory_space=pltpu.VMEM)
    dma = pltpu.SemaphoreType.DMA
    rows = NH * PR
    results = pl.pallas_call(
        kernel,
        out_shape=pltpu.VMEM((PR + 1, STEPS, width), BF16),
        in_specs=[hbm_spec] * 9,
        out_specs=vmem_spec,
        scratch_shapes=[
            pltpu.SMEM(lengths.shape, jnp.int32),
            pltpu.VMEM(tokens.shape, BF16),
            pltpu.VMEM((OWN, width), BF16),
            pltpu.VMEM((PR, HD), F32),
            pltpu.VMEM((width,), BF16),
            pltpu.VMEM((width, qcols), BF16),
            pltpu.VMEM((width, kvcols), BF16),
            pltpu.VMEM((qcols, width), BF16),
            pltpu.VMEM((lmax, KV_HEADS * HD), BF16),
            pltpu.VMEM((KV_HEADS * HD, lmax), BF16),
            pltpu.VMEM((lmax, KV_HEADS * HD), BF16),
            pltpu.VMEM((rows, width), BF16),
            pltpu.VMEM((rows // 2, width), BF16),
            pltpu.VMEM((8, HD), F32),
            pltpu.VMEM((NH - 1, 8, HD), F32),
            pltpu.VMEM((NF, 8, HD), F32),
            pltpu.VMEM((NY, NY, PR, qcols + kvcols), F32),
            pltpu.VMEM((2, NY, PR // 2, qcols + kvcols), F32),
            pltpu.VMEM((2, NY, PR // 2, qcols + kvcols), F32),
            pltpu.VMEM((2, NY, PR // 2, qcols + kvcols), F32),
            pltpu.VMEM((2, NY, PR // 2, qcols + kvcols), F32),
            pltpu.VMEM((2, NY - 1, PR // 2, qcols + kvcols), F32),
            pltpu.VMEM((NF * PR, HD), F32),
            pltpu.VMEM((NF, 2 * PR, HD), BF16),
            pltpu.VMEM((NF, 2 * PR, HD), BF16),
            pltpu.VMEM((HD, KV_HEADS * HD), BF16),
            pltpu.VMEM((HD, KV_HEADS * HD), BF16),
            pltpu.VMEM((8, 2 * KV_HEADS * HD), F32),
            pltpu.VMEM((KV_HEADS * OWN, lmax), F32),
            pltpu.VMEM((NF, PR, HD), BF16),
            pltpu.VMEM((2, 2, NF, PR, HD), BF16),
            pltpu.VMEM((NF * PR, HD), F32),
            pltpu.VMEM((2, 2, NY, PR, qcols), BF16),
            pltpu.VMEM((rows, width), F32),
            pltpu.VMEM((2, NX, OWN, width), BF16),
            pltpu.VMEM((NF - 1, OWN, width), BF16),
            dma((8,)),
            dma((CACHE_COPIES,)),
            dma((CACHE_COPIES,)),
            dma((NX - 1,)), dma((NX - 1,)),
            dma((NX,)), dma((NX,)),
            dma((NH - 1,)), dma((NH - 1,)),
            dma((NF - 1,)), dma((NF - 1,)),
            dma((2, 2, 6)), dma((2, 2, 6)),
            dma((2, 2, NY - 1)), dma((2, 2, NY - 1)),
            dma((NF - 1,)), dma((NF - 1,)),
            dma((NY,)), dma((2, 2)),
            dma((2, 2, NY - 1)), dma((2, 2, NY - 1)),
            dma((2, NX)), dma((NF - 1,)),
        ],
        compiler_params=pltpu.CompilerParams(
            collective_id=0, has_side_effects=True, vmem_limit_bytes=48 * 2**20
        ),
        name="decode_block",
    )(
        *[
            pltpu.with_memory_space_constraint(array, pltpu.HBM)
            for array in (
                lengths, freq, tokens, norm_gain, query_weight, w_keyval, w_out,
                cache_keys, cache_values,
            )
        ],
    )
    return pl.pallas_call(
        hand_out,
        out_shape=(
            jax.ShapeDtypeStruct(tokens.shape, BF16),
            jax.ShapeDtypeStruct((1, STEPS, 2 * KV_HEADS * HD), BF16),
        ),
        in_specs=[vmem_spec],
        out_specs=(any_spec, any_spec),
        scratch_shapes=[dma((2,))],
        name="hand_out",
    )(pltpu.with_memory_space_constraint(results, pltpu.VMEM))


def solution(mesh):
    in_specs = (
        P("ffn", None, "hid"),
        P("hid"),
        P("hid", "ffn"),
        P("hid", "ffn"),
        P("ffn", "hid"),
        P(("hid", "ffn"), None, None),
        P(("hid", "ffn"), None, None),
        P(),
    )
    out_specs = (P("ffn", None, "hid"), P(("hid", "ffn"), None, None))
    return jax.shard_map(body, mesh=mesh, in_specs=in_specs, out_specs=out_specs, check_vma=False)
```
